32 devices in a mesh: parts: 2 (over x), center: 8 (over z, y), sub: 2 (over core).
Axes of the slice: x: 2, y: 2, z: 4, core: 2. Of those that a mesh axis runs over, the one named last changes fastest.
Arguments:
- centers: bfloat16 [24576, 3072], P(('parts', 'center', 'sub')), parts along dimension 0
- weights: float32 [24576, 1000], P(('parts', 'center', 'sub')), parts along dimension 0, may hold values from -0.2 to 0.2
- targets: float32 [512, 1000], P('parts'), parts along dimension 0, may hold values from -6 to 6
- batch_index: int32 [512], P('parts'), parts along dimension 0, may hold values from 0 to 12287
- nys_index: int32 [10240], P(('parts', 'center', 'sub')), parts along dimension 0, may hold values from 0 to 12287, as said below
- eigvec: float32 [10240, 160], P(('parts', 'center', 'sub')), parts along dimension 0, may hold values from -0.078125 to 0.078125
- eigval: float32 [320], P('parts'), parts along dimension 0, may hold values from 0.05 to 1
Outputs:
- new_weights: float32 [24576, 1000], P(('parts', 'center', 'sub')), parts along dimension 0
- predictions: float32 [512, 1000], P('parts'), parts along dimension 0
The draws below stay inside these ranges and needn't reach their ends.
There are 2 independent parts, one for each index of `parts`. The reference program is written for one: setup_inputs(seed, part) draws one part's arguments, and reference() takes and returns one part's arrays. A program takes and returns all parts, laid end to end along the dimension named above; each array names one. Nothing has to cross between parts.
Inputs may be any that keep to these rules, and one draw needn't show every extreme that they name: `nys_index`: each Nystrom point of the k-th block of 320 entries lies in the k-th block of 768 centers.
All inputs are finite; a program needn't handle non-finite values.
Results may differ from the reference program's by a relative error of at most 0.0003.
Values may be sent and summed in bfloat16 or wider, within the bound.
No kernel may reach another device: no remote copies, remote signals or barrier semaphores. Data moves between devices by JAX's collectives and lax.ppermute only.
A program may use at most 64 MiB of HBM per device.

```python
import math
import jax
import jax.numpy as jnp
from jax import lax

D = 3072
C = 1000
Q = 160
M = 256
CEN_DEV = 768
NYS_DEV = 320
CENTERS = 12288
NYS = 5120


def draw_centers(key, part):
    key = jax.random.fold_in(key, 11)
    first, second = jax.random.split(key)
    scale = jnp.exp(jax.random.uniform(second, (CENTERS, 1), jnp.float32, math.log(0.3), math.log(3.0)))
    base = jax.random.normal(first, (CENTERS, D), jnp.float32)
    return (base * scale).astype(jnp.bfloat16)


def draw_nys_index(key, part):
    key = jax.random.fold_in(key, 12)
    offsets = jax.random.randint(key, (NYS,), 0, CEN_DEV)
    owner = jnp.arange(NYS, dtype=jnp.int32) // NYS_DEV
    return (owner * CEN_DEV + offsets).astype(jnp.int32)


def place_ends(drawn, rng, smallest, largest):
    longest = drawn.shape.index(max(drawn.shape))
    spots = []
    for shift in (0, 1):
        where = [jax.random.randint(jax.random.fold_in(rng, axis), (), 0, length) for axis, length in enumerate(drawn.shape)]
        where[longest] = (where[longest] + shift) % drawn.shape[longest]
        spots.append(tuple(where))
    return drawn.at[spots[0]].set(smallest).at[spots[1]].set(largest)


def block_scale(key, shape, cuts, low, largest):
    def one(axis_at, blocks):
        draws = jax.random.uniform(jax.random.fold_in(jax.random.fold_in(key, 6), axis_at), (blocks,), jnp.float32, low / len(cuts), largest / len(cuts))
        return jnp.repeat(jnp.exp(draws), shape[axis_at] // blocks).reshape((-1,) + (1,) * (len(shape) - axis_at - 1))

    level = one(*cuts[0])
    for cut in cuts[1:]:
        level = level * one(*cut)
    return level


def noise(rng, dims, deviation, bound, cuts=(), kind=jnp.bfloat16):
    factor_of = block_scale(rng, dims, cuts, -0.22, 0.18) if cuts else 1.0
    array = jax.random.normal(rng, dims, jnp.float32) * deviation * factor_of
    return jnp.minimum(jnp.maximum(array, -bound), bound).astype(kind)


def setup_inputs(seed: int = 0, part: int = 0) -> dict:
    arg_keys = jax.random.split(jax.random.key(seed), 8)
    own_keys = jax.random.split(jax.random.fold_in(arg_keys[7], part), 8)
    centers = draw_centers(jax.random.fold_in(jax.random.fold_in(arg_keys[7], part), 71), part)
    weights = noise(own_keys[1], (CENTERS, C), 0.03, 0.2, ((0, 16),), jnp.float32)
    targets = noise(own_keys[2], (M, C), 1.0, 6.0, (), jnp.float32)
    batch_index = place_ends(jax.random.randint(own_keys[3], (M,), 0, CENTERS), jax.random.fold_in(own_keys[3], 1), 0, CENTERS - 1).astype(jnp.int32)
    nys_index = draw_nys_index(jax.random.fold_in(jax.random.fold_in(arg_keys[7], part), 71), part)
    eigvec = noise(own_keys[5], (NYS, Q), NYS ** -0.5, 0.078125, ((0, 16),), jnp.float32)
    eigval = jnp.clip(jnp.exp(jax.random.uniform(own_keys[6], (Q,), jnp.float32, math.log(0.05), math.log(1.0))), 0.05, 1.0)
    return {"centers": centers, "weights": weights, "targets": targets, "batch_index": batch_index, "nys_index": nys_index, "eigvec": eigvec, "eigval": eigval}


def kernel(left, right):
    cross = jnp.dot(left, right.T, preferred_element_type=jnp.float32)
    lf = left.astype(jnp.float32)
    rf = right.astype(jnp.float32)
    lnorm = lax.optimization_barrier(jnp.sum(lf * lf, axis=1))
    rnorm = lax.optimization_barrier(jnp.sum(rf * rf, axis=1))
    square = jnp.maximum(lnorm[:, None] + rnorm[None, :] - 2.0 * cross, 0.0)
    return jnp.exp(-jnp.sqrt(square) / jnp.sqrt(jnp.float32(D)))

def reference(centers, weights, targets, batch_index, nys_index, eigvec, eigval):
    batch = centers[batch_index]
    nystrom = centers[nys_index]
    kb = kernel(batch, centers)
    ks = kernel(nystrom, batch)
    predictions = jnp.dot(kb, weights, precision=lax.Precision.HIGHEST)
    residual = predictions - targets
    mixed = jnp.dot(eigvec.T, ks, precision=lax.Precision.HIGHEST)
    proj = jnp.dot(mixed, residual, precision=lax.Precision.HIGHEST)
    lowest = jnp.min(eigval)
    scaled = (1.0 - lowest / eigval) / eigval
    correct = jnp.dot(eigvec, scaled[:, None] * proj, precision=lax.Precision.HIGHEST)
    new_weights = weights.at[batch_index].add(-0.25 * residual)
    new_weights = new_weights.at[nys_index].add(0.25 * correct)
    return (new_weights, predictions)
```

```python
import functools
import math

import jax
import jax.numpy as jnp
from jax import lax
from jax.experimental import pallas as pl
from jax.experimental.pallas import tpu as pltpu
from jax.sharding import PartitionSpec as P

F32 = jnp.float32
BF16 = jnp.bfloat16
AXES = ("center", "sub")
LEVELS = 4
CHUNKS = 1 << LEVELS
LANE = 128
NT = (((1,), (1,)), ((), ()))
NN = (((1,), (0,)), ((), ()))
TN = (((0,), (0,)), ((), ()))
VMEM_LIMIT = 56 * 1024 * 1024


def dot(a, b, dims):
    return lax.dot_general(a, b, dims, preferred_element_type=F32)


def position():
    return lax.axis_index("center") * 2 + lax.axis_index("sub")


def reversed_bits(value, bits):
    out = 0
    for bit in range(bits):
        out = out + ((value >> bit) & 1) * (1 << (bits - 1 - bit))
    return out


def column_of(row, width):
    return jnp.broadcast_to(row.astype(F32), (width, row.shape[1])).T


def two(x):
    high = x.astype(BF16)
    return high, (x - high.astype(F32)).astype(BF16)


def pick_rows(index_ref, columns, start, dtype, scale):
    column = column_of(index_ref[...] - start, LANE)
    lanes = lax.broadcasted_iota(jnp.int32, (1, LANE), 1).astype(F32)
    blocks = [
        jnp.where(column == lanes + float(LANE * k), scale, 0.0).astype(dtype)
        for k in range(columns // LANE)
    ]
    return jnp.concatenate(blocks, axis=1)


def pick_body(index_ref, centers_ref, keep_ref, send_ref, pick_ref):
    me = position()
    turn = reversed_bits(me, LEVELS)
    rows = index_ref.shape[1]
    size = rows // CHUNKS
    count = centers_ref.shape[0]

    @pl.when(pl.program_id(0) == 0)
    def _():
        pick = pick_rows(index_ref, count, me * count, F32, 1.0)
        for chunk in range(CHUNKS):
            to = pl.multiple_of((chunk ^ turn) * size, size)
            pick_ref[pl.ds(to, size), :] = pick[chunk * size : (chunk + 1) * size].astype(BF16)

    found = dot(pick_ref[...], centers_ref[...], NN).astype(BF16)
    keep_ref[...] = found[: rows // 2]
    send_ref[...] = found[rows // 2 :]


def pick_batch(batch_index, centers):
    rows = batch_index.shape[1]
    count, depth = centers.shape
    block = 1024
    half = jax.ShapeDtypeStruct((rows // 2, depth), BF16)
    return pl.pallas_call(
        pick_body,
        grid=(depth // block,),
        in_specs=[
            pl.BlockSpec((1, rows), lambda i: (0, 0)),
            pl.BlockSpec((count, block), lambda i: (0, i)),
        ],
        out_specs=[pl.BlockSpec((rows // 2, block), lambda i: (0, i))] * 2,
        out_shape=[half, half],
        scratch_shapes=[pltpu.VMEM((rows, count), BF16)],
        compiler_params=pltpu.CompilerParams(vmem_limit_bytes=VMEM_LIMIT),
        cost_estimate=pl.CostEstimate(
            flops=2 * rows * count * depth, bytes_accessed=2 * depth * (count + rows), transcendentals=0
        ),
        name="pick_batch",
    )(batch_index, centers)


def prepare_body(classes, index_ref, eigvec_ref, weights_ref, high_ref, low_ref, spread_ref, all_ref):
    me = position()
    turn = reversed_bits(me >> 1, LEVELS - 1)
    rank, points = eigvec_ref.shape
    count = weights_ref.shape[1]
    padded = high_ref.shape[0]
    size = padded // (CHUNKS // 2)
    local = index_ref[...] - me * count
    slots = lax.broadcasted_iota(jnp.int32, (count, points), 0)
    pick = jnp.where(slots == local, 1.0, 0.0).astype(BF16)
    vec = eigvec_ref[...]
    high = vec.astype(BF16)
    rest = vec - high.astype(F32)
    mid = rest.astype(BF16)
    low = (rest - mid.astype(F32)).astype(BF16)
    spread = dot(high, pick, NT) + dot(mid, pick, NT) + dot(low, pick, NT)
    spread_ref[...] = spread
    all_ref[:classes] = weights_ref[...]
    all_ref[classes : classes + rank] = spread
    all_ref[classes + rank :] = jnp.zeros((padded - classes - rank, count), F32)
    for chunk in range(CHUNKS // 2):
        to = pl.multiple_of((chunk ^ turn) * size, 8)
        high, low = two(all_ref[pl.ds(to, size), :])
        high_ref[chunk * size : (chunk + 1) * size] = high
        low_ref[chunk * size : (chunk + 1) * size] = low


def prepare(nys_index, eigvec, weights, padded):
    classes, count = weights.shape
    rank, points = eigvec.shape
    return pl.pallas_call(
        functools.partial(prepare_body, classes),
        out_shape=[
            jax.ShapeDtypeStruct((padded, count), BF16),
            jax.ShapeDtypeStruct((padded, count), BF16),
            jax.ShapeDtypeStruct((rank, count), F32),
        ],
        scratch_shapes=[pltpu.VMEM((padded, count), F32)],
        compiler_params=pltpu.CompilerParams(vmem_limit_bytes=VMEM_LIMIT),
        cost_estimate=pl.CostEstimate(
            flops=6 * rank * points * count, bytes_accessed=8 * padded * count, transcendentals=0
        ),
        name="prepare",
    )(nys_index, eigvec, weights)


def predict_body(mine_ref, other_ref, centers_ref, high_ref, low_ref, keep_ref, send_ref, batch_ref, norm_ref, total_ref):
    me = position()
    turn = reversed_bits(me, LEVELS)
    rows, depth = batch_ref.shape
    half = rows // 2
    size = rows // CHUNKS
    step = pl.program_id(0)

    @pl.when(step == 0)
    def _():
        for chunk in range(CHUNKS):
            ref = mine_ref if chunk < CHUNKS // 2 else other_ref
            at = chunk % (CHUNKS // 2) * size
            to = pl.multiple_of((chunk ^ turn) * size, size)
            batch_ref[pl.ds(to, size), :] = ref[at : at + size, :]
        batch = batch_ref[...].astype(F32)
        norm = jnp.sum(batch * batch, axis=1, keepdims=True)
        norm_ref[...] = jnp.broadcast_to(norm, (rows, LANE)).T[:8]
        total_ref[...] = jnp.zeros_like(total_ref)

    block = centers_ref[...]
    cross = dot(block, batch_ref[...], NT)
    wide = block.astype(F32)
    norm = jnp.sum(wide * wide, axis=1, keepdims=True)
    square = jnp.maximum(norm + norm_ref[0:1, :] - 2.0 * cross, 0.0)
    value = jnp.exp(jnp.sqrt(square) * (-1.0 / math.sqrt(depth)))
    value_high, value_low = two(value)
    high = high_ref[...]
    total_ref[...] += dot(high, value_high, NN) + (dot(high, value_low, NN) + dot(low_ref[...], value_high, NN))

    @pl.when(step == pl.num_programs(0) - 1)
    def _():
        first = total_ref[:, :half]
        second = total_ref[:, half:]
        lower = (me & 1) == 0
        keep_ref[...] = jnp.where(lower, first, second)
        send_ref[...] = jnp.where(lower, second, first)


def predict(mine, other, centers, high, low):
    half, depth = mine.shape
    rows = 2 * half
    count = centers.shape[0]
    padded = high.shape[0]
    block = 256
    out = jax.ShapeDtypeStruct((padded, half), F32)
    return pl.pallas_call(
        predict_body,
        grid=(count // block,),
        in_specs=[
            pl.BlockSpec((half, depth), lambda i: (0, 0)),
            pl.BlockSpec((half, depth), lambda i: (0, 0)),
            pl.BlockSpec((block, depth), lambda i: (i, 0)),
            pl.BlockSpec((padded, block), lambda i: (0, i)),
            pl.BlockSpec((padded, block), lambda i: (0, i)),
        ],
        out_specs=[pl.BlockSpec((padded, half), lambda i: (0, 0))] * 2,
        out_shape=[out, out],
        scratch_shapes=[
            pltpu.VMEM((rows, depth), BF16),
            pltpu.VMEM((8, rows), F32),
            pltpu.VMEM((padded, rows), F32),
        ],
        compiler_params=pltpu.CompilerParams(vmem_limit_bytes=VMEM_LIMIT),
        cost_estimate=pl.CostEstimate(
            flops=2 * rows * count * (depth + 3 * padded),
            bytes_accessed=2 * depth * (count + rows) + 4 * padded * (count + rows),
            transcendentals=2 * rows * count,
        ),
        name="predict",
    )(mine, other, centers, high, low)


def update_body(
    classes, mine_ref, other_ref, targets_ref, index_ref, eigval_ref, spread_ref, weights_ref,
    new_ref, out_ref, total_ref, high_ref, low_ref,
):
    me = position()
    step = pl.program_id(0)
    block = new_ref.shape[0]
    rank, count = spread_ref.shape
    half = mine_ref.shape[1]

    @pl.when(step == 0)
    def _():
        turn = reversed_bits(me >> 1, LEVELS - 1)
        size = mine_ref.shape[0] // (CHUNKS // 2)
        lower = (me & 1) == 0
        for chunk in range(CHUNKS // 2):
            to = pl.multiple_of((chunk ^ turn) * size, 8)
            mine = mine_ref[chunk * size : (chunk + 1) * size]
            other = other_ref[chunk * size : (chunk + 1) * size]
            total_ref[pl.ds(to, size), :half] = jnp.where(lower, mine, other)
            total_ref[pl.ds(to, size), half:] = jnp.where(lower, other, mine)
        value = eigval_ref[...]
        lowest = jnp.min(value, axis=1, keepdims=True)
        scaled = (1.0 - lowest / value) / value
        mixed_high, mixed_low = two(total_ref[classes : classes + rank].T * (0.25 * scaled))
        spread_high, spread_low = two(spread_ref[...])
        turned = dot(mixed_high, spread_high, NN) + (
            dot(mixed_high, spread_low, NN) + dot(mixed_low, spread_high, NN)
        )
        high, low = two(turned - pick_rows(index_ref, count, me * count, F32, 0.25))
        high_ref[...] = high
        low_ref[...] = low

    at = pl.multiple_of(step * block, 8)
    predictions = total_ref[pl.ds(at, block), :]
    out_ref[...] = predictions
    high, low = two(predictions - targets_ref[...])
    new_ref[...] = weights_ref[...] + (
        dot(high, high_ref[...], NN) + (dot(high, low_ref[...], NN) + dot(low, high_ref[...], NN))
    )


def update(mine, other, targets, batch_index, eigval, spread, weights):
    classes, count = weights.shape
    padded, half = mine.shape
    rows = 2 * half
    rank = spread.shape[0]
    block = 200
    whole = lambda shape: pl.BlockSpec(shape, lambda i: (0, 0))
    return pl.pallas_call(
        functools.partial(update_body, classes),
        grid=(classes // block,),
        in_specs=[
            whole((padded, half)),
            whole((padded, half)),
            pl.BlockSpec((block, rows), lambda i: (i, 0)),
            whole((1, rows)),
            whole((1, rank)),
            whole((rank, count)),
            pl.BlockSpec((block, count), lambda i: (i, 0)),
        ],
        out_specs=[
            pl.BlockSpec((block, count), lambda i: (i, 0)),
            pl.BlockSpec((block, rows), lambda i: (i, 0)),
        ],
        out_shape=[
            jax.ShapeDtypeStruct((classes, count), F32),
            jax.ShapeDtypeStruct((classes, rows), F32),
        ],
        scratch_shapes=[
            pltpu.VMEM((padded, rows), F32),
            pltpu.VMEM((rows, count), BF16),
            pltpu.VMEM((rows, count), BF16),
        ],
        compiler_params=pltpu.CompilerParams(vmem_limit_bytes=VMEM_LIMIT),
        cost_estimate=pl.CostEstimate(
            flops=6 * rows * count * (classes + rank),
            bytes_accessed=8 * classes * (count + rows),
            transcendentals=0,
        ),
        name="update",
    )(mine, other, targets, batch_index, eigval, spread, weights)


def swap(x, mask, devices):
    return lax.ppermute(x, AXES, [(i, i ^ mask) for i in range(devices)])


def total_of(keep, send, devices):
    for level in range(LEVELS):
        keep = keep + swap(send, 1 << level, devices)
        if level < LEVELS - 1:
            half = keep.shape[0] // 2
            keep, send = keep[:half], keep[half:]
    for level in range(LEVELS, int(math.log2(devices))):
        keep = keep + swap(keep, 1 << level, devices)
    for level in reversed(range(1, LEVELS)):
        keep = jnp.concatenate([keep, swap(keep, 1 << level, devices)])
    return keep, swap(keep, 1, devices)


def on_device(devices, centers, weights, targets, batch_index, nys_index, eigvec, eigval):
    rows = batch_index.shape[0]
    classes = weights.shape[1]
    rank = eigvec.shape[1]
    unit = 8 * CHUNKS // 2
    padded = -(-(classes + rank) // unit) * unit
    batch_index = batch_index.reshape(1, rows)
    mine, other = total_of(*pick_batch(batch_index, centers), devices)
    high, low, spread = prepare(nys_index.reshape(1, -1), eigvec.T, weights.T, padded)
    mine, other = total_of(*predict(mine, other, centers, high, low), devices)
    new_weights, predictions = update(
        mine, other, targets.T, batch_index, eigval.reshape(1, rank), spread, weights.T
    )
    return new_weights.T, predictions.T


def solution(mesh):
    devices = mesh.shape["center"] * mesh.shape["sub"]
    return jax.shard_map(
        functools.partial(on_device, devices),
        mesh=mesh,
        in_specs=(
            P(("parts", "center", "sub"), None),
            P(("parts", "center", "sub"), None),
            P("parts", None),
            P("parts"),
            P(("parts", "center", "sub")),
            P(("parts", "center", "sub"), None),
            P("parts"),
        ),
        out_specs=(P(("parts", "center", "sub"), None), P("parts", None)),
        check_vma=False,
    )
```

```python
import functools
import math

import jax
import jax.numpy as jnp
from jax import lax
from jax.experimental import pallas as pl
from jax.experimental.pallas import tpu as pltpu
from jax.sharding import PartitionSpec as P

F32 = jnp.float32
BF16 = jnp.bfloat16
LANE = 128
NT = (((1,), (1,)), ((), ()))
NN = (((1,), (0,)), ((), ()))
TN = (((0,), (0,)), ((), ()))
VMEM_LIMIT = 56 * 1024 * 1024


def dot(a, b, dims):
    return lax.dot_general(a, b, dims, preferred_element_type=F32)


def position():
    return lax.axis_index("center") * 2 + lax.axis_index("sub")


def column_of(row, width):
    return jnp.broadcast_to(row.astype(F32), (width, row.shape[1])).T


def two(x):
    high = x.astype(BF16)
    return high, (x - high.astype(F32)).astype(BF16)


def pick_rows(index_ref, columns, start, dtype, scale):
    column = column_of(index_ref[...] - start, LANE)
    lanes = lax.broadcasted_iota(jnp.int32, (1, LANE), 1).astype(F32)
    blocks = [
        jnp.where(column == lanes + float(LANE * k), scale, 0.0).astype(dtype)
        for k in range(columns // LANE)
    ]
    return jnp.concatenate(blocks, axis=1)


def pick_body(index_ref, centers_ref, keep_ref, send_ref, pick_ref):
    me = position()
    rows = index_ref.shape[1]
    half = rows // 2
    count = centers_ref.shape[0]

    @pl.when(pl.program_id(0) == 0)
    def _():
        pick = pick_rows(index_ref, count, me * count, F32, 1.0)
        mine = pl.multiple_of((me & 1) * half, half)
        pick_ref[pl.ds(mine, half), :] = pick[:half].astype(BF16)
        pick_ref[pl.ds(half - mine, half), :] = pick[half:].astype(BF16)

    found = dot(pick_ref[...], centers_ref[...], NN).astype(BF16)
    keep_ref[...] = found[:half]
    send_ref[...] = found[half:]


def pick_batch(batch_index, centers):
    rows = batch_index.shape[1]
    count, depth = centers.shape
    block = 1024
    half = jax.ShapeDtypeStruct((rows // 2, depth), BF16)
    return pl.pallas_call(
        pick_body,
        grid=(depth // block,),
        in_specs=[
            pl.BlockSpec((1, rows), lambda i: (0, 0)),
            pl.BlockSpec((count, block), lambda i: (0, i)),
        ],
        out_specs=[pl.BlockSpec((rows // 2, block), lambda i: (0, i))] * 2,
        out_shape=[half, half],
        scratch_shapes=[pltpu.VMEM((rows, count), BF16)],
        compiler_params=pltpu.CompilerParams(vmem_limit_bytes=VMEM_LIMIT),
        cost_estimate=pl.CostEstimate(
            flops=2 * rows * count * depth, bytes_accessed=2 * depth * (count + rows), transcendentals=0
        ),
        name="pick_batch",
    )(batch_index, centers)


def prepare_body(classes, index_ref, eigvec_ref, weights_ref, high_ref, low_ref, spread_ref):
    me = position()
    rank, points = eigvec_ref.shape
    count = weights_ref.shape[1]
    padded = high_ref.shape[0]
    local = index_ref[...] - me * count
    slots = lax.broadcasted_iota(jnp.int32, (count, points), 0)
    pick = jnp.where(slots == local, 1.0, 0.0).astype(BF16)
    vec = eigvec_ref[...]
    high = vec.astype(BF16)
    rest = vec - high.astype(F32)
    mid = rest.astype(BF16)
    low = (rest - mid.astype(F32)).astype(BF16)
    spread = dot(high, pick, NT) + dot(mid, pick, NT) + dot(low, pick, NT)
    spread_ref[...] = spread
    blank = jnp.zeros((padded - classes - rank, count), F32)
    stacked = jnp.concatenate([weights_ref[...], spread, blank])
    high_ref[...], low_ref[...] = two(stacked)


def prepare(nys_index, eigvec, weights, padded):
    classes, count = weights.shape
    rank, points = eigvec.shape
    return pl.pallas_call(
        functools.partial(prepare_body, classes),
        out_shape=[
            jax.ShapeDtypeStruct((padded, count), BF16),
            jax.ShapeDtypeStruct((padded, count), BF16),
            jax.ShapeDtypeStruct((rank, count), F32),
        ],
        compiler_params=pltpu.CompilerParams(vmem_limit_bytes=VMEM_LIMIT),
        cost_estimate=pl.CostEstimate(
            flops=6 * rank * points * count, bytes_accessed=8 * padded * count, transcendentals=0
        ),
        name="prepare",
    )(nys_index, eigvec, weights)


def predict_body(mine_ref, other_ref, centers_ref, high_ref, low_ref, keep_ref, send_ref, batch_ref, norm_ref, total_ref):
    me = position()
    rows, depth = batch_ref.shape
    half = rows // 2
    step = pl.program_id(0)

    @pl.when(step == 0)
    def _():
        at = pl.multiple_of((me & 1) * half, half)
        batch_ref[pl.ds(at, half), :] = mine_ref[...]
        batch_ref[pl.ds(half - at, half), :] = other_ref[...]
        batch = batch_ref[...].astype(F32)
        norm = jnp.sum(batch * batch, axis=1, keepdims=True)
        norm_ref[...] = jnp.broadcast_to(norm, (rows, LANE)).T[:8]
        total_ref[...] = jnp.zeros_like(total_ref)

    block = centers_ref[...]
    cross = dot(block, batch_ref[...], NT)
    wide = block.astype(F32)
    norm = jnp.sum(wide * wide, axis=1, keepdims=True)
    square = jnp.maximum(norm + norm_ref[0:1, :] - 2.0 * cross, 0.0)
    value = jnp.exp(jnp.sqrt(square) * (-1.0 / math.sqrt(depth)))
    value_high, value_low = two(value)
    high = high_ref[...]
    total_ref[...] += dot(high, value_high, NN) + (dot(high, value_low, NN) + dot(low_ref[...], value_high, NN))

    @pl.when(step == pl.num_programs(0) - 1)
    def _():
        first = total_ref[:, :half]
        second = total_ref[:, half:]
        lower = (me & 1) == 0
        keep_ref[...] = jnp.where(lower, first, second)
        send_ref[...] = jnp.where(lower, second, first)


def predict(mine, other, centers, high, low):
    half, depth = mine.shape
    rows = 2 * half
    count = centers.shape[0]
    padded = high.shape[0]
    block = 256
    out = jax.ShapeDtypeStruct((padded, half), F32)
    return pl.pallas_call(
        predict_body,
        grid=(count // block,),
        in_specs=[
            pl.BlockSpec((half, depth), lambda i: (0, 0)),
            pl.BlockSpec((half, depth), lambda i: (0, 0)),
            pl.BlockSpec((block, depth), lambda i: (i, 0)),
            pl.BlockSpec((padded, block), lambda i: (0, i)),
            pl.BlockSpec((padded, block), lambda i: (0, i)),
        ],
        out_specs=[pl.BlockSpec((padded, half), lambda i: (0, 0))] * 2,
        out_shape=[out, out],
        scratch_shapes=[
            pltpu.VMEM((rows, depth), BF16),
            pltpu.VMEM((8, rows), F32),
            pltpu.VMEM((padded, rows), F32),
        ],
        compiler_params=pltpu.CompilerParams(vmem_limit_bytes=VMEM_LIMIT),
        cost_estimate=pl.CostEstimate(
            flops=2 * rows * count * (depth + 3 * padded),
            bytes_accessed=2 * depth * (count + rows) + 4 * padded * (count + rows),
            transcendentals=2 * rows * count,
        ),
        name="predict",
    )(mine, other, centers, high, low)


def update_body(
    classes, mine_ref, other_ref, targets_ref, index_ref, eigval_ref, spread_ref, weights_ref,
    new_ref, out_ref, total_ref, high_ref, low_ref,
):
    me = position()
    step = pl.program_id(0)
    block = new_ref.shape[0]
    rank, count = spread_ref.shape
    half = mine_ref.shape[1]

    @pl.when(step == 0)
    def _():
        lower = (me & 1) == 0
        mine = mine_ref[...]
        other = other_ref[...]
        total_ref[:, :half] = jnp.where(lower, mine, other)
        total_ref[:, half:] = jnp.where(lower, other, mine)
        value = eigval_ref[...]
        lowest = jnp.min(value, axis=1, keepdims=True)
        scaled = (1.0 - lowest / value) / value
        mixed_high, mixed_low = two(total_ref[classes : classes + rank].T * (0.25 * scaled))
        spread_high, spread_low = two(spread_ref[...])
        turned = dot(mixed_high, spread_high, NN) + (
            dot(mixed_high, spread_low, NN) + dot(mixed_low, spread_high, NN)
        )
        high, low = two(turned - pick_rows(index_ref, count, me * count, F32, 0.25))
        high_ref[...] = high
        low_ref[...] = low

    at = pl.multiple_of(step * block, 8)
    predictions = total_ref[pl.ds(at, block), :]
    out_ref[...] = predictions
    high, low = two(predictions - targets_ref[...])
    new_ref[...] = weights_ref[...] + (
        dot(high, high_ref[...], NN) + (dot(high, low_ref[...], NN) + dot(low, high_ref[...], NN))
    )


def update(mine, other, targets, batch_index, eigval, spread, weights):
    classes, count = weights.shape
    padded, half = mine.shape
    rows = 2 * half
    rank = spread.shape[0]
    block = 200
    whole = lambda shape: pl.BlockSpec(shape, lambda i: (0, 0))
    return pl.pallas_call(
        functools.partial(update_body, classes),
        grid=(classes // block,),
        in_specs=[
            whole((padded, half)),
            whole((padded, half)),
            pl.BlockSpec((block, rows), lambda i: (i, 0)),
            whole((1, rows)),
            whole((1, rank)),
            whole((rank, count)),
            pl.BlockSpec((block, count), lambda i: (i, 0)),
        ],
        out_specs=[
            pl.BlockSpec((block, count), lambda i: (i, 0)),
            pl.BlockSpec((block, rows), lambda i: (i, 0)),
        ],
        out_shape=[
            jax.ShapeDtypeStruct((classes, count), F32),
            jax.ShapeDtypeStruct((classes, rows), F32),
        ],
        scratch_shapes=[
            pltpu.VMEM((padded, rows), F32),
            pltpu.VMEM((rows, count), BF16),
            pltpu.VMEM((rows, count), BF16),
        ],
        compiler_params=pltpu.CompilerParams(vmem_limit_bytes=VMEM_LIMIT),
        cost_estimate=pl.CostEstimate(
            flops=6 * rows * count * (classes + rank),
            bytes_accessed=8 * classes * (count + rows),
            transcendentals=0,
        ),
        name="update",
    )(mine, other, targets, batch_index, eigval, spread, weights)


def swap(x):
    return lax.ppermute(x, "sub", [(0, 1), (1, 0)])


def shuffle(x):
    return lax.all_to_all(x, "center", 0, 0, tiled=True)


def total_of(keep, send, chips):
    rows, width = keep.shape
    parts = shuffle(keep + swap(send)).reshape(chips, rows // chips, width)
    part = jnp.sum(parts.astype(F32), axis=0).astype(keep.dtype)
    whole = shuffle(jnp.broadcast_to(part, parts.shape).reshape(rows, width))
    return whole, swap(whole)


def on_device(chips, centers, weights, targets, batch_index, nys_index, eigvec, eigval):
    rows = batch_index.shape[0]
    classes = weights.shape[1]
    rank = eigvec.shape[1]
    unit = 8 * chips
    padded = -(-(classes + rank) // unit) * unit
    batch_index = batch_index.reshape(1, rows)
    mine, other = total_of(*pick_batch(batch_index, centers), chips)
    high, low, spread = prepare(nys_index.reshape(1, -1), eigvec.T, weights.T, padded)
    mine, other = total_of(*predict(mine, other, centers, high, low), chips)
    new_weights, predictions = update(
        mine, other, targets.T, batch_index, eigval.reshape(1, rank), spread, weights.T
    )
    return new_weights.T, predictions.T


def solution(mesh):
    return jax.shard_map(
        functools.partial(on_device, mesh.shape["center"]),
        mesh=mesh,
        in_specs=(
            P(("parts", "center", "sub"), None),
            P(("parts", "center", "sub"), None),
            P("parts", None),
            P("parts"),
            P(("parts", "center", "sub")),
            P(("parts", "center", "sub"), None),
            P("parts"),
        ),
        out_specs=(P(("parts", "center", "sub"), None), P("parts", None)),
        check_vma=False,
    )
```

```python
import functools
import math

import jax
import jax.numpy as jnp
from jax import lax
from jax.experimental import pallas as pl
from jax.experimental.pallas import tpu as pltpu
from jax.sharding import PartitionSpec as P

F32 = jnp.float32
BF16 = jnp.bfloat16
LANE = 128
NT = (((1,), (1,)), ((), ()))
NN = (((1,), (0,)), ((), ()))
TN = (((0,), (0,)), ((), ()))
VMEM_LIMIT = 56 * 1024 * 1024


def dot(a, b, dims):
    return lax.dot_general(a, b, dims, preferred_element_type=F32)


def position():
    return lax.axis_index("center") * 2 + lax.axis_index("sub")


def column_of(row, width):
    return jnp.broadcast_to(row.astype(F32), (width, row.shape[1])).T


def two(x):
    high = x.astype(BF16)
    return high, (x - high.astype(F32)).astype(BF16)


def pick_rows(index_ref, columns, start, dtype, scale):
    column = column_of(index_ref[...] - start, LANE)
    lanes = lax.broadcasted_iota(jnp.int32, (1, LANE), 1).astype(F32)
    blocks = [
        jnp.where(column == lanes + float(LANE * k), scale, 0.0).astype(dtype)
        for k in range(columns // LANE)
    ]
    return jnp.concatenate(blocks, axis=1)


def pick_body(index_ref, centers_ref, keep_ref, send_ref, pick_ref):
    me = position()
    rows = index_ref.shape[1]
    half = rows // 2
    count = centers_ref.shape[0]

    @pl.when(pl.program_id(0) == 0)
    def _():
        pick = pick_rows(index_ref, count, me * count, F32, 1.0)
        mine = pl.multiple_of((me & 1) * half, half)
        pick_ref[pl.ds(mine, half), :] = pick[:half].astype(BF16)
        pick_ref[pl.ds(half - mine, half), :] = pick[half:].astype(BF16)

    found = dot(pick_ref[...], centers_ref[...], NN).astype(BF16)
    keep_ref[...] = found[:half]
    send_ref[...] = found[half:]


def pick_batch(batch_index, centers):
    rows = batch_index.shape[1]
    count, depth = centers.shape
    block = 1024
    half = jax.ShapeDtypeStruct((rows // 2, depth), BF16)
    return pl.pallas_call(
        pick_body,
        grid=(depth // block,),
        in_specs=[
            pl.BlockSpec((1, rows), lambda i: (0, 0)),
            pl.BlockSpec((count, block), lambda i: (0, i)),
        ],
        out_specs=[pl.BlockSpec((rows // 2, block), lambda i: (0, i))] * 2,
        out_shape=[half, half],
        scratch_shapes=[pltpu.VMEM((rows, count), BF16)],
        compiler_params=pltpu.CompilerParams(vmem_limit_bytes=VMEM_LIMIT),
        cost_estimate=pl.CostEstimate(
            flops=2 * rows * count * depth, bytes_accessed=2 * depth * (count + rows), transcendentals=0
        ),
        name="pick_batch",
    )(batch_index, centers)


def prepare_body(classes, index_ref, eigvec_ref, weights_ref, high_ref, low_ref, spread_ref):
    me = position()
    rank, points = eigvec_ref.shape
    count = weights_ref.shape[1]
    padded = high_ref.shape[0]
    local = index_ref[...] - me * count
    slots = lax.broadcasted_iota(jnp.int32, (count, points), 0)
    pick = jnp.where(slots == local, 1.0, 0.0).astype(BF16)
    vec = eigvec_ref[...]
    high = vec.astype(BF16)
    rest = vec - high.astype(F32)
    mid = rest.astype(BF16)
    low = (rest - mid.astype(F32)).astype(BF16)
    spread = dot(high, pick, NT) + dot(mid, pick, NT) + dot(low, pick, NT)
    spread_ref[...] = spread
    blank = jnp.zeros((padded - classes - rank, count), F32)
    stacked = jnp.concatenate([weights_ref[...], spread, blank])
    high_ref[...], low_ref[...] = two(stacked)


def prepare(nys_index, eigvec, weights, padded):
    classes, count = weights.shape
    rank, points = eigvec.shape
    return pl.pallas_call(
        functools.partial(prepare_body, classes),
        out_shape=[
            jax.ShapeDtypeStruct((padded, count), BF16),
            jax.ShapeDtypeStruct((padded, count), BF16),
            jax.ShapeDtypeStruct((rank, count), F32),
        ],
        compiler_params=pltpu.CompilerParams(vmem_limit_bytes=VMEM_LIMIT),
        cost_estimate=pl.CostEstimate(
            flops=6 * rank * points * count, bytes_accessed=8 * padded * count, transcendentals=0
        ),
        name="prepare",
    )(nys_index, eigvec, weights)


def predict_body(mine_ref, other_ref, centers_ref, high_ref, low_ref, keep_ref, send_ref, batch_ref, norm_ref, total_ref):
    me = position()
    rows, depth = batch_ref.shape
    half = rows // 2
    step = pl.program_id(0)

    @pl.when(step == 0)
    def _():
        at = pl.multiple_of((me & 1) * half, half)
        batch_ref[pl.ds(at, half), :] = mine_ref[...]
        batch_ref[pl.ds(half - at, half), :] = other_ref[...]
        batch = batch_ref[...].astype(F32)
        norm = jnp.sum(batch * batch, axis=1, keepdims=True)
        norm_ref[...] = jnp.broadcast_to(norm, (rows, LANE)).T[:8]
        total_ref[...] = jnp.zeros_like(total_ref)

    block = centers_ref[...]
    cross = dot(block, batch_ref[...], NT)
    wide = block.astype(F32)
    norm = jnp.sum(wide * wide, axis=1, keepdims=True)
    square = jnp.maximum(norm + norm_ref[0:1, :] - 2.0 * cross, 0.0)
    value = jnp.exp(jnp.sqrt(square) * (-1.0 / math.sqrt(depth)))
    value_high, value_low = two(value)
    high = high_ref[...]
    total_ref[...] += dot(high, value_high, NN) + (dot(high, value_low, NN) + dot(low_ref[...], value_high, NN))

    @pl.when(step == pl.num_programs(0) - 1)
    def _():
        first = total_ref[:, :half]
        second = total_ref[:, half:]
        lower = (me & 1) == 0
        keep_ref[...] = jnp.where(lower, first, second)
        send_ref[...] = jnp.where(lower, second, first)


def predict(mine, other, centers, high, low):
    half, depth = mine.shape
    rows = 2 * half
    count = centers.shape[0]
    padded = high.shape[0]
    block = 256
    out = jax.ShapeDtypeStruct((padded, half), F32)
    return pl.pallas_call(
        predict_body,
        grid=(count // block,),
        in_specs=[
            pl.BlockSpec((half, depth), lambda i: (0, 0)),
            pl.BlockSpec((half, depth), lambda i: (0, 0)),
            pl.BlockSpec((block, depth), lambda i: (i, 0)),
            pl.BlockSpec((padded, block), lambda i: (0, i)),
            pl.BlockSpec((padded, block), lambda i: (0, i)),
        ],
        out_specs=[pl.BlockSpec((padded, half), lambda i: (0, 0))] * 2,
        out_shape=[out, out],
        scratch_shapes=[
            pltpu.VMEM((rows, depth), BF16),
            pltpu.VMEM((8, rows), F32),
            pltpu.VMEM((padded, rows), F32),
        ],
        compiler_params=pltpu.CompilerParams(vmem_limit_bytes=VMEM_LIMIT),
        cost_estimate=pl.CostEstimate(
            flops=2 * rows * count * (depth + 3 * padded),
            bytes_accessed=2 * depth * (count + rows) + 4 * padded * (count + rows),
            transcendentals=2 * rows * count,
        ),
        name="predict",
    )(mine, other, centers, high, low)


def update_body(
    classes, mine_ref, other_ref, targets_ref, index_ref, eigval_ref, spread_ref, weights_ref,
    new_ref, out_ref, total_ref, high_ref, low_ref,
):
    me = position()
    step = pl.program_id(0)
    block = new_ref.shape[0]
    rank, count = spread_ref.shape
    half = mine_ref.shape[1]

    @pl.when(step == 0)
    def _():
        lower = (me & 1) == 0
        mine = mine_ref[...]
        other = other_ref[...]
        total_ref[:, :half] = jnp.where(lower, mine, other)
        total_ref[:, half:] = jnp.where(lower, other, mine)
        value = eigval_ref[...]
        lowest = jnp.min(value, axis=1, keepdims=True)
        scaled = (1.0 - lowest / value) / value
        mixed_high, mixed_low = two(total_ref[classes : classes + rank].T * (0.25 * scaled))
        spread_high, spread_low = two(spread_ref[...])
        turned = dot(mixed_high, spread_high, NN) + (
            dot(mixed_high, spread_low, NN) + dot(mixed_low, spread_high, NN)
        )
        high, low = two(turned - pick_rows(index_ref, count, me * count, F32, 0.25))
        high_ref[...] = high
        low_ref[...] = low

    at = pl.multiple_of(step * block, 8)
    predictions = total_ref[pl.ds(at, block), :]
    out_ref[...] = predictions
    high, low = two(predictions - targets_ref[...])
    new_ref[...] = weights_ref[...] + (
        dot(high, high_ref[...], NN) + (dot(high, low_ref[...], NN) + dot(low, high_ref[...], NN))
    )


def update(mine, other, targets, batch_index, eigval, spread, weights):
    classes, count = weights.shape
    padded, half = mine.shape
    rows = 2 * half
    rank = spread.shape[0]
    block = 200
    whole = lambda shape: pl.BlockSpec(shape, lambda i: (0, 0))
    return pl.pallas_call(
        functools.partial(update_body, classes),
        grid=(classes // block,),
        in_specs=[
            whole((padded, half)),
            whole((padded, half)),
            pl.BlockSpec((block, rows), lambda i: (i, 0)),
            whole((1, rows)),
            whole((1, rank)),
            whole((rank, count)),
            pl.BlockSpec((block, count), lambda i: (i, 0)),
        ],
        out_specs=[
            pl.BlockSpec((block, count), lambda i: (i, 0)),
            pl.BlockSpec((block, rows), lambda i: (i, 0)),
        ],
        out_shape=[
            jax.ShapeDtypeStruct((classes, count), F32),
            jax.ShapeDtypeStruct((classes, rows), F32),
        ],
        scratch_shapes=[
            pltpu.VMEM((padded, rows), F32),
            pltpu.VMEM((rows, count), BF16),
            pltpu.VMEM((rows, count), BF16),
        ],
        compiler_params=pltpu.CompilerParams(vmem_limit_bytes=VMEM_LIMIT),
        cost_estimate=pl.CostEstimate(
            flops=6 * rows * count * (classes + rank),
            bytes_accessed=8 * classes * (count + rows),
            transcendentals=0,
        ),
        name="update",
    )(mine, other, targets, batch_index, eigval, spread, weights)


def swap(x):
    return lax.ppermute(x, "sub", [(0, 1), (1, 0)])


def shuffle(x):
    return lax.all_to_all(x, "center", 0, 0, tiled=True)


def total_of(keep, send, chips):
    rows, width = keep.shape
    parts = shuffle(keep + swap(send)).reshape(chips, rows // chips, width)
    part = jnp.sum(parts.astype(F32), axis=0).astype(keep.dtype)
    whole = lax.all_gather(part, "center", tiled=True)
    return whole, swap(whole)


def on_device(chips, centers, weights, targets, batch_index, nys_index, eigvec, eigval):
    rows = batch_index.shape[0]
    classes = weights.shape[1]
    rank = eigvec.shape[1]
    unit = 8 * chips
    padded = -(-(classes + rank) // unit) * unit
    batch_index = batch_index.reshape(1, rows)
    mine, other = total_of(*pick_batch(batch_index, centers), chips)
    high, low, spread = prepare(nys_index.reshape(1, -1), eigvec.T, weights.T, padded)
    mine, other = total_of(*predict(mine, other, centers, high, low), chips)
    new_weights, predictions = update(
        mine, other, targets.T, batch_index, eigval.reshape(1, rank), spread, weights.T
    )
    return new_weights.T, predictions.T


def solution(mesh):
    return jax.shard_map(
        functools.partial(on_device, mesh.shape["center"]),
        mesh=mesh,
        in_specs=(
            P(("parts", "center", "sub"), None),
            P(("parts", "center", "sub"), None),
            P("parts", None),
            P("parts"),
            P(("parts", "center", "sub")),
            P(("parts", "center", "sub"), None),
            P("parts"),
        ),
        out_specs=(P(("parts", "center", "sub"), None), P("parts", None)),
        check_vma=False,
    )
```

```python
import functools
import math

import jax
import jax.numpy as jnp
from jax import lax
from jax.experimental import pallas as pl
from jax.experimental.pallas import tpu as pltpu
from jax.sharding import PartitionSpec as P

F32 = jnp.float32
BF16 = jnp.bfloat16
AXES = ("center", "sub")
LEVELS = 4
CHUNKS = 1 << LEVELS
LANE = 128
PARTS = 2
NT = (((1,), (1,)), ((), ()))
NN = (((1,), (0,)), ((), ()))
VMEM_LIMIT = 24 * 1024 * 1024


def dot(a, b, dims):
    return lax.dot_general(a, b, dims, preferred_element_type=F32)


def position():
    return lax.axis_index("center") * 2 + lax.axis_index("sub")


def reversed_bits(value, bits):
    out = 0
    for bit in range(bits):
        out = out + ((value >> bit) & 1) * (1 << (bits - 1 - bit))
    return out


def column_of(row, width):
    return jnp.broadcast_to(row.astype(F32), (width, row.shape[1])).T


def two(x):
    high = x.astype(BF16)
    return high, (x - high.astype(F32)).astype(BF16)


def pick_rows(index_ref, columns, start, dtype, scale):
    column = column_of(index_ref[...] - start, LANE)
    lanes = lax.broadcasted_iota(jnp.int32, (1, LANE), 1).astype(F32)
    blocks = [
        jnp.where(column == lanes + float(LANE * k), scale, 0.0).astype(dtype)
        for k in range(columns // LANE)
    ]
    return jnp.concatenate(blocks, axis=1)


def params():
    return pltpu.CompilerParams(vmem_limit_bytes=VMEM_LIMIT)


def pick_body(index_ref, centers_ref, keep_ref, send_ref, pick_ref):
    me = position()
    turn = reversed_bits(me, LEVELS)
    rows = index_ref.shape[1]
    size = rows // CHUNKS
    count = centers_ref.shape[0]

    @pl.when(pl.program_id(0) == 0)
    def _():
        pick = pick_rows(index_ref, count, me * count, BF16, 1.0)
        for chunk in range(CHUNKS):
            to = pl.multiple_of((chunk ^ turn) * size, size)
            pick_ref[pl.ds(to, size), :] = pick[chunk * size : (chunk + 1) * size]

    found = dot(pick_ref[...], centers_ref[...], NN).astype(BF16)
    keep_ref[...] = found[: rows // 2]
    send_ref[...] = found[rows // 2 :]


def pick_batch(batch_index, centers, part):
    rows = batch_index.shape[1]
    count, depth = centers.shape
    block = depth // PARTS // 2
    half = jax.ShapeDtypeStruct((rows // 2, depth // PARTS), BF16)
    return pl.pallas_call(
        pick_body,
        grid=(2,),
        in_specs=[
            pl.BlockSpec((1, rows), lambda i: (0, 0)),
            pl.BlockSpec((count, block), lambda i: (0, 2 * part + i)),
        ],
        out_specs=[pl.BlockSpec((rows // 2, block), lambda i: (0, i))] * 2,
        out_shape=[half, half],
        scratch_shapes=[pltpu.VMEM((rows, count), BF16)],
        compiler_params=params(),
        cost_estimate=pl.CostEstimate(
            flops=2 * rows * count * depth // PARTS,
            bytes_accessed=2 * depth * (count + rows) // PARTS,
            transcendentals=0,
        ),
        name="pick_batch",
    )(batch_index, centers)


def spread_body(
    first, classes, index_ref, eigvec_ref, weights_ref,
    high1_ref, low1_ref, high2_ref, low2_ref, spread_ref, all_ref,
):
    me = position()
    turn = reversed_bits(me >> 1, LEVELS - 1)
    rank, points = eigvec_ref.shape
    count = weights_ref.shape[1]
    local = index_ref[...] - me * count
    slots = lax.broadcasted_iota(jnp.int32, (count, points), 0)
    pick = jnp.where(slots == local, 1.0, 0.0).astype(BF16)
    vec = eigvec_ref[...]
    high = vec.astype(BF16)
    rest = vec - high.astype(F32)
    mid = rest.astype(BF16)
    low = (rest - mid.astype(F32)).astype(BF16)
    spread = dot(high, pick, NT) + dot(mid, pick, NT) + dot(low, pick, NT)
    spread_ref[...] = spread
    all_ref[:rank] = spread
    all_ref[rank : rank + classes] = weights_ref[...]
    all_ref[rank + classes :] = jnp.zeros((all_ref.shape[0] - rank - classes, count), F32)
    for begin, high_ref, low_ref in ((0, high1_ref, low1_ref), (first, high2_ref, low2_ref)):
        size = high_ref.shape[0] // (CHUNKS // 2)
        for chunk in range(CHUNKS // 2):
            at = pl.multiple_of(begin + (chunk ^ turn) * size, 8)
            high, low = two(all_ref[pl.ds(at, size), :])
            high_ref[chunk * size : (chunk + 1) * size] = high
            low_ref[chunk * size : (chunk + 1) * size] = low


def spread_weights(nys_index, eigvec, weights, first, second):
    classes, count = weights.shape
    rank, points = eigvec.shape
    return pl.pallas_call(
        functools.partial(spread_body, first, classes),
        out_shape=[
            jax.ShapeDtypeStruct((first, count), BF16),
            jax.ShapeDtypeStruct((first, count), BF16),
            jax.ShapeDtypeStruct((second, count), BF16),
            jax.ShapeDtypeStruct((second, count), BF16),
            jax.ShapeDtypeStruct((rank, count), F32),
        ],
        scratch_shapes=[pltpu.VMEM((first + second, count), F32)],
        compiler_params=params(),
        cost_estimate=pl.CostEstimate(
            flops=6 * rank * points * count, bytes_accessed=8 * (first + second) * count, transcendentals=0
        ),
        name="spread_weights",
    )(nys_index, eigvec, weights)


def norms_body(centers_ref, norm_ref):
    wide = centers_ref[...].astype(F32)
    norm = jnp.sum(wide * wide, axis=1, keepdims=True)
    norm_ref[...] = jnp.broadcast_to(norm, norm_ref.shape)


def center_norms(centers):
    count, depth = centers.shape
    block = 256
    return pl.pallas_call(
        norms_body,
        grid=(count // block,),
        in_specs=[pl.BlockSpec((block, depth), lambda i: (i, 0))],
        out_specs=pl.BlockSpec((block, LANE), lambda i: (i, 0)),
        out_shape=jax.ShapeDtypeStruct((count, LANE), F32),
        compiler_params=params(),
        cost_estimate=pl.CostEstimate(flops=2 * count * depth, bytes_accessed=2 * count * depth, transcendentals=0),
        name="center_norms",
    )(centers)


def distance_step(mine_ref, other_ref, centers_ref, before, total_ref, batch_ref):
    step = pl.program_id(0)
    blocks, rows, block = batch_ref.shape
    size = rows // CHUNKS

    @pl.when(step == 0)
    def _():
        turn = reversed_bits(position(), LEVELS)
        for chunk in range(CHUNKS):
            ref = mine_ref if chunk < CHUNKS // 2 else other_ref
            at = chunk % (CHUNKS // 2) * size
            to = pl.multiple_of((chunk ^ turn) * size, size)
            for k in range(blocks):
                batch_ref[k, pl.ds(to, size), :] = ref[at : at + size, k * block : (k + 1) * block]
        norm = jnp.zeros((rows, 1), F32)
        for k in range(blocks):
            batch = batch_ref[k].astype(F32)
            norm = norm + jnp.sum(batch * batch, axis=1, keepdims=True)
        total_ref[...] = before() + jnp.broadcast_to(norm, (rows, LANE)).T[0:1]

    total_ref[...] -= 2.0 * dot(centers_ref[...], batch_ref[step], NT)


def product(me, high_ref, low_ref, value_high, value_low, keep_ref, send_ref):
    half = keep_ref.shape[1]
    high = high_ref[...]
    total = dot(high, value_high, NN) + (dot(high, value_low, NN) + dot(low_ref[...], value_high, NN))
    lower = (me & 1) == 0
    keep_ref[...] = jnp.where(lower, total[:, :half], total[:, half:])
    send_ref[...] = jnp.where(lower, total[:, half:], total[:, :half])


def distance_body(mine_ref, other_ref, centers_ref, norm_ref, total_ref, batch_ref):
    distance_step(mine_ref, other_ref, centers_ref, lambda: norm_ref[:, 0:1], total_ref, batch_ref)


def predict_body(
    depth, mine_ref, other_ref, centers_ref, before_ref, high_hbm, low_hbm,
    keep_ref, send_ref, value_high_ref, value_low_ref, total_ref, batch_ref, high_ref, low_ref, sems,
):
    copies = [
        pltpu.make_async_copy(high_hbm, high_ref, sems.at[0]),
        pltpu.make_async_copy(low_hbm, low_ref, sems.at[1]),
    ]

    @pl.when(pl.program_id(0) == 0)
    def _():
        for copy in copies:
            copy.start()

    distance_step(mine_ref, other_ref, centers_ref, lambda: before_ref[...], total_ref, batch_ref)

    @pl.when(pl.program_id(0) == pl.num_programs(0) - 1)
    def _():
        square = jnp.maximum(total_ref[...], 0.0)
        value_high, value_low = two(jnp.exp(jnp.sqrt(square) * (-1.0 / math.sqrt(depth))))
        value_high_ref[...] = value_high
        value_low_ref[...] = value_low
        for copy in copies:
            copy.wait()
        product(position(), high_ref, low_ref, value_high, value_low, keep_ref, send_ref)


def exchange_specs(half, depth, count, block, part):
    blocks = depth // block
    return [
        pl.BlockSpec((half, depth), lambda i: (0, 0)),
        pl.BlockSpec((half, depth), lambda i: (0, 0)),
        pl.BlockSpec((count, block), lambda i: (0, part * blocks + i)),
    ]


def distances(mine, other, centers, norms):
    half, depth = mine.shape
    rows = 2 * half
    count = centers.shape[0]
    block = 512
    return pl.pallas_call(
        distance_body,
        grid=(depth // block,),
        in_specs=exchange_specs(half, depth, count, block, 0) + [pl.BlockSpec((count, LANE), lambda i: (0, 0))],
        out_specs=pl.BlockSpec((count, rows), lambda i: (0, 0)),
        out_shape=jax.ShapeDtypeStruct((count, rows), F32),
        scratch_shapes=[pltpu.VMEM((depth // block, rows, block), BF16)],
        compiler_params=params(),
        cost_estimate=pl.CostEstimate(
            flops=2 * rows * count * depth, bytes_accessed=2 * depth * (count + rows), transcendentals=0
        ),
        name="distances",
    )(mine, other, centers, norms)


def predict(mine, other, centers, before, high, low):
    half, depth = mine.shape
    rows = 2 * half
    count = centers.shape[0]
    padded = high.shape[0]
    block = 512
    fixed = lambda shape: pl.BlockSpec(shape, lambda i: (0, 0))
    out = jax.ShapeDtypeStruct((padded, half), F32)
    value = jax.ShapeDtypeStruct((count, rows), BF16)
    return pl.pallas_call(
        functools.partial(predict_body, centers.shape[1]),
        grid=(depth // block,),
        in_specs=exchange_specs(half, depth, count, block, 1)
        + [fixed((count, rows)), pl.BlockSpec(memory_space=pl.ANY), pl.BlockSpec(memory_space=pl.ANY)],
        out_specs=[fixed((padded, half))] * 2 + [fixed((count, rows))] * 2,
        out_shape=[out, out, value, value],
        scratch_shapes=[
            pltpu.VMEM((count, rows), F32),
            pltpu.VMEM((depth // block, rows, block), BF16),
            pltpu.VMEM((padded, count), BF16),
            pltpu.VMEM((padded, count), BF16),
            pltpu.SemaphoreType.DMA((2,)),
        ],
        compiler_params=params(),
        cost_estimate=pl.CostEstimate(
            flops=2 * rows * count * (depth + 3 * padded),
            bytes_accessed=2 * depth * (count + rows) + 4 * padded * (count + rows),
            transcendentals=2 * rows * count,
        ),
        name="predict",
    )(mine, other, centers, before, high, low)


def more_body(high_ref, low_ref, value_high_ref, value_low_ref, keep_ref, send_ref):
    product(position(), high_ref, low_ref, value_high_ref[...], value_low_ref[...], keep_ref, send_ref)


def predict_more(high, low, value_high, value_low):
    padded = high.shape[0]
    count, rows = value_high.shape
    out = jax.ShapeDtypeStruct((padded, rows // 2), F32)
    return pl.pallas_call(
        more_body,
        out_shape=[out, out],
        compiler_params=params(),
        cost_estimate=pl.CostEstimate(
            flops=6 * rows * count * padded, bytes_accessed=4 * padded * (count + rows), transcendentals=0
        ),
        name="predict_more",
    )(high, low, value_high, value_low)


def gather_total(mine_ref, other_ref, total_ref):
    me = position()
    turn = reversed_bits(me >> 1, LEVELS - 1)
    half = mine_ref.shape[1]
    size = mine_ref.shape[0] // (CHUNKS // 2)
    lower = (me & 1) == 0
    for chunk in range(CHUNKS // 2):
        to = pl.multiple_of((chunk ^ turn) * size, 8)
        mine = mine_ref[chunk * size : (chunk + 1) * size]
        other = other_ref[chunk * size : (chunk + 1) * size]
        total_ref[pl.ds(to, size), :half] = jnp.where(lower, mine, other)
        total_ref[pl.ds(to, size), half:] = jnp.where(lower, other, mine)


def write_rows(begin, skip, total_ref, targets_ref, weights_ref, high_ref, low_ref, new_hbm, out_hbm, new_ref, sems):
    rows = new_ref.shape[0]
    blocks = sems.shape[0] - 1
    size = rows // blocks
    high_right = high_ref[...]
    low_right = low_ref[...]
    copies = [
        pltpu.make_async_copy(
            total_ref.at[pl.ds(skip, rows)], out_hbm.at[pl.ds(begin, rows)], sems.at[blocks]
        )
    ]
    copies[0].start()
    for k in range(blocks):
        at = slice(k * size, (k + 1) * size)
        from_ = slice(begin + k * size, begin + (k + 1) * size)
        high, low = two(total_ref[skip + k * size : skip + (k + 1) * size] - targets_ref[from_])
        new_ref[at] = weights_ref[from_] + (
            dot(high, high_right, NN) + (dot(high, low_right, NN) + dot(low, high_right, NN))
        )
        copy = pltpu.make_async_copy(
            new_ref.at[pl.ds(k * size, size)], new_hbm.at[pl.ds(begin + k * size, size)], sems.at[k]
        )
        copy.start()
        copies.append(copy)
    for copy in copies:
        copy.wait()


def update_body(
    mine_ref, other_ref, targets_ref, index_ref, eigval_ref, spread_ref, weights_ref,
    new_hbm, out_hbm, high_ref, low_ref, total_ref, new_ref, sems,
):
    me = position()
    rank, count = spread_ref.shape
    gather_total(mine_ref, other_ref, total_ref)
    value = eigval_ref[...]
    lowest = jnp.min(value, axis=1, keepdims=True)
    scaled = (1.0 - lowest / value) / value
    mixed_high, mixed_low = two(total_ref[:rank].T * (0.25 * scaled))
    spread_high, spread_low = two(spread_ref[...])
    turned = dot(mixed_high, spread_high, NN) + (
        dot(mixed_high, spread_low, NN) + dot(mixed_low, spread_high, NN)
    )
    high_ref[...], low_ref[...] = two(turned - pick_rows(index_ref, count, me * count, F32, 0.25))
    write_rows(0, rank, total_ref, targets_ref, weights_ref, high_ref, low_ref, new_hbm, out_hbm, new_ref, sems)


def update(mine, other, targets, batch_index, eigval, spread, weights):
    classes, count = weights.shape
    padded, half = mine.shape
    rows = 2 * half
    rank = spread.shape[0]
    here = padded - rank
    vmem = pl.BlockSpec(memory_space=pltpu.VMEM)
    hbm = pl.BlockSpec(memory_space=pl.ANY)
    right = jax.ShapeDtypeStruct((rows, count), BF16)
    return pl.pallas_call(
        update_body,
        in_specs=[vmem] * 7,
        out_specs=[hbm, hbm, vmem, vmem],
        out_shape=[
            jax.ShapeDtypeStruct((classes, count), F32),
            jax.ShapeDtypeStruct((classes, rows), F32),
            right,
            right,
        ],
        scratch_shapes=[
            pltpu.VMEM((padded, rows), F32),
            pltpu.VMEM((here, count), F32),
            pltpu.SemaphoreType.DMA((4,)),
        ],
        compiler_params=params(),
        cost_estimate=pl.CostEstimate(
            flops=6 * rows * count * (here + rank), bytes_accessed=8 * here * (count + rows), transcendentals=0
        ),
        name="update",
    )(mine, other, targets, batch_index, eigval, spread, weights)


def update_more_body(
    begin, mine_ref, other_ref, targets_ref, weights_ref, high_ref, low_ref, new_in, out_in,
    new_hbm, out_hbm, total_ref, new_ref, sems,
):
    gather_total(mine_ref, other_ref, total_ref)
    write_rows(begin, 0, total_ref, targets_ref, weights_ref, high_ref, low_ref, new_hbm, out_hbm, new_ref, sems)


def update_more(mine, other, targets, weights, high, low, new, out, begin):
    classes, count = weights.shape
    padded, half = mine.shape
    rows = 2 * half
    here = classes - begin
    vmem = pl.BlockSpec(memory_space=pltpu.VMEM)
    hbm = pl.BlockSpec(memory_space=pl.ANY)
    return pl.pallas_call(
        functools.partial(update_more_body, begin),
        in_specs=[vmem] * 6 + [hbm] * 2,
        out_specs=[hbm, hbm],
        out_shape=[
            jax.ShapeDtypeStruct((classes, count), F32),
            jax.ShapeDtypeStruct((classes, rows), F32),
        ],
        input_output_aliases={6: 0, 7: 1},
        scratch_shapes=[
            pltpu.VMEM((padded, rows), F32),
            pltpu.VMEM((here, count), F32),
            pltpu.SemaphoreType.DMA((6,)),
        ],
        compiler_params=params(),
        cost_estimate=pl.CostEstimate(
            flops=6 * rows * count * here, bytes_accessed=8 * here * (count + rows), transcendentals=0
        ),
        name="update_more",
    )(mine, other, targets, weights, high, low, new, out)


def swap(x, mask, devices):
    return lax.ppermute(x, AXES, [(i, i ^ mask) for i in range(devices)])


def total_of(keep, send, devices):
    for level in range(LEVELS):
        keep = keep + swap(send, 1 << level, devices)
        if level < LEVELS - 1:
            half = keep.shape[0] // 2
            keep, send = keep[:half], keep[half:]
    for level in range(LEVELS, int(math.log2(devices))):
        keep = keep + swap(keep, 1 << level, devices)
    for level in reversed(range(1, LEVELS)):
        keep = jnp.concatenate([keep, swap(keep, 1 << level, devices)])
    return keep, swap(keep, 1, devices)


def on_device(devices, centers, weights, targets, batch_index, nys_index, eigvec, eigval):
    rows = batch_index.shape[0]
    classes = weights.shape[1]
    rank = eigvec.shape[1]
    unit = 8 * CHUNKS // 2
    units = -(-(classes + rank) // unit)
    first = (units + 1) // 2 * unit
    second = units * unit - first
    begin = first - rank
    batch_index = batch_index.reshape(1, rows)
    weights = weights.T
    targets = targets.T
    halves = [total_of(*pick_batch(batch_index, centers, part), devices) for part in range(PARTS)]
    high1, low1, high2, low2, spread = spread_weights(nys_index.reshape(1, -1), eigvec.T, weights, first, second)
    before = distances(*halves[0], centers, center_norms(centers))
    keep, send, value_high, value_low = predict(*halves[1], centers, before, high1, low1)
    one = total_of(keep, send, devices)
    another = total_of(*predict_more(high2, low2, value_high, value_low), devices)
    new, out, high, low = update(*one, targets, batch_index, eigval.reshape(1, rank), spread, weights)
    new, out = update_more(*another, targets, weights, high, low, new, out, begin)
    return new.T, out.T


def solution(mesh):
    devices = mesh.shape["center"] * mesh.shape["sub"]
    return jax.shard_map(
        functools.partial(on_device, devices),
        mesh=mesh,
        in_specs=(
            P(("parts", "center", "sub"), None),
            P(("parts", "center", "sub"), None),
            P("parts", None),
            P("parts"),
            P(("parts", "center", "sub")),
            P(("parts", "center", "sub"), None),
            P("parts"),
        ),
        out_specs=(P(("parts", "center", "sub"), None), P("parts", None)),
        check_vma=False,
    )
```

```python
import functools
import math

import jax
import jax.numpy as jnp
from jax import lax
from jax.experimental import pallas as pl
from jax.experimental.pallas import tpu as pltpu
from jax.sharding import PartitionSpec as P

F32 = jnp.float32
BF16 = jnp.bfloat16
AXES = ("center", "sub")
HALVINGS = 2
CHUNKS = 1 << HALVINGS
LANE = 128
PARTS = 2
NT = (((1,), (1,)), ((), ()))
NN = (((1,), (0,)), ((), ()))
VMEM_LIMIT = 24 * 1024 * 1024


def dot(a, b, dims):
    return lax.dot_general(a, b, dims, preferred_element_type=F32)


def walk(sub, bits):
    order = list(range(bits))
    return order if sub == 0 else order[1:3] + order[:1] + order[3:]


def turns():
    center = lax.axis_index("center")
    return [
        sum(((center >> bit) & 1) << (HALVINGS - 1 - k) for k, bit in enumerate(walk(sub, HALVINGS + 1)[:HALVINGS]))
        for sub in range(2)
    ]


def column_of(row, width):
    return jnp.broadcast_to(row.astype(F32), (width, row.shape[1])).T


def two(x):
    high = x.astype(BF16)
    return high, (x - high.astype(F32)).astype(BF16)


def pick_rows(index_ref, columns, start, dtype, scale):
    column = column_of(index_ref[...] - start, LANE)
    lanes = lax.broadcasted_iota(jnp.int32, (1, LANE), 1).astype(F32)
    blocks = [
        jnp.where(column == lanes + float(LANE * k), scale, 0.0).astype(dtype)
        for k in range(columns // LANE)
    ]
    return jnp.concatenate(blocks, axis=1)


def params():
    return pltpu.CompilerParams(vmem_limit_bytes=VMEM_LIMIT)


def pick_body(first, index_hbm, centers_hbm, keep_ref, send_ref, pick_ref, index_ref, centers_ref, sems):
    sub = lax.axis_index("sub")
    blocks, count, block = centers_ref.shape
    rows = index_ref.shape[1]
    half = rows // 2
    size = half // CHUNKS
    copies = [pltpu.make_async_copy(index_hbm, index_ref, sems.at[blocks])] + [
        pltpu.make_async_copy(
            centers_hbm.at[:, pl.ds(first + k * block, block)], centers_ref.at[k], sems.at[k]
        )
        for k in range(blocks)
    ]
    for copy in copies:
        copy.start()
    copies[0].wait()
    start = (lax.axis_index("center") * 2 + sub) * count
    pick = pick_rows(index_ref, count, start, BF16, 1.0)
    for part, turn in enumerate(turns()):
        begin = jnp.where(sub == part, 0, half)
        for chunk in range(CHUNKS):
            to = pl.multiple_of(begin + (chunk ^ turn) * size, size)
            at = part * half + chunk * size
            pick_ref[pl.ds(to, size), :] = pick[at : at + size]
    for k in range(blocks):
        copies[k + 1].wait()
        found = dot(pick_ref[...], centers_ref[k], NN).astype(BF16)
        keep_ref[:, k * block : (k + 1) * block] = found[:half]
        send_ref[:, k * block : (k + 1) * block] = found[half:]


def pick_batch(batch_index, centers, part):
    rows = batch_index.shape[1]
    count, depth = centers.shape
    depth = depth // PARTS
    block = 512
    half = jax.ShapeDtypeStruct((rows // 2, depth), BF16)
    hbm = pl.BlockSpec(memory_space=pltpu.HBM)
    vmem = pl.BlockSpec(memory_space=pltpu.VMEM)
    return pl.pallas_call(
        functools.partial(pick_body, part * depth),
        in_specs=[hbm, hbm],
        out_specs=[vmem, vmem],
        out_shape=[half, half],
        scratch_shapes=[
            pltpu.VMEM((rows, count), BF16),
            pltpu.VMEM((1, rows), jnp.int32),
            pltpu.VMEM((depth // block, count, block), BF16),
            pltpu.SemaphoreType.DMA((depth // block + 1,)),
        ],
        compiler_params=params(),
        cost_estimate=pl.CostEstimate(
            flops=2 * rows * count * depth, bytes_accessed=2 * depth * (count + rows), transcendentals=0
        ),
        name="pick_batch",
    )(batch_index, centers)


def spread_body(
    first, classes, index_ref, eigvec_ref, weights_ref,
    high1_ref, low1_ref, high2_ref, low2_ref, spread_ref, all_ref,
):
    rank, points = eigvec_ref.shape
    count = weights_ref.shape[1]
    local = index_ref[...] - (lax.axis_index("center") * 2 + lax.axis_index("sub")) * count
    slots = lax.broadcasted_iota(jnp.int32, (count, points), 0)
    pick = jnp.where(slots == local, 1.0, 0.0).astype(BF16)
    vec = eigvec_ref[...]
    high = vec.astype(BF16)
    rest = vec - high.astype(F32)
    mid = rest.astype(BF16)
    low = (rest - mid.astype(F32)).astype(BF16)
    spread = dot(high, pick, NT) + dot(mid, pick, NT) + dot(low, pick, NT)
    spread_ref[...] = spread
    all_ref[:rank] = spread
    all_ref[rank : rank + classes] = weights_ref[...]
    all_ref[rank + classes :] = jnp.zeros((all_ref.shape[0] - rank - classes, count), F32)
    for begin, high_ref, low_ref in ((0, high1_ref, low1_ref), (first, high2_ref, low2_ref)):
        high_ref[...], low_ref[...] = two(all_ref[begin : begin + high_ref.shape[0]])


def spread_weights(nys_index, eigvec, weights, first, second):
    classes, count = weights.shape
    rank, points = eigvec.shape
    return pl.pallas_call(
        functools.partial(spread_body, first, classes),
        out_shape=[
            jax.ShapeDtypeStruct((first, count), BF16),
            jax.ShapeDtypeStruct((first, count), BF16),
            jax.ShapeDtypeStruct((second, count), BF16),
            jax.ShapeDtypeStruct((second, count), BF16),
            jax.ShapeDtypeStruct((rank, count), F32),
        ],
        scratch_shapes=[pltpu.VMEM((first + second, count), F32)],
        compiler_params=params(),
        cost_estimate=pl.CostEstimate(
            flops=6 * rank * points * count, bytes_accessed=8 * (first + second) * count, transcendentals=0
        ),
        name="spread_weights",
    )(nys_index, eigvec, weights)


def norms_body(centers_ref, norm_ref):
    wide = centers_ref[...].astype(F32)
    norm = jnp.sum(wide * wide, axis=1, keepdims=True)
    norm_ref[...] = jnp.broadcast_to(norm, norm_ref.shape)


def center_norms(centers):
    count, depth = centers.shape
    block = 256
    return pl.pallas_call(
        norms_body,
        grid=(count // block,),
        in_specs=[pl.BlockSpec((block, depth), lambda i: (i, 0))],
        out_specs=pl.BlockSpec((block, LANE), lambda i: (i, 0)),
        out_shape=jax.ShapeDtypeStruct((count, LANE), F32),
        compiler_params=params(),
        cost_estimate=pl.CostEstimate(flops=2 * count * depth, bytes_accessed=2 * count * depth, transcendentals=0),
        name="center_norms",
    )(centers)


def gather_batch(mine_ref, other_ref, batch_ref):
    lower = lax.axis_index("sub") == 0
    half = mine_ref.shape[0]
    size = half // CHUNKS
    for part, turn in enumerate(turns()):
        for chunk in range(CHUNKS):
            at = slice(chunk * size, (chunk + 1) * size)
            same = lower if part == 0 else jnp.logical_not(lower)
            to = pl.multiple_of(part * half + (chunk ^ turn) * size, size)
            batch_ref[pl.ds(to, size), :] = jnp.where(same, mine_ref[at], other_ref[at])


def nearer(first, centers_ref, batch_ref):
    rows, depth = batch_ref.shape
    batch = batch_ref[...].astype(F32)
    norm = jnp.sum(batch * batch, axis=1, keepdims=True)
    cross = dot(centers_ref[:, first : first + depth], batch_ref[...], NT)
    return jnp.broadcast_to(norm, (rows, LANE)).T[0:1] - 2.0 * cross


def product(high_ref, low_ref, value_high, value_low, total_ref, keep_ref, send_ref):
    half = keep_ref.shape[1]
    high = high_ref[...]
    total_ref[...] = dot(high, value_high, NN) + (dot(high, value_low, NN) + dot(low_ref[...], value_high, NN))
    lower = lax.axis_index("sub") == 0
    size = keep_ref.shape[0] // CHUNKS
    for chunk in range(CHUNKS):
        at = slice(chunk * size, (chunk + 1) * size)
        first, second = [
            total_ref[pl.ds(pl.multiple_of((chunk ^ turn) * size, 8), size), part * half : (part + 1) * half]
            for part, turn in enumerate(turns())
        ]
        keep_ref[at] = jnp.where(lower, first, second)
        send_ref[at] = jnp.where(lower, second, first)


def distance_body(mine_ref, other_ref, centers_ref, norm_ref, total_ref, batch_ref):
    gather_batch(mine_ref, other_ref, batch_ref)
    total_ref[...] = norm_ref[:, 0:1] + nearer(0, centers_ref, batch_ref)


def predict_body(
    mine_ref, other_ref, centers_ref, before_ref, high_ref, low_ref,
    keep_ref, send_ref, value_high_ref, value_low_ref, batch_ref, total_ref,
):
    depth = centers_ref.shape[1]
    gather_batch(mine_ref, other_ref, batch_ref)
    square = jnp.maximum(before_ref[...] + nearer(depth - batch_ref.shape[1], centers_ref, batch_ref), 0.0)
    value_high, value_low = two(jnp.exp(jnp.sqrt(square) * (-1.0 / math.sqrt(depth))))
    value_high_ref[...] = value_high
    value_low_ref[...] = value_low
    product(high_ref, low_ref, value_high, value_low, total_ref, keep_ref, send_ref)


def distances(mine, other, centers, norms):
    half, depth = mine.shape
    rows = 2 * half
    count = centers.shape[0]
    vmem = pl.BlockSpec(memory_space=pltpu.VMEM)
    return pl.pallas_call(
        distance_body,
        in_specs=[vmem] * 4,
        out_specs=vmem,
        out_shape=jax.ShapeDtypeStruct((count, rows), F32),
        scratch_shapes=[pltpu.VMEM((rows, depth), BF16)],
        compiler_params=params(),
        cost_estimate=pl.CostEstimate(
            flops=2 * rows * count * depth, bytes_accessed=2 * depth * (count + rows), transcendentals=0
        ),
        name="distances",
    )(mine, other, centers, norms)


def predict(mine, other, centers, before, high, low):
    half, depth = mine.shape
    rows = 2 * half
    count = centers.shape[0]
    padded = high.shape[0]
    out = jax.ShapeDtypeStruct((padded, half), F32)
    value = jax.ShapeDtypeStruct((count, rows), BF16)
    vmem = pl.BlockSpec(memory_space=pltpu.VMEM)
    return pl.pallas_call(
        predict_body,
        in_specs=[vmem] * 6,
        out_specs=[vmem] * 4,
        out_shape=[out, out, value, value],
        scratch_shapes=[pltpu.VMEM((rows, depth), BF16), pltpu.VMEM((padded, rows), F32)],
        compiler_params=params(),
        cost_estimate=pl.CostEstimate(
            flops=2 * rows * count * (depth + 3 * padded),
            bytes_accessed=2 * depth * (count + rows) + 4 * padded * (count + rows),
            transcendentals=2 * rows * count,
        ),
        name="predict",
    )(mine, other, centers, before, high, low)


def more_body(high_ref, low_ref, value_high_ref, value_low_ref, keep_ref, send_ref, total_ref):
    product(high_ref, low_ref, value_high_ref[...], value_low_ref[...], total_ref, keep_ref, send_ref)


def predict_more(high, low, value_high, value_low):
    padded = high.shape[0]
    count, rows = value_high.shape
    out = jax.ShapeDtypeStruct((padded, rows // 2), F32)
    return pl.pallas_call(
        more_body,
        out_shape=[out, out],
        scratch_shapes=[pltpu.VMEM((padded, rows), F32)],
        compiler_params=params(),
        cost_estimate=pl.CostEstimate(
            flops=6 * rows * count * padded, bytes_accessed=4 * padded * (count + rows), transcendentals=0
        ),
        name="predict_more",
    )(high, low, value_high, value_low)


def gather_total(mine_ref, other_ref, total_ref):
    lower = lax.axis_index("sub") == 0
    half = mine_ref.shape[1]
    size = mine_ref.shape[0] // CHUNKS
    for part, turn in enumerate(turns()):
        for chunk in range(CHUNKS):
            at = slice(chunk * size, (chunk + 1) * size)
            same = lower if part == 0 else jnp.logical_not(lower)
            to = pl.multiple_of((chunk ^ turn) * size, 8)
            total_ref[pl.ds(to, size), part * half : (part + 1) * half] = jnp.where(
                same, mine_ref[at], other_ref[at]
            )


def write_rows(begin, skip, total_ref, targets_ref, weights_ref, high_ref, low_ref, new_hbm, out_hbm, new_ref, sems):
    rows = new_ref.shape[0]
    blocks = sems.shape[0] - 1
    bounds = [8 * (rows // 8 * k // blocks) for k in range(blocks)] + [rows]
    high_right = high_ref[...]
    low_right = low_ref[...]
    copies = [
        pltpu.make_async_copy(
            total_ref.at[pl.ds(skip, rows)], out_hbm.at[pl.ds(begin, rows)], sems.at[blocks]
        )
    ]
    copies[0].start()
    for k in range(blocks):
        low_end, high_end = bounds[k : k + 2]
        here = slice(begin + low_end, begin + high_end)
        high, low = two(total_ref[skip + low_end : skip + high_end] - targets_ref[here])
        new_ref[low_end:high_end] = weights_ref[here] + (
            dot(high, high_right, NN) + (dot(high, low_right, NN) + dot(low, high_right, NN))
        )
        copy = pltpu.make_async_copy(
            new_ref.at[pl.ds(low_end, high_end - low_end)],
            new_hbm.at[pl.ds(begin + low_end, high_end - low_end)],
            sems.at[k],
        )
        copy.start()
        copies.append(copy)
    for copy in copies:
        copy.wait()


def update_body(
    mine_ref, other_ref, targets_ref, index_ref, eigval_ref, spread_ref, weights_ref,
    new_hbm, out_hbm, high_ref, low_ref, total_ref, new_ref, sems,
):
    start = (lax.axis_index("center") * 2 + lax.axis_index("sub")) * spread_ref.shape[1]
    rank, count = spread_ref.shape
    gather_total(mine_ref, other_ref, total_ref)
    value = eigval_ref[...]
    lowest = jnp.min(value, axis=1, keepdims=True)
    scaled = (1.0 - lowest / value) / value
    mixed_high, mixed_low = two(total_ref[:rank].T * (0.25 * scaled))
    spread_high, spread_low = two(spread_ref[...])
    turned = dot(mixed_high, spread_high, NN) + (
        dot(mixed_high, spread_low, NN) + dot(mixed_low, spread_high, NN)
    )
    high_ref[...], low_ref[...] = two(turned - pick_rows(index_ref, count, start, F32, 0.25))
    write_rows(0, rank, total_ref, targets_ref, weights_ref, high_ref, low_ref, new_hbm, out_hbm, new_ref, sems)


def update(mine, other, targets, batch_index, eigval, spread, weights):
    classes, count = weights.shape
    padded, half = mine.shape
    rows = 2 * half
    rank = spread.shape[0]
    here = padded - rank
    vmem = pl.BlockSpec(memory_space=pltpu.VMEM)
    hbm = pl.BlockSpec(memory_space=pl.ANY)
    right = jax.ShapeDtypeStruct((rows, count), BF16)
    return pl.pallas_call(
        update_body,
        in_specs=[vmem] * 7,
        out_specs=[hbm, hbm, vmem, vmem],
        out_shape=[
            jax.ShapeDtypeStruct((classes, count), F32),
            jax.ShapeDtypeStruct((classes, rows), F32),
            right,
            right,
        ],
        scratch_shapes=[
            pltpu.VMEM((padded, rows), F32),
            pltpu.VMEM((here, count), F32),
            pltpu.SemaphoreType.DMA((4,)),
        ],
        compiler_params=params(),
        cost_estimate=pl.CostEstimate(
            flops=6 * rows * count * (here + rank), bytes_accessed=8 * here * (count + rows), transcendentals=0
        ),
        name="update",
    )(mine, other, targets, batch_index, eigval, spread, weights)


def update_more_body(
    begin, mine_ref, other_ref, targets_ref, weights_ref, high_ref, low_ref, new_in, out_in,
    new_hbm, out_hbm, total_ref, new_ref, sems,
):
    gather_total(mine_ref, other_ref, total_ref)
    write_rows(begin, 0, total_ref, targets_ref, weights_ref, high_ref, low_ref, new_hbm, out_hbm, new_ref, sems)


def update_more(mine, other, targets, weights, high, low, new, out, begin):
    classes, count = weights.shape
    padded, half = mine.shape
    rows = 2 * half
    here = classes - begin
    vmem = pl.BlockSpec(memory_space=pltpu.VMEM)
    hbm = pl.BlockSpec(memory_space=pl.ANY)
    return pl.pallas_call(
        functools.partial(update_more_body, begin),
        in_specs=[vmem] * 6 + [hbm] * 2,
        out_specs=[hbm, hbm],
        out_shape=[
            jax.ShapeDtypeStruct((classes, count), F32),
            jax.ShapeDtypeStruct((classes, rows), F32),
        ],
        input_output_aliases={6: 0, 7: 1},
        scratch_shapes=[
            pltpu.VMEM((padded, rows), F32),
            pltpu.VMEM((here, count), F32),
            pltpu.SemaphoreType.DMA((6,)),
        ],
        compiler_params=params(),
        cost_estimate=pl.CostEstimate(
            flops=6 * rows * count * here, bytes_accessed=8 * here * (count + rows), transcendentals=0
        ),
        name="update_more",
    )(mine, other, targets, weights, high, low, new, out)


def swap(x, chips, level):
    bits = chips.bit_length() - 1
    flip = [1, 1] if level < 0 else [2 << walk(sub, bits)[level] for sub in range(2)]
    return lax.ppermute(x, AXES, [(i, i ^ flip[i & 1]) for i in range(2 * chips)])


def total_of(keep, send, chips, tied=()):
    keep = keep + swap(send, chips, -1)
    for level in range(chips.bit_length() - 1):
        if level >= HALVINGS:
            keep = keep + swap(keep, chips, level)
            continue
        half = keep.shape[0] // 2
        keep, send = keep[:half], keep[half:]
        if level == 1 and tied:
            send, *tied = lax.optimization_barrier((send, *tied))
        keep = keep + swap(send, chips, level)
    for level in reversed(range(HALVINGS)):
        keep = jnp.concatenate([keep, swap(keep, chips, level)])
    return [keep, swap(keep, chips, -1), *tied]


def on_device(chips, centers, weights, targets, batch_index, nys_index, eigvec, eigval):
    rows = batch_index.shape[0]
    classes = weights.shape[1]
    rank = eigvec.shape[1]
    unit = 8 * CHUNKS
    units = -(-(classes + rank) // unit)
    first = (units + 1) // 2 * unit
    second = units * unit - first
    begin = first - rank
    batch_index = batch_index.reshape(1, rows)
    weights = weights.T
    targets = targets.T
    picked = [pick_batch(batch_index, centers, part) for part in range(PARTS)]
    ready = [
        center_norms(centers),
        *spread_weights(nys_index.reshape(1, -1), eigvec.T, weights, first, second),
    ]
    mine, other, norms, high1, low1, high2, low2, spread = total_of(*picked[0], chips, ready)
    before = distances(mine, other, centers, norms)
    keep, send, value_high, value_low = predict(*total_of(*picked[1], chips), centers, before, high1, low1)
    one = total_of(keep, send, chips)
    another = total_of(*predict_more(high2, low2, value_high, value_low), chips)
    new, out, high, low = update(*one, targets, batch_index, eigval.reshape(1, rank), spread, weights)
    new, out = update_more(*another, targets, weights, high, low, new, out, begin)
    return new.T, out.T


def solution(mesh):
    return jax.shard_map(
        functools.partial(on_device, mesh.shape["center"]),
        mesh=mesh,
        in_specs=(
            P(("parts", "center", "sub"), None),
            P(("parts", "center", "sub"), None),
            P("parts", None),
            P("parts"),
            P(("parts", "center", "sub")),
            P(("parts", "center", "sub"), None),
            P("parts"),
        ),
        out_specs=(P(("parts", "center", "sub"), None), P("parts", None)),
        check_vma=False,
    )
```

```python
import functools
import math

import jax
import jax.numpy as jnp
from jax import lax
from jax.experimental import pallas as pl
from jax.experimental.pallas import tpu as pltpu
from jax.sharding import PartitionSpec as P

F32 = jnp.float32
BF16 = jnp.bfloat16
AXES = ("center", "sub")
HALVINGS = 2
CHUNKS = 1 << HALVINGS
LANE = 128
PARTS = 2
NT = (((1,), (1,)), ((), ()))
NN = (((1,), (0,)), ((), ()))
VMEM_LIMIT = 24 * 1024 * 1024


def dot(a, b, dims):
    return lax.dot_general(a, b, dims, preferred_element_type=F32)


def walk(sub, bits):
    order = list(range(bits))
    return order if sub == 0 else order[1::-1] + order[2:]


def turns():
    center = lax.axis_index("center")
    return [
        sum(((center >> bit) & 1) << (HALVINGS - 1 - k) for k, bit in enumerate(walk(sub, HALVINGS + 1)[:HALVINGS]))
        for sub in range(2)
    ]


def column_of(row, width):
    return jnp.broadcast_to(row.astype(F32), (width, row.shape[1])).T


def two(x):
    high = x.astype(BF16)
    return high, (x - high.astype(F32)).astype(BF16)


def pick_rows(index_ref, columns, start, dtype, scale):
    column = column_of(index_ref[...] - start, LANE)
    lanes = lax.broadcasted_iota(jnp.int32, (1, LANE), 1).astype(F32)
    blocks = [
        jnp.where(column == lanes + float(LANE * k), scale, 0.0).astype(dtype)
        for k in range(columns // LANE)
    ]
    return jnp.concatenate(blocks, axis=1)


def params():
    return pltpu.CompilerParams(vmem_limit_bytes=VMEM_LIMIT)


def pick_body(first, index_hbm, centers_hbm, keep_ref, send_ref, pick_ref, index_ref, centers_ref, sems):
    sub = lax.axis_index("sub")
    blocks, count, block = centers_ref.shape
    rows = index_ref.shape[1]
    half = rows // 2
    size = half // CHUNKS
    copies = [pltpu.make_async_copy(index_hbm, index_ref, sems.at[blocks])] + [
        pltpu.make_async_copy(
            centers_hbm.at[:, pl.ds(first + k * block, block)], centers_ref.at[k], sems.at[k]
        )
        for k in range(blocks)
    ]
    for copy in copies:
        copy.start()
    copies[0].wait()
    start = (lax.axis_index("center") * 2 + sub) * count
    pick = pick_rows(index_ref, count, start, BF16, 1.0)
    for part, turn in enumerate(turns()):
        begin = jnp.where(sub == part, 0, half)
        for chunk in range(CHUNKS):
            to = pl.multiple_of(begin + (chunk ^ turn) * size, size)
            at = part * half + chunk * size
            pick_ref[pl.ds(to, size), :] = pick[at : at + size]
    for k in range(blocks):
        copies[k + 1].wait()
        found = dot(pick_ref[...], centers_ref[k], NN).astype(BF16)
        keep_ref[:, k * block : (k + 1) * block] = found[:half]
        send_ref[:, k * block : (k + 1) * block] = found[half:]


def pick_batch(batch_index, centers, part):
    rows = batch_index.shape[1]
    count, depth = centers.shape
    depth = depth // PARTS
    block = 512
    half = jax.ShapeDtypeStruct((rows // 2, depth), BF16)
    hbm = pl.BlockSpec(memory_space=pltpu.HBM)
    vmem = pl.BlockSpec(memory_space=pltpu.VMEM)
    return pl.pallas_call(
        functools.partial(pick_body, part * depth),
        in_specs=[hbm, hbm],
        out_specs=[vmem, vmem],
        out_shape=[half, half],
        scratch_shapes=[
            pltpu.VMEM((rows, count), BF16),
            pltpu.VMEM((1, rows), jnp.int32),
            pltpu.VMEM((depth // block, count, block), BF16),
            pltpu.SemaphoreType.DMA((depth // block + 1,)),
        ],
        compiler_params=params(),
        cost_estimate=pl.CostEstimate(
            flops=2 * rows * count * depth, bytes_accessed=2 * depth * (count + rows), transcendentals=0
        ),
        name="pick_batch",
    )(batch_index, centers)


def spread_body(
    first, classes, index_ref, eigvec_ref, weights_ref,
    high1_ref, low1_ref, high2_ref, low2_ref, spread_ref, all_ref,
):
    rank, points = eigvec_ref.shape
    count = weights_ref.shape[1]
    local = index_ref[...] - (lax.axis_index("center") * 2 + lax.axis_index("sub")) * count
    slots = lax.broadcasted_iota(jnp.int32, (count, points), 0)
    pick = jnp.where(slots == local, 1.0, 0.0).astype(BF16)
    vec = eigvec_ref[...]
    high = vec.astype(BF16)
    rest = vec - high.astype(F32)
    mid = rest.astype(BF16)
    low = (rest - mid.astype(F32)).astype(BF16)
    spread = dot(high, pick, NT) + dot(mid, pick, NT) + dot(low, pick, NT)
    spread_ref[...] = spread
    all_ref[:rank] = spread
    all_ref[rank : rank + classes] = weights_ref[...]
    all_ref[rank + classes :] = jnp.zeros((all_ref.shape[0] - rank - classes, count), F32)
    for begin, high_ref, low_ref in ((0, high1_ref, low1_ref), (first, high2_ref, low2_ref)):
        high_ref[...], low_ref[...] = two(all_ref[begin : begin + high_ref.shape[0]])


def spread_weights(nys_index, eigvec, weights, first, second):
    classes, count = weights.shape
    rank, points = eigvec.shape
    return pl.pallas_call(
        functools.partial(spread_body, first, classes),
        out_shape=[
            jax.ShapeDtypeStruct((first, count), BF16),
            jax.ShapeDtypeStruct((first, count), BF16),
            jax.ShapeDtypeStruct((second, count), BF16),
            jax.ShapeDtypeStruct((second, count), BF16),
            jax.ShapeDtypeStruct((rank, count), F32),
        ],
        scratch_shapes=[pltpu.VMEM((first + second, count), F32)],
        compiler_params=params(),
        cost_estimate=pl.CostEstimate(
            flops=6 * rank * points * count, bytes_accessed=8 * (first + second) * count, transcendentals=0
        ),
        name="spread_weights",
    )(nys_index, eigvec, weights)


def norms_body(centers_ref, norm_ref):
    wide = centers_ref[...].astype(F32)
    norm = jnp.sum(wide * wide, axis=1, keepdims=True)
    norm_ref[...] = jnp.broadcast_to(norm, norm_ref.shape)


def center_norms(centers):
    count, depth = centers.shape
    block = 256
    return pl.pallas_call(
        norms_body,
        grid=(count // block,),
        in_specs=[pl.BlockSpec((block, depth), lambda i: (i, 0))],
        out_specs=pl.BlockSpec((block, LANE), lambda i: (i, 0)),
        out_shape=jax.ShapeDtypeStruct((count, LANE), F32),
        compiler_params=params(),
        cost_estimate=pl.CostEstimate(flops=2 * count * depth, bytes_accessed=2 * count * depth, transcendentals=0),
        name="center_norms",
    )(centers)


def gather_batch(mine_ref, other_ref, batch_ref):
    lower = lax.axis_index("sub") == 0
    half = mine_ref.shape[0]
    size = half // CHUNKS
    for part, turn in enumerate(turns()):
        for chunk in range(CHUNKS):
            at = slice(chunk * size, (chunk + 1) * size)
            same = lower if part == 0 else jnp.logical_not(lower)
            to = pl.multiple_of(part * half + (chunk ^ turn) * size, size)
            batch_ref[pl.ds(to, size), :] = jnp.where(same, mine_ref[at], other_ref[at])


def nearer(first, centers_ref, batch_ref):
    rows, depth = batch_ref.shape
    batch = batch_ref[...].astype(F32)
    norm = jnp.sum(batch * batch, axis=1, keepdims=True)
    cross = dot(centers_ref[:, first : first + depth], batch_ref[...], NT)
    return jnp.broadcast_to(norm, (rows, LANE)).T[0:1] - 2.0 * cross


def product(high_ref, low_ref, value_high, value_low, total_ref, keep_ref, send_ref):
    half = keep_ref.shape[1]
    high = high_ref[...]
    total_ref[...] = dot(high, value_high, NN) + (dot(high, value_low, NN) + dot(low_ref[...], value_high, NN))
    lower = lax.axis_index("sub") == 0
    size = keep_ref.shape[0] // CHUNKS
    for chunk in range(CHUNKS):
        at = slice(chunk * size, (chunk + 1) * size)
        first, second = [
            total_ref[pl.ds(pl.multiple_of((chunk ^ turn) * size, 8), size), part * half : (part + 1) * half]
            for part, turn in enumerate(turns())
        ]
        keep_ref[at] = jnp.where(lower, first, second)
        send_ref[at] = jnp.where(lower, second, first)


def distance_body(mine_ref, other_ref, centers_ref, norm_ref, total_ref, batch_ref):
    gather_batch(mine_ref, other_ref, batch_ref)
    total_ref[...] = norm_ref[:, 0:1] + nearer(0, centers_ref, batch_ref)


def predict_body(
    mine_ref, other_ref, centers_ref, before_ref, high_ref, low_ref,
    keep_ref, send_ref, value_high_ref, value_low_ref, batch_ref, total_ref,
):
    depth = centers_ref.shape[1]
    gather_batch(mine_ref, other_ref, batch_ref)
    square = jnp.maximum(before_ref[...] + nearer(depth - batch_ref.shape[1], centers_ref, batch_ref), 0.0)
    value_high, value_low = two(jnp.exp(jnp.sqrt(square) * (-1.0 / math.sqrt(depth))))
    value_high_ref[...] = value_high
    value_low_ref[...] = value_low
    product(high_ref, low_ref, value_high, value_low, total_ref, keep_ref, send_ref)


def distances(mine, other, centers, norms):
    half, depth = mine.shape
    rows = 2 * half
    count = centers.shape[0]
    vmem = pl.BlockSpec(memory_space=pltpu.VMEM)
    return pl.pallas_call(
        distance_body,
        in_specs=[vmem] * 4,
        out_specs=vmem,
        out_shape=jax.ShapeDtypeStruct((count, rows), F32),
        scratch_shapes=[pltpu.VMEM((rows, depth), BF16)],
        compiler_params=params(),
        cost_estimate=pl.CostEstimate(
            flops=2 * rows * count * depth, bytes_accessed=2 * depth * (count + rows), transcendentals=0
        ),
        name="distances",
    )(mine, other, centers, norms)


def predict(mine, other, centers, before, high, low):
    half, depth = mine.shape
    rows = 2 * half
    count = centers.shape[0]
    padded = high.shape[0]
    out = jax.ShapeDtypeStruct((padded, half), F32)
    value = jax.ShapeDtypeStruct((count, rows), BF16)
    vmem = pl.BlockSpec(memory_space=pltpu.VMEM)
    return pl.pallas_call(
        predict_body,
        in_specs=[vmem] * 6,
        out_specs=[vmem] * 4,
        out_shape=[out, out, value, value],
        scratch_shapes=[pltpu.VMEM((rows, depth), BF16), pltpu.VMEM((padded, rows), F32)],
        compiler_params=params(),
        cost_estimate=pl.CostEstimate(
            flops=2 * rows * count * (depth + 3 * padded),
            bytes_accessed=2 * depth * (count + rows) + 4 * padded * (count + rows),
            transcendentals=2 * rows * count,
        ),
        name="predict",
    )(mine, other, centers, before, high, low)


def more_body(high_ref, low_ref, value_high_ref, value_low_ref, keep_ref, send_ref, total_ref):
    product(high_ref, low_ref, value_high_ref[...], value_low_ref[...], total_ref, keep_ref, send_ref)


def predict_more(high, low, value_high, value_low):
    padded = high.shape[0]
    count, rows = value_high.shape
    out = jax.ShapeDtypeStruct((padded, rows // 2), F32)
    return pl.pallas_call(
        more_body,
        out_shape=[out, out],
        scratch_shapes=[pltpu.VMEM((padded, rows), F32)],
        compiler_params=params(),
        cost_estimate=pl.CostEstimate(
            flops=6 * rows * count * padded, bytes_accessed=4 * padded * (count + rows), transcendentals=0
        ),
        name="predict_more",
    )(high, low, value_high, value_low)


def gather_total(mine_ref, other_ref, total_ref):
    lower = lax.axis_index("sub") == 0
    half = mine_ref.shape[1]
    size = mine_ref.shape[0] // CHUNKS
    for part, turn in enumerate(turns()):
        for chunk in range(CHUNKS):
            at = slice(chunk * size, (chunk + 1) * size)
            same = lower if part == 0 else jnp.logical_not(lower)
            to = pl.multiple_of((chunk ^ turn) * size, 8)
            total_ref[pl.ds(to, size), part * half : (part + 1) * half] = jnp.where(
                same, mine_ref[at], other_ref[at]
            )


def write_rows(begin, skip, total_ref, targets_ref, weights_ref, high_ref, low_ref, new_hbm, out_hbm, new_ref, sems):
    rows = new_ref.shape[0]
    blocks = sems.shape[0] - 1
    bounds = [8 * (rows // 8 * k // blocks) for k in range(blocks)] + [rows]
    high_right = high_ref[...]
    low_right = low_ref[...]
    copies = [
        pltpu.make_async_copy(
            total_ref.at[pl.ds(skip, rows)], out_hbm.at[pl.ds(begin, rows)], sems.at[blocks]
        )
    ]
    copies[0].start()
    for k in range(blocks):
        low_end, high_end = bounds[k : k + 2]
        here = slice(begin + low_end, begin + high_end)
        high, low = two(total_ref[skip + low_end : skip + high_end] - targets_ref[here])
        new_ref[low_end:high_end] = weights_ref[here] + (
            dot(high, high_right, NN) + (dot(high, low_right, NN) + dot(low, high_right, NN))
        )
        copy = pltpu.make_async_copy(
            new_ref.at[pl.ds(low_end, high_end - low_end)],
            new_hbm.at[pl.ds(begin + low_end, high_end - low_end)],
            sems.at[k],
        )
        copy.start()
        copies.append(copy)
    for copy in copies:
        copy.wait()


def update_body(
    mine_ref, other_ref, targets_ref, index_ref, eigval_ref, spread_ref, weights_ref,
    new_hbm, out_hbm, high_ref, low_ref, total_ref, new_ref, sems,
):
    start = (lax.axis_index("center") * 2 + lax.axis_index("sub")) * spread_ref.shape[1]
    rank, count = spread_ref.shape
    gather_total(mine_ref, other_ref, total_ref)
    value = eigval_ref[...]
    lowest = jnp.min(value, axis=1, keepdims=True)
    scaled = (1.0 - lowest / value) / value
    mixed_high, mixed_low = two(total_ref[:rank].T * (0.25 * scaled))
    spread_high, spread_low = two(spread_ref[...])
    turned = dot(mixed_high, spread_high, NN) + (
        dot(mixed_high, spread_low, NN) + dot(mixed_low, spread_high, NN)
    )
    high_ref[...], low_ref[...] = two(turned - pick_rows(index_ref, count, start, F32, 0.25))
    write_rows(0, rank, total_ref, targets_ref, weights_ref, high_ref, low_ref, new_hbm, out_hbm, new_ref, sems)


def update(mine, other, targets, batch_index, eigval, spread, weights):
    classes, count = weights.shape
    padded, half = mine.shape
    rows = 2 * half
    rank = spread.shape[0]
    here = padded - rank
    vmem = pl.BlockSpec(memory_space=pltpu.VMEM)
    hbm = pl.BlockSpec(memory_space=pl.ANY)
    right = jax.ShapeDtypeStruct((rows, count), BF16)
    return pl.pallas_call(
        update_body,
        in_specs=[vmem] * 7,
        out_specs=[hbm, hbm, vmem, vmem],
        out_shape=[
            jax.ShapeDtypeStruct((classes, count), F32),
            jax.ShapeDtypeStruct((classes, rows), F32),
            right,
            right,
        ],
        scratch_shapes=[
            pltpu.VMEM((padded, rows), F32),
            pltpu.VMEM((here, count), F32),
            pltpu.SemaphoreType.DMA((4,)),
        ],
        compiler_params=params(),
        cost_estimate=pl.CostEstimate(
            flops=6 * rows * count * (here + rank), bytes_accessed=8 * here * (count + rows), transcendentals=0
        ),
        name="update",
    )(mine, other, targets, batch_index, eigval, spread, weights)


def update_more_body(
    begin, mine_ref, other_ref, targets_ref, weights_ref, high_ref, low_ref, new_in, out_in,
    new_hbm, out_hbm, total_ref, new_ref, sems,
):
    gather_total(mine_ref, other_ref, total_ref)
    write_rows(begin, 0, total_ref, targets_ref, weights_ref, high_ref, low_ref, new_hbm, out_hbm, new_ref, sems)


def update_more(mine, other, targets, weights, high, low, new, out, begin):
    classes, count = weights.shape
    padded, half = mine.shape
    rows = 2 * half
    here = classes - begin
    vmem = pl.BlockSpec(memory_space=pltpu.VMEM)
    hbm = pl.BlockSpec(memory_space=pl.ANY)
    return pl.pallas_call(
        functools.partial(update_more_body, begin),
        in_specs=[vmem] * 6 + [hbm] * 2,
        out_specs=[hbm, hbm],
        out_shape=[
            jax.ShapeDtypeStruct((classes, count), F32),
            jax.ShapeDtypeStruct((classes, rows), F32),
        ],
        input_output_aliases={6: 0, 7: 1},
        scratch_shapes=[
            pltpu.VMEM((padded, rows), F32),
            pltpu.VMEM((here, count), F32),
            pltpu.SemaphoreType.DMA((6,)),
        ],
        compiler_params=params(),
        cost_estimate=pl.CostEstimate(
            flops=6 * rows * count * here, bytes_accessed=8 * here * (count + rows), transcendentals=0
        ),
        name="update_more",
    )(mine, other, targets, weights, high, low, new, out)


def swap(x, chips, level):
    bits = chips.bit_length() - 1
    flip = [1, 1] if level < 0 else [2 << walk(sub, bits)[level] for sub in range(2)]
    return lax.ppermute(x, AXES, [(i, i ^ flip[i & 1]) for i in range(2 * chips)])


def total_of(keep, send, chips, tied=()):
    keep = keep + swap(send, chips, -1)
    for level in range(chips.bit_length() - 1):
        if level >= HALVINGS:
            keep = keep + swap(keep, chips, level)
            continue
        half = keep.shape[0] // 2
        keep, send = keep[:half], keep[half:]
        if level == 1 and tied:
            send, *tied = lax.optimization_barrier((send, *tied))
        keep = keep + swap(send, chips, level)
    for level in reversed(range(HALVINGS)):
        keep = jnp.concatenate([keep, swap(keep, chips, level)])
    return [keep, swap(keep, chips, -1), *tied]


def on_device(chips, centers, weights, targets, batch_index, nys_index, eigvec, eigval):
    rows = batch_index.shape[0]
    classes = weights.shape[1]
    rank = eigvec.shape[1]
    unit = 8 * CHUNKS
    units = -(-(classes + rank) // unit)
    first = (units + 1) // 2 * unit
    second = units * unit - first
    begin = first - rank
    batch_index = batch_index.reshape(1, rows)
    weights = weights.T
    targets = targets.T
    far = [pltpu.with_memory_space_constraint(x, pltpu.HBM) for x in (batch_index, centers)]
    picked = [pick_batch(*far, part) for part in range(PARTS)]
    ready = [
        center_norms(centers),
        *spread_weights(nys_index.reshape(1, -1), eigvec.T, weights, first, second),
    ]
    mine, other, norms, high1, low1, high2, low2, spread = total_of(*picked[0], chips, ready)
    before = distances(mine, other, centers, norms)
    keep, send, value_high, value_low = predict(*total_of(*picked[1], chips), centers, before, high1, low1)
    one = total_of(keep, send, chips)
    another = total_of(*predict_more(high2, low2, value_high, value_low), chips)
    new, out, high, low = update(*one, targets, batch_index, eigval.reshape(1, rank), spread, weights)
    new, out = update_more(*another, targets, weights, high, low, new, out, begin)
    return new.T, out.T


def solution(mesh):
    return jax.shard_map(
        functools.partial(on_device, mesh.shape["center"]),
        mesh=mesh,
        in_specs=(
            P(("parts", "center", "sub"), None),
            P(("parts", "center", "sub"), None),
            P("parts", None),
            P("parts"),
            P(("parts", "center", "sub")),
            P(("parts", "center", "sub"), None),
            P("parts"),
        ),
        out_specs=(P(("parts", "center", "sub"), None), P("parts", None)),
        check_vma=False,
    )
```

```python
import functools
import math

import jax
import jax.numpy as jnp
from jax import lax
from jax.experimental import pallas as pl
from jax.experimental.pallas import tpu as pltpu
from jax.sharding import PartitionSpec as P

F32 = jnp.float32
BF16 = jnp.bfloat16
AXES = ("center", "sub")
HALVINGS = 2
CHUNKS = 1 << HALVINGS
LANE = 128
PARTS = 2
UPDATES = 5
NT = (((1,), (1,)), ((), ()))
NN = (((1,), (0,)), ((), ()))
VMEM_LIMIT = 24 * 1024 * 1024


def dot(a, b, dims):
    return lax.dot_general(a, b, dims, preferred_element_type=F32)


def walk(sub, bits):
    order = list(range(bits))
    return order if sub == 0 else order[1::-1] + order[2:]


def turns():
    center = lax.axis_index("center")
    return [
        sum(((center >> bit) & 1) << (HALVINGS - 1 - k) for k, bit in enumerate(walk(sub, HALVINGS + 1)[:HALVINGS]))
        for sub in range(2)
    ]


def column_of(row, width):
    return jnp.broadcast_to(row.astype(F32), (width, row.shape[1])).T


def two(x):
    high = x.astype(BF16)
    return high, (x - high.astype(F32)).astype(BF16)


def pick_rows(index_ref, columns, start, dtype, scale):
    column = column_of(index_ref[...] - start, LANE)
    lanes = lax.broadcasted_iota(jnp.int32, (1, LANE), 1).astype(F32)
    blocks = [
        jnp.where(column == lanes + float(LANE * k), scale, 0.0).astype(dtype)
        for k in range(columns // LANE)
    ]
    return jnp.concatenate(blocks, axis=1)


def params():
    return pltpu.CompilerParams(vmem_limit_bytes=VMEM_LIMIT)


def pick_body(first, index_hbm, centers_hbm, keep_ref, send_ref, pick_ref, index_ref, centers_ref, sems):
    sub = lax.axis_index("sub")
    blocks, count, block = centers_ref.shape
    rows = index_ref.shape[1]
    half = rows // 2
    size = half // CHUNKS
    copies = [pltpu.make_async_copy(index_hbm, index_ref, sems.at[blocks])] + [
        pltpu.make_async_copy(
            centers_hbm.at[:, pl.ds(first + k * block, block)], centers_ref.at[k], sems.at[k]
        )
        for k in range(blocks)
    ]
    for copy in copies:
        copy.start()
    copies[0].wait()
    start = (lax.axis_index("center") * 2 + sub) * count
    pick = pick_rows(index_ref, count, start, BF16, 1.0)
    for part, turn in enumerate(turns()):
        begin = jnp.where(sub == part, 0, half)
        for chunk in range(CHUNKS):
            to = pl.multiple_of(begin + (chunk ^ turn) * size, size)
            at = part * half + chunk * size
            pick_ref[pl.ds(to, size), :] = pick[at : at + size]
    for k in range(blocks):
        copies[k + 1].wait()
        found = dot(pick_ref[...], centers_ref[k], NN).astype(BF16)
        keep_ref[:, k * block : (k + 1) * block] = found[:half]
        send_ref[:, k * block : (k + 1) * block] = found[half:]


def pick_batch(batch_index, centers, part):
    rows = batch_index.shape[1]
    count, depth = centers.shape
    depth = depth // PARTS
    block = 512
    half = jax.ShapeDtypeStruct((rows // 2, depth), BF16)
    hbm = pl.BlockSpec(memory_space=pltpu.HBM)
    vmem = pl.BlockSpec(memory_space=pltpu.VMEM)
    return pl.pallas_call(
        functools.partial(pick_body, part * depth),
        in_specs=[hbm, hbm],
        out_specs=[vmem, vmem],
        out_shape=[half, half],
        scratch_shapes=[
            pltpu.VMEM((rows, count), BF16),
            pltpu.VMEM((1, rows), jnp.int32),
            pltpu.VMEM((depth // block, count, block), BF16),
            pltpu.SemaphoreType.DMA((depth // block + 1,)),
        ],
        compiler_params=params(),
        cost_estimate=pl.CostEstimate(
            flops=2 * rows * count * depth, bytes_accessed=2 * depth * (count + rows), transcendentals=0
        ),
        name="pick_batch",
    )(batch_index, centers)


def spread_body(classes, index_ref, eigvec_ref, weights_ref, high_ref, low_ref, spread_ref):
    rank, points = eigvec_ref.shape
    count = weights_ref.shape[1]
    local = index_ref[...] - (lax.axis_index("center") * 2 + lax.axis_index("sub")) * count
    slots = lax.broadcasted_iota(jnp.int32, (count, points), 0)
    pick = jnp.where(slots == local, 1.0, 0.0).astype(BF16)
    vec = eigvec_ref[...]
    vec_high = vec.astype(BF16)
    rest = vec - vec_high.astype(F32)
    vec_mid = rest.astype(BF16)
    vec_low = (rest - vec_mid.astype(F32)).astype(BF16)
    spread = dot(vec_high, pick, NT) + dot(vec_mid, pick, NT) + dot(vec_low, pick, NT)
    spread_ref[...] = spread
    blank = jnp.zeros((high_ref.shape[0] - rank - classes, count), F32)
    for at, rows in ((0, spread), (rank, weights_ref[...]), (rank + classes, blank)):
        high_ref[at : at + rows.shape[0]], low_ref[at : at + rows.shape[0]] = two(rows)


def spread_weights(nys_index, eigvec, weights, padded):
    classes, count = weights.shape
    rank, points = eigvec.shape
    return pl.pallas_call(
        functools.partial(spread_body, classes),
        out_shape=[
            jax.ShapeDtypeStruct((padded, count), BF16),
            jax.ShapeDtypeStruct((padded, count), BF16),
            jax.ShapeDtypeStruct((rank, count), F32),
        ],
        compiler_params=params(),
        cost_estimate=pl.CostEstimate(
            flops=6 * rank * points * count, bytes_accessed=8 * padded * count, transcendentals=0
        ),
        name="spread_weights",
    )(nys_index, eigvec, weights)


def norms_body(centers_ref, norm_ref):
    wide = centers_ref[...].astype(F32)
    norm = jnp.sum(wide * wide, axis=1, keepdims=True)
    norm_ref[...] = jnp.broadcast_to(norm, norm_ref.shape)


def center_norms(centers):
    count, depth = centers.shape
    block = 256
    return pl.pallas_call(
        norms_body,
        grid=(count // block,),
        in_specs=[pl.BlockSpec((block, depth), lambda i: (i, 0))],
        out_specs=pl.BlockSpec((block, LANE), lambda i: (i, 0)),
        out_shape=jax.ShapeDtypeStruct((count, LANE), F32),
        compiler_params=params(),
        cost_estimate=pl.CostEstimate(flops=2 * count * depth, bytes_accessed=2 * count * depth, transcendentals=0),
        name="center_norms",
    )(centers)


def gather_batch(mine_ref, other_ref, batch_ref):
    lower = lax.axis_index("sub") == 0
    half = mine_ref.shape[0]
    size = half // CHUNKS
    for part, turn in enumerate(turns()):
        for chunk in range(CHUNKS):
            at = slice(chunk * size, (chunk + 1) * size)
            same = lower if part == 0 else jnp.logical_not(lower)
            to = pl.multiple_of(part * half + (chunk ^ turn) * size, size)
            batch_ref[pl.ds(to, size), :] = jnp.where(same, mine_ref[at], other_ref[at])


def nearer(first, centers_ref, batch_ref):
    rows, depth = batch_ref.shape
    batch = batch_ref[...].astype(F32)
    norm = jnp.sum(batch * batch, axis=1, keepdims=True)
    cross = dot(centers_ref[:, first : first + depth], batch_ref[...], NT)
    return jnp.broadcast_to(norm, (rows, LANE)).T[0:1] - 2.0 * cross


def product(high_ref, low_ref, value_high, value_low, total_ref, keep_ref, send_ref):
    half = keep_ref.shape[1]
    high = high_ref[...]
    total_ref[...] = dot(high, value_high, NN) + (dot(high, value_low, NN) + dot(low_ref[...], value_high, NN))
    lower = lax.axis_index("sub") == 0
    size = keep_ref.shape[0] // CHUNKS
    for chunk in range(CHUNKS):
        at = slice(chunk * size, (chunk + 1) * size)
        first, second = [
            total_ref[pl.ds(pl.multiple_of((chunk ^ turn) * size, 8), size), part * half : (part + 1) * half]
            for part, turn in enumerate(turns())
        ]
        keep_ref[at] = jnp.where(lower, first, second)
        send_ref[at] = jnp.where(lower, second, first)


def distance_body(mine_ref, other_ref, centers_ref, norm_ref, total_ref, batch_ref):
    gather_batch(mine_ref, other_ref, batch_ref)
    total_ref[...] = norm_ref[:, 0:1] + nearer(0, centers_ref, batch_ref)


def predict_body(
    mine_ref, other_ref, centers_ref, before_ref, high_ref, low_ref,
    keep_ref, send_ref, batch_ref, total_ref,
):
    depth = centers_ref.shape[1]
    gather_batch(mine_ref, other_ref, batch_ref)
    square = jnp.maximum(before_ref[...] + nearer(depth - batch_ref.shape[1], centers_ref, batch_ref), 0.0)
    value_high, value_low = two(jnp.exp(jnp.sqrt(square) * (-1.0 / math.sqrt(depth))))
    product(high_ref, low_ref, value_high, value_low, total_ref, keep_ref, send_ref)


def distances(mine, other, centers, norms):
    half, depth = mine.shape
    rows = 2 * half
    count = centers.shape[0]
    vmem = pl.BlockSpec(memory_space=pltpu.VMEM)
    return pl.pallas_call(
        distance_body,
        in_specs=[vmem] * 4,
        out_specs=vmem,
        out_shape=jax.ShapeDtypeStruct((count, rows), F32),
        scratch_shapes=[pltpu.VMEM((rows, depth), BF16)],
        compiler_params=params(),
        cost_estimate=pl.CostEstimate(
            flops=2 * rows * count * depth, bytes_accessed=2 * depth * (count + rows), transcendentals=0
        ),
        name="distances",
    )(mine, other, centers, norms)


def predict(mine, other, centers, before, high, low):
    half, depth = mine.shape
    rows = 2 * half
    count = centers.shape[0]
    padded = high.shape[0]
    out = jax.ShapeDtypeStruct((padded, half), F32)
    vmem = pl.BlockSpec(memory_space=pltpu.VMEM)
    return pl.pallas_call(
        predict_body,
        in_specs=[vmem] * 6,
        out_specs=[vmem] * 2,
        out_shape=[out, out],
        scratch_shapes=[pltpu.VMEM((rows, depth), BF16), pltpu.VMEM((padded, rows), F32)],
        compiler_params=params(),
        cost_estimate=pl.CostEstimate(
            flops=2 * rows * count * (depth + 3 * padded),
            bytes_accessed=2 * depth * (count + rows) + 4 * padded * (count + rows),
            transcendentals=2 * rows * count,
        ),
        name="predict",
    )(mine, other, centers, before, high, low)


def gather_total(mine_ref, other_ref, total_ref):
    lower = lax.axis_index("sub") == 0
    half = mine_ref.shape[1]
    size = mine_ref.shape[0] // CHUNKS
    for part, turn in enumerate(turns()):
        for chunk in range(CHUNKS):
            at = slice(chunk * size, (chunk + 1) * size)
            same = lower if part == 0 else jnp.logical_not(lower)
            to = pl.multiple_of((chunk ^ turn) * size, 8)
            total_ref[pl.ds(to, size), part * half : (part + 1) * half] = jnp.where(
                same, mine_ref[at], other_ref[at]
            )


def update_body(
    mine_ref, other_ref, targets_ref, index_ref, eigval_ref, spread_ref, weights_ref,
    new_hbm, out_hbm, total_ref, new_ref, sems,
):
    rank, count = spread_ref.shape
    classes = new_ref.shape[0]
    start = (lax.axis_index("center") * 2 + lax.axis_index("sub")) * count
    gather_total(mine_ref, other_ref, total_ref)
    copies = [pltpu.make_async_copy(total_ref.at[pl.ds(rank, classes)], out_hbm, sems.at[UPDATES])]
    copies[0].start()
    value = eigval_ref[...]
    lowest = jnp.min(value, axis=1, keepdims=True)
    scaled = (1.0 - lowest / value) / value
    mixed_high, mixed_low = two(total_ref[:rank].T * (0.25 * scaled))
    spread_high, spread_low = two(spread_ref[...])
    turned = dot(mixed_high, spread_high, NN) + (
        dot(mixed_high, spread_low, NN) + dot(mixed_low, spread_high, NN)
    )
    right_high, right_low = two(turned - pick_rows(index_ref, count, start, F32, 0.25))
    size = classes // UPDATES
    for k in range(UPDATES):
        at = slice(k * size, (k + 1) * size)
        high, low = two(total_ref[rank + k * size : rank + (k + 1) * size] - targets_ref[at])
        new_ref[at] = weights_ref[at] + (
            dot(high, right_high, NN) + (dot(high, right_low, NN) + dot(low, right_high, NN))
        )
        rows = pl.ds(k * size, size)
        copies.append(pltpu.make_async_copy(new_ref.at[rows], new_hbm.at[rows], sems.at[k]))
        copies[-1].start()
    for copy in copies:
        copy.wait()


def update(mine, other, targets, batch_index, eigval, spread, weights):
    classes, count = weights.shape
    padded, half = mine.shape
    rows = 2 * half
    rank = spread.shape[0]
    vmem = pl.BlockSpec(memory_space=pltpu.VMEM)
    hbm = pl.BlockSpec(memory_space=pl.ANY)
    return pl.pallas_call(
        update_body,
        in_specs=[vmem] * 7,
        out_specs=[hbm, hbm],
        out_shape=[
            jax.ShapeDtypeStruct((classes, count), F32),
            jax.ShapeDtypeStruct((classes, rows), F32),
        ],
        scratch_shapes=[
            pltpu.VMEM((padded, rows), F32),
            pltpu.VMEM((classes, count), F32),
            pltpu.SemaphoreType.DMA((UPDATES + 1,)),
        ],
        compiler_params=params(),
        cost_estimate=pl.CostEstimate(
            flops=6 * rows * count * (classes + rank), bytes_accessed=8 * classes * (count + rows), transcendentals=0
        ),
        name="update",
    )(mine, other, targets, batch_index, eigval, spread, weights)


def swap(x, chips, level):
    bits = chips.bit_length() - 1
    flip = [1, 1] if level < 0 else [2 << walk(sub, bits)[level] for sub in range(2)]
    return lax.ppermute(x, AXES, [(i, i ^ flip[i & 1]) for i in range(2 * chips)])


def total_of(keep, send, chips, tied=()):
    keep = keep + swap(send, chips, -1)
    for level in range(chips.bit_length() - 1):
        if level >= HALVINGS:
            keep = keep + swap(keep, chips, level)
            continue
        half = keep.shape[0] // 2
        keep, send = keep[:half], keep[half:]
        if level == 1 and tied:
            send, *tied = lax.optimization_barrier((send, *tied))
        keep = keep + swap(send, chips, level)
    for level in reversed(range(HALVINGS)):
        keep = jnp.concatenate([keep, swap(keep, chips, level)])
    return [keep, swap(keep, chips, -1), *tied]


def on_device(chips, centers, weights, targets, batch_index, nys_index, eigvec, eigval):
    rows = batch_index.shape[0]
    classes = weights.shape[1]
    rank = eigvec.shape[1]
    unit = 8 * CHUNKS
    padded = -(-(classes + rank) // unit) * unit
    batch_index = batch_index.reshape(1, rows)
    weights = weights.T
    targets = targets.T
    far = [pltpu.with_memory_space_constraint(x, pltpu.HBM) for x in (batch_index, centers)]
    picked = [pick_batch(*far, part) for part in range(PARTS)]
    ready = [
        center_norms(centers),
        *spread_weights(nys_index.reshape(1, -1), eigvec.T, weights, padded),
    ]
    mine, other, norms, high, low, spread = total_of(*picked[0], chips, ready)
    before = distances(mine, other, centers, norms)
    parts = predict(*total_of(*picked[1], chips), centers, before, high, low)
    new, out = update(*total_of(*parts, chips), targets, batch_index, eigval.reshape(1, rank), spread, weights)
    return new.T, out.T


def solution(mesh):
    return jax.shard_map(
        functools.partial(on_device, mesh.shape["center"]),
        mesh=mesh,
        in_specs=(
            P(("parts", "center", "sub"), None),
            P(("parts", "center", "sub"), None),
            P("parts", None),
            P("parts"),
            P(("parts", "center", "sub")),
            P(("parts", "center", "sub"), None),
            P("parts"),
        ),
        out_specs=(P(("parts", "center", "sub"), None), P("parts", None)),
        check_vma=False,
    )
```

```python
import functools
import math

import jax
import jax.numpy as jnp
from jax import lax
from jax.experimental import pallas as pl
from jax.experimental.pallas import tpu as pltpu
from jax.sharding import PartitionSpec as P

F32 = jnp.float32
BF16 = jnp.bfloat16
AXES = ("center", "sub")
HALVINGS = 2
CHUNKS = 1 << HALVINGS
LANE = 128
PARTS = 2
SLOTS = 32
NT = (((1,), (1,)), ((), ()))
NN = (((1,), (0,)), ((), ()))
VMEM_LIMIT = 24 * 1024 * 1024


def dot(a, b, dims):
    return lax.dot_general(a, b, dims, preferred_element_type=F32)


def walk(sub, bits):
    order = list(range(bits))
    return order if sub == 0 else order[1::-1] + order[2:]


def far_first(sub, bits):
    order = list(range(bits))[::-1]
    return order if sub == 0 else order[:-2] + order[:-3:-1]


def turns():
    center = lax.axis_index("center")
    return [
        sum(((center >> bit) & 1) << (HALVINGS - 1 - k) for k, bit in enumerate(walk(sub, HALVINGS + 1)[:HALVINGS]))
        for sub in range(2)
    ]


def column_of(row, width):
    return jnp.broadcast_to(row.astype(F32), (width, row.shape[1])).T


def two(x):
    high = x.astype(BF16)
    return high, (x - high.astype(F32)).astype(BF16)


def pick_rows(index_ref, columns, start, dtype, scale):
    column = column_of(index_ref[...] - start, LANE)
    lanes = lax.broadcasted_iota(jnp.int32, (1, LANE), 1).astype(F32)
    blocks = [
        jnp.where(column == lanes + float(LANE * k), scale, 0.0).astype(dtype)
        for k in range(columns // LANE)
    ]
    return jnp.concatenate(blocks, axis=1)


def params():
    return pltpu.CompilerParams(vmem_limit_bytes=VMEM_LIMIT)


def pick_body(first, index_hbm, centers_hbm, keep_ref, send_ref, pick_ref, index_ref, centers_ref, sems):
    sub = lax.axis_index("sub")
    blocks, count, block = centers_ref.shape
    rows = index_ref.shape[1]
    half = rows // 2
    size = half // CHUNKS
    copies = [pltpu.make_async_copy(index_hbm, index_ref, sems.at[blocks])] + [
        pltpu.make_async_copy(
            centers_hbm.at[:, pl.ds(first + k * block, block)], centers_ref.at[k], sems.at[k]
        )
        for k in range(blocks)
    ]
    for copy in copies:
        copy.start()
    copies[0].wait()
    start = (lax.axis_index("center") * 2 + sub) * count
    pick = pick_rows(index_ref, count, start, BF16, 1.0)
    for part, turn in enumerate(turns()):
        begin = jnp.where(sub == part, 0, half)
        for chunk in range(CHUNKS):
            to = pl.multiple_of(begin + (chunk ^ turn) * size, size)
            at = part * half + chunk * size
            pick_ref[pl.ds(to, size), :] = pick[at : at + size]
    for k in range(blocks):
        copies[k + 1].wait()
        found = dot(pick_ref[...], centers_ref[k], NN).astype(BF16)
        keep_ref[:, k * block : (k + 1) * block] = found[:half]
        send_ref[:, k * block : (k + 1) * block] = found[half:]


def pick_batch(batch_index, centers, part):
    rows = batch_index.shape[1]
    count, depth = centers.shape
    depth = depth // PARTS
    block = 512
    half = jax.ShapeDtypeStruct((rows // 2, depth), BF16)
    hbm = pl.BlockSpec(memory_space=pltpu.HBM)
    vmem = pl.BlockSpec(memory_space=pltpu.VMEM)
    return pl.pallas_call(
        functools.partial(pick_body, part * depth),
        in_specs=[hbm, hbm],
        out_specs=[vmem, vmem],
        out_shape=[half, half],
        scratch_shapes=[
            pltpu.VMEM((rows, count), BF16),
            pltpu.VMEM((1, rows), jnp.int32),
            pltpu.VMEM((depth // block, count, block), BF16),
            pltpu.SemaphoreType.DMA((depth // block + 1,)),
        ],
        compiler_params=params(),
        cost_estimate=pl.CostEstimate(
            flops=2 * rows * count * depth, bytes_accessed=2 * depth * (count + rows), transcendentals=0
        ),
        name="pick_batch",
    )(batch_index, centers)


def pack_body(first, index_hbm, rank_hbm, centers_hbm, out_ref, index_ref, rank_ref, centers_ref, sems):
    blocks, count, block = centers_ref.shape
    rows = index_ref.shape[1]
    copies = [
        pltpu.make_async_copy(index_hbm, index_ref, sems.at[blocks]),
        pltpu.make_async_copy(rank_hbm, rank_ref, sems.at[blocks + 1]),
    ] + [
        pltpu.make_async_copy(
            centers_hbm.at[:, pl.ds(first + k * block, block)], centers_ref.at[k], sems.at[k]
        )
        for k in range(blocks)
    ]
    for copy in copies:
        copy.start()
    copies[0].wait()
    copies[1].wait()
    start = (lax.axis_index("center") * 2 + lax.axis_index("sub")) * count
    local = index_ref[...] - start
    rank = jnp.where((local >= 0) & (local < count), rank_ref[...], -1)
    slots = lax.broadcasted_iota(jnp.int32, (SLOTS, rows), 0)
    to_slot = jnp.where(slots == rank, 1.0, 0.0).astype(BF16)
    pick = dot(to_slot, pick_rows(index_ref, count, start, BF16, 1.0), NN).astype(BF16)
    for k in range(blocks):
        copies[k + 2].wait()
        out_ref[:, k * block : (k + 1) * block] = dot(pick, centers_ref[k], NN).astype(BF16)


def pack_rows(batch_index, rank, centers, part):
    rows = batch_index.shape[1]
    count, depth = centers.shape
    depth = depth // PARTS
    block = 512
    hbm = pl.BlockSpec(memory_space=pltpu.HBM)
    return pl.pallas_call(
        functools.partial(pack_body, part * depth),
        in_specs=[hbm, hbm, hbm],
        out_specs=pl.BlockSpec(memory_space=pltpu.VMEM),
        out_shape=jax.ShapeDtypeStruct((SLOTS, depth), BF16),
        scratch_shapes=[
            pltpu.VMEM((1, rows), jnp.int32),
            pltpu.VMEM((1, rows), jnp.int32),
            pltpu.VMEM((depth // block, count, block), BF16),
            pltpu.SemaphoreType.DMA((depth // block + 2,)),
        ],
        compiler_params=params(),
        cost_estimate=pl.CostEstimate(
            flops=2 * SLOTS * count * depth, bytes_accessed=2 * depth * (count + SLOTS), transcendentals=0
        ),
        name="pack_rows",
    )(batch_index, rank, centers)


def spread_body(
    first, classes, index_ref, eigvec_ref, weights_ref,
    high1_ref, low1_ref, high2_ref, low2_ref, spread_ref, all_ref,
):
    rank, points = eigvec_ref.shape
    count = weights_ref.shape[1]
    local = index_ref[...] - (lax.axis_index("center") * 2 + lax.axis_index("sub")) * count
    slots = lax.broadcasted_iota(jnp.int32, (count, points), 0)
    pick = jnp.where(slots == local, 1.0, 0.0).astype(BF16)
    vec = eigvec_ref[...]
    high = vec.astype(BF16)
    rest = vec - high.astype(F32)
    mid = rest.astype(BF16)
    low = (rest - mid.astype(F32)).astype(BF16)
    spread = dot(high, pick, NT) + dot(mid, pick, NT) + dot(low, pick, NT)
    spread_ref[...] = spread
    all_ref[:rank] = spread
    all_ref[rank : rank + classes] = weights_ref[...]
    all_ref[rank + classes :] = jnp.zeros((all_ref.shape[0] - rank - classes, count), F32)
    for begin, high_ref, low_ref in ((0, high1_ref, low1_ref), (first, high2_ref, low2_ref)):
        high_ref[...], low_ref[...] = two(all_ref[begin : begin + high_ref.shape[0]])


def spread_weights(nys_index, eigvec, weights, first, second):
    classes, count = weights.shape
    rank, points = eigvec.shape
    return pl.pallas_call(
        functools.partial(spread_body, first, classes),
        out_shape=[
            jax.ShapeDtypeStruct((first, count), BF16),
            jax.ShapeDtypeStruct((first, count), BF16),
            jax.ShapeDtypeStruct((second, count), BF16),
            jax.ShapeDtypeStruct((second, count), BF16),
            jax.ShapeDtypeStruct((rank, count), F32),
        ],
        scratch_shapes=[pltpu.VMEM((first + second, count), F32)],
        compiler_params=params(),
        cost_estimate=pl.CostEstimate(
            flops=6 * rank * points * count, bytes_accessed=8 * (first + second) * count, transcendentals=0
        ),
        name="spread_weights",
    )(nys_index, eigvec, weights)


def norms_body(centers_ref, norm_ref):
    wide = centers_ref[...].astype(F32)
    norm = jnp.sum(wide * wide, axis=1, keepdims=True)
    norm_ref[...] = jnp.broadcast_to(norm, norm_ref.shape)


def center_norms(centers):
    count, depth = centers.shape
    block = 256
    return pl.pallas_call(
        norms_body,
        grid=(count // block,),
        in_specs=[pl.BlockSpec((block, depth), lambda i: (i, 0))],
        out_specs=pl.BlockSpec((block, LANE), lambda i: (i, 0)),
        out_shape=jax.ShapeDtypeStruct((count, LANE), F32),
        compiler_params=params(),
        cost_estimate=pl.CostEstimate(flops=2 * count * depth, bytes_accessed=2 * count * depth, transcendentals=0),
        name="center_norms",
    )(centers)


def gather_batch(mine_ref, other_ref, select_ref, batch_ref):
    half = mine_ref.shape[0]
    found = dot(select_ref[:, :half], mine_ref[...], NN) + dot(select_ref[:, half:], other_ref[...], NN)
    batch_ref[...] = found.astype(BF16)


def nearer(first, centers_ref, batch_ref):
    rows, depth = batch_ref.shape
    batch = batch_ref[...].astype(F32)
    norm = jnp.sum(batch * batch, axis=1, keepdims=True)
    cross = dot(centers_ref[:, first : first + depth], batch_ref[...], NT)
    return jnp.broadcast_to(norm, (rows, LANE)).T[0:1] - 2.0 * cross


def product(high_ref, low_ref, value_high, value_low, total_ref, keep_ref, send_ref):
    half = keep_ref.shape[1]
    high = high_ref[...]
    total_ref[...] = dot(high, value_high, NN) + (dot(high, value_low, NN) + dot(low_ref[...], value_high, NN))
    lower = lax.axis_index("sub") == 0
    size = keep_ref.shape[0] // CHUNKS
    for chunk in range(CHUNKS):
        at = slice(chunk * size, (chunk + 1) * size)
        first, second = [
            total_ref[pl.ds(pl.multiple_of((chunk ^ turn) * size, 8), size), part * half : (part + 1) * half]
            for part, turn in enumerate(turns())
        ]
        keep_ref[at] = jnp.where(lower, first, second)
        send_ref[at] = jnp.where(lower, second, first)


def distance_body(mine_ref, other_ref, select_ref, centers_ref, norm_ref, total_ref, batch_ref):
    gather_batch(mine_ref, other_ref, select_ref, batch_ref)
    total_ref[...] = norm_ref[:, 0:1] + nearer(0, centers_ref, batch_ref)


def predict_body(
    mine_ref, other_ref, select_ref, centers_ref, before_ref, high_ref, low_ref,
    keep_ref, send_ref, value_high_ref, value_low_ref, batch_ref, total_ref,
):
    depth = centers_ref.shape[1]
    gather_batch(mine_ref, other_ref, select_ref, batch_ref)
    square = jnp.maximum(before_ref[...] + nearer(depth - batch_ref.shape[1], centers_ref, batch_ref), 0.0)
    value_high, value_low = two(jnp.exp(jnp.sqrt(square) * (-1.0 / math.sqrt(depth))))
    value_high_ref[...] = value_high
    value_low_ref[...] = value_low
    product(high_ref, low_ref, value_high, value_low, total_ref, keep_ref, send_ref)


def distances(mine, other, select, centers, norms):
    depth = mine.shape[1]
    rows = select.shape[0]
    count = centers.shape[0]
    vmem = pl.BlockSpec(memory_space=pltpu.VMEM)
    return pl.pallas_call(
        distance_body,
        in_specs=[vmem] * 5,
        out_specs=vmem,
        out_shape=jax.ShapeDtypeStruct((count, rows), F32),
        scratch_shapes=[pltpu.VMEM((rows, depth), BF16)],
        compiler_params=params(),
        cost_estimate=pl.CostEstimate(
            flops=2 * rows * count * depth, bytes_accessed=2 * depth * (count + rows), transcendentals=0
        ),
        name="distances",
    )(mine, other, select, centers, norms)


def predict(mine, other, select, centers, before, high, low):
    depth = mine.shape[1]
    rows = select.shape[0]
    half = rows // 2
    count = centers.shape[0]
    padded = high.shape[0]
    out = jax.ShapeDtypeStruct((padded, half), F32)
    value = jax.ShapeDtypeStruct((count, rows), BF16)
    vmem = pl.BlockSpec(memory_space=pltpu.VMEM)
    return pl.pallas_call(
        predict_body,
        in_specs=[vmem] * 7,
        out_specs=[vmem] * 4,
        out_shape=[out, out, value, value],
        scratch_shapes=[pltpu.VMEM((rows, depth), BF16), pltpu.VMEM((padded, rows), F32)],
        compiler_params=params(),
        cost_estimate=pl.CostEstimate(
            flops=2 * rows * count * (depth + 3 * padded),
            bytes_accessed=2 * depth * (count + rows) + 4 * padded * (count + rows),
            transcendentals=2 * rows * count,
        ),
        name="predict",
    )(mine, other, select, centers, before, high, low)


def more_body(high_ref, low_ref, value_high_ref, value_low_ref, keep_ref, send_ref, total_ref):
    product(high_ref, low_ref, value_high_ref[...], value_low_ref[...], total_ref, keep_ref, send_ref)


def predict_more(high, low, value_high, value_low):
    padded = high.shape[0]
    count, rows = value_high.shape
    out = jax.ShapeDtypeStruct((padded, rows // 2), F32)
    return pl.pallas_call(
        more_body,
        out_shape=[out, out],
        scratch_shapes=[pltpu.VMEM((padded, rows), F32)],
        compiler_params=params(),
        cost_estimate=pl.CostEstimate(
            flops=6 * rows * count * padded, bytes_accessed=4 * padded * (count + rows), transcendentals=0
        ),
        name="predict_more",
    )(high, low, value_high, value_low)


def gather_total(mine_ref, other_ref, total_ref):
    lower = lax.axis_index("sub") == 0
    half = mine_ref.shape[1]
    size = mine_ref.shape[0] // CHUNKS
    for part, turn in enumerate(turns()):
        for chunk in range(CHUNKS):
            at = slice(chunk * size, (chunk + 1) * size)
            same = lower if part == 0 else jnp.logical_not(lower)
            to = pl.multiple_of((chunk ^ turn) * size, 8)
            total_ref[pl.ds(to, size), part * half : (part + 1) * half] = jnp.where(
                same, mine_ref[at], other_ref[at]
            )


def write_rows(begin, skip, total_ref, targets_ref, weights_ref, high_ref, low_ref, new_hbm, out_hbm, new_ref, sems):
    rows = new_ref.shape[0]
    blocks = sems.shape[0] - 1
    bounds = [8 * (rows // 8 * k // blocks) for k in range(blocks)] + [rows]
    high_right = high_ref[...]
    low_right = low_ref[...]
    copies = [
        pltpu.make_async_copy(
            total_ref.at[pl.ds(skip, rows)], out_hbm.at[pl.ds(begin, rows)], sems.at[blocks]
        )
    ]
    copies[0].start()
    for k in range(blocks):
        low_end, high_end = bounds[k : k + 2]
        here = slice(begin + low_end, begin + high_end)
        high, low = two(total_ref[skip + low_end : skip + high_end] - targets_ref[here])
        new_ref[low_end:high_end] = weights_ref[here] + (
            dot(high, high_right, NN) + (dot(high, low_right, NN) + dot(low, high_right, NN))
        )
        copy = pltpu.make_async_copy(
            new_ref.at[pl.ds(low_end, high_end - low_end)],
            new_hbm.at[pl.ds(begin + low_end, high_end - low_end)],
            sems.at[k],
        )
        copy.start()
        copies.append(copy)
    for copy in copies:
        copy.wait()


def update_body(
    mine_ref, other_ref, targets_ref, index_ref, eigval_ref, spread_ref, weights_ref,
    new_hbm, out_hbm, high_ref, low_ref, total_ref, new_ref, sems,
):
    start = (lax.axis_index("center") * 2 + lax.axis_index("sub")) * spread_ref.shape[1]
    rank, count = spread_ref.shape
    gather_total(mine_ref, other_ref, total_ref)
    value = eigval_ref[...]
    lowest = jnp.min(value, axis=1, keepdims=True)
    scaled = (1.0 - lowest / value) / value
    mixed_high, mixed_low = two(total_ref[:rank].T * (0.25 * scaled))
    spread_high, spread_low = two(spread_ref[...])
    turned = dot(mixed_high, spread_high, NN) + (
        dot(mixed_high, spread_low, NN) + dot(mixed_low, spread_high, NN)
    )
    high_ref[...], low_ref[...] = two(turned - pick_rows(index_ref, count, start, F32, 0.25))
    write_rows(0, rank, total_ref, targets_ref, weights_ref, high_ref, low_ref, new_hbm, out_hbm, new_ref, sems)


def update(mine, other, targets, batch_index, eigval, spread, weights):
    classes, count = weights.shape
    padded, half = mine.shape
    rows = 2 * half
    rank = spread.shape[0]
    here = padded - rank
    vmem = pl.BlockSpec(memory_space=pltpu.VMEM)
    hbm = pl.BlockSpec(memory_space=pl.ANY)
    right = jax.ShapeDtypeStruct((rows, count), BF16)
    return pl.pallas_call(
        update_body,
        in_specs=[vmem] * 7,
        out_specs=[hbm, hbm, vmem, vmem],
        out_shape=[
            jax.ShapeDtypeStruct((classes, count), F32),
            jax.ShapeDtypeStruct((classes, rows), F32),
            right,
            right,
        ],
        scratch_shapes=[
            pltpu.VMEM((padded, rows), F32),
            pltpu.VMEM((here, count), F32),
            pltpu.SemaphoreType.DMA((4,)),
        ],
        compiler_params=params(),
        cost_estimate=pl.CostEstimate(
            flops=6 * rows * count * (here + rank), bytes_accessed=8 * here * (count + rows), transcendentals=0
        ),
        name="update",
    )(mine, other, targets, batch_index, eigval, spread, weights)


def update_more_body(
    begin, mine_ref, other_ref, targets_ref, weights_ref, high_ref, low_ref, new_in, out_in,
    new_hbm, out_hbm, total_ref, new_ref, sems,
):
    gather_total(mine_ref, other_ref, total_ref)
    write_rows(begin, 0, total_ref, targets_ref, weights_ref, high_ref, low_ref, new_hbm, out_hbm, new_ref, sems)


def update_more(mine, other, targets, weights, high, low, new, out, begin):
    classes, count = weights.shape
    padded, half = mine.shape
    rows = 2 * half
    here = classes - begin
    vmem = pl.BlockSpec(memory_space=pltpu.VMEM)
    hbm = pl.BlockSpec(memory_space=pl.ANY)
    return pl.pallas_call(
        functools.partial(update_more_body, begin),
        in_specs=[vmem] * 6 + [hbm] * 2,
        out_specs=[hbm, hbm],
        out_shape=[
            jax.ShapeDtypeStruct((classes, count), F32),
            jax.ShapeDtypeStruct((classes, rows), F32),
        ],
        input_output_aliases={6: 0, 7: 1},
        scratch_shapes=[
            pltpu.VMEM((padded, rows), F32),
            pltpu.VMEM((here, count), F32),
            pltpu.SemaphoreType.DMA((6,)),
        ],
        compiler_params=params(),
        cost_estimate=pl.CostEstimate(
            flops=6 * rows * count * here, bytes_accessed=8 * here * (count + rows), transcendentals=0
        ),
        name="update_more",
    )(mine, other, targets, weights, high, low, new, out)


def swap(x, chips, order=None, level=0):
    flip = [2 << order(sub, chips.bit_length() - 1)[level] if order else 1 for sub in range(2)]
    return lax.ppermute(x, AXES, [(i, i ^ flip[i & 1]) for i in range(2 * chips)])


def tie(x, tied):
    x, *tied = lax.optimization_barrier((x, *tied))
    return x, tied


def total_of(keep, send, chips, tied=()):
    keep = keep + swap(send, chips)
    for level in range(chips.bit_length() - 1):
        if level >= HALVINGS:
            keep = keep + swap(keep, chips, walk, level)
            continue
        half = keep.shape[0] // 2
        keep, send = keep[:half], keep[half:]
        if level == 1 and tied:
            send, tied = tie(send, tied)
        keep = keep + swap(send, chips, walk, level)
    for level in reversed(range(HALVINGS)):
        keep = jnp.concatenate([keep, swap(keep, chips, walk, level)])
    return [keep, swap(keep, chips), *tied]


def all_of(keep, chips, tied=()):
    for level in range(chips.bit_length() - 1):
        if level == 1 and tied:
            keep, tied = tie(keep, tied)
        keep = jnp.concatenate([keep, swap(keep, chips, far_first, level)])
    return [keep, swap(keep, chips), *tied]


def one_hot(slot, slots):
    return (slot[:, None] == jnp.arange(slots, dtype=jnp.int32)[None, :]).astype(BF16)


def select_summed(rows):
    row = jnp.arange(rows, dtype=jnp.int32)
    half = rows // 2
    size = half // CHUNKS
    turn = jnp.stack(turns())[row // half]
    chunk = (row % half // size) ^ turn
    far = jnp.where(row // half == lax.axis_index("sub"), 0, half)
    return one_hot(far + chunk * size + row % size, rows)


def select_packed(owner, rank, chips):
    away = (owner >> 1) ^ lax.axis_index("center")
    places = [
        sum(((away >> bit) & 1) << k for k, bit in enumerate(far_first(sub, chips.bit_length() - 1)))
        for sub in range(2)
    ]
    place = jnp.where(owner & 1 == 0, *places)
    far = jnp.where(owner & 1 == lax.axis_index("sub"), 0, chips * SLOTS)
    return one_hot(far + place * SLOTS + rank, 2 * chips * SLOTS)


def step(packed, chips, owner, rank, centers, weights, targets, batch_index, nys_index, eigvec, eigval):
    rows = batch_index.shape[1]
    classes, count = weights.shape
    depth = eigvec.shape[0]
    unit = 8 * CHUNKS
    units = -(-(classes + depth) // unit)
    first = (units + 1) // 2 * unit
    second = units * unit - first
    far = [pltpu.with_memory_space_constraint(x, pltpu.HBM) for x in (batch_index, centers)]
    ready = [center_norms(centers), *spread_weights(nys_index, eigvec, weights, first, second)]
    if packed:
        rank_row = rank.reshape(1, rows)
        ready.append(select_packed(owner, rank, chips))
        slots = [pack_rows(far[0], rank_row, far[1], part) for part in range(PARTS)]
        mine, other, norms, high1, low1, high2, low2, spread, select = all_of(slots[0], chips, ready)
        late = all_of(slots[1], chips)
    else:
        ready.append(select_summed(rows))
        picked = [pick_batch(*far, part) for part in range(PARTS)]
        mine, other, norms, high1, low1, high2, low2, spread, select = total_of(*picked[0], chips, ready)
        late = total_of(*picked[1], chips)
    before = distances(mine, other, select, centers, norms)
    keep, send, value_high, value_low = predict(*late, select, centers, before, high1, low1)
    one = total_of(keep, send, chips)
    another = total_of(*predict_more(high2, low2, value_high, value_low), chips)
    new, out, high, low = update(*one, targets, batch_index, eigval, spread, weights)
    return update_more(*another, targets, weights, high, low, new, out, first - depth)


def on_device(chips, centers, weights, targets, batch_index, nys_index, eigvec, eigval):
    row = jnp.arange(batch_index.shape[0], dtype=jnp.int32)
    owner = batch_index // centers.shape[0]
    earlier = (owner[None, :] == owner[:, None]) & (row[None, :] < row[:, None])
    rank = jnp.sum(earlier.astype(jnp.int32), axis=1)
    new, out = lax.cond(
        jnp.max(rank) < SLOTS,
        functools.partial(step, True, chips),
        functools.partial(step, False, chips),
        owner,
        rank,
        centers,
        weights.T,
        targets.T,
        batch_index.reshape(1, -1),
        nys_index.reshape(1, -1),
        eigvec.T,
        eigval.reshape(1, -1),
    )
    return new.T, out.T


def solution(mesh):
    return jax.shard_map(
        functools.partial(on_device, mesh.shape["center"]),
        mesh=mesh,
        in_specs=(
            P(("parts", "center", "sub"), None),
            P(("parts", "center", "sub"), None),
            P("parts", None),
            P("parts"),
            P(("parts", "center", "sub")),
            P(("parts", "center", "sub"), None),
            P("parts"),
        ),
        out_specs=(P(("parts", "center", "sub"), None), P("parts", None)),
        check_vma=False,
    )
```

```python
import functools
import math

import jax
import jax.numpy as jnp
from jax import lax
from jax.experimental import pallas as pl
from jax.experimental.pallas import tpu as pltpu
from jax.sharding import PartitionSpec as P

F32 = jnp.float32
BF16 = jnp.bfloat16
AXES = ("center", "sub")
HALVINGS = 2
CHUNKS = 1 << HALVINGS
LANE = 128
PARTS = 2
SLOTS = 32
TIED = 2
NT = (((1,), (1,)), ((), ()))
NN = (((1,), (0,)), ((), ()))
VMEM_LIMIT = 24 * 1024 * 1024


def dot(a, b, dims):
    return lax.dot_general(a, b, dims, preferred_element_type=F32)


def walk(sub, bits):
    order = list(range(bits))
    return order if sub == 0 else order[1::-1] + order[2:]


def far_first(sub, bits):
    order = list(range(bits))[::-1]
    return order if sub == 0 else order[:-2] + order[:-3:-1]


def turns():
    center = lax.axis_index("center")
    return [
        sum(((center >> bit) & 1) << (HALVINGS - 1 - k) for k, bit in enumerate(walk(sub, HALVINGS + 1)[:HALVINGS]))
        for sub in range(2)
    ]


def column_of(row, width):
    return jnp.broadcast_to(row.astype(F32), (width, row.shape[1])).T


def two(x):
    high = x.astype(BF16)
    return high, (x - high.astype(F32)).astype(BF16)


def pick_rows(index_ref, columns, start, dtype, scale):
    column = column_of(index_ref[...] - start, LANE)
    lanes = lax.broadcasted_iota(jnp.int32, (1, LANE), 1).astype(F32)
    blocks = [
        jnp.where(column == lanes + float(LANE * k), scale, 0.0).astype(dtype)
        for k in range(columns // LANE)
    ]
    return jnp.concatenate(blocks, axis=1)


def params():
    return pltpu.CompilerParams(vmem_limit_bytes=VMEM_LIMIT)


def pack_body(first, offset_ref, index_hbm, centers_hbm, out_ref, index_ref, centers_ref, sems):
    blocks, count, block = centers_ref.shape
    rows = index_ref.shape[1]
    copies = [pltpu.make_async_copy(index_hbm, index_ref, sems.at[blocks])] + [
        pltpu.make_async_copy(
            centers_hbm.at[:, pl.ds(first + k * block, block)], centers_ref.at[k], sems.at[k]
        )
        for k in range(blocks)
    ]
    for copy in copies:
        copy.start()
    copies[0].wait()
    start = (lax.axis_index("center") * 2 + lax.axis_index("sub")) * count
    local = index_ref[...] - start
    here = jnp.where((local >= 0) & (local < count), 1.0, 0.0)
    earlier = lax.broadcasted_iota(jnp.int32, (rows, rows), 0) < lax.broadcasted_iota(jnp.int32, (rows, rows), 1)
    rank = dot(jnp.broadcast_to(here, (8, rows)).astype(BF16), jnp.where(earlier, 1.0, 0.0).astype(BF16), NN)[0:1]
    slots = (lax.broadcasted_iota(jnp.int32, (SLOTS, 1), 0) + offset_ref[0]).astype(F32)
    to_slot = jnp.where(slots == rank, here, 0.0).astype(BF16)
    pick = dot(to_slot, pick_rows(index_ref, count, start, BF16, 1.0), NN).astype(BF16)
    for k in range(blocks):
        copies[k + 1].wait()
        out_ref[:, k * block : (k + 1) * block] = dot(pick, centers_ref[k], NN).astype(BF16)


def pack_rows(offset, batch_index, centers, part):
    rows = batch_index.shape[1]
    count, depth = centers.shape
    depth = depth // PARTS
    block = 512
    hbm = pl.BlockSpec(memory_space=pltpu.HBM)
    return pl.pallas_call(
        functools.partial(pack_body, part * depth),
        in_specs=[pl.BlockSpec(memory_space=pltpu.SMEM), hbm, hbm],
        out_specs=pl.BlockSpec(memory_space=pltpu.VMEM),
        out_shape=jax.ShapeDtypeStruct((SLOTS, depth), BF16),
        scratch_shapes=[
            pltpu.VMEM((1, rows), jnp.int32),
            pltpu.VMEM((depth // block, count, block), BF16),
            pltpu.SemaphoreType.DMA((depth // block + 1,)),
        ],
        compiler_params=params(),
        cost_estimate=pl.CostEstimate(
            flops=2 * SLOTS * count * depth, bytes_accessed=2 * depth * (count + SLOTS), transcendentals=0
        ),
        name="pack_rows",
    )(offset, batch_index, centers)


def spread_body(
    first, classes, index_ref, eigvec_ref, weights_ref,
    high1_ref, low1_ref, high2_ref, low2_ref, spread_ref, all_ref,
):
    rank, points = eigvec_ref.shape
    count = weights_ref.shape[1]
    local = index_ref[...] - (lax.axis_index("center") * 2 + lax.axis_index("sub")) * count
    slots = lax.broadcasted_iota(jnp.int32, (count, points), 0)
    pick = jnp.where(slots == local, 1.0, 0.0).astype(BF16)
    vec = eigvec_ref[...]
    high = vec.astype(BF16)
    rest = vec - high.astype(F32)
    mid = rest.astype(BF16)
    low = (rest - mid.astype(F32)).astype(BF16)
    spread = dot(high, pick, NT) + dot(mid, pick, NT) + dot(low, pick, NT)
    spread_ref[...] = spread
    all_ref[:rank] = spread
    all_ref[rank : rank + classes] = weights_ref[...]
    all_ref[rank + classes :] = jnp.zeros((all_ref.shape[0] - rank - classes, count), F32)
    for begin, high_ref, low_ref in ((0, high1_ref, low1_ref), (first, high2_ref, low2_ref)):
        high_ref[...], low_ref[...] = two(all_ref[begin : begin + high_ref.shape[0]])


def spread_weights(nys_index, eigvec, weights, first, second):
    classes, count = weights.shape
    rank, points = eigvec.shape
    return pl.pallas_call(
        functools.partial(spread_body, first, classes),
        out_shape=[
            jax.ShapeDtypeStruct((first, count), BF16),
            jax.ShapeDtypeStruct((first, count), BF16),
            jax.ShapeDtypeStruct((second, count), BF16),
            jax.ShapeDtypeStruct((second, count), BF16),
            jax.ShapeDtypeStruct((rank, count), F32),
        ],
        scratch_shapes=[pltpu.VMEM((first + second, count), F32)],
        compiler_params=params(),
        cost_estimate=pl.CostEstimate(
            flops=6 * rank * points * count, bytes_accessed=8 * (first + second) * count, transcendentals=0
        ),
        name="spread_weights",
    )(nys_index, eigvec, weights)


def norms_body(centers_ref, norm_ref):
    wide = centers_ref[...].astype(F32)
    norm = jnp.sum(wide * wide, axis=1, keepdims=True)
    norm_ref[...] = jnp.broadcast_to(norm, norm_ref.shape)


def center_norms(centers):
    count, depth = centers.shape
    block = 256
    return pl.pallas_call(
        norms_body,
        grid=(count // block,),
        in_specs=[pl.BlockSpec((block, depth), lambda i: (i, 0))],
        out_specs=pl.BlockSpec((block, LANE), lambda i: (i, 0)),
        out_shape=jax.ShapeDtypeStruct((count, LANE), F32),
        compiler_params=params(),
        cost_estimate=pl.CostEstimate(flops=2 * count * depth, bytes_accessed=2 * count * depth, transcendentals=0),
        name="center_norms",
    )(centers)


def gather_batch(mine_ref, other_ref, select_ref, more_ref, batch_ref):
    half = mine_ref.shape[0]
    found = dot(select_ref[:, :half], mine_ref[...], NN) + dot(select_ref[:, half:], other_ref[...], NN)
    batch_ref[...] = (found + more_ref[...].astype(F32)).astype(BF16)


def nearer(first, centers_ref, batch_ref):
    rows, depth = batch_ref.shape
    batch = batch_ref[...].astype(F32)
    norm = jnp.sum(batch * batch, axis=1, keepdims=True)
    cross = dot(centers_ref[:, first : first + depth], batch_ref[...], NT)
    return jnp.broadcast_to(norm, (rows, LANE)).T[0:1] - 2.0 * cross


def product(high_ref, low_ref, value_high, value_low, total_ref, keep_ref, send_ref):
    half = keep_ref.shape[1]
    high = high_ref[...]
    total_ref[...] = dot(high, value_high, NN) + (dot(high, value_low, NN) + dot(low_ref[...], value_high, NN))
    lower = lax.axis_index("sub") == 0
    size = keep_ref.shape[0] // CHUNKS
    for chunk in range(CHUNKS):
        at = slice(chunk * size, (chunk + 1) * size)
        first, second = [
            total_ref[pl.ds(pl.multiple_of((chunk ^ turn) * size, 8), size), part * half : (part + 1) * half]
            for part, turn in enumerate(turns())
        ]
        keep_ref[at] = jnp.where(lower, first, second)
        send_ref[at] = jnp.where(lower, second, first)


def distance_body(mine_ref, other_ref, select_ref, more_ref, centers_ref, norm_ref, total_ref, batch_ref):
    gather_batch(mine_ref, other_ref, select_ref, more_ref, batch_ref)
    total_ref[...] = norm_ref[:, 0:1] + nearer(0, centers_ref, batch_ref)


def predict_body(
    mine_ref, other_ref, select_ref, more_ref, centers_ref, before_ref, high_ref, low_ref,
    keep_ref, send_ref, value_high_ref, value_low_ref, batch_ref, total_ref,
):
    depth = centers_ref.shape[1]
    gather_batch(mine_ref, other_ref, select_ref, more_ref, batch_ref)
    square = jnp.maximum(before_ref[...] + nearer(depth - batch_ref.shape[1], centers_ref, batch_ref), 0.0)
    value_high, value_low = two(jnp.exp(jnp.sqrt(square) * (-1.0 / math.sqrt(depth))))
    value_high_ref[...] = value_high
    value_low_ref[...] = value_low
    product(high_ref, low_ref, value_high, value_low, total_ref, keep_ref, send_ref)


def distances(mine, other, select, more, centers, norms):
    depth = mine.shape[1]
    rows = select.shape[0]
    count = centers.shape[0]
    vmem = pl.BlockSpec(memory_space=pltpu.VMEM)
    return pl.pallas_call(
        distance_body,
        in_specs=[vmem] * 6,
        out_specs=vmem,
        out_shape=jax.ShapeDtypeStruct((count, rows), F32),
        scratch_shapes=[pltpu.VMEM((rows, depth), BF16)],
        compiler_params=params(),
        cost_estimate=pl.CostEstimate(
            flops=2 * rows * count * depth, bytes_accessed=2 * depth * (count + rows), transcendentals=0
        ),
        name="distances",
    )(mine, other, select, more, centers, norms)


def predict(mine, other, select, more, centers, before, high, low):
    depth = mine.shape[1]
    rows = select.shape[0]
    half = rows // 2
    count = centers.shape[0]
    padded = high.shape[0]
    out = jax.ShapeDtypeStruct((padded, half), F32)
    value = jax.ShapeDtypeStruct((count, rows), BF16)
    vmem = pl.BlockSpec(memory_space=pltpu.VMEM)
    return pl.pallas_call(
        predict_body,
        in_specs=[vmem] * 8,
        out_specs=[vmem] * 4,
        out_shape=[out, out, value, value],
        scratch_shapes=[pltpu.VMEM((rows, depth), BF16), pltpu.VMEM((padded, rows), F32)],
        compiler_params=params(),
        cost_estimate=pl.CostEstimate(
            flops=2 * rows * count * (depth + 3 * padded),
            bytes_accessed=2 * depth * (count + rows) + 4 * padded * (count + rows),
            transcendentals=2 * rows * count,
        ),
        name="predict",
    )(mine, other, select, more, centers, before, high, low)


def more_body(high_ref, low_ref, value_high_ref, value_low_ref, keep_ref, send_ref, total_ref):
    product(high_ref, low_ref, value_high_ref[...], value_low_ref[...], total_ref, keep_ref, send_ref)


def predict_more(high, low, value_high, value_low):
    padded = high.shape[0]
    count, rows = value_high.shape
    out = jax.ShapeDtypeStruct((padded, rows // 2), F32)
    return pl.pallas_call(
        more_body,
        out_shape=[out, out],
        scratch_shapes=[pltpu.VMEM((padded, rows), F32)],
        compiler_params=params(),
        cost_estimate=pl.CostEstimate(
            flops=6 * rows * count * padded, bytes_accessed=4 * padded * (count + rows), transcendentals=0
        ),
        name="predict_more",
    )(high, low, value_high, value_low)


def gather_total(mine_ref, other_ref, total_ref):
    lower = lax.axis_index("sub") == 0
    half = mine_ref.shape[1]
    size = mine_ref.shape[0] // CHUNKS
    for part, turn in enumerate(turns()):
        for chunk in range(CHUNKS):
            at = slice(chunk * size, (chunk + 1) * size)
            same = lower if part == 0 else jnp.logical_not(lower)
            to = pl.multiple_of((chunk ^ turn) * size, 8)
            total_ref[pl.ds(to, size), part * half : (part + 1) * half] = jnp.where(
                same, mine_ref[at], other_ref[at]
            )


def write_rows(begin, skip, total_ref, targets_ref, weights_ref, high_ref, low_ref, new_hbm, out_hbm, new_ref, sems):
    rows = new_ref.shape[0]
    blocks = sems.shape[0] - 1
    bounds = [8 * (rows // 8 * k // blocks) for k in range(blocks)] + [rows]
    high_right = high_ref[...]
    low_right = low_ref[...]
    copies = [
        pltpu.make_async_copy(
            total_ref.at[pl.ds(skip, rows)], out_hbm.at[pl.ds(begin, rows)], sems.at[blocks]
        )
    ]
    copies[0].start()
    for k in range(blocks):
        low_end, high_end = bounds[k : k + 2]
        here = slice(begin + low_end, begin + high_end)
        high, low = two(total_ref[skip + low_end : skip + high_end] - targets_ref[here])
        new_ref[low_end:high_end] = weights_ref[here] + (
            dot(high, high_right, NN) + (dot(high, low_right, NN) + dot(low, high_right, NN))
        )
        copy = pltpu.make_async_copy(
            new_ref.at[pl.ds(low_end, high_end - low_end)],
            new_hbm.at[pl.ds(begin + low_end, high_end - low_end)],
            sems.at[k],
        )
        copy.start()
        copies.append(copy)
    for copy in copies:
        copy.wait()


def update_body(
    mine_ref, other_ref, targets_ref, index_ref, eigval_ref, spread_ref, weights_ref,
    new_hbm, out_hbm, high_ref, low_ref, total_ref, new_ref, sems,
):
    start = (lax.axis_index("center") * 2 + lax.axis_index("sub")) * spread_ref.shape[1]
    rank, count = spread_ref.shape
    gather_total(mine_ref, other_ref, total_ref)
    value = eigval_ref[...]
    lowest = jnp.min(value, axis=1, keepdims=True)
    scaled = (1.0 - lowest / value) / value
    mixed_high, mixed_low = two(total_ref[:rank].T * (0.25 * scaled))
    spread_high, spread_low = two(spread_ref[...])
    turned = dot(mixed_high, spread_high, NN) + (
        dot(mixed_high, spread_low, NN) + dot(mixed_low, spread_high, NN)
    )
    high_ref[...], low_ref[...] = two(turned - pick_rows(index_ref, count, start, F32, 0.25))
    write_rows(0, rank, total_ref, targets_ref, weights_ref, high_ref, low_ref, new_hbm, out_hbm, new_ref, sems)


def update(mine, other, targets, batch_index, eigval, spread, weights):
    classes, count = weights.shape
    padded, half = mine.shape
    rows = 2 * half
    rank = spread.shape[0]
    here = padded - rank
    vmem = pl.BlockSpec(memory_space=pltpu.VMEM)
    hbm = pl.BlockSpec(memory_space=pl.ANY)
    right = jax.ShapeDtypeStruct((rows, count), BF16)
    return pl.pallas_call(
        update_body,
        in_specs=[vmem] * 7,
        out_specs=[hbm, hbm, vmem, vmem],
        out_shape=[
            jax.ShapeDtypeStruct((classes, count), F32),
            jax.ShapeDtypeStruct((classes, rows), F32),
            right,
            right,
        ],
        scratch_shapes=[
            pltpu.VMEM((padded, rows), F32),
            pltpu.VMEM((here, count), F32),
            pltpu.SemaphoreType.DMA((4,)),
        ],
        compiler_params=params(),
        cost_estimate=pl.CostEstimate(
            flops=6 * rows * count * (here + rank), bytes_accessed=8 * here * (count + rows), transcendentals=0
        ),
        name="update",
    )(mine, other, targets, batch_index, eigval, spread, weights)


def update_more_body(
    begin, mine_ref, other_ref, targets_ref, weights_ref, high_ref, low_ref, new_in, out_in,
    new_hbm, out_hbm, total_ref, new_ref, sems,
):
    gather_total(mine_ref, other_ref, total_ref)
    write_rows(begin, 0, total_ref, targets_ref, weights_ref, high_ref, low_ref, new_hbm, out_hbm, new_ref, sems)


def update_more(mine, other, targets, weights, high, low, new, out, begin):
    classes, count = weights.shape
    padded, half = mine.shape
    rows = 2 * half
    here = classes - begin
    vmem = pl.BlockSpec(memory_space=pltpu.VMEM)
    hbm = pl.BlockSpec(memory_space=pl.ANY)
    return pl.pallas_call(
        functools.partial(update_more_body, begin),
        in_specs=[vmem] * 6 + [hbm] * 2,
        out_specs=[hbm, hbm],
        out_shape=[
            jax.ShapeDtypeStruct((classes, count), F32),
            jax.ShapeDtypeStruct((classes, rows), F32),
        ],
        input_output_aliases={6: 0, 7: 1},
        scratch_shapes=[
            pltpu.VMEM((padded, rows), F32),
            pltpu.VMEM((here, count), F32),
            pltpu.SemaphoreType.DMA((6,)),
        ],
        compiler_params=params(),
        cost_estimate=pl.CostEstimate(
            flops=6 * rows * count * here, bytes_accessed=8 * here * (count + rows), transcendentals=0
        ),
        name="update_more",
    )(mine, other, targets, weights, high, low, new, out)


def swap(x, chips, order=None, level=0):
    flip = [2 << order(sub, chips.bit_length() - 1)[level] if order else 1 for sub in range(2)]
    return lax.ppermute(x, AXES, [(i, i ^ flip[i & 1]) for i in range(2 * chips)])


def total_of(keep, send, chips):
    keep = keep + swap(send, chips)
    for level in range(chips.bit_length() - 1):
        if level >= HALVINGS:
            keep = keep + swap(keep, chips, walk, level)
            continue
        half = keep.shape[0] // 2
        keep = keep[:half] + swap(keep[half:], chips, walk, level)
    for level in reversed(range(HALVINGS)):
        keep = jnp.concatenate([keep, swap(keep, chips, walk, level)])
    return keep, swap(keep, chips)


def all_of(keep, chips, tied=()):
    for level in range(chips.bit_length() - 1):
        if level == TIED and tied:
            keep, *tied = lax.optimization_barrier((keep, *tied))
        keep = jnp.concatenate([keep, swap(keep, chips, far_first, level)])
    return [keep, swap(keep, chips), *tied]


def select_rows(owner, rank, offset, chips):
    away = (owner >> 1) ^ lax.axis_index("center")
    places = [
        sum(((away >> bit) & 1) << k for k, bit in enumerate(far_first(sub, chips.bit_length() - 1)))
        for sub in range(2)
    ]
    place = jnp.where(owner & 1 == 0, *places)
    far = jnp.where(owner & 1 == lax.axis_index("sub"), 0, chips * SLOTS)
    within = rank - offset
    slot = jnp.where((within >= 0) & (within < SLOTS), far + place * SLOTS + within, -1)
    return (slot[:, None] == jnp.arange(2 * chips * SLOTS, dtype=jnp.int32)[None, :]).astype(BF16)


def more_rows(owner, rank, batch_index, centers, chips):
    most = jnp.max(rank) + 1
    shape = (batch_index.shape[1], centers.shape[1] // PARTS)

    def one_pass(state):
        offset, *found = state
        select = select_rows(owner, rank, offset, chips)
        for part in range(PARTS):
            rows = pack_rows(offset.reshape(1), batch_index, centers, part)
            slots = jnp.concatenate(all_of(rows, chips))
            here = jnp.dot(select, slots, preferred_element_type=F32)
            found[part] = (found[part].astype(F32) + here).astype(BF16)
        return (offset + SLOTS, *found)

    blank = jnp.zeros(shape, BF16)
    return lax.while_loop(lambda state: state[0] < most, one_pass, (jnp.int32(SLOTS), blank, blank))[1:]


def on_device(chips, centers, weights, targets, batch_index, nys_index, eigvec, eigval):
    rows = batch_index.shape[0]
    classes = weights.shape[1]
    depth = eigvec.shape[1]
    unit = 8 * CHUNKS
    units = -(-(classes + depth) // unit)
    first = (units + 1) // 2 * unit
    second = units * unit - first
    row = jnp.arange(rows, dtype=jnp.int32)
    owner = batch_index // centers.shape[0]
    earlier = (owner[None, :] == owner[:, None]) & (row[None, :] < row[:, None])
    rank = jnp.sum(earlier.astype(jnp.int32), axis=1)
    batch_index = batch_index.reshape(1, rows)
    weights = weights.T
    targets = targets.T
    far = [pltpu.with_memory_space_constraint(x, pltpu.HBM) for x in (batch_index, centers)]
    packed = [pack_rows(jnp.zeros(1, jnp.int32), *far, part) for part in range(PARTS)]
    more = more_rows(owner, rank, *far, chips)
    ready = [
        center_norms(centers),
        *spread_weights(nys_index.reshape(1, -1), eigvec.T, weights, first, second),
        select_rows(owner, rank, 0, chips),
    ]
    mine, other, norms, high1, low1, high2, low2, spread, select = all_of(packed[0], chips, ready)
    before = distances(mine, other, select, more[0], centers, norms)
    late = all_of(packed[1], chips)
    keep, send, value_high, value_low = predict(*late, select, more[1], centers, before, high1, low1)
    one = total_of(keep, send, chips)
    another = total_of(*predict_more(high2, low2, value_high, value_low), chips)
    new, out, high, low = update(*one, targets, batch_index, eigval.reshape(1, depth), spread, weights)
    new, out = update_more(*another, targets, weights, high, low, new, out, first - depth)
    return new.T, out.T


def solution(mesh):
    return jax.shard_map(
        functools.partial(on_device, mesh.shape["center"]),
        mesh=mesh,
        in_specs=(
            P(("parts", "center", "sub"), None),
            P(("parts", "center", "sub"), None),
            P("parts", None),
            P("parts"),
            P(("parts", "center", "sub")),
            P(("parts", "center", "sub"), None),
            P("parts"),
        ),
        out_specs=(P(("parts", "center", "sub"), None), P("parts", None)),
        check_vma=False,
    )
```

```python
import functools
import math

import jax
import jax.numpy as jnp
from jax import lax
from jax.experimental import pallas as pl
from jax.experimental.pallas import tpu as pltpu
from jax.sharding import PartitionSpec as P

F32 = jnp.float32
BF16 = jnp.bfloat16
AXES = ("center", "sub")
HALVINGS = 2
CHUNKS = 1 << HALVINGS
LANE = 128
PARTS = 2
SLOTS = 32
NT = (((1,), (1,)), ((), ()))
NN = (((1,), (0,)), ((), ()))
VMEM_LIMIT = 24 * 1024 * 1024


def dot(a, b, dims):
    return lax.dot_general(a, b, dims, preferred_element_type=F32)


def walk(sub, bits):
    order = list(range(bits))
    return order if sub == 0 else order[1::-1] + order[2:]


def far_first(sub, bits):
    order = list(range(bits))[::-1]
    return order if sub == 0 else order[:-2] + order[:-3:-1]


def turns():
    center = lax.axis_index("center")
    return [
        sum(((center >> bit) & 1) << (HALVINGS - 1 - k) for k, bit in enumerate(walk(sub, HALVINGS + 1)[:HALVINGS]))
        for sub in range(2)
    ]


def column_of(row, width):
    return jnp.broadcast_to(row.astype(F32), (width, row.shape[1])).T


def two(x):
    high = x.astype(BF16)
    return high, (x - high.astype(F32)).astype(BF16)


def pick_rows(index_ref, columns, start, dtype, scale):
    column = column_of(index_ref[...] - start, LANE)
    lanes = lax.broadcasted_iota(jnp.int32, (1, LANE), 1).astype(F32)
    blocks = [
        jnp.where(column == lanes + float(LANE * k), scale, 0.0).astype(dtype)
        for k in range(columns // LANE)
    ]
    return jnp.concatenate(blocks, axis=1)


def params():
    return pltpu.CompilerParams(vmem_limit_bytes=VMEM_LIMIT)


def pick_body(first, index_hbm, centers_hbm, keep_ref, send_ref, pick_ref, index_ref, centers_ref, sems):
    sub = lax.axis_index("sub")
    blocks, count, block = centers_ref.shape
    rows = index_ref.shape[1]
    half = rows // 2
    size = half // CHUNKS
    copies = [pltpu.make_async_copy(index_hbm, index_ref, sems.at[blocks])] + [
        pltpu.make_async_copy(
            centers_hbm.at[:, pl.ds(first + k * block, block)], centers_ref.at[k], sems.at[k]
        )
        for k in range(blocks)
    ]
    for copy in copies:
        copy.start()
    copies[0].wait()
    start = (lax.axis_index("center") * 2 + sub) * count
    pick = pick_rows(index_ref, count, start, BF16, 1.0)
    for part, turn in enumerate(turns()):
        begin = jnp.where(sub == part, 0, half)
        for chunk in range(CHUNKS):
            to = pl.multiple_of(begin + (chunk ^ turn) * size, size)
            at = part * half + chunk * size
            pick_ref[pl.ds(to, size), :] = pick[at : at + size]
    for k in range(blocks):
        copies[k + 1].wait()
        found = dot(pick_ref[...], centers_ref[k], NN).astype(BF16)
        keep_ref[:, k * block : (k + 1) * block] = found[:half]
        send_ref[:, k * block : (k + 1) * block] = found[half:]


def pick_batch(batch_index, centers, part):
    rows = batch_index.shape[1]
    count, depth = centers.shape
    depth = depth // PARTS
    block = 512
    half = jax.ShapeDtypeStruct((rows // 2, depth), BF16)
    hbm = pl.BlockSpec(memory_space=pltpu.HBM)
    vmem = pl.BlockSpec(memory_space=pltpu.VMEM)
    return pl.pallas_call(
        functools.partial(pick_body, part * depth),
        in_specs=[hbm, hbm],
        out_specs=[vmem, vmem],
        out_shape=[half, half],
        scratch_shapes=[
            pltpu.VMEM((rows, count), BF16),
            pltpu.VMEM((1, rows), jnp.int32),
            pltpu.VMEM((depth // block, count, block), BF16),
            pltpu.SemaphoreType.DMA((depth // block + 1,)),
        ],
        compiler_params=params(),
        cost_estimate=pl.CostEstimate(
            flops=2 * rows * count * depth, bytes_accessed=2 * depth * (count + rows), transcendentals=0
        ),
        name="pick_batch",
    )(batch_index, centers)


def fits_body(count, index_hbm, fits_ref, index_ref, sem):
    copy = pltpu.make_async_copy(index_hbm, index_ref, sem)
    copy.start()
    copy.wait()
    devices = 2 * lax.axis_size("center")
    starts = lax.broadcasted_iota(jnp.int32, (devices, 1), 0) * count
    local = index_ref[...] - starts
    held = jnp.sum(jnp.where((local >= 0) & (local < count), 1.0, 0.0), axis=1, keepdims=True)
    fits_ref[0] = (jnp.max(held) <= SLOTS).astype(jnp.int32)


def rows_fit(batch_index, count):
    return pl.pallas_call(
        functools.partial(fits_body, count),
        in_specs=[pl.BlockSpec(memory_space=pltpu.HBM)],
        out_specs=pl.BlockSpec(memory_space=pltpu.SMEM),
        out_shape=jax.ShapeDtypeStruct((1,), jnp.int32),
        scratch_shapes=[pltpu.VMEM(batch_index.shape, jnp.int32), pltpu.SemaphoreType.DMA],
        compiler_params=params(),
        name="rows_fit",
    )(batch_index)[0]


def pack_body(first, index_hbm, centers_hbm, out_ref, index_ref, centers_ref, sems):
    blocks, count, block = centers_ref.shape
    rows = index_ref.shape[1]
    copies = [pltpu.make_async_copy(index_hbm, index_ref, sems.at[blocks])] + [
        pltpu.make_async_copy(
            centers_hbm.at[:, pl.ds(first + k * block, block)], centers_ref.at[k], sems.at[k]
        )
        for k in range(blocks)
    ]
    for copy in copies:
        copy.start()
    copies[0].wait()
    start = (lax.axis_index("center") * 2 + lax.axis_index("sub")) * count
    local = index_ref[...] - start
    here = jnp.where((local >= 0) & (local < count), 1.0, 0.0)
    earlier = lax.broadcasted_iota(jnp.int32, (rows, rows), 0) < lax.broadcasted_iota(jnp.int32, (rows, rows), 1)
    rank = dot(jnp.broadcast_to(here, (8, rows)).astype(BF16), jnp.where(earlier, 1.0, 0.0).astype(BF16), NN)[0:1]
    slots = lax.broadcasted_iota(jnp.int32, (SLOTS, 1), 0).astype(F32)
    to_slot = jnp.where(slots == rank, here, 0.0).astype(BF16)
    pick = dot(to_slot, pick_rows(index_ref, count, start, BF16, 1.0), NN).astype(BF16)
    for k in range(blocks):
        copies[k + 1].wait()
        out_ref[:, k * block : (k + 1) * block] = dot(pick, centers_ref[k], NN).astype(BF16)


def pack_rows(batch_index, centers, part):
    rows = batch_index.shape[1]
    count, depth = centers.shape
    depth = depth // PARTS
    block = 512
    hbm = pl.BlockSpec(memory_space=pltpu.HBM)
    return pl.pallas_call(
        functools.partial(pack_body, part * depth),
        in_specs=[hbm, hbm],
        out_specs=pl.BlockSpec(memory_space=pltpu.VMEM),
        out_shape=jax.ShapeDtypeStruct((SLOTS, depth), BF16),
        scratch_shapes=[
            pltpu.VMEM((1, rows), jnp.int32),
            pltpu.VMEM((depth // block, count, block), BF16),
            pltpu.SemaphoreType.DMA((depth // block + 1,)),
        ],
        compiler_params=params(),
        cost_estimate=pl.CostEstimate(
            flops=2 * SLOTS * count * depth, bytes_accessed=2 * depth * (count + SLOTS), transcendentals=0
        ),
        name="pack_rows",
    )(batch_index, centers)


def select_body(count, index_ref, select_ref):
    rows, slots = select_ref.shape
    chips = slots // (2 * SLOTS)
    index = index_ref[...]
    owner = jnp.zeros_like(index)
    for device in range(1, 2 * chips):
        owner = owner + jnp.where(index >= device * count, 1, 0)
    column = column_of(owner, LANE)
    same = jnp.concatenate([column] * (rows // LANE), axis=1) == owner.astype(F32)
    earlier = lax.broadcasted_iota(jnp.int32, (rows, rows), 0) < lax.broadcasted_iota(jnp.int32, (rows, rows), 1)
    rank = jnp.sum(jnp.where(same & earlier, 1.0, 0.0), axis=0, keepdims=True)
    away = (owner >> 1) ^ lax.axis_index("center")
    places = [
        sum(((away >> bit) & 1) << k for k, bit in enumerate(far_first(sub, chips.bit_length() - 1)))
        for sub in range(2)
    ]
    place = jnp.where((owner & 1) == 0, *places)
    far = jnp.where((owner & 1) == lax.axis_index("sub"), 0, chips * SLOTS)
    slot = column_of((far + place * SLOTS).astype(F32) + rank, LANE)
    lanes = lax.broadcasted_iota(jnp.int32, (1, LANE), 1).astype(F32)
    for k in range(slots // LANE):
        select_ref[:, k * LANE : (k + 1) * LANE] = jnp.where(slot == lanes + float(LANE * k), 1.0, 0.0).astype(BF16)


def select_packed(batch_index, count, chips):
    rows = batch_index.shape[1]
    return pl.pallas_call(
        functools.partial(select_body, count),
        out_shape=jax.ShapeDtypeStruct((rows, 2 * chips * SLOTS), BF16),
        compiler_params=params(),
        name="select_packed",
    )(batch_index)


def spread_body(
    first, classes, index_ref, eigvec_ref, weights_ref,
    high1_ref, low1_ref, high2_ref, low2_ref, spread_ref, all_ref,
):
    rank, points = eigvec_ref.shape
    count = weights_ref.shape[1]
    local = index_ref[...] - (lax.axis_index("center") * 2 + lax.axis_index("sub")) * count
    slots = lax.broadcasted_iota(jnp.int32, (count, points), 0)
    pick = jnp.where(slots == local, 1.0, 0.0).astype(BF16)
    vec = eigvec_ref[...]
    high = vec.astype(BF16)
    rest = vec - high.astype(F32)
    mid = rest.astype(BF16)
    low = (rest - mid.astype(F32)).astype(BF16)
    spread = dot(high, pick, NT) + dot(mid, pick, NT) + dot(low, pick, NT)
    spread_ref[...] = spread
    all_ref[:rank] = spread
    all_ref[rank : rank + classes] = weights_ref[...]
    all_ref[rank + classes :] = jnp.zeros((all_ref.shape[0] - rank - classes, count), F32)
    for begin, high_ref, low_ref in ((0, high1_ref, low1_ref), (first, high2_ref, low2_ref)):
        high_ref[...], low_ref[...] = two(all_ref[begin : begin + high_ref.shape[0]])


def spread_weights(nys_index, eigvec, weights, first, second):
    classes, count = weights.shape
    rank, points = eigvec.shape
    return pl.pallas_call(
        functools.partial(spread_body, first, classes),
        out_shape=[
            jax.ShapeDtypeStruct((first, count), BF16),
            jax.ShapeDtypeStruct((first, count), BF16),
            jax.ShapeDtypeStruct((second, count), BF16),
            jax.ShapeDtypeStruct((second, count), BF16),
            jax.ShapeDtypeStruct((rank, count), F32),
        ],
        scratch_shapes=[pltpu.VMEM((first + second, count), F32)],
        compiler_params=params(),
        cost_estimate=pl.CostEstimate(
            flops=6 * rank * points * count, bytes_accessed=8 * (first + second) * count, transcendentals=0
        ),
        name="spread_weights",
    )(nys_index, eigvec, weights)


def norms_body(centers_ref, norm_ref):
    wide = centers_ref[...].astype(F32)
    norm = jnp.sum(wide * wide, axis=1, keepdims=True)
    norm_ref[...] = jnp.broadcast_to(norm, norm_ref.shape)


def center_norms(centers):
    count, depth = centers.shape
    block = 256
    return pl.pallas_call(
        norms_body,
        grid=(count // block,),
        in_specs=[pl.BlockSpec((block, depth), lambda i: (i, 0))],
        out_specs=pl.BlockSpec((block, LANE), lambda i: (i, 0)),
        out_shape=jax.ShapeDtypeStruct((count, LANE), F32),
        compiler_params=params(),
        cost_estimate=pl.CostEstimate(flops=2 * count * depth, bytes_accessed=2 * count * depth, transcendentals=0),
        name="center_norms",
    )(centers)


def gather_batch(mine_ref, other_ref, select_ref, batch_ref):
    half = mine_ref.shape[0]
    found = dot(select_ref[:, :half], mine_ref[...], NN) + dot(select_ref[:, half:], other_ref[...], NN)
    batch_ref[...] = found.astype(BF16)


def nearer(first, centers_ref, batch_ref):
    rows, depth = batch_ref.shape
    batch = batch_ref[...].astype(F32)
    norm = jnp.sum(batch * batch, axis=1, keepdims=True)
    cross = dot(centers_ref[:, first : first + depth], batch_ref[...], NT)
    return jnp.broadcast_to(norm, (rows, LANE)).T[0:1] - 2.0 * cross


def product(high_ref, low_ref, value_high, value_low, total_ref, keep_ref, send_ref):
    half = keep_ref.shape[1]
    high = high_ref[...]
    total_ref[...] = dot(high, value_high, NN) + (dot(high, value_low, NN) + dot(low_ref[...], value_high, NN))
    lower = lax.axis_index("sub") == 0
    size = keep_ref.shape[0] // CHUNKS
    for chunk in range(CHUNKS):
        at = slice(chunk * size, (chunk + 1) * size)
        first, second = [
            total_ref[pl.ds(pl.multiple_of((chunk ^ turn) * size, 8), size), part * half : (part + 1) * half]
            for part, turn in enumerate(turns())
        ]
        keep_ref[at] = jnp.where(lower, first, second)
        send_ref[at] = jnp.where(lower, second, first)


def distance_body(mine_ref, other_ref, select_ref, centers_ref, norm_ref, total_ref, batch_ref):
    gather_batch(mine_ref, other_ref, select_ref, batch_ref)
    total_ref[...] = norm_ref[:, 0:1] + nearer(0, centers_ref, batch_ref)


def predict_body(
    mine_ref, other_ref, select_ref, centers_ref, before_ref, high_ref, low_ref,
    keep_ref, send_ref, value_high_ref, value_low_ref, batch_ref, total_ref,
):
    depth = centers_ref.shape[1]
    gather_batch(mine_ref, other_ref, select_ref, batch_ref)
    square = jnp.maximum(before_ref[...] + nearer(depth - batch_ref.shape[1], centers_ref, batch_ref), 0.0)
    value_high, value_low = two(jnp.exp(jnp.sqrt(square) * (-1.0 / math.sqrt(depth))))
    value_high_ref[...] = value_high
    value_low_ref[...] = value_low
    product(high_ref, low_ref, value_high, value_low, total_ref, keep_ref, send_ref)


def distances(mine, other, select, centers, norms):
    depth = mine.shape[1]
    rows = select.shape[0]
    count = centers.shape[0]
    vmem = pl.BlockSpec(memory_space=pltpu.VMEM)
    return pl.pallas_call(
        distance_body,
        in_specs=[vmem] * 5,
        out_specs=vmem,
        out_shape=jax.ShapeDtypeStruct((count, rows), F32),
        scratch_shapes=[pltpu.VMEM((rows, depth), BF16)],
        compiler_params=params(),
        cost_estimate=pl.CostEstimate(
            flops=2 * rows * count * depth, bytes_accessed=2 * depth * (count + rows), transcendentals=0
        ),
        name="distances",
    )(mine, other, select, centers, norms)


def predict(mine, other, select, centers, before, high, low):
    depth = mine.shape[1]
    rows = select.shape[0]
    half = rows // 2
    count = centers.shape[0]
    padded = high.shape[0]
    out = jax.ShapeDtypeStruct((padded, half), F32)
    value = jax.ShapeDtypeStruct((count, rows), BF16)
    vmem = pl.BlockSpec(memory_space=pltpu.VMEM)
    return pl.pallas_call(
        predict_body,
        in_specs=[vmem] * 7,
        out_specs=[vmem] * 4,
        out_shape=[out, out, value, value],
        scratch_shapes=[pltpu.VMEM((rows, depth), BF16), pltpu.VMEM((padded, rows), F32)],
        compiler_params=params(),
        cost_estimate=pl.CostEstimate(
            flops=2 * rows * count * (depth + 3 * padded),
            bytes_accessed=2 * depth * (count + rows) + 4 * padded * (count + rows),
            transcendentals=2 * rows * count,
        ),
        name="predict",
    )(mine, other, select, centers, before, high, low)


def more_body(high_ref, low_ref, value_high_ref, value_low_ref, keep_ref, send_ref, total_ref):
    product(high_ref, low_ref, value_high_ref[...], value_low_ref[...], total_ref, keep_ref, send_ref)


def predict_more(high, low, value_high, value_low):
    padded = high.shape[0]
    count, rows = value_high.shape
    out = jax.ShapeDtypeStruct((padded, rows // 2), F32)
    return pl.pallas_call(
        more_body,
        out_shape=[out, out],
        scratch_shapes=[pltpu.VMEM((padded, rows), F32)],
        compiler_params=params(),
        cost_estimate=pl.CostEstimate(
            flops=6 * rows * count * padded, bytes_accessed=4 * padded * (count + rows), transcendentals=0
        ),
        name="predict_more",
    )(high, low, value_high, value_low)


def gather_total(mine_ref, other_ref, total_ref):
    lower = lax.axis_index("sub") == 0
    half = mine_ref.shape[1]
    size = mine_ref.shape[0] // CHUNKS
    for part, turn in enumerate(turns()):
        for chunk in range(CHUNKS):
            at = slice(chunk * size, (chunk + 1) * size)
            same = lower if part == 0 else jnp.logical_not(lower)
            to = pl.multiple_of((chunk ^ turn) * size, 8)
            total_ref[pl.ds(to, size), part * half : (part + 1) * half] = jnp.where(
                same, mine_ref[at], other_ref[at]
            )


def write_rows(begin, skip, total_ref, targets_ref, weights_ref, high_ref, low_ref, new_hbm, out_hbm, new_ref, sems):
    rows = new_ref.shape[0]
    blocks = sems.shape[0] - 1
    bounds = [8 * (rows // 8 * k // blocks) for k in range(blocks)] + [rows]
    high_right = high_ref[...]
    low_right = low_ref[...]
    copies = [
        pltpu.make_async_copy(
            total_ref.at[pl.ds(skip, rows)], out_hbm.at[pl.ds(begin, rows)], sems.at[blocks]
        )
    ]
    copies[0].start()
    for k in range(blocks):
        low_end, high_end = bounds[k : k + 2]
        here = slice(begin + low_end, begin + high_end)
        high, low = two(total_ref[skip + low_end : skip + high_end] - targets_ref[here])
        new_ref[low_end:high_end] = weights_ref[here] + (
            dot(high, high_right, NN) + (dot(high, low_right, NN) + dot(low, high_right, NN))
        )
        copy = pltpu.make_async_copy(
            new_ref.at[pl.ds(low_end, high_end - low_end)],
            new_hbm.at[pl.ds(begin + low_end, high_end - low_end)],
            sems.at[k],
        )
        copy.start()
        copies.append(copy)
    for copy in copies:
        copy.wait()


def update_body(
    mine_ref, other_ref, targets_ref, index_ref, eigval_ref, spread_ref, weights_ref,
    new_hbm, out_hbm, high_ref, low_ref, total_ref, new_ref, sems,
):
    start = (lax.axis_index("center") * 2 + lax.axis_index("sub")) * spread_ref.shape[1]
    rank, count = spread_ref.shape
    gather_total(mine_ref, other_ref, total_ref)
    value = eigval_ref[...]
    lowest = jnp.min(value, axis=1, keepdims=True)
    scaled = (1.0 - lowest / value) / value
    mixed_high, mixed_low = two(total_ref[:rank].T * (0.25 * scaled))
    spread_high, spread_low = two(spread_ref[...])
    turned = dot(mixed_high, spread_high, NN) + (
        dot(mixed_high, spread_low, NN) + dot(mixed_low, spread_high, NN)
    )
    high_ref[...], low_ref[...] = two(turned - pick_rows(index_ref, count, start, F32, 0.25))
    write_rows(0, rank, total_ref, targets_ref, weights_ref, high_ref, low_ref, new_hbm, out_hbm, new_ref, sems)


def update(mine, other, targets, batch_index, eigval, spread, weights):
    classes, count = weights.shape
    padded, half = mine.shape
    rows = 2 * half
    rank = spread.shape[0]
    here = padded - rank
    vmem = pl.BlockSpec(memory_space=pltpu.VMEM)
    hbm = pl.BlockSpec(memory_space=pl.ANY)
    right = jax.ShapeDtypeStruct((rows, count), BF16)
    return pl.pallas_call(
        update_body,
        in_specs=[vmem] * 7,
        out_specs=[hbm, hbm, vmem, vmem],
        out_shape=[
            jax.ShapeDtypeStruct((classes, count), F32),
            jax.ShapeDtypeStruct((classes, rows), F32),
            right,
            right,
        ],
        scratch_shapes=[
            pltpu.VMEM((padded, rows), F32),
            pltpu.VMEM((here, count), F32),
            pltpu.SemaphoreType.DMA((4,)),
        ],
        compiler_params=params(),
        cost_estimate=pl.CostEstimate(
            flops=6 * rows * count * (here + rank), bytes_accessed=8 * here * (count + rows), transcendentals=0
        ),
        name="update",
    )(mine, other, targets, batch_index, eigval, spread, weights)


def update_more_body(
    begin, mine_ref, other_ref, targets_ref, weights_ref, high_ref, low_ref, new_in, out_in,
    new_hbm, out_hbm, total_ref, new_ref, sems,
):
    gather_total(mine_ref, other_ref, total_ref)
    write_rows(begin, 0, total_ref, targets_ref, weights_ref, high_ref, low_ref, new_hbm, out_hbm, new_ref, sems)


def update_more(mine, other, targets, weights, high, low, new, out, begin):
    classes, count = weights.shape
    padded, half = mine.shape
    rows = 2 * half
    here = classes - begin
    vmem = pl.BlockSpec(memory_space=pltpu.VMEM)
    hbm = pl.BlockSpec(memory_space=pl.ANY)
    return pl.pallas_call(
        functools.partial(update_more_body, begin),
        in_specs=[vmem] * 6 + [hbm] * 2,
        out_specs=[hbm, hbm],
        out_shape=[
            jax.ShapeDtypeStruct((classes, count), F32),
            jax.ShapeDtypeStruct((classes, rows), F32),
        ],
        input_output_aliases={6: 0, 7: 1},
        scratch_shapes=[
            pltpu.VMEM((padded, rows), F32),
            pltpu.VMEM((here, count), F32),
            pltpu.SemaphoreType.DMA((6,)),
        ],
        compiler_params=params(),
        cost_estimate=pl.CostEstimate(
            flops=6 * rows * count * here, bytes_accessed=8 * here * (count + rows), transcendentals=0
        ),
        name="update_more",
    )(mine, other, targets, weights, high, low, new, out)


def swap(x, chips, order=None, level=0):
    flip = [2 << order(sub, chips.bit_length() - 1)[level] if order else 1 for sub in range(2)]
    return lax.ppermute(x, AXES, [(i, i ^ flip[i & 1]) for i in range(2 * chips)])


def tie(x, tied):
    x, *tied = lax.optimization_barrier((x, *tied))
    return x, tied


def total_of(keep, send, chips, tied=()):
    keep = keep + swap(send, chips)
    for level in range(chips.bit_length() - 1):
        if level >= HALVINGS:
            keep = keep + swap(keep, chips, walk, level)
            continue
        half = keep.shape[0] // 2
        keep, send = keep[:half], keep[half:]
        if level == 1 and tied:
            send, tied = tie(send, tied)
        keep = keep + swap(send, chips, walk, level)
    for level in reversed(range(HALVINGS)):
        keep = jnp.concatenate([keep, swap(keep, chips, walk, level)])
    return [keep, swap(keep, chips), *tied]


def all_of(keep, chips, tied=()):
    for level in range(chips.bit_length() - 1):
        if level == 1 and tied:
            keep, tied = tie(keep, tied)
        keep = jnp.concatenate([keep, swap(keep, chips, far_first, level)])
    return [keep, swap(keep, chips), *tied]


def one_hot(slot, slots):
    return (slot[:, None] == jnp.arange(slots, dtype=jnp.int32)[None, :]).astype(BF16)


def select_summed(rows):
    row = jnp.arange(rows, dtype=jnp.int32)
    half = rows // 2
    size = half // CHUNKS
    turn = jnp.stack(turns())[row // half]
    chunk = (row % half // size) ^ turn
    far = jnp.where(row // half == lax.axis_index("sub"), 0, half)
    return one_hot(far + chunk * size + row % size, rows)


def step(packed, chips, centers, weights, targets, batch_index, nys_index, eigvec, eigval):
    rows = batch_index.shape[1]
    classes, count = weights.shape
    depth = eigvec.shape[0]
    unit = 8 * CHUNKS
    units = -(-(classes + depth) // unit)
    first = (units + 1) // 2 * unit
    second = units * unit - first
    far = [pltpu.with_memory_space_constraint(x, pltpu.HBM) for x in (batch_index, centers)]
    ready = [center_norms(centers), *spread_weights(nys_index.reshape(1, -1), eigvec, weights, first, second)]
    if packed:
        ready.append(select_packed(batch_index, count, chips))
        slots = [pack_rows(*far, part) for part in range(PARTS)]
        mine, other, norms, high1, low1, high2, low2, spread, select = all_of(slots[0], chips, ready)
        late = all_of(slots[1], chips)
    else:
        ready.append(select_summed(rows))
        picked = [pick_batch(*far, part) for part in range(PARTS)]
        mine, other, norms, high1, low1, high2, low2, spread, select = total_of(*picked[0], chips, ready)
        late = total_of(*picked[1], chips)
    before = distances(mine, other, select, centers, norms)
    keep, send, value_high, value_low = predict(*late, select, centers, before, high1, low1)
    one = total_of(keep, send, chips)
    another = total_of(*predict_more(high2, low2, value_high, value_low), chips)
    new, out, high, low = update(*one, targets, batch_index, eigval, spread, weights)
    return update_more(*another, targets, weights, high, low, new, out, first - depth)


def on_device(chips, centers, weights, targets, batch_index, nys_index, eigvec, eigval):
    batch_index = batch_index.reshape(1, -1)
    new, out = lax.cond(
        rows_fit(pltpu.with_memory_space_constraint(batch_index, pltpu.HBM), centers.shape[0]) > 0,
        functools.partial(step, True, chips),
        functools.partial(step, False, chips),
        centers,
        weights.T,
        targets.T,
        batch_index,
        nys_index,
        eigvec.T,
        eigval.reshape(1, -1),
    )
    return new.T, out.T


def solution(mesh):
    return jax.shard_map(
        functools.partial(on_device, mesh.shape["center"]),
        mesh=mesh,
        in_specs=(
            P(("parts", "center", "sub"), None),
            P(("parts", "center", "sub"), None),
            P("parts", None),
            P("parts"),
            P(("parts", "center", "sub")),
            P(("parts", "center", "sub"), None),
            P("parts"),
        ),
        out_specs=(P(("parts", "center", "sub"), None), P("parts", None)),
        check_vma=False,
    )
```

```python
import functools
import math

import jax
import jax.numpy as jnp
from jax import lax
from jax.experimental import pallas as pl
from jax.experimental.pallas import tpu as pltpu
from jax.sharding import PartitionSpec as P

F32 = jnp.float32
BF16 = jnp.bfloat16
AXES = ("center", "sub")
HALVINGS = 2
CHUNKS = 1 << HALVINGS
LANE = 128
PARTS = 2
SLOTS = 32
NT = (((1,), (1,)), ((), ()))
NN = (((1,), (0,)), ((), ()))
VMEM_LIMIT = 24 * 1024 * 1024


def dot(a, b, dims):
    return lax.dot_general(a, b, dims, preferred_element_type=F32)


def walk(sub, bits):
    order = list(range(bits))
    return order if sub == 0 else order[1::-1] + order[2:]


def far_first(sub, bits):
    order = list(range(bits))[::-1]
    return order if sub == 0 else order[:-2] + order[:-3:-1]


def turns():
    center = lax.axis_index("center")
    return [
        sum(((center >> bit) & 1) << (HALVINGS - 1 - k) for k, bit in enumerate(walk(sub, HALVINGS + 1)[:HALVINGS]))
        for sub in range(2)
    ]


def column_of(row, width):
    return jnp.broadcast_to(row.astype(F32), (width, row.shape[1])).T


def two(x):
    high = x.astype(BF16)
    return high, (x - high.astype(F32)).astype(BF16)


def pick_rows(index_ref, columns, start, dtype, scale):
    column = column_of(index_ref[...] - start, LANE)
    lanes = lax.broadcasted_iota(jnp.int32, (1, LANE), 1).astype(F32)
    blocks = [
        jnp.where(column == lanes + float(LANE * k), scale, 0.0).astype(dtype)
        for k in range(columns // LANE)
    ]
    return jnp.concatenate(blocks, axis=1)


def params():
    return pltpu.CompilerParams(vmem_limit_bytes=VMEM_LIMIT)


def pick_body(first, index_hbm, centers_hbm, keep_ref, send_ref, pick_ref, index_ref, centers_ref, sems):
    sub = lax.axis_index("sub")
    blocks, count, block = centers_ref.shape
    rows = index_ref.shape[1]
    half = rows // 2
    size = half // CHUNKS
    copies = [pltpu.make_async_copy(index_hbm, index_ref, sems.at[blocks])] + [
        pltpu.make_async_copy(
            centers_hbm.at[:, pl.ds(first + k * block, block)], centers_ref.at[k], sems.at[k]
        )
        for k in range(blocks)
    ]
    for copy in copies:
        copy.start()
    copies[0].wait()
    start = (lax.axis_index("center") * 2 + sub) * count
    pick = pick_rows(index_ref, count, start, BF16, 1.0)
    for part, turn in enumerate(turns()):
        begin = jnp.where(sub == part, 0, half)
        for chunk in range(CHUNKS):
            to = pl.multiple_of(begin + (chunk ^ turn) * size, size)
            at = part * half + chunk * size
            pick_ref[pl.ds(to, size), :] = pick[at : at + size]
    for k in range(blocks):
        copies[k + 1].wait()
        found = dot(pick_ref[...], centers_ref[k], NN).astype(BF16)
        keep_ref[:, k * block : (k + 1) * block] = found[:half]
        send_ref[:, k * block : (k + 1) * block] = found[half:]


def pick_batch(batch_index, centers, part):
    rows = batch_index.shape[1]
    count, depth = centers.shape
    depth = depth // PARTS
    block = 512
    half = jax.ShapeDtypeStruct((rows // 2, depth), BF16)
    hbm = pl.BlockSpec(memory_space=pltpu.HBM)
    vmem = pl.BlockSpec(memory_space=pltpu.VMEM)
    return pl.pallas_call(
        functools.partial(pick_body, part * depth),
        in_specs=[hbm, hbm],
        out_specs=[vmem, vmem],
        out_shape=[half, half],
        scratch_shapes=[
            pltpu.VMEM((rows, count), BF16),
            pltpu.VMEM((1, rows), jnp.int32),
            pltpu.VMEM((depth // block, count, block), BF16),
            pltpu.SemaphoreType.DMA((depth // block + 1,)),
        ],
        compiler_params=params(),
        cost_estimate=pl.CostEstimate(
            flops=2 * rows * count * depth, bytes_accessed=2 * depth * (count + rows), transcendentals=0
        ),
        name="pick_batch",
    )(batch_index, centers)


def pack_body(first, index_hbm, centers_hbm, out_ref, fits_ref, index_ref, centers_ref, sems):
    blocks, count, block = centers_ref.shape
    rows = index_ref.shape[1]
    copies = [pltpu.make_async_copy(index_hbm, index_ref, sems.at[blocks])] + [
        pltpu.make_async_copy(
            centers_hbm.at[:, pl.ds(first + k * block, block)], centers_ref.at[k], sems.at[k]
        )
        for k in range(blocks)
    ]
    for copy in copies:
        copy.start()
    copies[0].wait()
    starts = lax.broadcasted_iota(jnp.int32, (2 * lax.axis_size("center"), 1), 0) * count
    every = index_ref[...] - starts
    held = jnp.sum(jnp.where((every >= 0) & (every < count), 1.0, 0.0), axis=1, keepdims=True)
    fits_ref[0] = (jnp.max(held) <= SLOTS).astype(jnp.int32)
    start = (lax.axis_index("center") * 2 + lax.axis_index("sub")) * count
    local = index_ref[...] - start
    here = jnp.where((local >= 0) & (local < count), 1.0, 0.0)
    earlier = lax.broadcasted_iota(jnp.int32, (rows, rows), 0) < lax.broadcasted_iota(jnp.int32, (rows, rows), 1)
    rank = dot(jnp.broadcast_to(here, (8, rows)).astype(BF16), jnp.where(earlier, 1.0, 0.0).astype(BF16), NN)[0:1]
    slots = lax.broadcasted_iota(jnp.int32, (SLOTS, 1), 0).astype(F32)
    to_slot = jnp.where(slots == rank, here, 0.0).astype(BF16)
    pick = dot(to_slot, pick_rows(index_ref, count, start, BF16, 1.0), NN).astype(BF16)
    for k in range(blocks):
        copies[k + 1].wait()
        out_ref[:, k * block : (k + 1) * block] = dot(pick, centers_ref[k], NN).astype(BF16)


def pack_rows(batch_index, centers, part):
    rows = batch_index.shape[1]
    count, depth = centers.shape
    depth = depth // PARTS
    block = 512
    hbm = pl.BlockSpec(memory_space=pltpu.HBM)
    return pl.pallas_call(
        functools.partial(pack_body, part * depth),
        in_specs=[hbm, hbm],
        out_specs=[pl.BlockSpec(memory_space=pltpu.VMEM), pl.BlockSpec(memory_space=pltpu.SMEM)],
        out_shape=[jax.ShapeDtypeStruct((SLOTS, depth), BF16), jax.ShapeDtypeStruct((1,), jnp.int32)],
        scratch_shapes=[
            pltpu.VMEM((1, rows), jnp.int32),
            pltpu.VMEM((depth // block, count, block), BF16),
            pltpu.SemaphoreType.DMA((depth // block + 1,)),
        ],
        compiler_params=params(),
        cost_estimate=pl.CostEstimate(
            flops=2 * SLOTS * count * depth, bytes_accessed=2 * depth * (count + SLOTS), transcendentals=0
        ),
        name="pack_rows",
    )(batch_index, centers)


def select_body(count, index_ref, select_ref):
    rows, slots = select_ref.shape
    chips = slots // (2 * SLOTS)
    index = index_ref[...]
    owner = jnp.zeros_like(index)
    for device in range(1, 2 * chips):
        owner = owner + jnp.where(index >= device * count, 1, 0)
    column = column_of(owner, LANE)
    same = jnp.concatenate([column] * (rows // LANE), axis=1) == owner.astype(F32)
    earlier = lax.broadcasted_iota(jnp.int32, (rows, rows), 0) < lax.broadcasted_iota(jnp.int32, (rows, rows), 1)
    rank = jnp.sum(jnp.where(same & earlier, 1.0, 0.0), axis=0, keepdims=True)
    away = (owner >> 1) ^ lax.axis_index("center")
    places = [
        sum(((away >> bit) & 1) << k for k, bit in enumerate(far_first(sub, chips.bit_length() - 1)))
        for sub in range(2)
    ]
    place = jnp.where((owner & 1) == 0, *places)
    far = jnp.where((owner & 1) == lax.axis_index("sub"), 0, chips * SLOTS)
    slot = column_of((far + place * SLOTS).astype(F32) + rank, LANE)
    lanes = lax.broadcasted_iota(jnp.int32, (1, LANE), 1).astype(F32)
    for k in range(slots // LANE):
        select_ref[:, k * LANE : (k + 1) * LANE] = jnp.where(slot == lanes + float(LANE * k), 1.0, 0.0).astype(BF16)


def select_packed(batch_index, count, chips):
    rows = batch_index.shape[1]
    return pl.pallas_call(
        functools.partial(select_body, count),
        out_shape=jax.ShapeDtypeStruct((rows, 2 * chips * SLOTS), BF16),
        compiler_params=params(),
        name="select_packed",
    )(batch_index)


def spread_body(
    first, classes, index_ref, eigvec_ref, weights_ref,
    high1_ref, low1_ref, high2_ref, low2_ref, spread_ref, all_ref,
):
    rank, points = eigvec_ref.shape
    count = weights_ref.shape[1]
    local = index_ref[...] - (lax.axis_index("center") * 2 + lax.axis_index("sub")) * count
    slots = lax.broadcasted_iota(jnp.int32, (count, points), 0)
    pick = jnp.where(slots == local, 1.0, 0.0).astype(BF16)
    vec = eigvec_ref[...]
    high = vec.astype(BF16)
    rest = vec - high.astype(F32)
    mid = rest.astype(BF16)
    low = (rest - mid.astype(F32)).astype(BF16)
    spread = dot(high, pick, NT) + dot(mid, pick, NT) + dot(low, pick, NT)
    spread_ref[...] = spread
    all_ref[:rank] = spread
    all_ref[rank : rank + classes] = weights_ref[...]
    all_ref[rank + classes :] = jnp.zeros((all_ref.shape[0] - rank - classes, count), F32)
    for begin, high_ref, low_ref in ((0, high1_ref, low1_ref), (first, high2_ref, low2_ref)):
        high_ref[...], low_ref[...] = two(all_ref[begin : begin + high_ref.shape[0]])


def spread_weights(nys_index, eigvec, weights, first, second):
    classes, count = weights.shape
    rank, points = eigvec.shape
    return pl.pallas_call(
        functools.partial(spread_body, first, classes),
        out_shape=[
            jax.ShapeDtypeStruct((first, count), BF16),
            jax.ShapeDtypeStruct((first, count), BF16),
            jax.ShapeDtypeStruct((second, count), BF16),
            jax.ShapeDtypeStruct((second, count), BF16),
            jax.ShapeDtypeStruct((rank, count), F32),
        ],
        scratch_shapes=[pltpu.VMEM((first + second, count), F32)],
        compiler_params=params(),
        cost_estimate=pl.CostEstimate(
            flops=6 * rank * points * count, bytes_accessed=8 * (first + second) * count, transcendentals=0
        ),
        name="spread_weights",
    )(nys_index, eigvec, weights)


def norms_body(centers_ref, norm_ref):
    wide = centers_ref[...].astype(F32)
    norm = jnp.sum(wide * wide, axis=1, keepdims=True)
    norm_ref[...] = jnp.broadcast_to(norm, norm_ref.shape)


def center_norms(centers):
    count, depth = centers.shape
    block = 256
    return pl.pallas_call(
        norms_body,
        grid=(count // block,),
        in_specs=[pl.BlockSpec((block, depth), lambda i: (i, 0))],
        out_specs=pl.BlockSpec((block, LANE), lambda i: (i, 0)),
        out_shape=jax.ShapeDtypeStruct((count, LANE), F32),
        compiler_params=params(),
        cost_estimate=pl.CostEstimate(flops=2 * count * depth, bytes_accessed=2 * count * depth, transcendentals=0),
        name="center_norms",
    )(centers)


def gather_batch(piece_refs, select_ref, batch_ref):
    found = 0.0
    for k, ref in enumerate(piece_refs):
        size = ref.shape[0]
        found = found + dot(select_ref[:, k * size : (k + 1) * size], ref[...], NN)
    batch_ref[...] = found.astype(BF16)


def nearer(first, centers_ref, batch_ref):
    rows, depth = batch_ref.shape
    batch = batch_ref[...].astype(F32)
    norm = jnp.sum(batch * batch, axis=1, keepdims=True)
    cross = dot(centers_ref[:, first : first + depth], batch_ref[...], NT)
    return jnp.broadcast_to(norm, (rows, LANE)).T[0:1] - 2.0 * cross


def product(high_ref, low_ref, value_high, value_low, total_ref, keep_ref, send_ref):
    half = keep_ref.shape[1]
    high = high_ref[...]
    total_ref[...] = dot(high, value_high, NN) + (dot(high, value_low, NN) + dot(low_ref[...], value_high, NN))
    lower = lax.axis_index("sub") == 0
    size = keep_ref.shape[0] // CHUNKS
    for chunk in range(CHUNKS):
        at = slice(chunk * size, (chunk + 1) * size)
        first, second = [
            total_ref[pl.ds(pl.multiple_of((chunk ^ turn) * size, 8), size), part * half : (part + 1) * half]
            for part, turn in enumerate(turns())
        ]
        keep_ref[at] = jnp.where(lower, first, second)
        send_ref[at] = jnp.where(lower, second, first)


def distance_body(*refs):
    *piece_refs, select_ref, centers_ref, norm_ref, total_ref, batch_ref = refs
    gather_batch(piece_refs, select_ref, batch_ref)
    total_ref[...] = norm_ref[:, 0:1] + nearer(0, centers_ref, batch_ref)


def predict_body(*refs):
    *piece_refs, select_ref, centers_ref, before_ref, high_ref, low_ref = refs[:-6]
    keep_ref, send_ref, value_high_ref, value_low_ref, batch_ref, total_ref = refs[-6:]
    depth = centers_ref.shape[1]
    gather_batch(piece_refs, select_ref, batch_ref)
    square = jnp.maximum(before_ref[...] + nearer(depth - batch_ref.shape[1], centers_ref, batch_ref), 0.0)
    value_high, value_low = two(jnp.exp(jnp.sqrt(square) * (-1.0 / math.sqrt(depth))))
    value_high_ref[...] = value_high
    value_low_ref[...] = value_low
    product(high_ref, low_ref, value_high, value_low, total_ref, keep_ref, send_ref)


def distances(pieces, select, centers, norms):
    depth = pieces[0].shape[1]
    rows = select.shape[0]
    count = centers.shape[0]
    vmem = pl.BlockSpec(memory_space=pltpu.VMEM)
    return pl.pallas_call(
        distance_body,
        in_specs=[vmem] * (len(pieces) + 3),
        out_specs=vmem,
        out_shape=jax.ShapeDtypeStruct((count, rows), F32),
        scratch_shapes=[pltpu.VMEM((rows, depth), BF16)],
        compiler_params=params(),
        cost_estimate=pl.CostEstimate(
            flops=2 * rows * count * depth, bytes_accessed=2 * depth * (count + rows), transcendentals=0
        ),
        name="distances",
    )(*pieces, select, centers, norms)


def predict(pieces, select, centers, before, high, low):
    depth = pieces[0].shape[1]
    rows = select.shape[0]
    half = rows // 2
    count = centers.shape[0]
    padded = high.shape[0]
    out = jax.ShapeDtypeStruct((padded, half), F32)
    value = jax.ShapeDtypeStruct((count, rows), BF16)
    vmem = pl.BlockSpec(memory_space=pltpu.VMEM)
    return pl.pallas_call(
        predict_body,
        in_specs=[vmem] * (len(pieces) + 5),
        out_specs=[vmem] * 4,
        out_shape=[out, out, value, value],
        scratch_shapes=[pltpu.VMEM((rows, depth), BF16), pltpu.VMEM((padded, rows), F32)],
        compiler_params=params(),
        cost_estimate=pl.CostEstimate(
            flops=2 * rows * count * (depth + 3 * padded),
            bytes_accessed=2 * depth * (count + rows) + 4 * padded * (count + rows),
            transcendentals=2 * rows * count,
        ),
        name="predict",
    )(*pieces, select, centers, before, high, low)


def more_body(high_ref, low_ref, value_high_ref, value_low_ref, keep_ref, send_ref, total_ref):
    product(high_ref, low_ref, value_high_ref[...], value_low_ref[...], total_ref, keep_ref, send_ref)


def predict_more(high, low, value_high, value_low):
    padded = high.shape[0]
    count, rows = value_high.shape
    out = jax.ShapeDtypeStruct((padded, rows // 2), F32)
    return pl.pallas_call(
        more_body,
        out_shape=[out, out],
        scratch_shapes=[pltpu.VMEM((padded, rows), F32)],
        compiler_params=params(),
        cost_estimate=pl.CostEstimate(
            flops=6 * rows * count * padded, bytes_accessed=4 * padded * (count + rows), transcendentals=0
        ),
        name="predict_more",
    )(high, low, value_high, value_low)


def gather_total(piece_refs, total_ref):
    lower = lax.axis_index("sub") == 0
    rows, half = piece_refs[0].shape
    size = 2 * rows // CHUNKS
    for part, turn in enumerate(turns()):
        for chunk in range(CHUNKS):
            second, at = divmod(chunk * size, rows)
            mine, other = [ref[at : at + size] for ref in (piece_refs[second], piece_refs[2 + second])]
            same = lower if part == 0 else jnp.logical_not(lower)
            to = pl.multiple_of((chunk ^ turn) * size, 8)
            total_ref[pl.ds(to, size), part * half : (part + 1) * half] = jnp.where(same, mine, other)


def write_rows(begin, skip, total_ref, targets_ref, weights_ref, high_ref, low_ref, new_hbm, out_hbm, new_ref, sems):
    rows = new_ref.shape[0]
    blocks = sems.shape[0] - 1
    bounds = [8 * (rows // 8 * k // blocks) for k in range(blocks)] + [rows]
    high_right = high_ref[...]
    low_right = low_ref[...]
    copies = [
        pltpu.make_async_copy(
            total_ref.at[pl.ds(skip, rows)], out_hbm.at[pl.ds(begin, rows)], sems.at[blocks]
        )
    ]
    copies[0].start()
    for k in range(blocks):
        low_end, high_end = bounds[k : k + 2]
        here = slice(begin + low_end, begin + high_end)
        high, low = two(total_ref[skip + low_end : skip + high_end] - targets_ref[here])
        new_ref[low_end:high_end] = weights_ref[here] + (
            dot(high, high_right, NN) + (dot(high, low_right, NN) + dot(low, high_right, NN))
        )
        copy = pltpu.make_async_copy(
            new_ref.at[pl.ds(low_end, high_end - low_end)],
            new_hbm.at[pl.ds(begin + low_end, high_end - low_end)],
            sems.at[k],
        )
        copy.start()
        copies.append(copy)
    for copy in copies:
        copy.wait()


def update_body(
    keep_ref, got_ref, near_ref, far_ref, targets_ref, index_ref, eigval_ref, spread_ref, weights_ref,
    new_hbm, out_hbm, high_ref, low_ref, total_ref, new_ref, sems,
):
    start = (lax.axis_index("center") * 2 + lax.axis_index("sub")) * spread_ref.shape[1]
    rank, count = spread_ref.shape
    gather_total((keep_ref, got_ref, near_ref, far_ref), total_ref)
    value = eigval_ref[...]
    lowest = jnp.min(value, axis=1, keepdims=True)
    scaled = (1.0 - lowest / value) / value
    mixed_high, mixed_low = two(total_ref[:rank].T * (0.25 * scaled))
    spread_high, spread_low = two(spread_ref[...])
    turned = dot(mixed_high, spread_high, NN) + (
        dot(mixed_high, spread_low, NN) + dot(mixed_low, spread_high, NN)
    )
    high_ref[...], low_ref[...] = two(turned - pick_rows(index_ref, count, start, F32, 0.25))
    write_rows(0, rank, total_ref, targets_ref, weights_ref, high_ref, low_ref, new_hbm, out_hbm, new_ref, sems)


def update(pieces, targets, batch_index, eigval, spread, weights):
    classes, count = weights.shape
    padded, rows = 2 * pieces[0].shape[0], 2 * pieces[0].shape[1]
    rank = spread.shape[0]
    here = padded - rank
    vmem = pl.BlockSpec(memory_space=pltpu.VMEM)
    hbm = pl.BlockSpec(memory_space=pl.ANY)
    right = jax.ShapeDtypeStruct((rows, count), BF16)
    return pl.pallas_call(
        update_body,
        in_specs=[vmem] * 9,
        out_specs=[hbm, hbm, vmem, vmem],
        out_shape=[
            jax.ShapeDtypeStruct((classes, count), F32),
            jax.ShapeDtypeStruct((classes, rows), F32),
            right,
            right,
        ],
        scratch_shapes=[
            pltpu.VMEM((padded, rows), F32),
            pltpu.VMEM((here, count), F32),
            pltpu.SemaphoreType.DMA((4,)),
        ],
        compiler_params=params(),
        cost_estimate=pl.CostEstimate(
            flops=6 * rows * count * (here + rank), bytes_accessed=8 * here * (count + rows), transcendentals=0
        ),
        name="update",
    )(*pieces, targets, batch_index, eigval, spread, weights)


def update_more_body(
    begin, keep_ref, got_ref, near_ref, far_ref, targets_ref, weights_ref, high_ref, low_ref, new_in, out_in,
    new_hbm, out_hbm, total_ref, new_ref, sems,
):
    gather_total((keep_ref, got_ref, near_ref, far_ref), total_ref)
    write_rows(begin, 0, total_ref, targets_ref, weights_ref, high_ref, low_ref, new_hbm, out_hbm, new_ref, sems)


def update_more(pieces, targets, weights, high, low, new, out, begin):
    classes, count = weights.shape
    padded, rows = 2 * pieces[0].shape[0], 2 * pieces[0].shape[1]
    here = classes - begin
    vmem = pl.BlockSpec(memory_space=pltpu.VMEM)
    hbm = pl.BlockSpec(memory_space=pl.ANY)
    return pl.pallas_call(
        functools.partial(update_more_body, begin),
        in_specs=[vmem] * 8 + [hbm] * 2,
        out_specs=[hbm, hbm],
        out_shape=[
            jax.ShapeDtypeStruct((classes, count), F32),
            jax.ShapeDtypeStruct((classes, rows), F32),
        ],
        input_output_aliases={8: 0, 9: 1},
        scratch_shapes=[
            pltpu.VMEM((padded, rows), F32),
            pltpu.VMEM((here, count), F32),
            pltpu.SemaphoreType.DMA((6,)),
        ],
        compiler_params=params(),
        cost_estimate=pl.CostEstimate(
            flops=6 * rows * count * here, bytes_accessed=8 * here * (count + rows), transcendentals=0
        ),
        name="update_more",
    )(*pieces, targets, weights, high, low, new, out)


def swap(x, chips, order=None, level=0):
    flip = [2 << order(sub, chips.bit_length() - 1)[level] if order else 1 for sub in range(2)]
    return lax.ppermute(x, AXES, [(i, i ^ flip[i & 1]) for i in range(2 * chips)])


def tie(x, *others):
    return lax.optimization_barrier((x, *others))


def settle(keeps, gots, combine):
    first = combine(keeps[0], gots[0])
    got, _ = tie(gots[1], first)
    return [first, combine(keeps[1], got)]


def stack(keep, got):
    return jnp.concatenate([keep, got])


def add(keep, got):
    return keep + got


def pieces_of(keeps, gots, chips):
    return [(keep, got, swap(keep, chips), swap(got, chips)) for keep, got in zip(keeps, gots)]


def totals(parts, chips):
    keeps = [keep for keep, _ in parts]
    gots = [swap(send, chips) for _, send in parts]
    gots[0], keeps[1] = tie(gots[0], keeps[1])
    keeps = settle(keeps, gots, add)
    for level in range(chips.bit_length() - 1):
        sends = keeps
        if level < HALVINGS:
            half = [keep.shape[0] // 2 for keep in keeps]
            sends = [keep[at:] for keep, at in zip(keeps, half)]
            keeps = [keep[:at] for keep, at in zip(keeps, half)]
        keeps = settle(keeps, [swap(send, chips, walk, level) for send in sends], add)
    for level in reversed(range(HALVINGS)):
        gots = [swap(keep, chips, walk, level) for keep in keeps]
        if level:
            keeps = settle(keeps, gots, stack)
    return pieces_of(keeps, gots, chips)


def gathered(keeps, chips, tied):
    bits = chips.bit_length() - 1
    for level in range(bits):
        if level == 1:
            keeps[0], *tied = tie(keeps[0], *tied)
        gots = [swap(keep, chips, far_first, level) for keep in keeps]
        if level < bits - 1:
            keeps = settle(keeps, gots, stack)
    return pieces_of(keeps, gots, chips), tied


def one_hot(slot, slots):
    return (slot[:, None] == jnp.arange(slots, dtype=jnp.int32)[None, :]).astype(BF16)


def select_summed(rows):
    row = jnp.arange(rows, dtype=jnp.int32)
    half = rows // 2
    size = half // CHUNKS
    turn = jnp.stack(turns())[row // half]
    chunk = (row % half // size) ^ turn
    far = jnp.where(row // half == lax.axis_index("sub"), 0, half)
    return one_hot(far + chunk * size + row % size, rows)


def step(packed, chips, slots, centers, weights, targets, batch_index, nys_index, eigvec, eigval):
    rows = batch_index.shape[1]
    classes, count = weights.shape
    depth = eigvec.shape[0]
    unit = 8 * CHUNKS
    units = -(-(classes + depth) // unit)
    first = (units + 1) // 2 * unit
    second = units * unit - first
    far = [pltpu.with_memory_space_constraint(x, pltpu.HBM) for x in (batch_index, centers)]
    ready = [center_norms(centers), *spread_weights(nys_index.reshape(1, -1), eigvec, weights, first, second)]
    if packed:
        ready.append(select_packed(batch_index, count, chips))
        halves, ready = gathered([slots, pack_rows(*far, 1)[0]], chips, ready)
    else:
        ready.append(select_summed(rows))
        halves = totals([pick_batch(*far, part) for part in range(PARTS)], chips)
    norms, high1, low1, high2, low2, spread, select = ready
    before = distances(halves[0], select, centers, norms)
    keep, send, value_high, value_low = predict(halves[1], select, centers, before, high1, low1)
    one, another = totals([(keep, send), predict_more(high2, low2, value_high, value_low)], chips)
    new, out, high, low = update(one, targets, batch_index, eigval, spread, weights)
    return update_more(another, targets, weights, high, low, new, out, first - depth)


def on_device(chips, centers, weights, targets, batch_index, nys_index, eigvec, eigval):
    batch_index = batch_index.reshape(1, -1)
    far = [pltpu.with_memory_space_constraint(x, pltpu.HBM) for x in (batch_index, centers)]
    slots, fits = pack_rows(*far, 0)
    new, out = lax.cond(
        fits[0] > 0,
        functools.partial(step, True, chips),
        functools.partial(step, False, chips),
        slots,
        centers,
        weights.T,
        targets.T,
        batch_index,
        nys_index,
        eigvec.T,
        eigval.reshape(1, -1),
    )
    return new.T, out.T


def solution(mesh):
    return jax.shard_map(
        functools.partial(on_device, mesh.shape["center"]),
        mesh=mesh,
        in_specs=(
            P(("parts", "center", "sub"), None),
            P(("parts", "center", "sub"), None),
            P("parts", None),
            P("parts"),
            P(("parts", "center", "sub")),
            P(("parts", "center", "sub"), None),
            P("parts"),
        ),
        out_specs=(P(("parts", "center", "sub"), None), P("parts", None)),
        check_vma=False,
    )
```

```python
import functools
import math

import jax
import jax.numpy as jnp
from jax import lax
from jax.experimental import pallas as pl
from jax.experimental.pallas import tpu as pltpu
from jax.sharding import PartitionSpec as P

F32 = jnp.float32
BF16 = jnp.bfloat16
AXES = ("center", "sub")
HALVINGS = 2
CHUNKS = 1 << HALVINGS
LANE = 128
PARTS = 2
SLOTS = 32
NT = (((1,), (1,)), ((), ()))
NN = (((1,), (0,)), ((), ()))
VMEM_LIMIT = 24 * 1024 * 1024


def dot(a, b, dims):
    return lax.dot_general(a, b, dims, preferred_element_type=F32)


def walk(sub, bits):
    order = list(range(bits))
    return order if sub == 0 else order[1::-1] + order[2:]


def far_first(sub, bits):
    order = list(range(bits))[::-1]
    return order if sub == 0 else order[:-2] + order[:-3:-1]


def turns():
    center = lax.axis_index("center")
    return [
        sum(((center >> bit) & 1) << (HALVINGS - 1 - k) for k, bit in enumerate(walk(sub, HALVINGS + 1)[:HALVINGS]))
        for sub in range(2)
    ]


def column_of(row, width):
    return jnp.broadcast_to(row.astype(F32), (width, row.shape[1])).T


def two(x):
    high = x.astype(BF16)
    return high, (x - high.astype(F32)).astype(BF16)


def pick_rows(index_ref, columns, start, dtype, scale):
    column = column_of(index_ref[...] - start, LANE)
    lanes = lax.broadcasted_iota(jnp.int32, (1, LANE), 1).astype(F32)
    blocks = [
        jnp.where(column == lanes + float(LANE * k), scale, 0.0).astype(dtype)
        for k in range(columns // LANE)
    ]
    return jnp.concatenate(blocks, axis=1)


def params():
    return pltpu.CompilerParams(vmem_limit_bytes=VMEM_LIMIT)


def pick_body(first, index_hbm, centers_hbm, keep_ref, send_ref, pick_ref, index_ref, centers_ref, sems):
    sub = lax.axis_index("sub")
    blocks, count, block = centers_ref.shape
    rows = index_ref.shape[1]
    half = rows // 2
    size = half // CHUNKS
    copies = [pltpu.make_async_copy(index_hbm, index_ref, sems.at[blocks])] + [
        pltpu.make_async_copy(
            centers_hbm.at[:, pl.ds(first + k * block, block)], centers_ref.at[k], sems.at[k]
        )
        for k in range(blocks)
    ]
    for copy in copies:
        copy.start()
    copies[0].wait()
    start = (lax.axis_index("center") * 2 + sub) * count
    pick = pick_rows(index_ref, count, start, BF16, 1.0)
    for part, turn in enumerate(turns()):
        begin = jnp.where(sub == part, 0, half)
        for chunk in range(CHUNKS):
            to = pl.multiple_of(begin + (chunk ^ turn) * size, size)
            at = part * half + chunk * size
            pick_ref[pl.ds(to, size), :] = pick[at : at + size]
    for k in range(blocks):
        copies[k + 1].wait()
        found = dot(pick_ref[...], centers_ref[k], NN).astype(BF16)
        keep_ref[:, k * block : (k + 1) * block] = found[:half]
        send_ref[:, k * block : (k + 1) * block] = found[half:]


def pick_batch(batch_index, centers, part):
    rows = batch_index.shape[1]
    count, depth = centers.shape
    depth = depth // PARTS
    block = 512
    half = jax.ShapeDtypeStruct((rows // 2, depth), BF16)
    hbm = pl.BlockSpec(memory_space=pltpu.HBM)
    vmem = pl.BlockSpec(memory_space=pltpu.VMEM)
    return pl.pallas_call(
        functools.partial(pick_body, part * depth),
        in_specs=[hbm, hbm],
        out_specs=[vmem, vmem],
        out_shape=[half, half],
        scratch_shapes=[
            pltpu.VMEM((rows, count), BF16),
            pltpu.VMEM((1, rows), jnp.int32),
            pltpu.VMEM((depth // block, count, block), BF16),
            pltpu.SemaphoreType.DMA((depth // block + 1,)),
        ],
        compiler_params=params(),
        cost_estimate=pl.CostEstimate(
            flops=2 * rows * count * depth, bytes_accessed=2 * depth * (count + rows), transcendentals=0
        ),
        name="pick_batch",
    )(batch_index, centers)


def fits_body(count, index_hbm, fits_ref, index_ref, sem):
    copy = pltpu.make_async_copy(index_hbm, index_ref, sem)
    copy.start()
    copy.wait()
    devices = 2 * lax.axis_size("center")
    starts = lax.broadcasted_iota(jnp.int32, (devices, 1), 0) * count
    local = index_ref[...] - starts
    held = jnp.sum(jnp.where((local >= 0) & (local < count), 1.0, 0.0), axis=1, keepdims=True)
    fits_ref[0] = (jnp.max(held) <= SLOTS).astype(jnp.int32)


def rows_fit(batch_index, count):
    return pl.pallas_call(
        functools.partial(fits_body, count),
        in_specs=[pl.BlockSpec(memory_space=pltpu.HBM)],
        out_specs=pl.BlockSpec(memory_space=pltpu.SMEM),
        out_shape=jax.ShapeDtypeStruct((1,), jnp.int32),
        scratch_shapes=[pltpu.VMEM(batch_index.shape, jnp.int32), pltpu.SemaphoreType.DMA],
        compiler_params=params(),
        name="rows_fit",
    )(batch_index)[0]


def pack_body(first, index_hbm, centers_hbm, out_ref, index_ref, centers_ref, sems):
    blocks, count, block = centers_ref.shape
    rows = index_ref.shape[1]
    copies = [pltpu.make_async_copy(index_hbm, index_ref, sems.at[blocks])] + [
        pltpu.make_async_copy(
            centers_hbm.at[:, pl.ds(first + k * block, block)], centers_ref.at[k], sems.at[k]
        )
        for k in range(blocks)
    ]
    for copy in copies:
        copy.start()
    copies[0].wait()
    start = (lax.axis_index("center") * 2 + lax.axis_index("sub")) * count
    local = index_ref[...] - start
    here = jnp.where((local >= 0) & (local < count), 1.0, 0.0)
    earlier = lax.broadcasted_iota(jnp.int32, (rows, rows), 0) < lax.broadcasted_iota(jnp.int32, (rows, rows), 1)
    rank = dot(jnp.broadcast_to(here, (8, rows)).astype(BF16), jnp.where(earlier, 1.0, 0.0).astype(BF16), NN)[0:1]
    slots = lax.broadcasted_iota(jnp.int32, (SLOTS, 1), 0).astype(F32)
    to_slot = jnp.where(slots == rank, here, 0.0).astype(BF16)
    pick = dot(to_slot, pick_rows(index_ref, count, start, BF16, 1.0), NN).astype(BF16)
    for k in range(blocks):
        copies[k + 1].wait()
        out_ref[:, k * block : (k + 1) * block] = dot(pick, centers_ref[k], NN).astype(BF16)


def pack_rows(batch_index, centers, part):
    rows = batch_index.shape[1]
    count, depth = centers.shape
    depth = depth // PARTS
    block = 512
    hbm = pl.BlockSpec(memory_space=pltpu.HBM)
    return pl.pallas_call(
        functools.partial(pack_body, part * depth),
        in_specs=[hbm, hbm],
        out_specs=pl.BlockSpec(memory_space=pltpu.VMEM),
        out_shape=jax.ShapeDtypeStruct((SLOTS, depth), BF16),
        scratch_shapes=[
            pltpu.VMEM((1, rows), jnp.int32),
            pltpu.VMEM((depth // block, count, block), BF16),
            pltpu.SemaphoreType.DMA((depth // block + 1,)),
        ],
        compiler_params=params(),
        cost_estimate=pl.CostEstimate(
            flops=2 * SLOTS * count * depth, bytes_accessed=2 * depth * (count + SLOTS), transcendentals=0
        ),
        name="pack_rows",
    )(batch_index, centers)


def select_body(count, index_ref, select_ref):
    rows, slots = select_ref.shape
    chips = slots // (2 * SLOTS)
    index = index_ref[...]
    owner = jnp.zeros_like(index)
    for device in range(1, 2 * chips):
        owner = owner + jnp.where(index >= device * count, 1, 0)
    column = column_of(owner, LANE)
    same = jnp.concatenate([column] * (rows // LANE), axis=1) == owner.astype(F32)
    earlier = lax.broadcasted_iota(jnp.int32, (rows, rows), 0) < lax.broadcasted_iota(jnp.int32, (rows, rows), 1)
    rank = jnp.sum(jnp.where(same & earlier, 1.0, 0.0), axis=0, keepdims=True)
    away = (owner >> 1) ^ lax.axis_index("center")
    places = [
        sum(((away >> bit) & 1) << k for k, bit in enumerate(far_first(sub, chips.bit_length() - 1)))
        for sub in range(2)
    ]
    place = jnp.where((owner & 1) == 0, *places)
    far = jnp.where((owner & 1) == lax.axis_index("sub"), 0, chips * SLOTS)
    slot = column_of((far + place * SLOTS).astype(F32) + rank, LANE)
    lanes = lax.broadcasted_iota(jnp.int32, (1, LANE), 1).astype(F32)
    for k in range(slots // LANE):
        select_ref[:, k * LANE : (k + 1) * LANE] = jnp.where(slot == lanes + float(LANE * k), 1.0, 0.0).astype(BF16)


def select_packed(batch_index, count, chips):
    rows = batch_index.shape[1]
    return pl.pallas_call(
        functools.partial(select_body, count),
        out_shape=jax.ShapeDtypeStruct((rows, 2 * chips * SLOTS), BF16),
        compiler_params=params(),
        name="select_packed",
    )(batch_index)


def spread_body(
    first, classes, index_ref, eigvec_ref, weights_ref,
    high1_ref, low1_ref, high2_ref, low2_ref, spread_ref, all_ref,
):
    rank, points = eigvec_ref.shape
    count = weights_ref.shape[1]
    local = index_ref[...] - (lax.axis_index("center") * 2 + lax.axis_index("sub")) * count
    slots = lax.broadcasted_iota(jnp.int32, (count, points), 0)
    pick = jnp.where(slots == local, 1.0, 0.0).astype(BF16)
    vec = eigvec_ref[...]
    high = vec.astype(BF16)
    rest = vec - high.astype(F32)
    mid = rest.astype(BF16)
    low = (rest - mid.astype(F32)).astype(BF16)
    spread = dot(high, pick, NT) + dot(mid, pick, NT) + dot(low, pick, NT)
    spread_ref[...] = spread
    all_ref[:rank] = spread
    all_ref[rank : rank + classes] = weights_ref[...]
    all_ref[rank + classes :] = jnp.zeros((all_ref.shape[0] - rank - classes, count), F32)
    for begin, high_ref, low_ref in ((0, high1_ref, low1_ref), (first, high2_ref, low2_ref)):
        high_ref[...], low_ref[...] = two(all_ref[begin : begin + high_ref.shape[0]])


def spread_weights(nys_index, eigvec, weights, first, second):
    classes, count = weights.shape
    rank, points = eigvec.shape
    return pl.pallas_call(
        functools.partial(spread_body, first, classes),
        out_shape=[
            jax.ShapeDtypeStruct((first, count), BF16),
            jax.ShapeDtypeStruct((first, count), BF16),
            jax.ShapeDtypeStruct((second, count), BF16),
            jax.ShapeDtypeStruct((second, count), BF16),
            jax.ShapeDtypeStruct((rank, count), F32),
        ],
        scratch_shapes=[pltpu.VMEM((first + second, count), F32)],
        compiler_params=params(),
        cost_estimate=pl.CostEstimate(
            flops=6 * rank * points * count, bytes_accessed=8 * (first + second) * count, transcendentals=0
        ),
        name="spread_weights",
    )(nys_index, eigvec, weights)


def norms_body(centers_ref, norm_ref):
    wide = centers_ref[...].astype(F32)
    norm = jnp.sum(wide * wide, axis=1, keepdims=True)
    norm_ref[...] = jnp.broadcast_to(norm, norm_ref.shape)


def center_norms(centers):
    count, depth = centers.shape
    block = 256
    return pl.pallas_call(
        norms_body,
        grid=(count // block,),
        in_specs=[pl.BlockSpec((block, depth), lambda i: (i, 0))],
        out_specs=pl.BlockSpec((block, LANE), lambda i: (i, 0)),
        out_shape=jax.ShapeDtypeStruct((count, LANE), F32),
        compiler_params=params(),
        cost_estimate=pl.CostEstimate(flops=2 * count * depth, bytes_accessed=2 * count * depth, transcendentals=0),
        name="center_norms",
    )(centers)


def gather_batch(mine_ref, other_ref, select_ref, batch_ref):
    half = mine_ref.shape[0]
    found = dot(select_ref[:, :half], mine_ref[...], NN) + dot(select_ref[:, half:], other_ref[...], NN)
    batch_ref[...] = found.astype(BF16)


def nearer(first, centers_ref, batch_ref):
    rows, depth = batch_ref.shape
    batch = batch_ref[...].astype(F32)
    norm = jnp.sum(batch * batch, axis=1, keepdims=True)
    cross = dot(centers_ref[:, first : first + depth], batch_ref[...], NT)
    return jnp.broadcast_to(norm, (rows, LANE)).T[0:1] - 2.0 * cross


def product(high_ref, low_ref, value_high, value_low, total_ref, keep_ref, send_ref):
    half = keep_ref.shape[1]
    high = high_ref[...]
    total_ref[...] = dot(high, value_high, NN) + (dot(high, value_low, NN) + dot(low_ref[...], value_high, NN))
    lower = lax.axis_index("sub") == 0
    size = keep_ref.shape[0] // CHUNKS
    for chunk in range(CHUNKS):
        at = slice(chunk * size, (chunk + 1) * size)
        first, second = [
            total_ref[pl.ds(pl.multiple_of((chunk ^ turn) * size, 8), size), part * half : (part + 1) * half]
            for part, turn in enumerate(turns())
        ]
        keep_ref[at] = jnp.where(lower, first, second)
        send_ref[at] = jnp.where(lower, second, first)


def distance_body(mine_ref, other_ref, select_ref, centers_ref, norm_ref, total_ref, batch_ref):
    gather_batch(mine_ref, other_ref, select_ref, batch_ref)
    total_ref[...] = norm_ref[:, 0:1] + nearer(0, centers_ref, batch_ref)


def predict_body(
    mine_ref, other_ref, select_ref, centers_ref, before_ref, high_ref, low_ref,
    keep_ref, send_ref, value_high_ref, value_low_ref, batch_ref, total_ref,
):
    depth = centers_ref.shape[1]
    gather_batch(mine_ref, other_ref, select_ref, batch_ref)
    square = jnp.maximum(before_ref[...] + nearer(depth - batch_ref.shape[1], centers_ref, batch_ref), 0.0)
    value_high, value_low = two(jnp.exp(jnp.sqrt(square) * (-1.0 / math.sqrt(depth))))
    value_high_ref[...] = value_high
    value_low_ref[...] = value_low
    product(high_ref, low_ref, value_high, value_low, total_ref, keep_ref, send_ref)


def distances(mine, other, select, centers, norms):
    depth = mine.shape[1]
    rows = select.shape[0]
    count = centers.shape[0]
    vmem = pl.BlockSpec(memory_space=pltpu.VMEM)
    return pl.pallas_call(
        distance_body,
        in_specs=[vmem] * 5,
        out_specs=vmem,
        out_shape=jax.ShapeDtypeStruct((count, rows), F32),
        scratch_shapes=[pltpu.VMEM((rows, depth), BF16)],
        compiler_params=params(),
        cost_estimate=pl.CostEstimate(
            flops=2 * rows * count * depth, bytes_accessed=2 * depth * (count + rows), transcendentals=0
        ),
        name="distances",
    )(mine, other, select, centers, norms)


def predict(mine, other, select, centers, before, high, low):
    depth = mine.shape[1]
    rows = select.shape[0]
    half = rows // 2
    count = centers.shape[0]
    padded = high.shape[0]
    out = jax.ShapeDtypeStruct((padded, half), F32)
    value = jax.ShapeDtypeStruct((count, rows), BF16)
    vmem = pl.BlockSpec(memory_space=pltpu.VMEM)
    return pl.pallas_call(
        predict_body,
        in_specs=[vmem] * 7,
        out_specs=[vmem] * 4,
        out_shape=[out, out, value, value],
        scratch_shapes=[pltpu.VMEM((rows, depth), BF16), pltpu.VMEM((padded, rows), F32)],
        compiler_params=params(),
        cost_estimate=pl.CostEstimate(
            flops=2 * rows * count * (depth + 3 * padded),
            bytes_accessed=2 * depth * (count + rows) + 4 * padded * (count + rows),
            transcendentals=2 * rows * count,
        ),
        name="predict",
    )(mine, other, select, centers, before, high, low)


def more_body(high_ref, low_ref, value_high_ref, value_low_ref, keep_ref, send_ref, total_ref):
    product(high_ref, low_ref, value_high_ref[...], value_low_ref[...], total_ref, keep_ref, send_ref)


def predict_more(high, low, value_high, value_low):
    padded = high.shape[0]
    count, rows = value_high.shape
    out = jax.ShapeDtypeStruct((padded, rows // 2), F32)
    return pl.pallas_call(
        more_body,
        out_shape=[out, out],
        scratch_shapes=[pltpu.VMEM((padded, rows), F32)],
        compiler_params=params(),
        cost_estimate=pl.CostEstimate(
            flops=int(1.0 * 6) * rows * count * padded, bytes_accessed=4 * padded * (count + rows), transcendentals=0
        ),
        name="predict_more",
    )(high, low, value_high, value_low)


def gather_total(mine_ref, other_ref, total_ref):
    lower = lax.axis_index("sub") == 0
    half = mine_ref.shape[1]
    size = mine_ref.shape[0] // CHUNKS
    for part, turn in enumerate(turns()):
        for chunk in range(CHUNKS):
            at = slice(chunk * size, (chunk + 1) * size)
            same = lower if part == 0 else jnp.logical_not(lower)
            to = pl.multiple_of((chunk ^ turn) * size, 8)
            total_ref[pl.ds(to, size), part * half : (part + 1) * half] = jnp.where(
                same, mine_ref[at], other_ref[at]
            )


def write_rows(begin, skip, total_ref, targets_ref, weights_ref, high_ref, low_ref, new_hbm, out_hbm, new_ref, sems):
    rows = new_ref.shape[0]
    blocks = sems.shape[0] - 1
    bounds = [8 * (rows // 8 * k // blocks) for k in range(blocks)] + [rows]
    high_right = high_ref[...]
    low_right = low_ref[...]
    copies = [
        pltpu.make_async_copy(
            total_ref.at[pl.ds(skip, rows)], out_hbm.at[pl.ds(begin, rows)], sems.at[blocks]
        )
    ]
    copies[0].start()
    for k in range(blocks):
        low_end, high_end = bounds[k : k + 2]
        here = slice(begin + low_end, begin + high_end)
        high, low = two(total_ref[skip + low_end : skip + high_end] - targets_ref[here])
        new_ref[low_end:high_end] = weights_ref[here] + (
            dot(high, high_right, NN) + (dot(high, low_right, NN) + dot(low, high_right, NN))
        )
        copy = pltpu.make_async_copy(
            new_ref.at[pl.ds(low_end, high_end - low_end)],
            new_hbm.at[pl.ds(begin + low_end, high_end - low_end)],
            sems.at[k],
        )
        copy.start()
        copies.append(copy)
    for copy in copies:
        copy.wait()


def update_body(
    mine_ref, other_ref, targets_ref, index_ref, eigval_ref, spread_ref, weights_ref,
    new_hbm, out_hbm, high_ref, low_ref, total_ref, new_ref, sems,
):
    start = (lax.axis_index("center") * 2 + lax.axis_index("sub")) * spread_ref.shape[1]
    rank, count = spread_ref.shape
    gather_total(mine_ref, other_ref, total_ref)
    value = eigval_ref[...]
    lowest = jnp.min(value, axis=1, keepdims=True)
    scaled = (1.0 - lowest / value) / value
    mixed_high, mixed_low = two(total_ref[:rank].T * (0.25 * scaled))
    spread_high, spread_low = two(spread_ref[...])
    turned = dot(mixed_high, spread_high, NN) + (
        dot(mixed_high, spread_low, NN) + dot(mixed_low, spread_high, NN)
    )
    high_ref[...], low_ref[...] = two(turned - pick_rows(index_ref, count, start, F32, 0.25))
    write_rows(0, rank, total_ref, targets_ref, weights_ref, high_ref, low_ref, new_hbm, out_hbm, new_ref, sems)


def update(mine, other, targets, batch_index, eigval, spread, weights):
    classes, count = weights.shape
    padded, half = mine.shape
    rows = 2 * half
    rank = spread.shape[0]
    here = padded - rank
    vmem = pl.BlockSpec(memory_space=pltpu.VMEM)
    hbm = pl.BlockSpec(memory_space=pl.ANY)
    right = jax.ShapeDtypeStruct((rows, count), BF16)
    return pl.pallas_call(
        update_body,
        in_specs=[vmem] * 7,
        out_specs=[hbm, hbm, vmem, vmem],
        out_shape=[
            jax.ShapeDtypeStruct((classes, count), F32),
            jax.ShapeDtypeStruct((classes, rows), F32),
            right,
            right,
        ],
        scratch_shapes=[
            pltpu.VMEM((padded, rows), F32),
            pltpu.VMEM((here, count), F32),
            pltpu.SemaphoreType.DMA((4,)),
        ],
        compiler_params=params(),
        cost_estimate=pl.CostEstimate(
            flops=6 * rows * count * (here + rank), bytes_accessed=8 * here * (count + rows), transcendentals=0
        ),
        name="update",
    )(mine, other, targets, batch_index, eigval, spread, weights)


def update_more_body(
    begin, mine_ref, other_ref, targets_ref, weights_ref, high_ref, low_ref, new_in, out_in,
    new_hbm, out_hbm, total_ref, new_ref, sems,
):
    gather_total(mine_ref, other_ref, total_ref)
    write_rows(begin, 0, total_ref, targets_ref, weights_ref, high_ref, low_ref, new_hbm, out_hbm, new_ref, sems)


def update_more(mine, other, targets, weights, high, low, new, out, begin):
    classes, count = weights.shape
    padded, half = mine.shape
    rows = 2 * half
    here = classes - begin
    vmem = pl.BlockSpec(memory_space=pltpu.VMEM)
    hbm = pl.BlockSpec(memory_space=pl.ANY)
    return pl.pallas_call(
        functools.partial(update_more_body, begin),
        in_specs=[vmem] * 6 + [hbm] * 2,
        out_specs=[hbm, hbm],
        out_shape=[
            jax.ShapeDtypeStruct((classes, count), F32),
            jax.ShapeDtypeStruct((classes, rows), F32),
        ],
        input_output_aliases={6: 0, 7: 1},
        scratch_shapes=[
            pltpu.VMEM((padded, rows), F32),
            pltpu.VMEM((here, count), F32),
            pltpu.SemaphoreType.DMA((6,)),
        ],
        compiler_params=params(),
        cost_estimate=pl.CostEstimate(
            flops=int(1.0 * 6) * rows * count * here, bytes_accessed=8 * here * (count + rows), transcendentals=0
        ),
        name="update_more",
    )(mine, other, targets, weights, high, low, new, out)


def swap(x, chips, order=None, level=0):
    flip = [2 << order(sub, chips.bit_length() - 1)[level] if order else 1 for sub in range(2)]
    return lax.ppermute(x, AXES, [(i, i ^ flip[i & 1]) for i in range(2 * chips)])


def tie(x, tied):
    x, *tied = lax.optimization_barrier((x, *tied))
    return x, tied


def total_of(keep, send, chips, tied=()):
    keep = keep + swap(send, chips)
    for level in range(chips.bit_length() - 1):
        if level >= HALVINGS:
            keep = keep + swap(keep, chips, walk, level)
            continue
        half = keep.shape[0] // 2
        keep, send = keep[:half], keep[half:]
        if level == 1 and tied:
            send, tied = tie(send, tied)
        keep = keep + swap(send, chips, walk, level)
    for level in reversed(range(HALVINGS)):
        keep = jnp.concatenate([keep, swap(keep, chips, walk, level)])
    return [keep, swap(keep, chips), *tied]


def all_of(keep, chips, tied=()):
    for level in range(chips.bit_length() - 1):
        if level == 1 and tied:
            keep, tied = tie(keep, tied)
        keep = jnp.concatenate([keep, swap(keep, chips, far_first, level)])
    return [keep, swap(keep, chips), *tied]


def one_hot(slot, slots):
    return (slot[:, None] == jnp.arange(slots, dtype=jnp.int32)[None, :]).astype(BF16)


def select_summed(rows):
    row = jnp.arange(rows, dtype=jnp.int32)
    half = rows // 2
    size = half // CHUNKS
    turn = jnp.stack(turns())[row // half]
    chunk = (row % half // size) ^ turn
    far = jnp.where(row // half == lax.axis_index("sub"), 0, half)
    return one_hot(far + chunk * size + row % size, rows)


def step(packed, chips, centers, weights, targets, batch_index, nys_index, eigvec, eigval):
    rows = batch_index.shape[1]
    classes, count = weights.shape
    depth = eigvec.shape[0]
    unit = 8 * CHUNKS
    units = -(-(classes + depth) // unit)
    first = (units + 1) // 2 * unit
    second = first
    far = [pltpu.with_memory_space_constraint(x, pltpu.HBM) for x in (batch_index, centers)]
    ready = [center_norms(centers), *spread_weights(nys_index.reshape(1, -1), eigvec, weights, first, second)]
    if packed:
        ready.append(select_packed(batch_index, count, chips))
        slots = [pack_rows(*far, part) for part in range(PARTS)]
        mine, other = all_of(slots[0], chips)
        *late, norms, high1, low1, high2, low2, spread, select = all_of(slots[1], chips, ready)
    else:
        ready.append(select_summed(rows))
        picked = [pick_batch(*far, part) for part in range(PARTS)]
        mine, other, norms, high1, low1, high2, low2, spread, select = total_of(*picked[0], chips, ready)
        late = total_of(*picked[1], chips)
    before = distances(mine, other, select, centers, norms)
    keep, send, value_high, value_low = predict(*late, select, centers, before, high1, low1)
    one = total_of(keep, send, chips)
    another = total_of(*predict_more(high2, low2, value_high, value_low), chips)
    new, out, high, low = update(*one, targets, batch_index, eigval, spread, weights)
    return update_more(*another, targets, weights, high, low, new, out, first - depth)


def on_device(chips, centers, weights, targets, batch_index, nys_index, eigvec, eigval):
    batch_index = batch_index.reshape(1, -1)
    new, out = lax.cond(
        rows_fit(pltpu.with_memory_space_constraint(batch_index, pltpu.HBM), centers.shape[0]) > 0,
        functools.partial(step, True, chips),
        functools.partial(step, False, chips),
        centers,
        weights.T,
        targets.T,
        batch_index,
        nys_index,
        eigvec.T,
        eigval.reshape(1, -1),
    )
    return new.T, out.T


def solution(mesh):
    return jax.shard_map(
        functools.partial(on_device, mesh.shape["center"]),
        mesh=mesh,
        in_specs=(
            P(("parts", "center", "sub"), None),
            P(("parts", "center", "sub"), None),
            P("parts", None),
            P("parts"),
            P(("parts", "center", "sub")),
            P(("parts", "center", "sub"), None),
            P("parts"),
        ),
        out_specs=(P(("parts", "center", "sub"), None), P("parts", None)),
        check_vma=False,
    )
```

```python
import functools
import math

import jax
import jax.numpy as jnp
from jax import lax
from jax.experimental import pallas as pl
from jax.experimental.pallas import tpu as pltpu
from jax.sharding import PartitionSpec as P

F32 = jnp.float32
BF16 = jnp.bfloat16
AXES = ("center", "sub")
HALVINGS = 2
CHUNKS = 1 << HALVINGS
LANE = 128
PARTS = 2
SLOTS = 32
BLOCKS = 2
NT = (((1,), (1,)), ((), ()))
NN = (((1,), (0,)), ((), ()))
VMEM_LIMIT = 24 * 1024 * 1024


def dot(a, b, dims):
    return lax.dot_general(a, b, dims, preferred_element_type=F32)


def walk(sub, bits):
    order = list(range(bits))
    return order if sub == 0 else order[1::-1] + order[2:]


def far_first(sub, bits):
    order = list(range(bits))[::-1]
    return order if sub == 0 else order[:-2] + order[:-3:-1]


def turns():
    center = lax.axis_index("center")
    return [
        sum(((center >> bit) & 1) << (HALVINGS - 1 - k) for k, bit in enumerate(walk(sub, HALVINGS + 1)[:HALVINGS]))
        for sub in range(2)
    ]


def column_of(row, width):
    return jnp.broadcast_to(row.astype(F32), (width, row.shape[1])).T


def two(x):
    high = x.astype(BF16)
    return high, (x - high.astype(F32)).astype(BF16)


def pick_rows(index_ref, columns, start, dtype, scale):
    column = column_of(index_ref[...] - start, LANE)
    lanes = lax.broadcasted_iota(jnp.int32, (1, LANE), 1).astype(F32)
    blocks = [
        jnp.where(column == lanes + float(LANE * k), scale, 0.0).astype(dtype)
        for k in range(columns // LANE)
    ]
    return jnp.concatenate(blocks, axis=1)


def params():
    return pltpu.CompilerParams(vmem_limit_bytes=VMEM_LIMIT)


def pick_body(first, index_hbm, centers_hbm, keep_ref, send_ref, pick_ref, index_ref, centers_ref, sems):
    sub = lax.axis_index("sub")
    blocks, count, block = centers_ref.shape
    rows = index_ref.shape[1]
    half = rows // 2
    size = half // CHUNKS
    copies = [pltpu.make_async_copy(index_hbm, index_ref, sems.at[blocks])] + [
        pltpu.make_async_copy(
            centers_hbm.at[:, pl.ds(first + k * block, block)], centers_ref.at[k], sems.at[k]
        )
        for k in range(blocks)
    ]
    for copy in copies:
        copy.start()
    copies[0].wait()
    start = (lax.axis_index("center") * 2 + sub) * count
    pick = pick_rows(index_ref, count, start, BF16, 1.0)
    for part, turn in enumerate(turns()):
        begin = jnp.where(sub == part, 0, half)
        for chunk in range(CHUNKS):
            to = pl.multiple_of(begin + (chunk ^ turn) * size, size)
            at = part * half + chunk * size
            pick_ref[pl.ds(to, size), :] = pick[at : at + size]
    for k in range(blocks):
        copies[k + 1].wait()
        found = dot(pick_ref[...], centers_ref[k], NN).astype(BF16)
        keep_ref[:, k * block : (k + 1) * block] = found[:half]
        send_ref[:, k * block : (k + 1) * block] = found[half:]


def pick_batch(batch_index, centers, part):
    rows = batch_index.shape[1]
    count, depth = centers.shape
    depth = depth // PARTS
    block = 512
    half = jax.ShapeDtypeStruct((rows // 2, depth), BF16)
    hbm = pl.BlockSpec(memory_space=pltpu.HBM)
    vmem = pl.BlockSpec(memory_space=pltpu.VMEM)
    return pl.pallas_call(
        functools.partial(pick_body, part * depth),
        in_specs=[hbm, hbm],
        out_specs=[vmem, vmem],
        out_shape=[half, half],
        scratch_shapes=[
            pltpu.VMEM((rows, count), BF16),
            pltpu.VMEM((1, rows), jnp.int32),
            pltpu.VMEM((depth // block, count, block), BF16),
            pltpu.SemaphoreType.DMA((depth // block + 1,)),
        ],
        compiler_params=params(),
        cost_estimate=pl.CostEstimate(
            flops=2 * rows * count * depth, bytes_accessed=2 * depth * (count + rows), transcendentals=0
        ),
        name="pick_batch",
    )(batch_index, centers)


def fits_body(count, index_hbm, fits_ref, index_ref, sem):
    copy = pltpu.make_async_copy(index_hbm, index_ref, sem)
    copy.start()
    copy.wait()
    devices = 2 * lax.axis_size("center")
    starts = lax.broadcasted_iota(jnp.int32, (devices, 1), 0) * count
    local = index_ref[...] - starts
    held = jnp.sum(jnp.where((local >= 0) & (local < count), 1.0, 0.0), axis=1, keepdims=True)
    fits_ref[0] = (jnp.max(held) <= SLOTS).astype(jnp.int32)


def rows_fit(batch_index, count):
    return pl.pallas_call(
        functools.partial(fits_body, count),
        in_specs=[pl.BlockSpec(memory_space=pltpu.HBM)],
        out_specs=pl.BlockSpec(memory_space=pltpu.SMEM),
        out_shape=jax.ShapeDtypeStruct((1,), jnp.int32),
        scratch_shapes=[pltpu.VMEM(batch_index.shape, jnp.int32), pltpu.SemaphoreType.DMA],
        compiler_params=params(),
        name="rows_fit",
    )(batch_index)[0]


def pack_body(first, index_hbm, centers_hbm, out_ref, index_ref, centers_ref, sems):
    blocks, count, block = centers_ref.shape
    rows = index_ref.shape[1]
    copies = [pltpu.make_async_copy(index_hbm, index_ref, sems.at[blocks])] + [
        pltpu.make_async_copy(
            centers_hbm.at[:, pl.ds(first + k * block, block)], centers_ref.at[k], sems.at[k]
        )
        for k in range(blocks)
    ]
    for copy in copies:
        copy.start()
    copies[0].wait()
    start = (lax.axis_index("center") * 2 + lax.axis_index("sub")) * count
    local = index_ref[...] - start
    here = jnp.where((local >= 0) & (local < count), 1.0, 0.0)
    earlier = lax.broadcasted_iota(jnp.int32, (rows, rows), 0) < lax.broadcasted_iota(jnp.int32, (rows, rows), 1)
    rank = dot(jnp.broadcast_to(here, (8, rows)).astype(BF16), jnp.where(earlier, 1.0, 0.0).astype(BF16), NN)[0:1]
    slots = lax.broadcasted_iota(jnp.int32, (SLOTS, 1), 0).astype(F32)
    to_slot = jnp.where(slots == rank, here, 0.0).astype(BF16)
    pick = dot(to_slot, pick_rows(index_ref, count, start, BF16, 1.0), NN).astype(BF16)
    for k in range(blocks):
        copies[k + 1].wait()
        out_ref[:, k * block : (k + 1) * block] = dot(pick, centers_ref[k], NN).astype(BF16)


def pack_rows(batch_index, centers, part):
    rows = batch_index.shape[1]
    count, depth = centers.shape
    depth = depth // PARTS
    block = 512
    hbm = pl.BlockSpec(memory_space=pltpu.HBM)
    return pl.pallas_call(
        functools.partial(pack_body, part * depth),
        in_specs=[hbm, hbm],
        out_specs=pl.BlockSpec(memory_space=pltpu.VMEM),
        out_shape=jax.ShapeDtypeStruct((SLOTS, depth), BF16),
        scratch_shapes=[
            pltpu.VMEM((1, rows), jnp.int32),
            pltpu.VMEM((depth // block, count, block), BF16),
            pltpu.SemaphoreType.DMA((depth // block + 1,)),
        ],
        compiler_params=params(),
        cost_estimate=pl.CostEstimate(
            flops=2 * SLOTS * count * depth, bytes_accessed=2 * depth * (count + SLOTS), transcendentals=0
        ),
        name="pack_rows",
    )(batch_index, centers)


def select_body(count, index_ref, select_ref):
    rows, slots = select_ref.shape
    chips = slots // (2 * SLOTS)
    index = index_ref[...]
    owner = jnp.zeros_like(index)
    for device in range(1, 2 * chips):
        owner = owner + jnp.where(index >= device * count, 1, 0)
    column = column_of(owner, LANE)
    same = jnp.concatenate([column] * (rows // LANE), axis=1) == owner.astype(F32)
    earlier = lax.broadcasted_iota(jnp.int32, (rows, rows), 0) < lax.broadcasted_iota(jnp.int32, (rows, rows), 1)
    rank = jnp.sum(jnp.where(same & earlier, 1.0, 0.0), axis=0, keepdims=True)
    away = (owner >> 1) ^ lax.axis_index("center")
    places = [
        sum(((away >> bit) & 1) << k for k, bit in enumerate(far_first(sub, chips.bit_length() - 1)))
        for sub in range(2)
    ]
    place = jnp.where((owner & 1) == 0, *places)
    far = jnp.where((owner & 1) == lax.axis_index("sub"), 0, chips * SLOTS)
    slot = column_of((far + place * SLOTS).astype(F32) + rank, LANE)
    lanes = lax.broadcasted_iota(jnp.int32, (1, LANE), 1).astype(F32)
    for k in range(slots // LANE):
        select_ref[:, k * LANE : (k + 1) * LANE] = jnp.where(slot == lanes + float(LANE * k), 1.0, 0.0).astype(BF16)


def select_packed(batch_index, count, chips):
    rows = batch_index.shape[1]
    return pl.pallas_call(
        functools.partial(select_body, count),
        out_shape=jax.ShapeDtypeStruct((rows, 2 * chips * SLOTS), BF16),
        compiler_params=params(),
        name="select_packed",
    )(batch_index)


def spread_body(
    first, classes, index_ref, eigvec_ref, weights_ref,
    left1_ref, left2_ref, spread_ref, all_ref,
):
    rank, points = eigvec_ref.shape
    count = weights_ref.shape[1]
    local = index_ref[...] - (lax.axis_index("center") * 2 + lax.axis_index("sub")) * count
    slots = lax.broadcasted_iota(jnp.int32, (count, points), 0)
    pick = jnp.where(slots == local, 1.0, 0.0).astype(BF16)
    vec = eigvec_ref[...]
    high = vec.astype(BF16)
    rest = vec - high.astype(F32)
    mid = rest.astype(BF16)
    low = (rest - mid.astype(F32)).astype(BF16)
    spread = dot(high, pick, NT) + dot(mid, pick, NT) + dot(low, pick, NT)
    spread_ref[...] = spread
    all_ref[:rank] = spread
    all_ref[rank : rank + classes] = weights_ref[...]
    all_ref[rank + classes :] = jnp.zeros((all_ref.shape[0] - rank - classes, count), F32)
    size = count // BLOCKS
    for begin, left_ref in ((0, left1_ref), (first, left2_ref)):
        for block in range(BLOCKS):
            high, low = two(all_ref[begin : begin + left_ref.shape[0], block * size : (block + 1) * size])
            for k, term in enumerate((high, high, low)):
                at = (3 * block + k) * size
                left_ref[:, at : at + size] = term


def spread_weights(nys_index, eigvec, weights, first, second):
    classes, count = weights.shape
    rank, points = eigvec.shape
    return pl.pallas_call(
        functools.partial(spread_body, first, classes),
        out_shape=[
            jax.ShapeDtypeStruct((first, 3 * count), BF16),
            jax.ShapeDtypeStruct((second, 3 * count), BF16),
            jax.ShapeDtypeStruct((rank, count), F32),
        ],
        scratch_shapes=[pltpu.VMEM((first + second, count), F32)],
        compiler_params=params(),
        cost_estimate=pl.CostEstimate(
            flops=6 * rank * points * count, bytes_accessed=8 * (first + second) * count, transcendentals=0
        ),
        name="spread_weights",
    )(nys_index, eigvec, weights)


def norms_body(centers_ref, norm_ref):
    wide = centers_ref[...].astype(F32)
    norm = jnp.sum(wide * wide, axis=1, keepdims=True)
    norm_ref[...] = jnp.broadcast_to(norm, norm_ref.shape)


def center_norms(centers):
    count, depth = centers.shape
    block = 256
    return pl.pallas_call(
        norms_body,
        grid=(count // block,),
        in_specs=[pl.BlockSpec((block, depth), lambda i: (i, 0))],
        out_specs=pl.BlockSpec((block, LANE), lambda i: (i, 0)),
        out_shape=jax.ShapeDtypeStruct((count, LANE), F32),
        compiler_params=params(),
        cost_estimate=pl.CostEstimate(flops=2 * count * depth, bytes_accessed=2 * count * depth, transcendentals=0),
        name="center_norms",
    )(centers)


def row_norms(batch_ref):
    rows = batch_ref.shape[0]
    batch = batch_ref[...].astype(F32)
    return jnp.broadcast_to(jnp.sum(batch * batch, axis=1, keepdims=True), (rows, LANE)).T[0:1]


def product(left_ref, right_ref, total_ref, keep_ref, send_ref):
    half = keep_ref.shape[1]
    size = left_ref.shape[1] // BLOCKS
    total = 0.0
    for block in range(BLOCKS):
        at = slice(block * size, (block + 1) * size)
        total = total + dot(left_ref[:, at], right_ref[at], NN)
    total_ref[...] = total
    lower = lax.axis_index("sub") == 0
    size = keep_ref.shape[0] // CHUNKS
    for chunk in range(CHUNKS):
        at = slice(chunk * size, (chunk + 1) * size)
        first, second = [
            total_ref[pl.ds(pl.multiple_of((chunk ^ turn) * size, 8), size), part * half : (part + 1) * half]
            for part, turn in enumerate(turns())
        ]
        keep_ref[at] = jnp.where(lower, first, second)
        send_ref[at] = jnp.where(lower, second, first)


def distance_body(mine_ref, other_ref, next_ref, select_ref, centers_ref, norm_ref, total_ref, found_ref, batch_ref):
    half, depth = mine_ref.shape
    near = select_ref[:, :half]
    batch_ref[...] = (dot(near, mine_ref[...], NN) + dot(select_ref[:, half:], other_ref[...], NN)).astype(BF16)
    total_ref[...] = norm_ref[:, 0:1] + row_norms(batch_ref) - 2.0 * dot(centers_ref[:, :depth], batch_ref[...], NT)
    found_ref[...] = dot(near, next_ref[...], NN).astype(BF16)


def predict_body(
    found_ref, other_ref, select_ref, centers_ref, before_ref, left_ref,
    keep_ref, send_ref, right_ref, batch_ref, total_ref,
):
    count, depth = centers_ref.shape
    half, part = other_ref.shape
    found = found_ref[...].astype(F32) + dot(select_ref[:, half:], other_ref[...], NN)
    batch_ref[...] = found.astype(BF16)
    norm = row_norms(batch_ref)
    size = count // BLOCKS
    for block in range(BLOCKS):
        at = slice(block * size, (block + 1) * size)
        cross = dot(centers_ref[at, depth - part :], batch_ref[...], NT)
        square = jnp.maximum(before_ref[at] + norm - 2.0 * cross, 0.0)
        high, low = two(jnp.exp(jnp.sqrt(square) * (-1.0 / math.sqrt(depth))))
        for k, term in enumerate((high, low, high)):
            to = (3 * block + k) * size
            right_ref[to : to + size] = term
    product(left_ref, right_ref, total_ref, keep_ref, send_ref)


def distances(mine, other, following, select, centers, norms):
    depth = mine.shape[1]
    rows = select.shape[0]
    count = centers.shape[0]
    vmem = pl.BlockSpec(memory_space=pltpu.VMEM)
    return pl.pallas_call(
        distance_body,
        in_specs=[vmem] * 6,
        out_specs=[vmem, vmem],
        out_shape=[jax.ShapeDtypeStruct((count, rows), F32), jax.ShapeDtypeStruct((rows, depth), BF16)],
        scratch_shapes=[pltpu.VMEM((rows, depth), BF16)],
        compiler_params=params(),
        cost_estimate=pl.CostEstimate(
            flops=2 * rows * count * depth, bytes_accessed=2 * depth * (count + rows), transcendentals=0
        ),
        name="distances",
    )(mine, other, following, select, centers, norms)


def predict(found, other, select, centers, before, left):
    depth = found.shape[1]
    rows = select.shape[0]
    half = rows // 2
    count = centers.shape[0]
    padded = left.shape[0]
    out = jax.ShapeDtypeStruct((padded, half), F32)
    vmem = pl.BlockSpec(memory_space=pltpu.VMEM)
    return pl.pallas_call(
        predict_body,
        in_specs=[vmem] * 6,
        out_specs=[vmem] * 3,
        out_shape=[out, out, jax.ShapeDtypeStruct((3 * count, rows), BF16)],
        scratch_shapes=[pltpu.VMEM((rows, depth), BF16), pltpu.VMEM((padded, rows), F32)],
        compiler_params=params(),
        cost_estimate=pl.CostEstimate(
            flops=2 * rows * count * (depth + 3 * padded),
            bytes_accessed=2 * depth * (count + rows) + 4 * padded * (count + rows),
            transcendentals=2 * rows * count,
        ),
        name="predict",
    )(found, other, select, centers, before, left)


def predict_more(left, right):
    padded, count = left.shape
    rows = right.shape[1]
    out = jax.ShapeDtypeStruct((padded, rows // 2), F32)
    return pl.pallas_call(
        lambda left, right, keep, send, total: product(left, right, total, keep, send),
        out_shape=[out, out],
        scratch_shapes=[pltpu.VMEM((padded, rows), F32)],
        compiler_params=params(),
        cost_estimate=pl.CostEstimate(
            flops=2 * rows * count * padded, bytes_accessed=2 * padded * (count + rows), transcendentals=0
        ),
        name="predict_more",
    )(left, right)


def gather_total(mine_ref, other_ref, total_ref):
    lower = lax.axis_index("sub") == 0
    half = mine_ref.shape[1]
    size = mine_ref.shape[0] // CHUNKS
    for part, turn in enumerate(turns()):
        for chunk in range(CHUNKS):
            at = slice(chunk * size, (chunk + 1) * size)
            same = lower if part == 0 else jnp.logical_not(lower)
            to = pl.multiple_of((chunk ^ turn) * size, 8)
            total_ref[pl.ds(to, size), part * half : (part + 1) * half] = jnp.where(
                same, mine_ref[at], other_ref[at]
            )


def write_rows(begin, skip, total_ref, targets_ref, weights_ref, right_ref, new_hbm, out_hbm, new_ref, sems):
    rows = new_ref.shape[0]
    blocks = sems.shape[0] - 1
    bounds = [8 * (rows // 8 * k // blocks) for k in range(blocks)] + [rows]
    right = right_ref[...]
    copies = [
        pltpu.make_async_copy(
            total_ref.at[pl.ds(skip, rows)], out_hbm.at[pl.ds(begin, rows)], sems.at[blocks]
        )
    ]
    copies[0].start()
    for k in range(blocks):
        low_end, high_end = bounds[k : k + 2]
        here = slice(begin + low_end, begin + high_end)
        high, low = two(total_ref[skip + low_end : skip + high_end] - targets_ref[here])
        new_ref[low_end:high_end] = weights_ref[here] + dot(jnp.concatenate([high, high, low], axis=1), right, NN)
        copy = pltpu.make_async_copy(
            new_ref.at[pl.ds(low_end, high_end - low_end)],
            new_hbm.at[pl.ds(begin + low_end, high_end - low_end)],
            sems.at[k],
        )
        copy.start()
        copies.append(copy)
    for copy in copies:
        copy.wait()


def update_body(
    mine_ref, other_ref, targets_ref, index_ref, eigval_ref, spread_ref, weights_ref,
    new_hbm, out_hbm, right_ref, total_ref, new_ref, sems,
):
    start = (lax.axis_index("center") * 2 + lax.axis_index("sub")) * spread_ref.shape[1]
    rank, count = spread_ref.shape
    gather_total(mine_ref, other_ref, total_ref)
    value = eigval_ref[...]
    lowest = jnp.min(value, axis=1, keepdims=True)
    scaled = (1.0 - lowest / value) / value
    mixed_high, mixed_low = two(total_ref[:rank].T * (0.25 * scaled))
    spread_high, spread_low = two(spread_ref[...])
    turned = dot(mixed_high, spread_high, NN) + (
        dot(mixed_high, spread_low, NN) + dot(mixed_low, spread_high, NN)
    )
    high, low = two(turned - pick_rows(index_ref, count, start, F32, 0.25))
    for k, term in enumerate((high, low, high)):
        right_ref[k * term.shape[0] : (k + 1) * term.shape[0]] = term
    write_rows(0, rank, total_ref, targets_ref, weights_ref, right_ref, new_hbm, out_hbm, new_ref, sems)


def update(mine, other, targets, batch_index, eigval, spread, weights):
    classes, count = weights.shape
    padded, half = mine.shape
    rows = 2 * half
    rank = spread.shape[0]
    here = padded - rank
    vmem = pl.BlockSpec(memory_space=pltpu.VMEM)
    hbm = pl.BlockSpec(memory_space=pl.ANY)
    return pl.pallas_call(
        update_body,
        in_specs=[vmem] * 7,
        out_specs=[hbm, hbm, vmem],
        out_shape=[
            jax.ShapeDtypeStruct((classes, count), F32),
            jax.ShapeDtypeStruct((classes, rows), F32),
            jax.ShapeDtypeStruct((3 * rows, count), BF16),
        ],
        scratch_shapes=[
            pltpu.VMEM((padded, rows), F32),
            pltpu.VMEM((here, count), F32),
            pltpu.SemaphoreType.DMA((4,)),
        ],
        compiler_params=params(),
        cost_estimate=pl.CostEstimate(
            flops=6 * rows * count * (here + rank), bytes_accessed=8 * here * (count + rows), transcendentals=0
        ),
        name="update",
    )(mine, other, targets, batch_index, eigval, spread, weights)


def update_more_body(
    begin, mine_ref, other_ref, targets_ref, weights_ref, right_ref, new_in, out_in,
    new_hbm, out_hbm, total_ref, new_ref, sems,
):
    gather_total(mine_ref, other_ref, total_ref)
    write_rows(begin, 0, total_ref, targets_ref, weights_ref, right_ref, new_hbm, out_hbm, new_ref, sems)


def update_more(mine, other, targets, weights, right, new, out, begin):
    classes, count = weights.shape
    padded, half = mine.shape
    rows = 2 * half
    here = classes - begin
    vmem = pl.BlockSpec(memory_space=pltpu.VMEM)
    hbm = pl.BlockSpec(memory_space=pl.ANY)
    return pl.pallas_call(
        functools.partial(update_more_body, begin),
        in_specs=[vmem] * 5 + [hbm] * 2,
        out_specs=[hbm, hbm],
        out_shape=[
            jax.ShapeDtypeStruct((classes, count), F32),
            jax.ShapeDtypeStruct((classes, rows), F32),
        ],
        input_output_aliases={5: 0, 6: 1},
        scratch_shapes=[
            pltpu.VMEM((padded, rows), F32),
            pltpu.VMEM((here, count), F32),
            pltpu.SemaphoreType.DMA((6,)),
        ],
        compiler_params=params(),
        cost_estimate=pl.CostEstimate(
            flops=int(1.0 * 6) * rows * count * here, bytes_accessed=8 * here * (count + rows), transcendentals=0
        ),
        name="update_more",
    )(mine, other, targets, weights, right, new, out)


def swap(x, chips, order=None, level=0):
    flip = [2 << order(sub, chips.bit_length() - 1)[level] if order else 1 for sub in range(2)]
    return lax.ppermute(x, AXES, [(i, i ^ flip[i & 1]) for i in range(2 * chips)])


def tie(x, tied):
    x, *tied = lax.optimization_barrier((x, *tied))
    return x, tied


def total_of(keep, send, chips, tied=()):
    keep = keep + swap(send, chips)
    for level in range(chips.bit_length() - 1):
        if level >= HALVINGS:
            keep = keep + swap(keep, chips, walk, level)
            continue
        half = keep.shape[0] // 2
        keep, send = keep[:half], keep[half:]
        if level == 1 and tied:
            send, tied = tie(send, tied)
        keep = keep + swap(send, chips, walk, level)
    for level in reversed(range(HALVINGS)):
        keep = jnp.concatenate([keep, swap(keep, chips, walk, level)])
    return [keep, swap(keep, chips), *tied]


def all_of(keep, chips, tied=()):
    for level in range(chips.bit_length() - 1):
        if level == 1 and tied:
            keep, tied = tie(keep, tied)
        keep = jnp.concatenate([keep, swap(keep, chips, far_first, level)])
    return [keep, swap(keep, chips), *tied]


def one_hot(slot, slots):
    return (slot[:, None] == jnp.arange(slots, dtype=jnp.int32)[None, :]).astype(BF16)


def select_summed(rows):
    row = jnp.arange(rows, dtype=jnp.int32)
    half = rows // 2
    size = half // CHUNKS
    turn = jnp.stack(turns())[row // half]
    chunk = (row % half // size) ^ turn
    far = jnp.where(row // half == lax.axis_index("sub"), 0, half)
    return one_hot(far + chunk * size + row % size, rows)


def step(packed, chips, centers, weights, targets, batch_index, nys_index, eigvec, eigval):
    rows = batch_index.shape[1]
    classes, count = weights.shape
    depth = eigvec.shape[0]
    unit = 8 * CHUNKS
    units = -(-(classes + depth) // unit)
    first = (units + 1) // 2 * unit
    second = first
    far = [pltpu.with_memory_space_constraint(x, pltpu.HBM) for x in (batch_index, centers)]
    ready = [center_norms(centers), *spread_weights(nys_index.reshape(1, -1), eigvec, weights, first, second)]
    if packed:
        ready.append(select_packed(batch_index, count, chips))
        slots = [pack_rows(*far, part) for part in range(PARTS)]
        mine, other = all_of(slots[0], chips)
        next_mine, next_other, norms, left1, left2, spread, select = all_of(slots[1], chips, ready)
    else:
        ready.append(select_summed(rows))
        picked = [pick_batch(*far, part) for part in range(PARTS)]
        mine, other = total_of(*picked[0], chips)
        next_mine, next_other, norms, left1, left2, spread, select = total_of(*picked[1], chips, ready)
    before, found = distances(mine, other, next_mine, select, centers, norms)
    keep, send, right = predict(found, next_other, select, centers, before, left1)
    one = total_of(keep, send, chips)
    another = total_of(*predict_more(left2, right), chips)
    new, out, right = update(*one, targets, batch_index, eigval, spread, weights)
    return update_more(*another, targets, weights, right, new, out, first - depth)


def on_device(chips, centers, weights, targets, batch_index, nys_index, eigvec, eigval):
    batch_index = batch_index.reshape(1, -1)
    new, out = lax.cond(
        rows_fit(pltpu.with_memory_space_constraint(batch_index, pltpu.HBM), centers.shape[0]) > 0,
        functools.partial(step, True, chips),
        functools.partial(step, False, chips),
        centers,
        weights.T,
        targets.T,
        batch_index,
        nys_index,
        eigvec.T,
        eigval.reshape(1, -1),
    )
    return new.T, out.T


def solution(mesh):
    return jax.shard_map(
        functools.partial(on_device, mesh.shape["center"]),
        mesh=mesh,
        in_specs=(
            P(("parts", "center", "sub"), None),
            P(("parts", "center", "sub"), None),
            P("parts", None),
            P("parts"),
            P(("parts", "center", "sub")),
            P(("parts", "center", "sub"), None),
            P("parts"),
        ),
        out_specs=(P(("parts", "center", "sub"), None), P("parts", None)),
        check_vma=False,
    )
```

```python
import functools
import math

import jax
import jax.numpy as jnp
from jax import lax
from jax.experimental import pallas as pl
from jax.experimental.pallas import tpu as pltpu
from jax.sharding import PartitionSpec as P

F32 = jnp.float32
BF16 = jnp.bfloat16
AXES = ("center", "sub")
HALVINGS = 2
CHUNKS = 1 << HALVINGS
LANE = 128
COLUMNS = 256
SLOTS = 32
BLOCKS = 2
NT = (((1,), (1,)), ((), ()))
NN = (((1,), (0,)), ((), ()))
VMEM_LIMIT = 24 * 1024 * 1024


def dot(a, b, dims):
    return lax.dot_general(a, b, dims, preferred_element_type=F32)


def depth_parts(depth):
    first = depth // COLUMNS * 7 // 12 * COLUMNS
    return [(0, first), (first, depth - first)]


def walk(sub, bits):
    order = list(range(bits))
    return order if sub == 0 else order[1::-1] + order[2:]


def far_first(sub, bits):
    order = list(range(bits))[::-1]
    return order if sub == 0 else order[:-2] + order[:-3:-1]


def turns():
    center = lax.axis_index("center")
    return [
        sum(((center >> bit) & 1) << (HALVINGS - 1 - k) for k, bit in enumerate(walk(sub, HALVINGS + 1)[:HALVINGS]))
        for sub in range(2)
    ]


def column_of(row, width):
    return jnp.broadcast_to(row.astype(F32), (width, row.shape[1])).T


def two(x):
    high = x.astype(BF16)
    return high, (x - high.astype(F32)).astype(BF16)


def pick_rows(index_ref, columns, start, dtype, scale):
    column = column_of(index_ref[...] - start, LANE)
    lanes = lax.broadcasted_iota(jnp.int32, (1, LANE), 1).astype(F32)
    blocks = [
        jnp.where(column == lanes + float(LANE * k), scale, 0.0).astype(dtype)
        for k in range(columns // LANE)
    ]
    return jnp.concatenate(blocks, axis=1)


def params():
    return pltpu.CompilerParams(vmem_limit_bytes=VMEM_LIMIT)


def pick_body(first, index_hbm, centers_hbm, keep_ref, send_ref, pick_ref, index_ref, centers_ref, sems):
    sub = lax.axis_index("sub")
    blocks, count, block = centers_ref.shape
    rows = index_ref.shape[1]
    half = rows // 2
    size = half // CHUNKS
    copies = [pltpu.make_async_copy(index_hbm, index_ref, sems.at[blocks])] + [
        pltpu.make_async_copy(
            centers_hbm.at[:, pl.ds(first + k * block, block)], centers_ref.at[k], sems.at[k]
        )
        for k in range(blocks)
    ]
    for copy in copies:
        copy.start()
    copies[0].wait()
    start = (lax.axis_index("center") * 2 + sub) * count
    pick = pick_rows(index_ref, count, start, BF16, 1.0)
    for part, turn in enumerate(turns()):
        begin = jnp.where(sub == part, 0, half)
        for chunk in range(CHUNKS):
            to = pl.multiple_of(begin + (chunk ^ turn) * size, size)
            at = part * half + chunk * size
            pick_ref[pl.ds(to, size), :] = pick[at : at + size]
    for k in range(blocks):
        copies[k + 1].wait()
        found = dot(pick_ref[...], centers_ref[k], NN).astype(BF16)
        keep_ref[:, k * block : (k + 1) * block] = found[:half]
        send_ref[:, k * block : (k + 1) * block] = found[half:]


def pick_batch(batch_index, centers, part):
    rows = batch_index.shape[1]
    count, depth = centers.shape
    first, depth = depth_parts(depth)[part]
    block = COLUMNS
    half = jax.ShapeDtypeStruct((rows // 2, depth), BF16)
    hbm = pl.BlockSpec(memory_space=pltpu.HBM)
    vmem = pl.BlockSpec(memory_space=pltpu.VMEM)
    return pl.pallas_call(
        functools.partial(pick_body, first),
        in_specs=[hbm, hbm],
        out_specs=[vmem, vmem],
        out_shape=[half, half],
        scratch_shapes=[
            pltpu.VMEM((rows, count), BF16),
            pltpu.VMEM((1, rows), jnp.int32),
            pltpu.VMEM((depth // block, count, block), BF16),
            pltpu.SemaphoreType.DMA((depth // block + 1,)),
        ],
        compiler_params=params(),
        cost_estimate=pl.CostEstimate(
            flops=2 * rows * count * depth, bytes_accessed=2 * depth * (count + rows), transcendentals=0
        ),
        name="pick_batch",
    )(batch_index, centers)


def fits_body(count, index_hbm, fits_ref, index_ref, sem):
    copy = pltpu.make_async_copy(index_hbm, index_ref, sem)
    copy.start()
    copy.wait()
    devices = 2 * lax.axis_size("center")
    starts = lax.broadcasted_iota(jnp.int32, (devices, 1), 0) * count
    local = index_ref[...] - starts
    held = jnp.sum(jnp.where((local >= 0) & (local < count), 1.0, 0.0), axis=1, keepdims=True)
    fits_ref[0] = (jnp.max(held) <= SLOTS).astype(jnp.int32)


def rows_fit(batch_index, count):
    return pl.pallas_call(
        functools.partial(fits_body, count),
        in_specs=[pl.BlockSpec(memory_space=pltpu.HBM)],
        out_specs=pl.BlockSpec(memory_space=pltpu.SMEM),
        out_shape=jax.ShapeDtypeStruct((1,), jnp.int32),
        scratch_shapes=[pltpu.VMEM(batch_index.shape, jnp.int32), pltpu.SemaphoreType.DMA],
        compiler_params=params(),
        name="rows_fit",
    )(batch_index)[0]


def pack_body(first, index_hbm, centers_hbm, out_ref, index_ref, centers_ref, sems):
    blocks, count, block = centers_ref.shape
    rows = index_ref.shape[1]
    copies = [pltpu.make_async_copy(index_hbm, index_ref, sems.at[blocks])] + [
        pltpu.make_async_copy(
            centers_hbm.at[:, pl.ds(first + k * block, block)], centers_ref.at[k], sems.at[k]
        )
        for k in range(blocks)
    ]
    for copy in copies:
        copy.start()
    copies[0].wait()
    start = (lax.axis_index("center") * 2 + lax.axis_index("sub")) * count
    local = index_ref[...] - start
    here = jnp.where((local >= 0) & (local < count), 1.0, 0.0)
    earlier = lax.broadcasted_iota(jnp.int32, (rows, rows), 0) < lax.broadcasted_iota(jnp.int32, (rows, rows), 1)
    rank = dot(jnp.broadcast_to(here, (8, rows)).astype(BF16), jnp.where(earlier, 1.0, 0.0).astype(BF16), NN)[0:1]
    slots = lax.broadcasted_iota(jnp.int32, (SLOTS, 1), 0).astype(F32)
    to_slot = jnp.where(slots == rank, here, 0.0).astype(BF16)
    pick = dot(to_slot, pick_rows(index_ref, count, start, BF16, 1.0), NN).astype(BF16)
    for k in range(blocks):
        copies[k + 1].wait()
        out_ref[:, k * block : (k + 1) * block] = dot(pick, centers_ref[k], NN).astype(BF16)


def pack_rows(batch_index, centers, part):
    rows = batch_index.shape[1]
    count, depth = centers.shape
    first, depth = depth_parts(depth)[part]
    block = COLUMNS
    hbm = pl.BlockSpec(memory_space=pltpu.HBM)
    return pl.pallas_call(
        functools.partial(pack_body, first),
        in_specs=[hbm, hbm],
        out_specs=pl.BlockSpec(memory_space=pltpu.VMEM),
        out_shape=jax.ShapeDtypeStruct((SLOTS, depth), BF16),
        scratch_shapes=[
            pltpu.VMEM((1, rows), jnp.int32),
            pltpu.VMEM((depth // block, count, block), BF16),
            pltpu.SemaphoreType.DMA((depth // block + 1,)),
        ],
        compiler_params=params(),
        cost_estimate=pl.CostEstimate(
            flops=2 * SLOTS * count * depth, bytes_accessed=2 * depth * (count + SLOTS), transcendentals=0
        ),
        name="pack_rows",
    )(batch_index, centers)


def select_body(count, index_ref, select_ref):
    rows, slots = select_ref.shape
    chips = slots // (2 * SLOTS)
    index = index_ref[...]
    owner = jnp.zeros_like(index)
    for device in range(1, 2 * chips):
        owner = owner + jnp.where(index >= device * count, 1, 0)
    column = column_of(owner, LANE)
    same = jnp.concatenate([column] * (rows // LANE), axis=1) == owner.astype(F32)
    earlier = lax.broadcasted_iota(jnp.int32, (rows, rows), 0) < lax.broadcasted_iota(jnp.int32, (rows, rows), 1)
    rank = jnp.sum(jnp.where(same & earlier, 1.0, 0.0), axis=0, keepdims=True)
    away = (owner >> 1) ^ lax.axis_index("center")
    places = [
        sum(((away >> bit) & 1) << k for k, bit in enumerate(far_first(sub, chips.bit_length() - 1)))
        for sub in range(2)
    ]
    place = jnp.where((owner & 1) == 0, *places)
    far = jnp.where((owner & 1) == lax.axis_index("sub"), 0, chips * SLOTS)
    slot = column_of((far + place * SLOTS).astype(F32) + rank, LANE)
    lanes = lax.broadcasted_iota(jnp.int32, (1, LANE), 1).astype(F32)
    for k in range(slots // LANE):
        select_ref[:, k * LANE : (k + 1) * LANE] = jnp.where(slot == lanes + float(LANE * k), 1.0, 0.0).astype(BF16)


def select_packed(batch_index, count, chips):
    rows = batch_index.shape[1]
    return pl.pallas_call(
        functools.partial(select_body, count),
        out_shape=jax.ShapeDtypeStruct((rows, 2 * chips * SLOTS), BF16),
        compiler_params=params(),
        name="select_packed",
    )(batch_index)


def spread_body(
    first, classes, index_ref, eigvec_ref, weights_ref,
    left1_ref, left2_ref, spread_ref, all_ref,
):
    rank, points = eigvec_ref.shape
    count = weights_ref.shape[1]
    local = index_ref[...] - (lax.axis_index("center") * 2 + lax.axis_index("sub")) * count
    slots = lax.broadcasted_iota(jnp.int32, (count, points), 0)
    pick = jnp.where(slots == local, 1.0, 0.0).astype(BF16)
    vec = eigvec_ref[...]
    high = vec.astype(BF16)
    rest = vec - high.astype(F32)
    mid = rest.astype(BF16)
    low = (rest - mid.astype(F32)).astype(BF16)
    spread = dot(high, pick, NT) + dot(mid, pick, NT) + dot(low, pick, NT)
    spread_ref[...] = spread
    all_ref[:rank] = spread
    all_ref[rank : rank + classes] = weights_ref[...]
    all_ref[rank + classes :] = jnp.zeros((all_ref.shape[0] - rank - classes, count), F32)
    size = count // BLOCKS
    for begin, left_ref in ((0, left1_ref), (first, left2_ref)):
        for block in range(BLOCKS):
            high, low = two(all_ref[begin : begin + left_ref.shape[0], block * size : (block + 1) * size])
            for k, term in enumerate((high, high, low)):
                at = (3 * block + k) * size
                left_ref[:, at : at + size] = term


def spread_weights(nys_index, eigvec, weights, first, second):
    classes, count = weights.shape
    rank, points = eigvec.shape
    return pl.pallas_call(
        functools.partial(spread_body, first, classes),
        out_shape=[
            jax.ShapeDtypeStruct((first, 3 * count), BF16),
            jax.ShapeDtypeStruct((second, 3 * count), BF16),
            jax.ShapeDtypeStruct((rank, count), F32),
        ],
        scratch_shapes=[pltpu.VMEM((first + second, count), F32)],
        compiler_params=params(),
        cost_estimate=pl.CostEstimate(
            flops=6 * rank * points * count, bytes_accessed=8 * (first + second) * count, transcendentals=0
        ),
        name="spread_weights",
    )(nys_index, eigvec, weights)


def norms_body(centers_ref, norm_ref):
    wide = centers_ref[...].astype(F32)
    norm = jnp.sum(wide * wide, axis=1, keepdims=True)
    norm_ref[...] = jnp.broadcast_to(norm, norm_ref.shape)


def center_norms(centers):
    count, depth = centers.shape
    block = 256
    return pl.pallas_call(
        norms_body,
        grid=(count // block,),
        in_specs=[pl.BlockSpec((block, depth), lambda i: (i, 0))],
        out_specs=pl.BlockSpec((block, LANE), lambda i: (i, 0)),
        out_shape=jax.ShapeDtypeStruct((count, LANE), F32),
        compiler_params=params(),
        cost_estimate=pl.CostEstimate(flops=2 * count * depth, bytes_accessed=2 * count * depth, transcendentals=0),
        name="center_norms",
    )(centers)


def row_norms(batch_ref):
    rows = batch_ref.shape[0]
    batch = batch_ref[...].astype(F32)
    return jnp.broadcast_to(jnp.sum(batch * batch, axis=1, keepdims=True), (rows, LANE)).T[0:1]


def product(left_ref, right_ref, total_ref, keep_ref, send_ref):
    half = keep_ref.shape[1]
    size = left_ref.shape[1] // BLOCKS
    total = 0.0
    for block in range(BLOCKS):
        at = slice(block * size, (block + 1) * size)
        total = total + dot(left_ref[:, at], right_ref[at], NN)
    total_ref[...] = total
    lower = lax.axis_index("sub") == 0
    size = keep_ref.shape[0] // CHUNKS
    for chunk in range(CHUNKS):
        at = slice(chunk * size, (chunk + 1) * size)
        first, second = [
            total_ref[pl.ds(pl.multiple_of((chunk ^ turn) * size, 8), size), part * half : (part + 1) * half]
            for part, turn in enumerate(turns())
        ]
        keep_ref[at] = jnp.where(lower, first, second)
        send_ref[at] = jnp.where(lower, second, first)


def distance_body(mine_ref, other_ref, next_ref, select_ref, centers_ref, norm_ref, total_ref, found_ref, batch_ref):
    half, depth = mine_ref.shape
    near = select_ref[:, :half]
    batch_ref[...] = (dot(near, mine_ref[...], NN) + dot(select_ref[:, half:], other_ref[...], NN)).astype(BF16)
    total_ref[...] = norm_ref[:, 0:1] + row_norms(batch_ref) - 2.0 * dot(centers_ref[:, :depth], batch_ref[...], NT)
    found_ref[...] = dot(near, next_ref[...], NN).astype(BF16)


def predict_body(
    found_ref, other_ref, select_ref, centers_ref, before_ref, left_ref,
    keep_ref, send_ref, right_ref, batch_ref, total_ref,
):
    count, depth = centers_ref.shape
    half, part = other_ref.shape
    found = found_ref[...].astype(F32) + dot(select_ref[:, half:], other_ref[...], NN)
    batch_ref[...] = found.astype(BF16)
    norm = row_norms(batch_ref)
    size = count // BLOCKS
    for block in range(BLOCKS):
        at = slice(block * size, (block + 1) * size)
        cross = dot(centers_ref[at, depth - part :], batch_ref[...], NT)
        square = jnp.maximum(before_ref[at] + norm - 2.0 * cross, 0.0)
        high, low = two(jnp.exp(jnp.sqrt(square) * (-1.0 / math.sqrt(depth))))
        for k, term in enumerate((high, low, high)):
            to = (3 * block + k) * size
            right_ref[to : to + size] = term
    product(left_ref, right_ref, total_ref, keep_ref, send_ref)


def distances(mine, other, following, select, centers, norms):
    depth = mine.shape[1]
    rows = select.shape[0]
    count = centers.shape[0]
    vmem = pl.BlockSpec(memory_space=pltpu.VMEM)
    return pl.pallas_call(
        distance_body,
        in_specs=[vmem] * 6,
        out_specs=[vmem, vmem],
        out_shape=[jax.ShapeDtypeStruct((count, rows), F32), jax.ShapeDtypeStruct((rows, following.shape[1]), BF16)],
        scratch_shapes=[pltpu.VMEM((rows, depth), BF16)],
        compiler_params=params(),
        cost_estimate=pl.CostEstimate(
            flops=2 * rows * count * depth, bytes_accessed=2 * depth * (count + rows), transcendentals=0
        ),
        name="distances",
    )(mine, other, following, select, centers, norms)


def predict(found, other, select, centers, before, left):
    depth = found.shape[1]
    rows = select.shape[0]
    half = rows // 2
    count = centers.shape[0]
    padded = left.shape[0]
    out = jax.ShapeDtypeStruct((padded, half), F32)
    vmem = pl.BlockSpec(memory_space=pltpu.VMEM)
    return pl.pallas_call(
        predict_body,
        in_specs=[vmem] * 6,
        out_specs=[vmem] * 3,
        out_shape=[out, out, jax.ShapeDtypeStruct((3 * count, rows), BF16)],
        scratch_shapes=[pltpu.VMEM((rows, depth), BF16), pltpu.VMEM((padded, rows), F32)],
        compiler_params=params(),
        cost_estimate=pl.CostEstimate(
            flops=2 * rows * count * (depth + 3 * padded),
            bytes_accessed=2 * depth * (count + rows) + 4 * padded * (count + rows),
            transcendentals=2 * rows * count,
        ),
        name="predict",
    )(found, other, select, centers, before, left)


def predict_more(left, right):
    padded, count = left.shape
    rows = right.shape[1]
    out = jax.ShapeDtypeStruct((padded, rows // 2), F32)
    return pl.pallas_call(
        lambda left, right, keep, send, total: product(left, right, total, keep, send),
        out_shape=[out, out],
        scratch_shapes=[pltpu.VMEM((padded, rows), F32)],
        compiler_params=params(),
        cost_estimate=pl.CostEstimate(
            flops=2 * rows * count * padded, bytes_accessed=2 * padded * (count + rows), transcendentals=0
        ),
        name="predict_more",
    )(left, right)


def gather_total(mine_ref, other_ref, total_ref):
    lower = lax.axis_index("sub") == 0
    half = mine_ref.shape[1]
    size = mine_ref.shape[0] // CHUNKS
    for part, turn in enumerate(turns()):
        for chunk in range(CHUNKS):
            at = slice(chunk * size, (chunk + 1) * size)
            same = lower if part == 0 else jnp.logical_not(lower)
            to = pl.multiple_of((chunk ^ turn) * size, 8)
            total_ref[pl.ds(to, size), part * half : (part + 1) * half] = jnp.where(
                same, mine_ref[at], other_ref[at]
            )


def write_rows(begin, skip, total_ref, targets_ref, weights_ref, right_ref, new_hbm, out_hbm, new_ref, sems):
    rows = new_ref.shape[0]
    blocks = sems.shape[0] - 1
    bounds = [8 * (rows // 8 * k // blocks) for k in range(blocks)] + [rows]
    right = right_ref[...]
    copies = [
        pltpu.make_async_copy(
            total_ref.at[pl.ds(skip, rows)], out_hbm.at[pl.ds(begin, rows)], sems.at[blocks]
        )
    ]
    copies[0].start()
    for k in range(blocks):
        low_end, high_end = bounds[k : k + 2]
        here = slice(begin + low_end, begin + high_end)
        high, low = two(total_ref[skip + low_end : skip + high_end] - targets_ref[here])
        new_ref[low_end:high_end] = weights_ref[here] + dot(jnp.concatenate([high, high, low], axis=1), right, NN)
        copy = pltpu.make_async_copy(
            new_ref.at[pl.ds(low_end, high_end - low_end)],
            new_hbm.at[pl.ds(begin + low_end, high_end - low_end)],
            sems.at[k],
        )
        copy.start()
        copies.append(copy)
    for copy in copies:
        copy.wait()


def update_body(
    mine_ref, other_ref, targets_ref, index_ref, eigval_ref, spread_ref, weights_ref,
    new_hbm, out_hbm, right_ref, total_ref, new_ref, sems,
):
    start = (lax.axis_index("center") * 2 + lax.axis_index("sub")) * spread_ref.shape[1]
    rank, count = spread_ref.shape
    gather_total(mine_ref, other_ref, total_ref)
    value = eigval_ref[...]
    lowest = jnp.min(value, axis=1, keepdims=True)
    scaled = (1.0 - lowest / value) / value
    mixed_high, mixed_low = two(total_ref[:rank].T * (0.25 * scaled))
    spread_high, spread_low = two(spread_ref[...])
    turned = dot(mixed_high, spread_high, NN) + (
        dot(mixed_high, spread_low, NN) + dot(mixed_low, spread_high, NN)
    )
    high, low = two(turned - pick_rows(index_ref, count, start, F32, 0.25))
    for k, term in enumerate((high, low, high)):
        right_ref[k * term.shape[0] : (k + 1) * term.shape[0]] = term
    write_rows(0, rank, total_ref, targets_ref, weights_ref, right_ref, new_hbm, out_hbm, new_ref, sems)


def update(mine, other, targets, batch_index, eigval, spread, weights):
    classes, count = weights.shape
    padded, half = mine.shape
    rows = 2 * half
    rank = spread.shape[0]
    here = padded - rank
    vmem = pl.BlockSpec(memory_space=pltpu.VMEM)
    hbm = pl.BlockSpec(memory_space=pl.ANY)
    return pl.pallas_call(
        update_body,
        in_specs=[vmem] * 7,
        out_specs=[hbm, hbm, vmem],
        out_shape=[
            jax.ShapeDtypeStruct((classes, count), F32),
            jax.ShapeDtypeStruct((classes, rows), F32),
            jax.ShapeDtypeStruct((3 * rows, count), BF16),
        ],
        scratch_shapes=[
            pltpu.VMEM((padded, rows), F32),
            pltpu.VMEM((here, count), F32),
            pltpu.SemaphoreType.DMA((4,)),
        ],
        compiler_params=params(),
        cost_estimate=pl.CostEstimate(
            flops=6 * rows * count * (here + rank), bytes_accessed=8 * here * (count + rows), transcendentals=0
        ),
        name="update",
    )(mine, other, targets, batch_index, eigval, spread, weights)


def update_more_body(
    begin, mine_ref, other_ref, targets_ref, weights_ref, right_ref, new_in, out_in,
    new_hbm, out_hbm, total_ref, new_ref, sems,
):
    gather_total(mine_ref, other_ref, total_ref)
    write_rows(begin, 0, total_ref, targets_ref, weights_ref, right_ref, new_hbm, out_hbm, new_ref, sems)


def update_more(mine, other, targets, weights, right, new, out, begin):
    classes, count = weights.shape
    padded, half = mine.shape
    rows = 2 * half
    here = classes - begin
    vmem = pl.BlockSpec(memory_space=pltpu.VMEM)
    hbm = pl.BlockSpec(memory_space=pl.ANY)
    return pl.pallas_call(
        functools.partial(update_more_body, begin),
        in_specs=[vmem] * 5 + [hbm] * 2,
        out_specs=[hbm, hbm],
        out_shape=[
            jax.ShapeDtypeStruct((classes, count), F32),
            jax.ShapeDtypeStruct((classes, rows), F32),
        ],
        input_output_aliases={5: 0, 6: 1},
        scratch_shapes=[
            pltpu.VMEM((padded, rows), F32),
            pltpu.VMEM((here, count), F32),
            pltpu.SemaphoreType.DMA((6,)),
        ],
        compiler_params=params(),
        cost_estimate=pl.CostEstimate(
            flops=int(1.0 * 6) * rows * count * here, bytes_accessed=8 * here * (count + rows), transcendentals=0
        ),
        name="update_more",
    )(mine, other, targets, weights, right, new, out)


def swap(x, chips, order=None, level=0):
    flip = [2 << order(sub, chips.bit_length() - 1)[level] if order else 1 for sub in range(2)]
    return lax.ppermute(x, AXES, [(i, i ^ flip[i & 1]) for i in range(2 * chips)])


def tie(x, tied):
    x, *tied = lax.optimization_barrier((x, *tied))
    return x, tied


def total_of(keep, send, chips, tied=()):
    keep = keep + swap(send, chips)
    for level in range(chips.bit_length() - 1):
        if level >= HALVINGS:
            keep = keep + swap(keep, chips, walk, level)
            continue
        half = keep.shape[0] // 2
        keep, send = keep[:half], keep[half:]
        if level == 1 and tied:
            send, tied = tie(send, tied)
        keep = keep + swap(send, chips, walk, level)
    for level in reversed(range(HALVINGS)):
        keep = jnp.concatenate([keep, swap(keep, chips, walk, level)])
    return [keep, swap(keep, chips), *tied]


def all_of(keep, chips, tied=()):
    for level in range(chips.bit_length() - 1):
        if level == 1 and tied:
            keep, tied = tie(keep, tied)
        keep = jnp.concatenate([keep, swap(keep, chips, far_first, level)])
    return [keep, swap(keep, chips), *tied]


def one_hot(slot, slots):
    return (slot[:, None] == jnp.arange(slots, dtype=jnp.int32)[None, :]).astype(BF16)


def select_summed(rows):
    row = jnp.arange(rows, dtype=jnp.int32)
    half = rows // 2
    size = half // CHUNKS
    turn = jnp.stack(turns())[row // half]
    chunk = (row % half // size) ^ turn
    far = jnp.where(row // half == lax.axis_index("sub"), 0, half)
    return one_hot(far + chunk * size + row % size, rows)


def step(packed, chips, centers, weights, targets, batch_index, nys_index, eigvec, eigval):
    rows = batch_index.shape[1]
    classes, count = weights.shape
    depth = eigvec.shape[0]
    unit = 8 * CHUNKS
    units = -(-(classes + depth) // unit)
    first = (units + 1) // 2 * unit
    second = first
    far = [pltpu.with_memory_space_constraint(x, pltpu.HBM) for x in (batch_index, centers)]
    ready = [center_norms(centers), *spread_weights(nys_index.reshape(1, -1), eigvec, weights, first, second)]
    if packed:
        ready.append(select_packed(batch_index, count, chips))
        slots = [pack_rows(*far, part) for part in range(2)]
        mine, other = all_of(slots[0], chips)
        next_mine, next_other, norms, left1, left2, spread, select = all_of(slots[1], chips, ready)
    else:
        ready.append(select_summed(rows))
        picked = [pick_batch(*far, part) for part in range(2)]
        mine, other = total_of(*picked[0], chips)
        next_mine, next_other, norms, left1, left2, spread, select = total_of(*picked[1], chips, ready)
    before, found = distances(mine, other, next_mine, select, centers, norms)
    keep, send, right = predict(found, next_other, select, centers, before, left1)
    one = total_of(keep, send, chips)
    another = total_of(*predict_more(left2, right), chips)
    new, out, right = update(*one, targets, batch_index, eigval, spread, weights)
    return update_more(*another, targets, weights, right, new, out, first - depth)


def on_device(chips, centers, weights, targets, batch_index, nys_index, eigvec, eigval):
    batch_index = batch_index.reshape(1, -1)
    new, out = lax.cond(
        rows_fit(pltpu.with_memory_space_constraint(batch_index, pltpu.HBM), centers.shape[0]) > 0,
        functools.partial(step, True, chips),
        functools.partial(step, False, chips),
        centers,
        weights.T,
        targets.T,
        batch_index,
        nys_index,
        eigvec.T,
        eigval.reshape(1, -1),
    )
    return new.T, out.T


def solution(mesh):
    return jax.shard_map(
        functools.partial(on_device, mesh.shape["center"]),
        mesh=mesh,
        in_specs=(
            P(("parts", "center", "sub"), None),
            P(("parts", "center", "sub"), None),
            P("parts", None),
            P("parts"),
            P(("parts", "center", "sub")),
            P(("parts", "center", "sub"), None),
            P("parts"),
        ),
        out_specs=(P(("parts", "center", "sub"), None), P("parts", None)),
        check_vma=False,
    )
```

```python
import functools
import math

import jax
import jax.numpy as jnp
from jax import lax
from jax.experimental import pallas as pl
from jax.experimental.pallas import tpu as pltpu
from jax.sharding import PartitionSpec as P

F32 = jnp.float32
BF16 = jnp.bfloat16
AXES = ("center", "sub")
HALVINGS = 2
CHUNKS = 1 << HALVINGS
LANE = 128
PARTS = 2
SLOTS = 32
GROUP_SLOTS = 96
BLOCKS = 2
NT = (((1,), (1,)), ((), ()))
NN = (((1,), (0,)), ((), ()))
VMEM_LIMIT = 24 * 1024 * 1024


def dot(a, b, dims):
    return lax.dot_general(a, b, dims, preferred_element_type=F32)


def walk(sub, bits):
    order = list(range(bits))
    return order if sub == 0 else order[1::-1] + order[2:]


def far_first(sub, bits):
    order = list(range(bits))[::-1]
    return order if sub == 0 else order[:-2] + order[:-3:-1]


def turns():
    center = lax.axis_index("center")
    return [
        sum(((center >> bit) & 1) << (HALVINGS - 1 - k) for k, bit in enumerate(walk(sub, HALVINGS + 1)[:HALVINGS]))
        for sub in range(2)
    ]


def column_of(row, width):
    return jnp.broadcast_to(row.astype(F32), (width, row.shape[1])).T


def two(x):
    high = x.astype(BF16)
    return high, (x - high.astype(F32)).astype(BF16)


def pick_rows(index_ref, columns, start, dtype, scale):
    column = column_of(index_ref[...] - start, LANE)
    lanes = lax.broadcasted_iota(jnp.int32, (1, LANE), 1).astype(F32)
    blocks = [
        jnp.where(column == lanes + float(LANE * k), scale, 0.0).astype(dtype)
        for k in range(columns // LANE)
    ]
    return jnp.concatenate(blocks, axis=1)


def params():
    return pltpu.CompilerParams(vmem_limit_bytes=VMEM_LIMIT)


def pick_body(first, index_hbm, centers_hbm, keep_ref, send_ref, pick_ref, index_ref, centers_ref, sems):
    sub = lax.axis_index("sub")
    blocks, count, block = centers_ref.shape
    rows = index_ref.shape[1]
    half = rows // 2
    size = half // CHUNKS
    copies = [pltpu.make_async_copy(index_hbm, index_ref, sems.at[blocks])] + [
        pltpu.make_async_copy(
            centers_hbm.at[:, pl.ds(first + k * block, block)], centers_ref.at[k], sems.at[k]
        )
        for k in range(blocks)
    ]
    for copy in copies:
        copy.start()
    copies[0].wait()
    start = (lax.axis_index("center") * 2 + sub) * count
    pick = pick_rows(index_ref, count, start, BF16, 1.0)
    for part, turn in enumerate(turns()):
        begin = jnp.where(sub == part, 0, half)
        for chunk in range(CHUNKS):
            to = pl.multiple_of(begin + (chunk ^ turn) * size, size)
            at = part * half + chunk * size
            pick_ref[pl.ds(to, size), :] = pick[at : at + size]
    for k in range(blocks):
        copies[k + 1].wait()
        found = dot(pick_ref[...], centers_ref[k], NN).astype(BF16)
        keep_ref[:, k * block : (k + 1) * block] = found[:half]
        send_ref[:, k * block : (k + 1) * block] = found[half:]


def pick_batch(batch_index, centers, part):
    rows = batch_index.shape[1]
    count, depth = centers.shape
    depth = depth // PARTS
    block = 512
    half = jax.ShapeDtypeStruct((rows // 2, depth), BF16)
    hbm = pl.BlockSpec(memory_space=pltpu.HBM)
    vmem = pl.BlockSpec(memory_space=pltpu.VMEM)
    return pl.pallas_call(
        functools.partial(pick_body, part * depth),
        in_specs=[hbm, hbm],
        out_specs=[vmem, vmem],
        out_shape=[half, half],
        scratch_shapes=[
            pltpu.VMEM((rows, count), BF16),
            pltpu.VMEM((1, rows), jnp.int32),
            pltpu.VMEM((depth // block, count, block), BF16),
            pltpu.SemaphoreType.DMA((depth // block + 1,)),
        ],
        compiler_params=params(),
        cost_estimate=pl.CostEstimate(
            flops=2 * rows * count * depth, bytes_accessed=2 * depth * (count + rows), transcendentals=0
        ),
        name="pick_batch",
    )(batch_index, centers)


def group_of(device, chips):
    bits = chips.bit_length() - 1
    masks = [sum(1 << bit for bit in far_first(sub, bits)[:2]) for sub in range(2)]
    center = device >> 1
    return (jnp.where((device & 1) == 0, center & ~masks[0], center & ~masks[1]) << 1) + (device & 1)


def owners(index, count, chips):
    owner = jnp.zeros_like(index)
    for device in range(1, 2 * chips):
        owner = owner + jnp.where(index >= device * count, 1, 0)
    return owner


def fits_body(count, index_hbm, fits_ref, index_ref, sem):
    copy = pltpu.make_async_copy(index_hbm, index_ref, sem)
    copy.start()
    copy.wait()
    chips = lax.axis_size("center")
    owner = owners(index_ref[...], count, chips)
    device = lax.broadcasted_iota(jnp.int32, (2 * chips, 1), 0)
    held = jnp.sum(jnp.where(owner == device, 1.0, 0.0), axis=1, keepdims=True)
    same = group_of(owner, chips) == group_of(device, chips)
    shared = jnp.sum(jnp.where(same, 1.0, 0.0), axis=1, keepdims=True)
    over = jnp.max(jnp.maximum(held - SLOTS, shared - GROUP_SLOTS))
    fits_ref[0] = (over <= 0.0).astype(jnp.int32)


def rows_fit(batch_index, count):
    return pl.pallas_call(
        functools.partial(fits_body, count),
        in_specs=[pl.BlockSpec(memory_space=pltpu.HBM)],
        out_specs=pl.BlockSpec(memory_space=pltpu.SMEM),
        out_shape=jax.ShapeDtypeStruct((1,), jnp.int32),
        scratch_shapes=[pltpu.VMEM(batch_index.shape, jnp.int32), pltpu.SemaphoreType.DMA],
        compiler_params=params(),
        name="rows_fit",
    )(batch_index)[0]


def pack_body(first, index_hbm, centers_hbm, out_ref, index_ref, centers_ref, sems):
    blocks, count, block = centers_ref.shape
    rows = index_ref.shape[1]
    copies = [pltpu.make_async_copy(index_hbm, index_ref, sems.at[blocks])] + [
        pltpu.make_async_copy(
            centers_hbm.at[:, pl.ds(first + k * block, block)], centers_ref.at[k], sems.at[k]
        )
        for k in range(blocks)
    ]
    for copy in copies:
        copy.start()
    copies[0].wait()
    start = (lax.axis_index("center") * 2 + lax.axis_index("sub")) * count
    local = index_ref[...] - start
    here = jnp.where((local >= 0) & (local < count), 1.0, 0.0)
    earlier = lax.broadcasted_iota(jnp.int32, (rows, rows), 0) < lax.broadcasted_iota(jnp.int32, (rows, rows), 1)
    rank = dot(jnp.broadcast_to(here, (8, rows)).astype(BF16), jnp.where(earlier, 1.0, 0.0).astype(BF16), NN)[0:1]
    slots = lax.broadcasted_iota(jnp.int32, (SLOTS, 1), 0).astype(F32)
    to_slot = jnp.where(slots == rank, here, 0.0).astype(BF16)
    pick = dot(to_slot, pick_rows(index_ref, count, start, BF16, 1.0), NN).astype(BF16)
    for k in range(blocks):
        copies[k + 1].wait()
        out_ref[:, k * block : (k + 1) * block] = dot(pick, centers_ref[k], NN).astype(BF16)


def pack_rows(batch_index, centers, part):
    rows = batch_index.shape[1]
    count, depth = centers.shape
    depth = depth // PARTS
    block = 512
    hbm = pl.BlockSpec(memory_space=pltpu.HBM)
    return pl.pallas_call(
        functools.partial(pack_body, part * depth),
        in_specs=[hbm, hbm],
        out_specs=pl.BlockSpec(memory_space=pltpu.VMEM),
        out_shape=jax.ShapeDtypeStruct((SLOTS, depth), BF16),
        scratch_shapes=[
            pltpu.VMEM((1, rows), jnp.int32),
            pltpu.VMEM((depth // block, count, block), BF16),
            pltpu.SemaphoreType.DMA((depth // block + 1,)),
        ],
        compiler_params=params(),
        cost_estimate=pl.CostEstimate(
            flops=2 * SLOTS * count * depth, bytes_accessed=2 * depth * (count + SLOTS), transcendentals=0
        ),
        name="pack_rows",
    )(batch_index, centers)


def select_body(count, index_ref, select_ref, squeeze_ref):
    rows, slots = select_ref.shape
    chips = lax.axis_size("center")
    center, sub = lax.axis_index("center"), lax.axis_index("sub")
    owner = owners(index_ref[...], count, chips)
    group = group_of(owner, chips)
    earlier = lax.broadcasted_iota(jnp.int32, (rows, rows), 0) < lax.broadcasted_iota(jnp.int32, (rows, rows), 1)

    def rank_among(key):
        column = jnp.concatenate([column_of(key, LANE)] * (rows // LANE), axis=1)
        return jnp.sum(jnp.where((column == key.astype(F32)) & earlier, 1.0, 0.0), axis=0, keepdims=True)

    away = (owner >> 1) ^ center
    orders = [far_first(side, chips.bit_length() - 1) for side in range(2)]

    def place(low, high):
        places = [
            sum(((away >> bit) & 1) << k for k, bit in enumerate(order[low:high])) + jnp.zeros_like(away)
            for order in orders
        ]
        return jnp.where((owner & 1) == 0, *places).astype(F32)

    lanes = lax.broadcasted_iota(jnp.int32, (1, LANE), 1).astype(F32)
    rank = rank_among(group)
    far = jnp.where((owner & 1) == sub, 0, slots // 2).astype(F32)
    slot = column_of(far + place(2, None) * float(GROUP_SLOTS) + rank, LANE)
    for k in range(slots // LANE):
        select_ref[:, k * LANE : (k + 1) * LANE] = jnp.where(slot == lanes + float(LANE * k), 1.0, 0.0).astype(BF16)
    before = column_of(place(0, 2) * float(SLOTS) + rank_among(owner), LANE)
    spots = lax.broadcasted_iota(jnp.int32, (GROUP_SLOTS, 1), 0).astype(F32)
    mine = group == group_of(center * 2 + sub, chips)
    to_spot = jnp.where((spots == rank) & mine, 1.0, 0.0).astype(BF16)
    squeeze_ref[...] = dot(to_spot, jnp.where(before == lanes, 1.0, 0.0).astype(BF16), NN).astype(BF16)


def select_packed(batch_index, count, chips):
    rows = batch_index.shape[1]
    half = -(-chips // 4 * GROUP_SLOTS // LANE) * LANE
    return pl.pallas_call(
        functools.partial(select_body, count),
        out_shape=[
            jax.ShapeDtypeStruct((rows, 2 * half), BF16),
            jax.ShapeDtypeStruct((GROUP_SLOTS, 4 * SLOTS), BF16),
        ],
        compiler_params=params(),
        name="select_packed",
    )(batch_index)


def squeeze_body(squeeze_ref, keep_ref, got_ref, out_ref):
    rows = keep_ref.shape[0]
    found = dot(squeeze_ref[:, :rows], keep_ref[...], NN) + dot(squeeze_ref[:, rows:], got_ref[...], NN)
    out_ref[...] = found.astype(BF16)


def squeeze_slots(squeeze, keep, got):
    depth = keep.shape[1]
    return pl.pallas_call(
        squeeze_body,
        out_shape=jax.ShapeDtypeStruct((squeeze.shape[0], depth), BF16),
        compiler_params=params(),
        cost_estimate=pl.CostEstimate(
            flops=40 * squeeze.size * depth, bytes_accessed=4 * squeeze.shape[1] * depth, transcendentals=0
        ),
        name="squeeze_slots",
    )(squeeze, keep, got)


def spread_body(
    first, classes, index_ref, eigvec_ref, weights_ref,
    left1_ref, left2_ref, spread_ref, all_ref,
):
    rank, points = eigvec_ref.shape
    count = weights_ref.shape[1]
    local = index_ref[...] - (lax.axis_index("center") * 2 + lax.axis_index("sub")) * count
    slots = lax.broadcasted_iota(jnp.int32, (count, points), 0)
    pick = jnp.where(slots == local, 1.0, 0.0).astype(BF16)
    vec = eigvec_ref[...]
    high = vec.astype(BF16)
    rest = vec - high.astype(F32)
    mid = rest.astype(BF16)
    low = (rest - mid.astype(F32)).astype(BF16)
    spread = dot(high, pick, NT) + dot(mid, pick, NT) + dot(low, pick, NT)
    spread_ref[...] = spread
    all_ref[:rank] = spread
    all_ref[rank : rank + classes] = weights_ref[...]
    all_ref[rank + classes :] = jnp.zeros((all_ref.shape[0] - rank - classes, count), F32)
    size = count // BLOCKS
    for begin, left_ref in ((0, left1_ref), (first, left2_ref)):
        for block in range(BLOCKS):
            high, low = two(all_ref[begin : begin + left_ref.shape[0], block * size : (block + 1) * size])
            for k, term in enumerate((high, high, low)):
                at = (3 * block + k) * size
                left_ref[:, at : at + size] = term


def spread_weights(nys_index, eigvec, weights, first, second):
    classes, count = weights.shape
    rank, points = eigvec.shape
    return pl.pallas_call(
        functools.partial(spread_body, first, classes),
        out_shape=[
            jax.ShapeDtypeStruct((first, 3 * count), BF16),
            jax.ShapeDtypeStruct((second, 3 * count), BF16),
            jax.ShapeDtypeStruct((rank, count), F32),
        ],
        scratch_shapes=[pltpu.VMEM((first + second, count), F32)],
        compiler_params=params(),
        cost_estimate=pl.CostEstimate(
            flops=6 * rank * points * count, bytes_accessed=8 * (first + second) * count, transcendentals=0
        ),
        name="spread_weights",
    )(nys_index, eigvec, weights)


def norms_body(centers_ref, norm_ref):
    wide = centers_ref[...].astype(F32)
    norm = jnp.sum(wide * wide, axis=1, keepdims=True)
    norm_ref[...] = jnp.broadcast_to(norm, norm_ref.shape)


def center_norms(centers):
    count, depth = centers.shape
    block = 256
    return pl.pallas_call(
        norms_body,
        grid=(count // block,),
        in_specs=[pl.BlockSpec((block, depth), lambda i: (i, 0))],
        out_specs=pl.BlockSpec((block, LANE), lambda i: (i, 0)),
        out_shape=jax.ShapeDtypeStruct((count, LANE), F32),
        compiler_params=params(),
        cost_estimate=pl.CostEstimate(flops=2 * count * depth, bytes_accessed=2 * count * depth, transcendentals=0),
        name="center_norms",
    )(centers)


def row_norms(batch_ref):
    rows = batch_ref.shape[0]
    batch = batch_ref[...].astype(F32)
    return jnp.broadcast_to(jnp.sum(batch * batch, axis=1, keepdims=True), (rows, LANE)).T[0:1]


def product(left_ref, right_ref, total_ref, keep_ref, send_ref):
    half = keep_ref.shape[1]
    size = left_ref.shape[1] // BLOCKS
    total = 0.0
    for block in range(BLOCKS):
        at = slice(block * size, (block + 1) * size)
        total = total + dot(left_ref[:, at], right_ref[at], NN)
    total_ref[...] = total
    lower = lax.axis_index("sub") == 0
    size = keep_ref.shape[0] // CHUNKS
    for chunk in range(CHUNKS):
        at = slice(chunk * size, (chunk + 1) * size)
        first, second = [
            total_ref[pl.ds(pl.multiple_of((chunk ^ turn) * size, 8), size), part * half : (part + 1) * half]
            for part, turn in enumerate(turns())
        ]
        keep_ref[at] = jnp.where(lower, first, second)
        send_ref[at] = jnp.where(lower, second, first)


def distance_body(mine_ref, other_ref, next_ref, select_ref, centers_ref, norm_ref, total_ref, found_ref, batch_ref):
    half, depth = mine_ref.shape
    wide = select_ref.shape[1] // 2
    near = select_ref[:, :half]
    far = select_ref[:, wide : wide + half]
    batch_ref[...] = (dot(near, mine_ref[...], NN) + dot(far, other_ref[...], NN)).astype(BF16)
    total_ref[...] = norm_ref[:, 0:1] + row_norms(batch_ref) - 2.0 * dot(centers_ref[:, :depth], batch_ref[...], NT)
    found_ref[...] = dot(near, next_ref[...], NN).astype(BF16)


def predict_body(
    found_ref, other_ref, select_ref, centers_ref, before_ref, left_ref,
    keep_ref, send_ref, right_ref, batch_ref, total_ref,
):
    count, depth = centers_ref.shape
    half, part = other_ref.shape
    wide = select_ref.shape[1] // 2
    found = found_ref[...].astype(F32) + dot(select_ref[:, wide : wide + half], other_ref[...], NN)
    batch_ref[...] = found.astype(BF16)
    norm = row_norms(batch_ref)
    size = count // BLOCKS
    for block in range(BLOCKS):
        at = slice(block * size, (block + 1) * size)
        cross = dot(centers_ref[at, depth - part :], batch_ref[...], NT)
        square = jnp.maximum(before_ref[at] + norm - 2.0 * cross, 0.0)
        high, low = two(jnp.exp(jnp.sqrt(square) * (-1.0 / math.sqrt(depth))))
        for k, term in enumerate((high, low, high)):
            to = (3 * block + k) * size
            right_ref[to : to + size] = term
    product(left_ref, right_ref, total_ref, keep_ref, send_ref)


def distances(mine, other, following, select, centers, norms):
    depth = mine.shape[1]
    rows = select.shape[0]
    count = centers.shape[0]
    vmem = pl.BlockSpec(memory_space=pltpu.VMEM)
    return pl.pallas_call(
        distance_body,
        in_specs=[vmem] * 6,
        out_specs=[vmem, vmem],
        out_shape=[jax.ShapeDtypeStruct((count, rows), F32), jax.ShapeDtypeStruct((rows, depth), BF16)],
        scratch_shapes=[pltpu.VMEM((rows, depth), BF16)],
        compiler_params=params(),
        cost_estimate=pl.CostEstimate(
            flops=2 * rows * count * depth, bytes_accessed=2 * depth * (count + rows), transcendentals=0
        ),
        name="distances",
    )(mine, other, following, select, centers, norms)


def predict(found, other, select, centers, before, left):
    depth = found.shape[1]
    rows = select.shape[0]
    half = rows // 2
    count = centers.shape[0]
    padded = left.shape[0]
    out = jax.ShapeDtypeStruct((padded, half), F32)
    vmem = pl.BlockSpec(memory_space=pltpu.VMEM)
    return pl.pallas_call(
        predict_body,
        in_specs=[vmem] * 6,
        out_specs=[vmem] * 3,
        out_shape=[out, out, jax.ShapeDtypeStruct((3 * count, rows), BF16)],
        scratch_shapes=[pltpu.VMEM((rows, depth), BF16), pltpu.VMEM((padded, rows), F32)],
        compiler_params=params(),
        cost_estimate=pl.CostEstimate(
            flops=2 * rows * count * (depth + 3 * padded),
            bytes_accessed=2 * depth * (count + rows) + 4 * padded * (count + rows),
            transcendentals=2 * rows * count,
        ),
        name="predict",
    )(found, other, select, centers, before, left)


def predict_more(left, right):
    padded, count = left.shape
    rows = right.shape[1]
    out = jax.ShapeDtypeStruct((padded, rows // 2), F32)
    return pl.pallas_call(
        lambda left, right, keep, send, total: product(left, right, total, keep, send),
        out_shape=[out, out],
        scratch_shapes=[pltpu.VMEM((padded, rows), F32)],
        compiler_params=params(),
        cost_estimate=pl.CostEstimate(
            flops=2 * rows * count * padded, bytes_accessed=2 * padded * (count + rows), transcendentals=0
        ),
        name="predict_more",
    )(left, right)


def gather_total(mine_ref, other_ref, total_ref):
    lower = lax.axis_index("sub") == 0
    half = mine_ref.shape[1]
    size = mine_ref.shape[0] // CHUNKS
    for part, turn in enumerate(turns()):
        for chunk in range(CHUNKS):
            at = slice(chunk * size, (chunk + 1) * size)
            same = lower if part == 0 else jnp.logical_not(lower)
            to = pl.multiple_of((chunk ^ turn) * size, 8)
            total_ref[pl.ds(to, size), part * half : (part + 1) * half] = jnp.where(
                same, mine_ref[at], other_ref[at]
            )


def write_rows(begin, skip, total_ref, targets_ref, weights_ref, right_ref, new_hbm, out_hbm, new_ref, sems):
    rows = new_ref.shape[0]
    blocks = sems.shape[0] - 1
    bounds = [8 * (rows // 8 * k // blocks) for k in range(blocks)] + [rows]
    right = right_ref[...]
    copies = [
        pltpu.make_async_copy(
            total_ref.at[pl.ds(skip, rows)], out_hbm.at[pl.ds(begin, rows)], sems.at[blocks]
        )
    ]
    copies[0].start()
    for k in range(blocks):
        low_end, high_end = bounds[k : k + 2]
        here = slice(begin + low_end, begin + high_end)
        high, low = two(total_ref[skip + low_end : skip + high_end] - targets_ref[here])
        new_ref[low_end:high_end] = weights_ref[here] + dot(jnp.concatenate([high, high, low], axis=1), right, NN)
        copy = pltpu.make_async_copy(
            new_ref.at[pl.ds(low_end, high_end - low_end)],
            new_hbm.at[pl.ds(begin + low_end, high_end - low_end)],
            sems.at[k],
        )
        copy.start()
        copies.append(copy)
    for copy in copies:
        copy.wait()


def update_body(
    mine_ref, other_ref, targets_ref, index_ref, eigval_ref, spread_ref, weights_ref,
    new_hbm, out_hbm, right_ref, total_ref, new_ref, sems,
):
    start = (lax.axis_index("center") * 2 + lax.axis_index("sub")) * spread_ref.shape[1]
    rank, count = spread_ref.shape
    gather_total(mine_ref, other_ref, total_ref)
    value = eigval_ref[...]
    lowest = jnp.min(value, axis=1, keepdims=True)
    scaled = (1.0 - lowest / value) / value
    mixed_high, mixed_low = two(total_ref[:rank].T * (0.25 * scaled))
    spread_high, spread_low = two(spread_ref[...])
    turned = dot(mixed_high, spread_high, NN) + (
        dot(mixed_high, spread_low, NN) + dot(mixed_low, spread_high, NN)
    )
    high, low = two(turned - pick_rows(index_ref, count, start, F32, 0.25))
    for k, term in enumerate((high, low, high)):
        right_ref[k * term.shape[0] : (k + 1) * term.shape[0]] = term
    write_rows(0, rank, total_ref, targets_ref, weights_ref, right_ref, new_hbm, out_hbm, new_ref, sems)


def update(mine, other, targets, batch_index, eigval, spread, weights):
    classes, count = weights.shape
    padded, half = mine.shape
    rows = 2 * half
    rank = spread.shape[0]
    here = padded - rank
    vmem = pl.BlockSpec(memory_space=pltpu.VMEM)
    hbm = pl.BlockSpec(memory_space=pl.ANY)
    return pl.pallas_call(
        update_body,
        in_specs=[vmem] * 7,
        out_specs=[hbm, hbm, vmem],
        out_shape=[
            jax.ShapeDtypeStruct((classes, count), F32),
            jax.ShapeDtypeStruct((classes, rows), F32),
            jax.ShapeDtypeStruct((3 * rows, count), BF16),
        ],
        scratch_shapes=[
            pltpu.VMEM((padded, rows), F32),
            pltpu.VMEM((here, count), F32),
            pltpu.SemaphoreType.DMA((4,)),
        ],
        compiler_params=params(),
        cost_estimate=pl.CostEstimate(
            flops=6 * rows * count * (here + rank), bytes_accessed=8 * here * (count + rows), transcendentals=0
        ),
        name="update",
    )(mine, other, targets, batch_index, eigval, spread, weights)


def update_more_body(
    begin, mine_ref, other_ref, targets_ref, weights_ref, right_ref, new_in, out_in,
    new_hbm, out_hbm, total_ref, new_ref, sems,
):
    gather_total(mine_ref, other_ref, total_ref)
    write_rows(begin, 0, total_ref, targets_ref, weights_ref, right_ref, new_hbm, out_hbm, new_ref, sems)


def update_more(mine, other, targets, weights, right, new, out, begin):
    classes, count = weights.shape
    padded, half = mine.shape
    rows = 2 * half
    here = classes - begin
    vmem = pl.BlockSpec(memory_space=pltpu.VMEM)
    hbm = pl.BlockSpec(memory_space=pl.ANY)
    return pl.pallas_call(
        functools.partial(update_more_body, begin),
        in_specs=[vmem] * 5 + [hbm] * 2,
        out_specs=[hbm, hbm],
        out_shape=[
            jax.ShapeDtypeStruct((classes, count), F32),
            jax.ShapeDtypeStruct((classes, rows), F32),
        ],
        input_output_aliases={5: 0, 6: 1},
        scratch_shapes=[
            pltpu.VMEM((padded, rows), F32),
            pltpu.VMEM((here, count), F32),
            pltpu.SemaphoreType.DMA((6,)),
        ],
        compiler_params=params(),
        cost_estimate=pl.CostEstimate(
            flops=int(1.0 * 6) * rows * count * here, bytes_accessed=8 * here * (count + rows), transcendentals=0
        ),
        name="update_more",
    )(mine, other, targets, weights, right, new, out)


def swap(x, chips, order=None, level=0):
    flip = [2 << order(sub, chips.bit_length() - 1)[level] if order else 1 for sub in range(2)]
    return lax.ppermute(x, AXES, [(i, i ^ flip[i & 1]) for i in range(2 * chips)])


def tie(x, tied):
    x, *tied = lax.optimization_barrier((x, *tied))
    return x, tied


def total_of(keep, send, chips, tied=()):
    keep = keep + swap(send, chips)
    for level in range(chips.bit_length() - 1):
        if level >= HALVINGS:
            keep = keep + swap(keep, chips, walk, level)
            continue
        half = keep.shape[0] // 2
        keep, send = keep[:half], keep[half:]
        if level == 1 and tied:
            send, tied = tie(send, tied)
        keep = keep + swap(send, chips, walk, level)
    for level in reversed(range(HALVINGS)):
        keep = jnp.concatenate([keep, swap(keep, chips, walk, level)])
    return [keep, swap(keep, chips), *tied]


def gathered(first, second, squeeze, chips, ready):
    for level in range(chips.bit_length() - 1):
        if level == 1:
            second, ready = tie(second, ready)
        got = swap(first, chips, far_first, level)
        late = swap(second, chips, far_first, level)
        if level == 1:
            got, _ = tie(got, [second])
            first = squeeze_slots(squeeze, first, got)
            second = squeeze_slots(squeeze, second, late)
        else:
            first = jnp.concatenate([first, got])
            second = jnp.concatenate([second, late])
    return [first, swap(first, chips), second, swap(second, chips), *ready]


def one_hot(slot, slots):
    return (slot[:, None] == jnp.arange(slots, dtype=jnp.int32)[None, :]).astype(BF16)


def select_summed(rows):
    row = jnp.arange(rows, dtype=jnp.int32)
    half = rows // 2
    size = half // CHUNKS
    turn = jnp.stack(turns())[row // half]
    chunk = (row % half // size) ^ turn
    far = jnp.where(row // half == lax.axis_index("sub"), 0, half)
    return one_hot(far + chunk * size + row % size, rows)


def step(packed, chips, centers, weights, targets, batch_index, nys_index, eigvec, eigval):
    rows = batch_index.shape[1]
    classes, count = weights.shape
    depth = eigvec.shape[0]
    unit = 8 * CHUNKS
    units = -(-(classes + depth) // unit)
    first = (units + 1) // 2 * unit
    second = first
    far = [pltpu.with_memory_space_constraint(x, pltpu.HBM) for x in (batch_index, centers)]
    ready = [center_norms(centers), *spread_weights(nys_index.reshape(1, -1), eigvec, weights, first, second)]
    if packed:
        select, squeeze = select_packed(batch_index, count, chips)
        ready.append(select)
        slots = [pack_rows(*far, part) for part in range(PARTS)]
        mine, other, next_mine, next_other, *ready = gathered(*slots, squeeze, chips, ready)
        norms, left1, left2, spread, select = ready
    else:
        ready.append(select_summed(rows))
        picked = [pick_batch(*far, part) for part in range(PARTS)]
        mine, other = total_of(*picked[0], chips)
        next_mine, next_other, norms, left1, left2, spread, select = total_of(*picked[1], chips, ready)
    before, found = distances(mine, other, next_mine, select, centers, norms)
    keep, send, right = predict(found, next_other, select, centers, before, left1)
    one = total_of(keep, send, chips)
    another = total_of(*predict_more(left2, right), chips)
    new, out, right = update(*one, targets, batch_index, eigval, spread, weights)
    return update_more(*another, targets, weights, right, new, out, first - depth)


def on_device(chips, centers, weights, targets, batch_index, nys_index, eigvec, eigval):
    batch_index = batch_index.reshape(1, -1)
    new, out = lax.cond(
        rows_fit(pltpu.with_memory_space_constraint(batch_index, pltpu.HBM), centers.shape[0]) > 0,
        functools.partial(step, True, chips),
        functools.partial(step, False, chips),
        centers,
        weights.T,
        targets.T,
        batch_index,
        nys_index,
        eigvec.T,
        eigval.reshape(1, -1),
    )
    return new.T, out.T


def solution(mesh):
    return jax.shard_map(
        functools.partial(on_device, mesh.shape["center"]),
        mesh=mesh,
        in_specs=(
            P(("parts", "center", "sub"), None),
            P(("parts", "center", "sub"), None),
            P("parts", None),
            P("parts"),
            P(("parts", "center", "sub")),
            P(("parts", "center", "sub"), None),
            P("parts"),
        ),
        out_specs=(P(("parts", "center", "sub"), None), P("parts", None)),
        check_vma=False,
    )
```

```python
import functools
import math

import jax
import jax.numpy as jnp
from jax import lax
from jax.experimental import pallas as pl
from jax.experimental.pallas import tpu as pltpu
from jax.sharding import PartitionSpec as P

F32 = jnp.float32
BF16 = jnp.bfloat16
AXES = ("center", "sub")
HALVINGS = 2
CHUNKS = 1 << HALVINGS
LANE = 128
PARTS = 2
SLOTS = 32
GROUP_SLOTS = 96
BLOCKS = 2
NT = (((1,), (1,)), ((), ()))
NN = (((1,), (0,)), ((), ()))
VMEM_LIMIT = 24 * 1024 * 1024


def dot(a, b, dims):
    return lax.dot_general(a, b, dims, preferred_element_type=F32)


def walk(sub, bits):
    order = list(range(bits))
    return order if sub == 1 else order[1::-1] + order[2:]


def far_first(sub, bits):
    order = list(range(bits))[::-1]
    return order if sub == 1 else order[:-2] + order[:-3:-1]


def turns():
    center = lax.axis_index("center")
    return [
        sum(((center >> bit) & 1) << (HALVINGS - 1 - k) for k, bit in enumerate(walk(sub, HALVINGS + 1)[:HALVINGS]))
        for sub in range(2)
    ]


def column_of(row, width):
    return jnp.broadcast_to(row.astype(F32), (width, row.shape[1])).T


def two(x):
    high = x.astype(BF16)
    return high, (x - high.astype(F32)).astype(BF16)


def pick_rows(index_ref, columns, start, dtype, scale):
    column = column_of(index_ref[...] - start, LANE)
    lanes = lax.broadcasted_iota(jnp.int32, (1, LANE), 1).astype(F32)
    blocks = [
        jnp.where(column == lanes + float(LANE * k), scale, 0.0).astype(dtype)
        for k in range(columns // LANE)
    ]
    return jnp.concatenate(blocks, axis=1)


def params():
    return pltpu.CompilerParams(vmem_limit_bytes=VMEM_LIMIT)


def pick_body(first, index_hbm, centers_hbm, keep_ref, send_ref, pick_ref, index_ref, centers_ref, sems):
    sub = lax.axis_index("sub")
    blocks, count, block = centers_ref.shape
    rows = index_ref.shape[1]
    half = rows // 2
    size = half // CHUNKS
    copies = [pltpu.make_async_copy(index_hbm, index_ref, sems.at[blocks])] + [
        pltpu.make_async_copy(
            centers_hbm.at[:, pl.ds(first + k * block, block)], centers_ref.at[k], sems.at[k]
        )
        for k in range(blocks)
    ]
    for copy in copies:
        copy.start()
    copies[0].wait()
    start = (lax.axis_index("center") * 2 + sub) * count
    pick = pick_rows(index_ref, count, start, BF16, 1.0)
    for part, turn in enumerate(turns()):
        begin = jnp.where(sub == part, 0, half)
        for chunk in range(CHUNKS):
            to = pl.multiple_of(begin + (chunk ^ turn) * size, size)
            at = part * half + chunk * size
            pick_ref[pl.ds(to, size), :] = pick[at : at + size]
    for k in range(blocks):
        copies[k + 1].wait()
        found = dot(pick_ref[...], centers_ref[k], NN).astype(BF16)
        keep_ref[:, k * block : (k + 1) * block] = found[:half]
        send_ref[:, k * block : (k + 1) * block] = found[half:]


def pick_batch(batch_index, centers, part):
    rows = batch_index.shape[1]
    count, depth = centers.shape
    depth = depth // PARTS
    block = 512
    half = jax.ShapeDtypeStruct((rows // 2, depth), BF16)
    hbm = pl.BlockSpec(memory_space=pltpu.HBM)
    vmem = pl.BlockSpec(memory_space=pltpu.VMEM)
    return pl.pallas_call(
        functools.partial(pick_body, part * depth),
        in_specs=[hbm, hbm],
        out_specs=[vmem, vmem],
        out_shape=[half, half],
        scratch_shapes=[
            pltpu.VMEM((rows, count), BF16),
            pltpu.VMEM((1, rows), jnp.int32),
            pltpu.VMEM((depth // block, count, block), BF16),
            pltpu.SemaphoreType.DMA((depth // block + 1,)),
        ],
        compiler_params=params(),
        cost_estimate=pl.CostEstimate(
            flops=2 * rows * count * depth, bytes_accessed=2 * depth * (count + rows), transcendentals=0
        ),
        name="pick_batch",
    )(batch_index, centers)


def group_of(device, chips):
    bits = chips.bit_length() - 1
    masks = [sum(1 << bit for bit in far_first(sub, bits)[:2]) for sub in range(2)]
    center = device >> 1
    return (jnp.where((device & 1) == 0, center & ~masks[0], center & ~masks[1]) << 1) + (device & 1)


def owners(index, count, chips):
    owner = jnp.zeros_like(index)
    for device in range(1, 2 * chips):
        owner = owner + jnp.where(index >= device * count, 1, 0)
    return owner


def fits_body(count, index_hbm, fits_ref, index_ref, sem):
    copy = pltpu.make_async_copy(index_hbm, index_ref, sem)
    copy.start()
    copy.wait()
    chips = lax.axis_size("center")
    owner = owners(index_ref[...], count, chips)
    device = lax.broadcasted_iota(jnp.int32, (2 * chips, 1), 0)
    held = jnp.sum(jnp.where(owner == device, 1.0, 0.0), axis=1, keepdims=True)
    same = group_of(owner, chips) == group_of(device, chips)
    shared = jnp.sum(jnp.where(same, 1.0, 0.0), axis=1, keepdims=True)
    over = jnp.max(jnp.maximum(held - SLOTS, shared - GROUP_SLOTS))
    fits_ref[0] = (over <= 0.0).astype(jnp.int32)


def rows_fit(batch_index, count):
    return pl.pallas_call(
        functools.partial(fits_body, count),
        in_specs=[pl.BlockSpec(memory_space=pltpu.HBM)],
        out_specs=pl.BlockSpec(memory_space=pltpu.SMEM),
        out_shape=jax.ShapeDtypeStruct((1,), jnp.int32),
        scratch_shapes=[pltpu.VMEM(batch_index.shape, jnp.int32), pltpu.SemaphoreType.DMA],
        compiler_params=params(),
        name="rows_fit",
    )(batch_index)[0]


def pack_body(first, index_hbm, centers_hbm, out_ref, index_ref, centers_ref, sems):
    blocks, count, block = centers_ref.shape
    rows = index_ref.shape[1]
    copies = [pltpu.make_async_copy(index_hbm, index_ref, sems.at[blocks])] + [
        pltpu.make_async_copy(
            centers_hbm.at[:, pl.ds(first + k * block, block)], centers_ref.at[k], sems.at[k]
        )
        for k in range(blocks)
    ]
    for copy in copies:
        copy.start()
    copies[0].wait()
    start = (lax.axis_index("center") * 2 + lax.axis_index("sub")) * count
    local = index_ref[...] - start
    here = jnp.where((local >= 0) & (local < count), 1.0, 0.0)
    earlier = lax.broadcasted_iota(jnp.int32, (rows, rows), 0) < lax.broadcasted_iota(jnp.int32, (rows, rows), 1)
    rank = dot(jnp.broadcast_to(here, (8, rows)).astype(BF16), jnp.where(earlier, 1.0, 0.0).astype(BF16), NN)[0:1]
    slots = lax.broadcasted_iota(jnp.int32, (SLOTS, 1), 0).astype(F32)
    to_slot = jnp.where(slots == rank, here, 0.0).astype(BF16)
    pick = dot(to_slot, pick_rows(index_ref, count, start, BF16, 1.0), NN).astype(BF16)
    for k in range(blocks):
        copies[k + 1].wait()
        out_ref[:, k * block : (k + 1) * block] = dot(pick, centers_ref[k], NN).astype(BF16)


def pack_rows(batch_index, centers, part):
    rows = batch_index.shape[1]
    count, depth = centers.shape
    depth = depth // PARTS
    block = 512
    hbm = pl.BlockSpec(memory_space=pltpu.HBM)
    return pl.pallas_call(
        functools.partial(pack_body, part * depth),
        in_specs=[hbm, hbm],
        out_specs=pl.BlockSpec(memory_space=pltpu.VMEM),
        out_shape=jax.ShapeDtypeStruct((SLOTS, depth), BF16),
        scratch_shapes=[
            pltpu.VMEM((1, rows), jnp.int32),
            pltpu.VMEM((depth // block, count, block), BF16),
            pltpu.SemaphoreType.DMA((depth // block + 1,)),
        ],
        compiler_params=params(),
        cost_estimate=pl.CostEstimate(
            flops=2 * SLOTS * count * depth, bytes_accessed=2 * depth * (count + SLOTS), transcendentals=0
        ),
        name="pack_rows",
    )(batch_index, centers)


def select_body(count, index_ref, select_ref, squeeze_ref):
    rows, slots = select_ref.shape
    chips = lax.axis_size("center")
    center, sub = lax.axis_index("center"), lax.axis_index("sub")
    owner = owners(index_ref[...], count, chips)
    group = group_of(owner, chips)
    earlier = lax.broadcasted_iota(jnp.int32, (rows, rows), 0) < lax.broadcasted_iota(jnp.int32, (rows, rows), 1)

    def rank_among(key):
        column = jnp.concatenate([column_of(key, LANE)] * (rows // LANE), axis=1)
        return jnp.sum(jnp.where((column == key.astype(F32)) & earlier, 1.0, 0.0), axis=0, keepdims=True)

    away = (owner >> 1) ^ center
    orders = [far_first(side, chips.bit_length() - 1) for side in range(2)]

    def place(low, high):
        places = [
            sum(((away >> bit) & 1) << k for k, bit in enumerate(order[low:high])) + jnp.zeros_like(away)
            for order in orders
        ]
        return jnp.where((owner & 1) == 0, *places).astype(F32)

    lanes = lax.broadcasted_iota(jnp.int32, (1, LANE), 1).astype(F32)
    rank = rank_among(group)
    far = jnp.where((owner & 1) == sub, 0, slots // 2).astype(F32)
    slot = column_of(far + place(2, None) * float(GROUP_SLOTS) + rank, LANE)
    for k in range(slots // LANE):
        select_ref[:, k * LANE : (k + 1) * LANE] = jnp.where(slot == lanes + float(LANE * k), 1.0, 0.0).astype(BF16)
    before = column_of(place(0, 2) * float(SLOTS) + rank_among(owner), LANE)
    spots = lax.broadcasted_iota(jnp.int32, (GROUP_SLOTS, 1), 0).astype(F32)
    mine = group == group_of(center * 2 + sub, chips)
    to_spot = jnp.where((spots == rank) & mine, 1.0, 0.0).astype(BF16)
    squeeze_ref[...] = dot(to_spot, jnp.where(before == lanes, 1.0, 0.0).astype(BF16), NN).astype(BF16)


def select_packed(batch_index, count, chips):
    rows = batch_index.shape[1]
    half = -(-chips // 4 * GROUP_SLOTS // LANE) * LANE
    return pl.pallas_call(
        functools.partial(select_body, count),
        out_shape=[
            jax.ShapeDtypeStruct((rows, 2 * half), BF16),
            jax.ShapeDtypeStruct((GROUP_SLOTS, 4 * SLOTS), BF16),
        ],
        compiler_params=params(),
        name="select_packed",
    )(batch_index)


def squeeze_body(squeeze_ref, keep_ref, got_ref, out_ref):
    rows = keep_ref.shape[0]
    found = dot(squeeze_ref[:, :rows], keep_ref[...], NN) + dot(squeeze_ref[:, rows:], got_ref[...], NN)
    out_ref[...] = found.astype(BF16)


def squeeze_slots(squeeze, keep, got):
    depth = keep.shape[1]
    return pl.pallas_call(
        squeeze_body,
        out_shape=jax.ShapeDtypeStruct((squeeze.shape[0], depth), BF16),
        compiler_params=params(),
        cost_estimate=pl.CostEstimate(
            flops=40 * squeeze.size * depth, bytes_accessed=4 * squeeze.shape[1] * depth, transcendentals=0
        ),
        name="squeeze_slots",
    )(squeeze, keep, got)


def spread_body(
    first, classes, index_ref, eigvec_ref, weights_ref,
    left1_ref, left2_ref, spread_ref, all_ref,
):
    rank, points = eigvec_ref.shape
    count = weights_ref.shape[1]
    local = index_ref[...] - (lax.axis_index("center") * 2 + lax.axis_index("sub")) * count
    slots = lax.broadcasted_iota(jnp.int32, (count, points), 0)
    pick = jnp.where(slots == local, 1.0, 0.0).astype(BF16)
    vec = eigvec_ref[...]
    high = vec.astype(BF16)
    rest = vec - high.astype(F32)
    mid = rest.astype(BF16)
    low = (rest - mid.astype(F32)).astype(BF16)
    spread = dot(high, pick, NT) + dot(mid, pick, NT) + dot(low, pick, NT)
    spread_ref[...] = spread
    all_ref[:rank] = spread
    all_ref[rank : rank + classes] = weights_ref[...]
    all_ref[rank + classes :] = jnp.zeros((all_ref.shape[0] - rank - classes, count), F32)
    size = count // BLOCKS
    for begin, left_ref in ((0, left1_ref), (first, left2_ref)):
        for block in range(BLOCKS):
            high, low = two(all_ref[begin : begin + left_ref.shape[0], block * size : (block + 1) * size])
            for k, term in enumerate((high, high, low)):
                at = (3 * block + k) * size
                left_ref[:, at : at + size] = term


def spread_weights(nys_index, eigvec, weights, first, second):
    classes, count = weights.shape
    rank, points = eigvec.shape
    return pl.pallas_call(
        functools.partial(spread_body, first, classes),
        out_shape=[
            jax.ShapeDtypeStruct((first, 3 * count), BF16),
            jax.ShapeDtypeStruct((second, 3 * count), BF16),
            jax.ShapeDtypeStruct((rank, count), F32),
        ],
        scratch_shapes=[pltpu.VMEM((first + second, count), F32)],
        compiler_params=params(),
        cost_estimate=pl.CostEstimate(
            flops=6 * rank * points * count, bytes_accessed=8 * (first + second) * count, transcendentals=0
        ),
        name="spread_weights",
    )(nys_index, eigvec, weights)


def norms_body(centers_ref, norm_ref):
    wide = centers_ref[...].astype(F32)
    norm = jnp.sum(wide * wide, axis=1, keepdims=True)
    norm_ref[...] = jnp.broadcast_to(norm, norm_ref.shape)


def center_norms(centers):
    count, depth = centers.shape
    block = 256
    return pl.pallas_call(
        norms_body,
        grid=(count // block,),
        in_specs=[pl.BlockSpec((block, depth), lambda i: (i, 0))],
        out_specs=pl.BlockSpec((block, LANE), lambda i: (i, 0)),
        out_shape=jax.ShapeDtypeStruct((count, LANE), F32),
        compiler_params=params(),
        cost_estimate=pl.CostEstimate(flops=2 * count * depth, bytes_accessed=2 * count * depth, transcendentals=0),
        name="center_norms",
    )(centers)


def row_norms(batch_ref):
    rows = batch_ref.shape[0]
    batch = batch_ref[...].astype(F32)
    return jnp.broadcast_to(jnp.sum(batch * batch, axis=1, keepdims=True), (rows, LANE)).T[0:1]


def product(left_ref, right_ref, total_ref, keep_ref, send_ref):
    half = keep_ref.shape[1]
    size = left_ref.shape[1] // BLOCKS
    total = 0.0
    for block in range(BLOCKS):
        at = slice(block * size, (block + 1) * size)
        total = total + dot(left_ref[:, at], right_ref[at], NN)
    total_ref[...] = total
    lower = lax.axis_index("sub") == 0
    size = keep_ref.shape[0] // CHUNKS
    for chunk in range(CHUNKS):
        at = slice(chunk * size, (chunk + 1) * size)
        first, second = [
            total_ref[pl.ds(pl.multiple_of((chunk ^ turn) * size, 8), size), part * half : (part + 1) * half]
            for part, turn in enumerate(turns())
        ]
        keep_ref[at] = jnp.where(lower, first, second)
        send_ref[at] = jnp.where(lower, second, first)


def distance_body(mine_ref, other_ref, next_ref, select_ref, centers_ref, norm_ref, total_ref, found_ref, batch_ref):
    half, depth = mine_ref.shape
    wide = select_ref.shape[1] // 2
    near = select_ref[:, :half]
    far = select_ref[:, wide : wide + half]
    batch_ref[...] = (dot(near, mine_ref[...], NN) + dot(far, other_ref[...], NN)).astype(BF16)
    total_ref[...] = norm_ref[:, 0:1] + row_norms(batch_ref) - 2.0 * dot(centers_ref[:, :depth], batch_ref[...], NT)
    found_ref[...] = dot(near, next_ref[...], NN).astype(BF16)


def predict_body(
    found_ref, other_ref, select_ref, centers_ref, before_ref, left_ref,
    keep_ref, send_ref, right_ref, batch_ref, total_ref,
):
    count, depth = centers_ref.shape
    half, part = other_ref.shape
    wide = select_ref.shape[1] // 2
    found = found_ref[...].astype(F32) + dot(select_ref[:, wide : wide + half], other_ref[...], NN)
    batch_ref[...] = found.astype(BF16)
    norm = row_norms(batch_ref)
    size = count // BLOCKS
    for block in range(BLOCKS):
        at = slice(block * size, (block + 1) * size)
        cross = dot(centers_ref[at, depth - part :], batch_ref[...], NT)
        square = jnp.maximum(before_ref[at] + norm - 2.0 * cross, 0.0)
        high, low = two(jnp.exp(jnp.sqrt(square) * (-1.0 / math.sqrt(depth))))
        for k, term in enumerate((high, low, high)):
            to = (3 * block + k) * size
            right_ref[to : to + size] = term
    product(left_ref, right_ref, total_ref, keep_ref, send_ref)


def distances(mine, other, following, select, centers, norms):
    depth = mine.shape[1]
    rows = select.shape[0]
    count = centers.shape[0]
    vmem = pl.BlockSpec(memory_space=pltpu.VMEM)
    return pl.pallas_call(
        distance_body,
        in_specs=[vmem] * 6,
        out_specs=[vmem, vmem],
        out_shape=[jax.ShapeDtypeStruct((count, rows), F32), jax.ShapeDtypeStruct((rows, depth), BF16)],
        scratch_shapes=[pltpu.VMEM((rows, depth), BF16)],
        compiler_params=params(),
        cost_estimate=pl.CostEstimate(
            flops=2 * rows * count * depth, bytes_accessed=2 * depth * (count + rows), transcendentals=0
        ),
        name="distances",
    )(mine, other, following, select, centers, norms)


def predict(found, other, select, centers, before, left):
    depth = found.shape[1]
    rows = select.shape[0]
    half = rows // 2
    count = centers.shape[0]
    padded = left.shape[0]
    out = jax.ShapeDtypeStruct((padded, half), F32)
    vmem = pl.BlockSpec(memory_space=pltpu.VMEM)
    return pl.pallas_call(
        predict_body,
        in_specs=[vmem] * 6,
        out_specs=[vmem] * 3,
        out_shape=[out, out, jax.ShapeDtypeStruct((3 * count, rows), BF16)],
        scratch_shapes=[pltpu.VMEM((rows, depth), BF16), pltpu.VMEM((padded, rows), F32)],
        compiler_params=params(),
        cost_estimate=pl.CostEstimate(
            flops=2 * rows * count * (depth + 3 * padded),
            bytes_accessed=2 * depth * (count + rows) + 4 * padded * (count + rows),
            transcendentals=2 * rows * count,
        ),
        name="predict",
    )(found, other, select, centers, before, left)


def predict_more(left, right):
    padded, count = left.shape
    rows = right.shape[1]
    out = jax.ShapeDtypeStruct((padded, rows // 2), F32)
    return pl.pallas_call(
        lambda left, right, keep, send, total: product(left, right, total, keep, send),
        out_shape=[out, out],
        scratch_shapes=[pltpu.VMEM((padded, rows), F32)],
        compiler_params=params(),
        cost_estimate=pl.CostEstimate(
            flops=2 * rows * count * padded, bytes_accessed=2 * padded * (count + rows), transcendentals=0
        ),
        name="predict_more",
    )(left, right)


def gather_total(mine_ref, other_ref, total_ref):
    lower = lax.axis_index("sub") == 0
    half = mine_ref.shape[1]
    size = mine_ref.shape[0] // CHUNKS
    for part, turn in enumerate(turns()):
        for chunk in range(CHUNKS):
            at = slice(chunk * size, (chunk + 1) * size)
            same = lower if part == 0 else jnp.logical_not(lower)
            to = pl.multiple_of((chunk ^ turn) * size, 8)
            total_ref[pl.ds(to, size), part * half : (part + 1) * half] = jnp.where(
                same, mine_ref[at], other_ref[at]
            )


def write_rows(begin, skip, total_ref, targets_ref, weights_ref, right_ref, new_hbm, out_hbm, new_ref, sems):
    rows = new_ref.shape[0]
    blocks = sems.shape[0] - 1
    bounds = [8 * (rows // 8 * k // blocks) for k in range(blocks)] + [rows]
    right = right_ref[...]
    copies = [
        pltpu.make_async_copy(
            total_ref.at[pl.ds(skip, rows)], out_hbm.at[pl.ds(begin, rows)], sems.at[blocks]
        )
    ]
    copies[0].start()
    for k in range(blocks):
        low_end, high_end = bounds[k : k + 2]
        here = slice(begin + low_end, begin + high_end)
        high, low = two(total_ref[skip + low_end : skip + high_end] - targets_ref[here])
        new_ref[low_end:high_end] = weights_ref[here] + dot(jnp.concatenate([high, high, low], axis=1), right, NN)
        copy = pltpu.make_async_copy(
            new_ref.at[pl.ds(low_end, high_end - low_end)],
            new_hbm.at[pl.ds(begin + low_end, high_end - low_end)],
            sems.at[k],
        )
        copy.start()
        copies.append(copy)
    for copy in copies:
        copy.wait()


def update_body(
    mine_ref, other_ref, targets_ref, index_ref, eigval_ref, spread_ref, weights_ref,
    new_hbm, out_hbm, right_ref, total_ref, new_ref, sems,
):
    start = (lax.axis_index("center") * 2 + lax.axis_index("sub")) * spread_ref.shape[1]
    rank, count = spread_ref.shape
    gather_total(mine_ref, other_ref, total_ref)
    value = eigval_ref[...]
    lowest = jnp.min(value, axis=1, keepdims=True)
    scaled = (1.0 - lowest / value) / value
    mixed_high, mixed_low = two(total_ref[:rank].T * (0.25 * scaled))
    spread_high, spread_low = two(spread_ref[...])
    turned = dot(mixed_high, spread_high, NN) + (
        dot(mixed_high, spread_low, NN) + dot(mixed_low, spread_high, NN)
    )
    high, low = two(turned - pick_rows(index_ref, count, start, F32, 0.25))
    for k, term in enumerate((high, low, high)):
        right_ref[k * term.shape[0] : (k + 1) * term.shape[0]] = term
    write_rows(0, rank, total_ref, targets_ref, weights_ref, right_ref, new_hbm, out_hbm, new_ref, sems)


def update(mine, other, targets, batch_index, eigval, spread, weights):
    classes, count = weights.shape
    padded, half = mine.shape
    rows = 2 * half
    rank = spread.shape[0]
    here = padded - rank
    vmem = pl.BlockSpec(memory_space=pltpu.VMEM)
    hbm = pl.BlockSpec(memory_space=pl.ANY)
    return pl.pallas_call(
        update_body,
        in_specs=[vmem] * 7,
        out_specs=[hbm, hbm, vmem],
        out_shape=[
            jax.ShapeDtypeStruct((classes, count), F32),
            jax.ShapeDtypeStruct((classes, rows), F32),
            jax.ShapeDtypeStruct((3 * rows, count), BF16),
        ],
        scratch_shapes=[
            pltpu.VMEM((padded, rows), F32),
            pltpu.VMEM((here, count), F32),
            pltpu.SemaphoreType.DMA((4,)),
        ],
        compiler_params=params(),
        cost_estimate=pl.CostEstimate(
            flops=6 * rows * count * (here + rank), bytes_accessed=8 * here * (count + rows), transcendentals=0
        ),
        name="update",
    )(mine, other, targets, batch_index, eigval, spread, weights)


def update_more_body(
    begin, mine_ref, other_ref, targets_ref, weights_ref, right_ref, new_in, out_in,
    new_hbm, out_hbm, total_ref, new_ref, sems,
):
    gather_total(mine_ref, other_ref, total_ref)
    write_rows(begin, 0, total_ref, targets_ref, weights_ref, right_ref, new_hbm, out_hbm, new_ref, sems)


def update_more(mine, other, targets, weights, right, new, out, begin):
    classes, count = weights.shape
    padded, half = mine.shape
    rows = 2 * half
    here = classes - begin
    vmem = pl.BlockSpec(memory_space=pltpu.VMEM)
    hbm = pl.BlockSpec(memory_space=pl.ANY)
    return pl.pallas_call(
        functools.partial(update_more_body, begin),
        in_specs=[vmem] * 5 + [hbm] * 2,
        out_specs=[hbm, hbm],
        out_shape=[
            jax.ShapeDtypeStruct((classes, count), F32),
            jax.ShapeDtypeStruct((classes, rows), F32),
        ],
        input_output_aliases={5: 0, 6: 1},
        scratch_shapes=[
            pltpu.VMEM((padded, rows), F32),
            pltpu.VMEM((here, count), F32),
            pltpu.SemaphoreType.DMA((6,)),
        ],
        compiler_params=params(),
        cost_estimate=pl.CostEstimate(
            flops=int(1.0 * 6) * rows * count * here, bytes_accessed=8 * here * (count + rows), transcendentals=0
        ),
        name="update_more",
    )(mine, other, targets, weights, right, new, out)


def swap(x, chips, order=None, level=0):
    flip = [2 << order(sub, chips.bit_length() - 1)[level] if order else 1 for sub in range(2)]
    return lax.ppermute(x, AXES, [(i, i ^ flip[i & 1]) for i in range(2 * chips)])


def tie(x, tied):
    x, *tied = lax.optimization_barrier((x, *tied))
    return x, tied


def total_of(keep, send, chips, tied=()):
    keep = keep + swap(send, chips)
    for level in range(chips.bit_length() - 1):
        if level >= HALVINGS:
            keep = keep + swap(keep, chips, walk, level)
            continue
        half = keep.shape[0] // 2
        keep, send = keep[:half], keep[half:]
        if level == 1 and tied:
            send, tied = tie(send, tied)
        keep = keep + swap(send, chips, walk, level)
    for level in reversed(range(HALVINGS)):
        keep = jnp.concatenate([keep, swap(keep, chips, walk, level)])
    return [keep, swap(keep, chips), *tied]


def gathered(first, second, squeeze, chips, ready):
    for level in range(chips.bit_length() - 1):
        if level == 1:
            second, ready = tie(second, ready)
        got = swap(first, chips, far_first, level)
        late = swap(second, chips, far_first, level)
        if level == 1:
            got, _ = tie(got, [second])
            first = squeeze_slots(squeeze, first, got)
            second = squeeze_slots(squeeze, second, late)
        else:
            first = jnp.concatenate([first, got])
            second = jnp.concatenate([second, late])
    return [first, swap(first, chips), second, swap(second, chips), *ready]


def one_hot(slot, slots):
    return (slot[:, None] == jnp.arange(slots, dtype=jnp.int32)[None, :]).astype(BF16)


def select_summed(rows):
    row = jnp.arange(rows, dtype=jnp.int32)
    half = rows // 2
    size = half // CHUNKS
    turn = jnp.stack(turns())[row // half]
    chunk = (row % half // size) ^ turn
    far = jnp.where(row // half == lax.axis_index("sub"), 0, half)
    return one_hot(far + chunk * size + row % size, rows)


def step(packed, chips, centers, weights, targets, batch_index, nys_index, eigvec, eigval):
    rows = batch_index.shape[1]
    classes, count = weights.shape
    depth = eigvec.shape[0]
    unit = 8 * CHUNKS
    units = -(-(classes + depth) // unit)
    first = (units + 1) // 2 * unit
    second = first
    far = [pltpu.with_memory_space_constraint(x, pltpu.HBM) for x in (batch_index, centers)]
    ready = [center_norms(centers), *spread_weights(nys_index.reshape(1, -1), eigvec, weights, first, second)]
    if packed:
        select, squeeze = select_packed(batch_index, count, chips)
        ready.append(select)
        slots = [pack_rows(*far, part) for part in range(PARTS)]
        mine, other, next_mine, next_other, *ready = gathered(*slots, squeeze, chips, ready)
        norms, left1, left2, spread, select = ready
    else:
        ready.append(select_summed(rows))
        picked = [pick_batch(*far, part) for part in range(PARTS)]
        mine, other = total_of(*picked[0], chips)
        next_mine, next_other, norms, left1, left2, spread, select = total_of(*picked[1], chips, ready)
    before, found = distances(mine, other, next_mine, select, centers, norms)
    keep, send, right = predict(found, next_other, select, centers, before, left1)
    one = total_of(keep, send, chips)
    another = total_of(*predict_more(left2, right), chips)
    new, out, right = update(*one, targets, batch_index, eigval, spread, weights)
    return update_more(*another, targets, weights, right, new, out, first - depth)


def on_device(chips, centers, weights, targets, batch_index, nys_index, eigvec, eigval):
    batch_index = batch_index.reshape(1, -1)
    new, out = lax.cond(
        rows_fit(pltpu.with_memory_space_constraint(batch_index, pltpu.HBM), centers.shape[0]) > 0,
        functools.partial(step, True, chips),
        functools.partial(step, False, chips),
        centers,
        weights.T,
        targets.T,
        batch_index,
        nys_index,
        eigvec.T,
        eigval.reshape(1, -1),
    )
    return new.T, out.T


def solution(mesh):
    return jax.shard_map(
        functools.partial(on_device, mesh.shape["center"]),
        mesh=mesh,
        in_specs=(
            P(("parts", "center", "sub"), None),
            P(("parts", "center", "sub"), None),
            P("parts", None),
            P("parts"),
            P(("parts", "center", "sub")),
            P(("parts", "center", "sub"), None),
            P("parts"),
        ),
        out_specs=(P(("parts", "center", "sub"), None), P("parts", None)),
        check_vma=False,
    )
```

```python
import functools
import math

import jax
import jax.numpy as jnp
from jax import lax
from jax.experimental import pallas as pl
from jax.experimental.pallas import tpu as pltpu
from jax.sharding import PartitionSpec as P

F32 = jnp.float32
BF16 = jnp.bfloat16
AXES = ("center", "sub")
HALVINGS = 2
CHUNKS = 1 << HALVINGS
LANE = 128
PARTS = 2
SLOTS = 32
GROUP_SLOTS = 96
BLOCKS = 3
NT = (((1,), (1,)), ((), ()))
NN = (((1,), (0,)), ((), ()))
VMEM_LIMIT = 24 * 1024 * 1024


def dot(a, b, dims):
    return lax.dot_general(a, b, dims, preferred_element_type=F32)


def walk(sub, bits):
    order = list(range(bits))
    return order if sub == 1 else order[1::-1] + order[2:]


def far_first(sub, bits):
    order = list(range(bits))[::-1]
    return order if sub == 1 else order[:-2] + order[:-3:-1]


def turns():
    center = lax.axis_index("center")
    return [
        sum(((center >> bit) & 1) << (HALVINGS - 1 - k) for k, bit in enumerate(walk(sub, HALVINGS + 1)[:HALVINGS]))
        for sub in range(2)
    ]


def column_of(row, width):
    return jnp.broadcast_to(row.astype(F32), (width, row.shape[1])).T


def two(x):
    high = x.astype(BF16)
    return high, (x - high.astype(F32)).astype(BF16)


def pick_rows(index_ref, columns, start, dtype, scale):
    column = column_of(index_ref[...] - start, LANE)
    lanes = lax.broadcasted_iota(jnp.int32, (1, LANE), 1).astype(F32)
    blocks = [
        jnp.where(column == lanes + float(LANE * k), scale, 0.0).astype(dtype)
        for k in range(columns // LANE)
    ]
    return jnp.concatenate(blocks, axis=1)


def params():
    return pltpu.CompilerParams(vmem_limit_bytes=VMEM_LIMIT)


def pick_body(first, index_hbm, centers_hbm, keep_ref, send_ref, pick_ref, index_ref, centers_ref, sems):
    sub = lax.axis_index("sub")
    blocks, count, block = centers_ref.shape
    rows = index_ref.shape[1]
    half = rows // 2
    size = half // CHUNKS
    copies = [pltpu.make_async_copy(index_hbm, index_ref, sems.at[blocks])] + [
        pltpu.make_async_copy(
            centers_hbm.at[:, pl.ds(first + k * block, block)], centers_ref.at[k], sems.at[k]
        )
        for k in range(blocks)
    ]
    for copy in copies:
        copy.start()
    copies[0].wait()
    start = (lax.axis_index("center") * 2 + sub) * count
    pick = pick_rows(index_ref, count, start, BF16, 1.0)
    for part, turn in enumerate(turns()):
        begin = jnp.where(sub == part, 0, half)
        for chunk in range(CHUNKS):
            to = pl.multiple_of(begin + (chunk ^ turn) * size, size)
            at = part * half + chunk * size
            pick_ref[pl.ds(to, size), :] = pick[at : at + size]
    for k in range(blocks):
        copies[k + 1].wait()
        found = dot(pick_ref[...], centers_ref[k], NN).astype(BF16)
        keep_ref[:, k * block : (k + 1) * block] = found[:half]
        send_ref[:, k * block : (k + 1) * block] = found[half:]


def pick_batch(batch_index, centers, part):
    rows = batch_index.shape[1]
    count, depth = centers.shape
    depth = depth // PARTS
    block = 512
    half = jax.ShapeDtypeStruct((rows // 2, depth), BF16)
    hbm = pl.BlockSpec(memory_space=pltpu.HBM)
    vmem = pl.BlockSpec(memory_space=pltpu.VMEM)
    return pl.pallas_call(
        functools.partial(pick_body, part * depth),
        in_specs=[hbm, hbm],
        out_specs=[vmem, vmem],
        out_shape=[half, half],
        scratch_shapes=[
            pltpu.VMEM((rows, count), BF16),
            pltpu.VMEM((1, rows), jnp.int32),
            pltpu.VMEM((depth // block, count, block), BF16),
            pltpu.SemaphoreType.DMA((depth // block + 1,)),
        ],
        compiler_params=params(),
        cost_estimate=pl.CostEstimate(
            flops=2 * rows * count * depth, bytes_accessed=2 * depth * (count + rows), transcendentals=0
        ),
        name="pick_batch",
    )(batch_index, centers)


def group_of(device, chips):
    bits = chips.bit_length() - 1
    masks = [sum(1 << bit for bit in far_first(sub, bits)[:2]) for sub in range(2)]
    center = device >> 1
    return (jnp.where((device & 1) == 0, center & ~masks[0], center & ~masks[1]) << 1) + (device & 1)


def owners(index, count, chips):
    owner = jnp.zeros_like(index)
    for device in range(1, 2 * chips):
        owner = owner + jnp.where(index >= device * count, 1, 0)
    return owner


def fits_body(count, index_hbm, fits_ref, index_ref, sem):
    copy = pltpu.make_async_copy(index_hbm, index_ref, sem)
    copy.start()
    copy.wait()
    chips = lax.axis_size("center")
    owner = owners(index_ref[...], count, chips)
    device = lax.broadcasted_iota(jnp.int32, (2 * chips, 1), 0)
    held = jnp.sum(jnp.where(owner == device, 1.0, 0.0), axis=1, keepdims=True)
    same = group_of(owner, chips) == group_of(device, chips)
    shared = jnp.sum(jnp.where(same, 1.0, 0.0), axis=1, keepdims=True)
    over = jnp.max(jnp.maximum(held - SLOTS, shared - GROUP_SLOTS))
    fits_ref[0] = (over <= 0.0).astype(jnp.int32)


def rows_fit(batch_index, count):
    return pl.pallas_call(
        functools.partial(fits_body, count),
        in_specs=[pl.BlockSpec(memory_space=pltpu.HBM)],
        out_specs=pl.BlockSpec(memory_space=pltpu.SMEM),
        out_shape=jax.ShapeDtypeStruct((1,), jnp.int32),
        scratch_shapes=[pltpu.VMEM(batch_index.shape, jnp.int32), pltpu.SemaphoreType.DMA],
        compiler_params=params(),
        name="rows_fit",
    )(batch_index)[0]


def pack_body(first, index_hbm, centers_hbm, out_ref, index_ref, centers_ref, sems):
    blocks, count, block = centers_ref.shape
    rows = index_ref.shape[1]
    copies = [pltpu.make_async_copy(index_hbm, index_ref, sems.at[blocks])] + [
        pltpu.make_async_copy(
            centers_hbm.at[:, pl.ds(first + k * block, block)], centers_ref.at[k], sems.at[k]
        )
        for k in range(blocks)
    ]
    for copy in copies:
        copy.start()
    copies[0].wait()
    start = (lax.axis_index("center") * 2 + lax.axis_index("sub")) * count
    local = index_ref[...] - start
    here = jnp.where((local >= 0) & (local < count), 1.0, 0.0)
    earlier = lax.broadcasted_iota(jnp.int32, (rows, rows), 0) < lax.broadcasted_iota(jnp.int32, (rows, rows), 1)
    rank = dot(jnp.broadcast_to(here, (8, rows)).astype(BF16), jnp.where(earlier, 1.0, 0.0).astype(BF16), NN)[0:1]
    slots = lax.broadcasted_iota(jnp.int32, (SLOTS, 1), 0).astype(F32)
    to_slot = jnp.where(slots == rank, here, 0.0).astype(BF16)
    pick = dot(to_slot, pick_rows(index_ref, count, start, BF16, 1.0), NN).astype(BF16)
    for k in range(blocks):
        copies[k + 1].wait()
        out_ref[:, k * block : (k + 1) * block] = dot(pick, centers_ref[k], NN).astype(BF16)


def pack_rows(batch_index, centers, part):
    rows = batch_index.shape[1]
    count, depth = centers.shape
    depth = depth // PARTS
    block = 512
    hbm = pl.BlockSpec(memory_space=pltpu.HBM)
    return pl.pallas_call(
        functools.partial(pack_body, part * depth),
        in_specs=[hbm, hbm],
        out_specs=pl.BlockSpec(memory_space=pltpu.VMEM),
        out_shape=jax.ShapeDtypeStruct((SLOTS, depth), BF16),
        scratch_shapes=[
            pltpu.VMEM((1, rows), jnp.int32),
            pltpu.VMEM((depth // block, count, block), BF16),
            pltpu.SemaphoreType.DMA((depth // block + 1,)),
        ],
        compiler_params=params(),
        cost_estimate=pl.CostEstimate(
            flops=2 * SLOTS * count * depth, bytes_accessed=2 * depth * (count + SLOTS), transcendentals=0
        ),
        name="pack_rows",
    )(batch_index, centers)


def select_body(count, index_ref, select_ref, squeeze_ref):
    rows, slots = select_ref.shape
    chips = lax.axis_size("center")
    center, sub = lax.axis_index("center"), lax.axis_index("sub")
    owner = owners(index_ref[...], count, chips)
    group = group_of(owner, chips)
    earlier = lax.broadcasted_iota(jnp.int32, (rows, rows), 0) < lax.broadcasted_iota(jnp.int32, (rows, rows), 1)

    def rank_among(key):
        column = jnp.concatenate([column_of(key, LANE)] * (rows // LANE), axis=1)
        return jnp.sum(jnp.where((column == key.astype(F32)) & earlier, 1.0, 0.0), axis=0, keepdims=True)

    away = (owner >> 1) ^ center
    orders = [far_first(side, chips.bit_length() - 1) for side in range(2)]

    def place(low, high):
        places = [
            sum(((away >> bit) & 1) << k for k, bit in enumerate(order[low:high])) + jnp.zeros_like(away)
            for order in orders
        ]
        return jnp.where((owner & 1) == 0, *places).astype(F32)

    lanes = lax.broadcasted_iota(jnp.int32, (1, LANE), 1).astype(F32)
    rank = rank_among(group)
    far = jnp.where((owner & 1) == sub, 0, slots // 2).astype(F32)
    slot = column_of(far + place(2, None) * float(GROUP_SLOTS) + rank, LANE)
    for k in range(slots // LANE):
        select_ref[:, k * LANE : (k + 1) * LANE] = jnp.where(slot == lanes + float(LANE * k), 1.0, 0.0).astype(BF16)
    before = column_of(place(0, 2) * float(SLOTS) + rank_among(owner), LANE)
    spots = lax.broadcasted_iota(jnp.int32, (GROUP_SLOTS, 1), 0).astype(F32)
    mine = group == group_of(center * 2 + sub, chips)
    to_spot = jnp.where((spots == rank) & mine, 1.0, 0.0).astype(BF16)
    squeeze_ref[...] = dot(to_spot, jnp.where(before == lanes, 1.0, 0.0).astype(BF16), NN).astype(BF16)


def select_packed(batch_index, count, chips):
    rows = batch_index.shape[1]
    half = -(-chips // 4 * GROUP_SLOTS // LANE) * LANE
    return pl.pallas_call(
        functools.partial(select_body, count),
        out_shape=[
            jax.ShapeDtypeStruct((rows, 2 * half), BF16),
            jax.ShapeDtypeStruct((GROUP_SLOTS, 4 * SLOTS), BF16),
        ],
        compiler_params=params(),
        name="select_packed",
    )(batch_index)


def squeeze_body(squeeze_ref, keep_ref, got_ref, out_ref):
    rows = keep_ref.shape[0]
    found = dot(squeeze_ref[:, :rows], keep_ref[...], NN) + dot(squeeze_ref[:, rows:], got_ref[...], NN)
    out_ref[...] = found.astype(BF16)


def squeeze_slots(squeeze, keep, got):
    depth = keep.shape[1]
    return pl.pallas_call(
        squeeze_body,
        out_shape=jax.ShapeDtypeStruct((squeeze.shape[0], depth), BF16),
        compiler_params=params(),
        cost_estimate=pl.CostEstimate(
            flops=40 * squeeze.size * depth, bytes_accessed=4 * squeeze.shape[1] * depth, transcendentals=0
        ),
        name="squeeze_slots",
    )(squeeze, keep, got)


def spread_body(
    first, classes, index_ref, eigvec_ref, weights_ref,
    left1_ref, left2_ref, spread_ref, all_ref,
):
    rank, points = eigvec_ref.shape
    count = weights_ref.shape[1]
    local = index_ref[...] - (lax.axis_index("center") * 2 + lax.axis_index("sub")) * count
    slots = lax.broadcasted_iota(jnp.int32, (count, points), 0)
    pick = jnp.where(slots == local, 1.0, 0.0).astype(BF16)
    vec = eigvec_ref[...]
    high = vec.astype(BF16)
    rest = vec - high.astype(F32)
    mid = rest.astype(BF16)
    low = (rest - mid.astype(F32)).astype(BF16)
    spread = dot(high, pick, NT) + dot(mid, pick, NT) + dot(low, pick, NT)
    spread_ref[...] = spread
    all_ref[:rank] = spread
    all_ref[rank : rank + classes] = weights_ref[...]
    all_ref[rank + classes :] = jnp.zeros((all_ref.shape[0] - rank - classes, count), F32)
    size = count // BLOCKS
    for begin, left_ref in ((0, left1_ref), (first, left2_ref)):
        for block in range(BLOCKS):
            high, low = two(all_ref[begin : begin + left_ref.shape[0], block * size : (block + 1) * size])
            for k, term in enumerate((high, high, low)):
                at = (3 * block + k) * size
                left_ref[:, at : at + size] = term


def spread_weights(nys_index, eigvec, weights, first, second):
    classes, count = weights.shape
    rank, points = eigvec.shape
    return pl.pallas_call(
        functools.partial(spread_body, first, classes),
        out_shape=[
            jax.ShapeDtypeStruct((first, 3 * count), BF16),
            jax.ShapeDtypeStruct((second, 3 * count), BF16),
            jax.ShapeDtypeStruct((rank, count), F32),
        ],
        scratch_shapes=[pltpu.VMEM((first + second, count), F32)],
        compiler_params=params(),
        cost_estimate=pl.CostEstimate(
            flops=6 * rank * points * count, bytes_accessed=8 * (first + second) * count, transcendentals=0
        ),
        name="spread_weights",
    )(nys_index, eigvec, weights)


def norms_body(centers_ref, norm_ref):
    wide = centers_ref[...].astype(F32)
    norm = jnp.sum(wide * wide, axis=1, keepdims=True)
    norm_ref[...] = jnp.broadcast_to(norm, norm_ref.shape)


def center_norms(centers):
    count, depth = centers.shape
    block = 256
    return pl.pallas_call(
        norms_body,
        grid=(count // block,),
        in_specs=[pl.BlockSpec((block, depth), lambda i: (i, 0))],
        out_specs=pl.BlockSpec((block, LANE), lambda i: (i, 0)),
        out_shape=jax.ShapeDtypeStruct((count, LANE), F32),
        compiler_params=params(),
        cost_estimate=pl.CostEstimate(flops=2 * count * depth, bytes_accessed=2 * count * depth, transcendentals=0),
        name="center_norms",
    )(centers)


def row_norms(batch_ref):
    rows = batch_ref.shape[0]
    batch = batch_ref[...].astype(F32)
    return jnp.broadcast_to(jnp.sum(batch * batch, axis=1, keepdims=True), (rows, LANE)).T[0:1]


def product(left_ref, right_ref, total_ref, keep_ref, send_ref):
    half = keep_ref.shape[1]
    size = left_ref.shape[1] // BLOCKS
    total = 0.0
    for block in range(BLOCKS):
        at = slice(block * size, (block + 1) * size)
        total = total + dot(left_ref[:, at], right_ref[at], NN)
    total_ref[...] = total
    lower = lax.axis_index("sub") == 0
    size = keep_ref.shape[0] // CHUNKS
    for chunk in range(CHUNKS):
        at = slice(chunk * size, (chunk + 1) * size)
        first, second = [
            total_ref[pl.ds(pl.multiple_of((chunk ^ turn) * size, 8), size), part * half : (part + 1) * half]
            for part, turn in enumerate(turns())
        ]
        keep_ref[at] = jnp.where(lower, first, second)
        send_ref[at] = jnp.where(lower, second, first)


def distance_body(mine_ref, other_ref, next_ref, select_ref, centers_ref, norm_ref, total_ref, found_ref, batch_ref):
    half, depth = mine_ref.shape
    wide = select_ref.shape[1] // 2
    near = select_ref[:, :half]
    far = select_ref[:, wide : wide + half]
    batch_ref[...] = (dot(near, mine_ref[...], NN) + dot(far, other_ref[...], NN)).astype(BF16)
    total_ref[...] = norm_ref[:, 0:1] + row_norms(batch_ref) - 2.0 * dot(centers_ref[:, :depth], batch_ref[...], NT)
    found_ref[...] = dot(near, next_ref[...], NN).astype(BF16)


def predict_body(
    found_ref, other_ref, select_ref, centers_ref, before_ref, left_ref,
    keep_ref, send_ref, right_ref, batch_ref, total_ref,
):
    count, depth = centers_ref.shape
    half, part = other_ref.shape
    wide = select_ref.shape[1] // 2
    found = found_ref[...].astype(F32) + dot(select_ref[:, wide : wide + half], other_ref[...], NN)
    batch_ref[...] = found.astype(BF16)
    norm = row_norms(batch_ref)
    size = count // BLOCKS
    for block in range(BLOCKS):
        at = slice(block * size, (block + 1) * size)
        cross = dot(centers_ref[at, depth - part :], batch_ref[...], NT)
        square = jnp.maximum(before_ref[at] + norm - 2.0 * cross, 0.0)
        high, low = two(jnp.exp(jnp.sqrt(square) * (-1.0 / math.sqrt(depth))))
        for k, term in enumerate((high, low, high)):
            to = (3 * block + k) * size
            right_ref[to : to + size] = term
    product(left_ref, right_ref, total_ref, keep_ref, send_ref)


def distances(mine, other, following, select, centers, norms):
    depth = mine.shape[1]
    rows = select.shape[0]
    count = centers.shape[0]
    vmem = pl.BlockSpec(memory_space=pltpu.VMEM)
    return pl.pallas_call(
        distance_body,
        in_specs=[vmem] * 6,
        out_specs=[vmem, vmem],
        out_shape=[jax.ShapeDtypeStruct((count, rows), F32), jax.ShapeDtypeStruct((rows, depth), BF16)],
        scratch_shapes=[pltpu.VMEM((rows, depth), BF16)],
        compiler_params=params(),
        cost_estimate=pl.CostEstimate(
            flops=2 * rows * count * depth, bytes_accessed=2 * depth * (count + rows), transcendentals=0
        ),
        name="distances",
    )(mine, other, following, select, centers, norms)


def predict(found, other, select, centers, before, left):
    depth = found.shape[1]
    rows = select.shape[0]
    half = rows // 2
    count = centers.shape[0]
    padded = left.shape[0]
    out = jax.ShapeDtypeStruct((padded, half), F32)
    vmem = pl.BlockSpec(memory_space=pltpu.VMEM)
    return pl.pallas_call(
        predict_body,
        in_specs=[vmem] * 6,
        out_specs=[vmem] * 3,
        out_shape=[out, out, jax.ShapeDtypeStruct((3 * count, rows), BF16)],
        scratch_shapes=[pltpu.VMEM((rows, depth), BF16), pltpu.VMEM((padded, rows), F32)],
        compiler_params=params(),
        cost_estimate=pl.CostEstimate(
            flops=2 * rows * count * (depth + 3 * padded),
            bytes_accessed=2 * depth * (count + rows) + 4 * padded * (count + rows),
            transcendentals=2 * rows * count,
        ),
        name="predict",
    )(found, other, select, centers, before, left)


def predict_more(left, right):
    padded, count = left.shape
    rows = right.shape[1]
    out = jax.ShapeDtypeStruct((padded, rows // 2), F32)
    return pl.pallas_call(
        lambda left, right, keep, send, total: product(left, right, total, keep, send),
        out_shape=[out, out],
        scratch_shapes=[pltpu.VMEM((padded, rows), F32)],
        compiler_params=params(),
        cost_estimate=pl.CostEstimate(
            flops=2 * rows * count * padded, bytes_accessed=2 * padded * (count + rows), transcendentals=0
        ),
        name="predict_more",
    )(left, right)


def gather_total(mine_ref, other_ref, total_ref):
    lower = lax.axis_index("sub") == 0
    half = mine_ref.shape[1]
    size = mine_ref.shape[0] // CHUNKS
    for part, turn in enumerate(turns()):
        for chunk in range(CHUNKS):
            at = slice(chunk * size, (chunk + 1) * size)
            same = lower if part == 0 else jnp.logical_not(lower)
            to = pl.multiple_of((chunk ^ turn) * size, 8)
            total_ref[pl.ds(to, size), part * half : (part + 1) * half] = jnp.where(
                same, mine_ref[at], other_ref[at]
            )


def write_rows(begin, skip, total_ref, targets_ref, weights_ref, right_ref, new_hbm, out_hbm, new_ref, sems):
    rows = new_ref.shape[0]
    blocks = sems.shape[0] - 1
    bounds = [8 * (rows // 8 * k // blocks) for k in range(blocks)] + [rows]
    right = right_ref[...]
    copies = [
        pltpu.make_async_copy(
            total_ref.at[pl.ds(skip, rows)], out_hbm.at[pl.ds(begin, rows)], sems.at[blocks]
        )
    ]
    copies[0].start()
    for k in range(blocks):
        low_end, high_end = bounds[k : k + 2]
        here = slice(begin + low_end, begin + high_end)
        high, low = two(total_ref[skip + low_end : skip + high_end] - targets_ref[here])
        new_ref[low_end:high_end] = weights_ref[here] + dot(jnp.concatenate([high, high, low], axis=1), right, NN)
        copy = pltpu.make_async_copy(
            new_ref.at[pl.ds(low_end, high_end - low_end)],
            new_hbm.at[pl.ds(begin + low_end, high_end - low_end)],
            sems.at[k],
        )
        copy.start()
        copies.append(copy)
    for copy in copies:
        copy.wait()


def update_body(
    mine_ref, other_ref, targets_ref, index_ref, eigval_ref, spread_ref, weights_ref,
    new_hbm, out_hbm, right_ref, total_ref, new_ref, sems,
):
    start = (lax.axis_index("center") * 2 + lax.axis_index("sub")) * spread_ref.shape[1]
    rank, count = spread_ref.shape
    gather_total(mine_ref, other_ref, total_ref)
    value = eigval_ref[...]
    lowest = jnp.min(value, axis=1, keepdims=True)
    scaled = (1.0 - lowest / value) / value
    mixed_high, mixed_low = two(total_ref[:rank].T * (0.25 * scaled))
    spread_high, spread_low = two(spread_ref[...])
    turned = dot(mixed_high, spread_high, NN) + (
        dot(mixed_high, spread_low, NN) + dot(mixed_low, spread_high, NN)
    )
    high, low = two(turned - pick_rows(index_ref, count, start, F32, 0.25))
    for k, term in enumerate((high, low, high)):
        right_ref[k * term.shape[0] : (k + 1) * term.shape[0]] = term
    write_rows(0, rank, total_ref, targets_ref, weights_ref, right_ref, new_hbm, out_hbm, new_ref, sems)


def update(mine, other, targets, batch_index, eigval, spread, weights):
    classes, count = weights.shape
    padded, half = mine.shape
    rows = 2 * half
    rank = spread.shape[0]
    here = padded - rank
    vmem = pl.BlockSpec(memory_space=pltpu.VMEM)
    hbm = pl.BlockSpec(memory_space=pl.ANY)
    return pl.pallas_call(
        update_body,
        in_specs=[vmem] * 7,
        out_specs=[hbm, hbm, vmem],
        out_shape=[
            jax.ShapeDtypeStruct((classes, count), F32),
            jax.ShapeDtypeStruct((classes, rows), F32),
            jax.ShapeDtypeStruct((3 * rows, count), BF16),
        ],
        scratch_shapes=[
            pltpu.VMEM((padded, rows), F32),
            pltpu.VMEM((here, count), F32),
            pltpu.SemaphoreType.DMA((8,)),
        ],
        compiler_params=params(),
        cost_estimate=pl.CostEstimate(
            flops=6 * rows * count * (here + rank), bytes_accessed=8 * here * (count + rows), transcendentals=0
        ),
        name="update",
    )(mine, other, targets, batch_index, eigval, spread, weights)


def update_more_body(
    begin, mine_ref, other_ref, targets_ref, weights_ref, right_ref, new_in, out_in,
    new_hbm, out_hbm, total_ref, new_ref, sems,
):
    gather_total(mine_ref, other_ref, total_ref)
    write_rows(begin, 0, total_ref, targets_ref, weights_ref, right_ref, new_hbm, out_hbm, new_ref, sems)


def update_more(mine, other, targets, weights, right, new, out, begin):
    classes, count = weights.shape
    padded, half = mine.shape
    rows = 2 * half
    here = classes - begin
    vmem = pl.BlockSpec(memory_space=pltpu.VMEM)
    hbm = pl.BlockSpec(memory_space=pl.ANY)
    return pl.pallas_call(
        functools.partial(update_more_body, begin),
        in_specs=[vmem] * 5 + [hbm] * 2,
        out_specs=[hbm, hbm],
        out_shape=[
            jax.ShapeDtypeStruct((classes, count), F32),
            jax.ShapeDtypeStruct((classes, rows), F32),
        ],
        input_output_aliases={5: 0, 6: 1},
        scratch_shapes=[
            pltpu.VMEM((padded, rows), F32),
            pltpu.VMEM((here, count), F32),
            pltpu.SemaphoreType.DMA((9,)),
        ],
        compiler_params=params(),
        cost_estimate=pl.CostEstimate(
            flops=int(1.0 * 6) * rows * count * here, bytes_accessed=8 * here * (count + rows), transcendentals=0
        ),
        name="update_more",
    )(mine, other, targets, weights, right, new, out)


def swap(x, chips, order=None, level=0):
    flip = [2 << order(sub, chips.bit_length() - 1)[level] if order else 1 for sub in range(2)]
    return lax.ppermute(x, AXES, [(i, i ^ flip[i & 1]) for i in range(2 * chips)])


def tie(x, tied):
    x, *tied = lax.optimization_barrier((x, *tied))
    return x, tied


def total_of(keep, send, chips, tied=()):
    keep = keep + swap(send, chips)
    for level in range(chips.bit_length() - 1):
        if level >= HALVINGS:
            keep = keep + swap(keep, chips, walk, level)
            continue
        half = keep.shape[0] // 2
        keep, send = keep[:half], keep[half:]
        if level == 1 and tied:
            send, tied = tie(send, tied)
        keep = keep + swap(send, chips, walk, level)
    for level in reversed(range(HALVINGS)):
        keep = jnp.concatenate([keep, swap(keep, chips, walk, level)])
    return [keep, swap(keep, chips), *tied]


def gathered(first, second, squeeze, chips, ready):
    for level in range(chips.bit_length() - 1):
        if level == 1:
            second, ready = tie(second, ready)
        got = swap(first, chips, far_first, level)
        late = swap(second, chips, far_first, level)
        if level == 1:
            got, _ = tie(got, [second])
            first = squeeze_slots(squeeze, first, got)
            second = squeeze_slots(squeeze, second, late)
        else:
            first = jnp.concatenate([first, got])
            second = jnp.concatenate([second, late])
    return [first, swap(first, chips), second, swap(second, chips), *ready]


def one_hot(slot, slots):
    return (slot[:, None] == jnp.arange(slots, dtype=jnp.int32)[None, :]).astype(BF16)


def select_summed(rows):
    row = jnp.arange(rows, dtype=jnp.int32)
    half = rows // 2
    size = half // CHUNKS
    turn = jnp.stack(turns())[row // half]
    chunk = (row % half // size) ^ turn
    far = jnp.where(row // half == lax.axis_index("sub"), 0, half)
    return one_hot(far + chunk * size + row % size, rows)


def step(packed, chips, centers, weights, targets, batch_index, nys_index, eigvec, eigval):
    rows = batch_index.shape[1]
    classes, count = weights.shape
    depth = eigvec.shape[0]
    unit = 8 * CHUNKS
    units = -(-(classes + depth) // unit)
    first = (units + 1) // 2 * unit
    second = first
    far = [pltpu.with_memory_space_constraint(x, pltpu.HBM) for x in (batch_index, centers)]
    ready = [center_norms(centers), *spread_weights(nys_index.reshape(1, -1), eigvec, weights, first, second)]
    if packed:
        select, squeeze = select_packed(batch_index, count, chips)
        ready.append(select)
        slots = [pack_rows(*far, part) for part in range(PARTS)]
        mine, other, next_mine, next_other, *ready = gathered(*slots, squeeze, chips, ready)
        norms, left1, left2, spread, select = ready
    else:
        ready.append(select_summed(rows))
        picked = [pick_batch(*far, part) for part in range(PARTS)]
        mine, other = total_of(*picked[0], chips)
        next_mine, next_other, norms, left1, left2, spread, select = total_of(*picked[1], chips, ready)
    before, found = distances(mine, other, next_mine, select, centers, norms)
    keep, send, right = predict(found, next_other, select, centers, before, left1)
    one = total_of(keep, send, chips)
    another = total_of(*predict_more(left2, right), chips)
    new, out, right = update(*one, targets, batch_index, eigval, spread, weights)
    return update_more(*another, targets, weights, right, new, out, first - depth)


def on_device(chips, centers, weights, targets, batch_index, nys_index, eigvec, eigval):
    batch_index = batch_index.reshape(1, -1)
    new, out = lax.cond(
        rows_fit(pltpu.with_memory_space_constraint(batch_index, pltpu.HBM), centers.shape[0]) > 0,
        functools.partial(step, True, chips),
        functools.partial(step, False, chips),
        centers,
        weights.T,
        targets.T,
        batch_index,
        nys_index,
        eigvec.T,
        eigval.reshape(1, -1),
    )
    return new.T, out.T


def solution(mesh):
    return jax.shard_map(
        functools.partial(on_device, mesh.shape["center"]),
        mesh=mesh,
        in_specs=(
            P(("parts", "center", "sub"), None),
            P(("parts", "center", "sub"), None),
            P("parts", None),
            P("parts"),
            P(("parts", "center", "sub")),
            P(("parts", "center", "sub"), None),
            P("parts"),
        ),
        out_specs=(P(("parts", "center", "sub"), None), P("parts", None)),
        check_vma=False,
    )
```

```python
import functools
import math

import jax
import jax.numpy as jnp
from jax import lax
from jax.experimental import pallas as pl
from jax.experimental.pallas import tpu as pltpu
from jax.sharding import PartitionSpec as P

F32 = jnp.float32
BF16 = jnp.bfloat16
AXES = ("center", "sub")
HALVINGS = 2
CHUNKS = 1 << HALVINGS
LANE = 128
PARTS = 2
SLOTS = 32
GROUP_SLOTS = 96
BLOCKS = 3
NT = (((1,), (1,)), ((), ()))
NN = (((1,), (0,)), ((), ()))
VMEM_LIMIT = 24 * 1024 * 1024


def dot(a, b, dims):
    return lax.dot_general(a, b, dims, preferred_element_type=F32)


def walk(sub, bits):
    order = list(range(bits))
    return order if sub == 1 else order[1::-1] + order[2:]


def far_first(sub, bits):
    order = list(range(bits))[::-1]
    return order if sub == 1 else order[:-2] + order[:-3:-1]


def turns():
    center = lax.axis_index("center")
    return [
        sum(((center >> bit) & 1) << (HALVINGS - 1 - k) for k, bit in enumerate(walk(sub, HALVINGS + 1)[:HALVINGS]))
        for sub in range(2)
    ]


def column_of(row, width):
    return jnp.broadcast_to(row.astype(F32), (width, row.shape[1])).T


def two(x):
    high = x.astype(BF16)
    return high, (x - high.astype(F32)).astype(BF16)


def pick_rows(index_ref, columns, start, dtype, scale):
    column = column_of(index_ref[...] - start, LANE)
    lanes = lax.broadcasted_iota(jnp.int32, (1, LANE), 1).astype(F32)
    blocks = [
        jnp.where(column == lanes + float(LANE * k), scale, 0.0).astype(dtype)
        for k in range(columns // LANE)
    ]
    return jnp.concatenate(blocks, axis=1)


def params():
    return pltpu.CompilerParams(vmem_limit_bytes=VMEM_LIMIT)


def pick_body(first, index_hbm, centers_hbm, keep_ref, send_ref, pick_ref, index_ref, centers_ref, sems):
    sub = lax.axis_index("sub")
    blocks, count, block = centers_ref.shape
    rows = index_ref.shape[1]
    half = rows // 2
    size = half // CHUNKS
    copies = [pltpu.make_async_copy(index_hbm, index_ref, sems.at[blocks])] + [
        pltpu.make_async_copy(
            centers_hbm.at[:, pl.ds(first + k * block, block)], centers_ref.at[k], sems.at[k]
        )
        for k in range(blocks)
    ]
    for copy in copies:
        copy.start()
    copies[0].wait()
    start = (lax.axis_index("center") * 2 + sub) * count
    pick = pick_rows(index_ref, count, start, BF16, 1.0)
    for part, turn in enumerate(turns()):
        begin = jnp.where(sub == part, 0, half)
        for chunk in range(CHUNKS):
            to = pl.multiple_of(begin + (chunk ^ turn) * size, size)
            at = part * half + chunk * size
            pick_ref[pl.ds(to, size), :] = pick[at : at + size]
    for k in range(blocks):
        copies[k + 1].wait()
        found = dot(pick_ref[...], centers_ref[k], NN).astype(BF16)
        keep_ref[:, k * block : (k + 1) * block] = found[:half]
        send_ref[:, k * block : (k + 1) * block] = found[half:]


def pick_batch(batch_index, centers, part):
    rows = batch_index.shape[1]
    count, depth = centers.shape
    depth = depth // PARTS
    block = 512
    half = jax.ShapeDtypeStruct((rows // 2, depth), BF16)
    hbm = pl.BlockSpec(memory_space=pltpu.HBM)
    vmem = pl.BlockSpec(memory_space=pltpu.VMEM)
    return pl.pallas_call(
        functools.partial(pick_body, part * depth),
        in_specs=[hbm, hbm],
        out_specs=[vmem, vmem],
        out_shape=[half, half],
        scratch_shapes=[
            pltpu.VMEM((rows, count), BF16),
            pltpu.VMEM((1, rows), jnp.int32),
            pltpu.VMEM((depth // block, count, block), BF16),
            pltpu.SemaphoreType.DMA((depth // block + 1,)),
        ],
        compiler_params=params(),
        cost_estimate=pl.CostEstimate(
            flops=2 * rows * count * depth, bytes_accessed=2 * depth * (count + rows), transcendentals=0
        ),
        name="pick_batch",
    )(batch_index, centers)


def group_of(device, chips):
    bits = chips.bit_length() - 1
    masks = [sum(1 << bit for bit in far_first(sub, bits)[:2]) for sub in range(2)]
    center = device >> 1
    return (jnp.where((device & 1) == 0, center & ~masks[0], center & ~masks[1]) << 1) + (device & 1)


def owners(index, count, chips):
    owner = jnp.zeros_like(index)
    for device in range(1, 2 * chips):
        owner = owner + jnp.where(index >= device * count, 1, 0)
    return owner


def fits_body(count, index_hbm, fits_ref, index_ref, sem):
    copy = pltpu.make_async_copy(index_hbm, index_ref, sem)
    copy.start()
    copy.wait()
    chips = lax.axis_size("center")
    owner = owners(index_ref[...], count, chips)
    device = lax.broadcasted_iota(jnp.int32, (2 * chips, 1), 0)
    held = jnp.sum(jnp.where(owner == device, 1.0, 0.0), axis=1, keepdims=True)
    same = group_of(owner, chips) == group_of(device, chips)
    shared = jnp.sum(jnp.where(same, 1.0, 0.0), axis=1, keepdims=True)
    over = jnp.max(jnp.maximum(held - SLOTS, shared - GROUP_SLOTS))
    fits_ref[0] = (over <= 0.0).astype(jnp.int32)


def rows_fit(batch_index, count):
    return pl.pallas_call(
        functools.partial(fits_body, count),
        in_specs=[pl.BlockSpec(memory_space=pltpu.HBM)],
        out_specs=pl.BlockSpec(memory_space=pltpu.SMEM),
        out_shape=jax.ShapeDtypeStruct((1,), jnp.int32),
        scratch_shapes=[pltpu.VMEM(batch_index.shape, jnp.int32), pltpu.SemaphoreType.DMA],
        compiler_params=params(),
        name="rows_fit",
    )(batch_index)[0]


def pack_body(first, index_hbm, centers_hbm, out_ref, index_ref, centers_ref, sems):
    blocks, count, block = centers_ref.shape
    rows = index_ref.shape[1]
    copies = [pltpu.make_async_copy(index_hbm, index_ref, sems.at[blocks])] + [
        pltpu.make_async_copy(
            centers_hbm.at[:, pl.ds(first + k * block, block)], centers_ref.at[k], sems.at[k]
        )
        for k in range(blocks)
    ]
    for copy in copies:
        copy.start()
    copies[0].wait()
    start = (lax.axis_index("center") * 2 + lax.axis_index("sub")) * count
    local = index_ref[...] - start
    here = jnp.where((local >= 0) & (local < count), 1.0, 0.0)
    earlier = lax.broadcasted_iota(jnp.int32, (rows, rows), 0) < lax.broadcasted_iota(jnp.int32, (rows, rows), 1)
    rank = dot(jnp.broadcast_to(here, (8, rows)).astype(BF16), jnp.where(earlier, 1.0, 0.0).astype(BF16), NN)[0:1]
    slots = lax.broadcasted_iota(jnp.int32, (SLOTS, 1), 0).astype(F32)
    to_slot = jnp.where(slots == rank, here, 0.0).astype(BF16)
    pick = dot(to_slot, pick_rows(index_ref, count, start, BF16, 1.0), NN).astype(BF16)
    for k in range(blocks):
        copies[k + 1].wait()
        out_ref[:, k * block : (k + 1) * block] = dot(pick, centers_ref[k], NN).astype(BF16)


def pack_rows(batch_index, centers, part):
    rows = batch_index.shape[1]
    count, depth = centers.shape
    depth = depth // PARTS
    block = 512
    hbm = pl.BlockSpec(memory_space=pltpu.HBM)
    return pl.pallas_call(
        functools.partial(pack_body, part * depth),
        in_specs=[hbm, hbm],
        out_specs=pl.BlockSpec(memory_space=pltpu.VMEM),
        out_shape=jax.ShapeDtypeStruct((SLOTS, depth), BF16),
        scratch_shapes=[
            pltpu.VMEM((1, rows), jnp.int32),
            pltpu.VMEM((depth // block, count, block), BF16),
            pltpu.SemaphoreType.DMA((depth // block + 1,)),
        ],
        compiler_params=params(),
        cost_estimate=pl.CostEstimate(
            flops=2 * SLOTS * count * depth, bytes_accessed=2 * depth * (count + SLOTS), transcendentals=0
        ),
        name="pack_rows",
    )(batch_index, centers)


def select_body(count, index_ref, select_ref, squeeze_ref):
    rows, slots = select_ref.shape
    chips = lax.axis_size("center")
    center, sub = lax.axis_index("center"), lax.axis_index("sub")
    owner = owners(index_ref[...], count, chips)
    group = group_of(owner, chips)
    earlier = lax.broadcasted_iota(jnp.int32, (rows, rows), 0) < lax.broadcasted_iota(jnp.int32, (rows, rows), 1)

    def rank_among(key):
        column = jnp.concatenate([column_of(key, LANE)] * (rows // LANE), axis=1)
        return jnp.sum(jnp.where((column == key.astype(F32)) & earlier, 1.0, 0.0), axis=0, keepdims=True)

    away = (owner >> 1) ^ center
    orders = [far_first(side, chips.bit_length() - 1) for side in range(2)]

    def place(low, high):
        places = [
            sum(((away >> bit) & 1) << k for k, bit in enumerate(order[low:high])) + jnp.zeros_like(away)
            for order in orders
        ]
        return jnp.where((owner & 1) == 0, *places).astype(F32)

    lanes = lax.broadcasted_iota(jnp.int32, (1, LANE), 1).astype(F32)
    rank = rank_among(group)
    far = jnp.where((owner & 1) == sub, 0, slots // 2).astype(F32)
    slot = column_of(far + place(2, None) * float(GROUP_SLOTS) + rank, LANE)
    for k in range(slots // LANE):
        select_ref[:, k * LANE : (k + 1) * LANE] = jnp.where(slot == lanes + float(LANE * k), 1.0, 0.0).astype(BF16)
    before = column_of(place(0, 2) * float(SLOTS) + rank_among(owner), LANE)
    spots = lax.broadcasted_iota(jnp.int32, (GROUP_SLOTS, 1), 0).astype(F32)
    mine = group == group_of(center * 2 + sub, chips)
    to_spot = jnp.where((spots == rank) & mine, 1.0, 0.0).astype(BF16)
    squeeze_ref[...] = dot(to_spot, jnp.where(before == lanes, 1.0, 0.0).astype(BF16), NN).astype(BF16)


def select_packed(batch_index, count, chips):
    rows = batch_index.shape[1]
    half = -(-chips // 4 * GROUP_SLOTS // LANE) * LANE
    return pl.pallas_call(
        functools.partial(select_body, count),
        out_shape=[
            jax.ShapeDtypeStruct((rows, 2 * half), BF16),
            jax.ShapeDtypeStruct((GROUP_SLOTS, 4 * SLOTS), BF16),
        ],
        compiler_params=params(),
        name="select_packed",
    )(batch_index)


def squeeze_body(squeeze_ref, keep_ref, got_ref, out_ref):
    rows = keep_ref.shape[0]
    found = dot(squeeze_ref[:, :rows], keep_ref[...], NN) + dot(squeeze_ref[:, rows:], got_ref[...], NN)
    out_ref[...] = found.astype(BF16)


def squeeze_slots(squeeze, keep, got):
    depth = keep.shape[1]
    return pl.pallas_call(
        squeeze_body,
        out_shape=jax.ShapeDtypeStruct((squeeze.shape[0], depth), BF16),
        compiler_params=params(),
        cost_estimate=pl.CostEstimate(
            flops=40 * squeeze.size * depth, bytes_accessed=4 * squeeze.shape[1] * depth, transcendentals=0
        ),
        name="squeeze_slots",
    )(squeeze, keep, got)


def spread_body(
    first, classes, index_ref, eigvec_ref, weights_ref,
    left1_ref, left2_ref, spread_ref, all_ref,
):
    rank, points = eigvec_ref.shape
    count = weights_ref.shape[1]
    local = index_ref[...] - (lax.axis_index("center") * 2 + lax.axis_index("sub")) * count
    slots = lax.broadcasted_iota(jnp.int32, (count, points), 0)
    pick = jnp.where(slots == local, 1.0, 0.0).astype(BF16)
    vec = eigvec_ref[...]
    high = vec.astype(BF16)
    rest = vec - high.astype(F32)
    mid = rest.astype(BF16)
    low = (rest - mid.astype(F32)).astype(BF16)
    spread = dot(high, pick, NT) + dot(mid, pick, NT) + dot(low, pick, NT)
    spread_ref[...] = spread
    all_ref[:rank] = spread
    all_ref[rank : rank + classes] = weights_ref[...]
    all_ref[rank + classes :] = jnp.zeros((all_ref.shape[0] - rank - classes, count), F32)
    size = count // BLOCKS
    for begin, left_ref in ((0, left1_ref), (first, left2_ref)):
        for block in range(BLOCKS):
            high, low = two(all_ref[begin : begin + left_ref.shape[0], block * size : (block + 1) * size])
            for k, term in enumerate((high, high, low)):
                at = (3 * block + k) * size
                left_ref[:, at : at + size] = term


def spread_weights(nys_index, eigvec, weights, first, second):
    classes, count = weights.shape
    rank, points = eigvec.shape
    return pl.pallas_call(
        functools.partial(spread_body, first, classes),
        out_shape=[
            jax.ShapeDtypeStruct((first, 3 * count), BF16),
            jax.ShapeDtypeStruct((second, 3 * count), BF16),
            jax.ShapeDtypeStruct((rank, count), F32),
        ],
        scratch_shapes=[pltpu.VMEM((first + second, count), F32)],
        compiler_params=params(),
        cost_estimate=pl.CostEstimate(
            flops=6 * rank * points * count, bytes_accessed=8 * (first + second) * count, transcendentals=0
        ),
        name="spread_weights",
    )(nys_index, eigvec, weights)


def norms_body(centers_ref, norm_ref):
    wide = centers_ref[...].astype(F32)
    norm = jnp.sum(wide * wide, axis=1, keepdims=True)
    norm_ref[...] = jnp.broadcast_to(norm, norm_ref.shape)


def center_norms(centers):
    count, depth = centers.shape
    block = 256
    return pl.pallas_call(
        norms_body,
        grid=(count // block,),
        in_specs=[pl.BlockSpec((block, depth), lambda i: (i, 0))],
        out_specs=pl.BlockSpec((block, LANE), lambda i: (i, 0)),
        out_shape=jax.ShapeDtypeStruct((count, LANE), F32),
        compiler_params=params(),
        cost_estimate=pl.CostEstimate(flops=2 * count * depth, bytes_accessed=2 * count * depth, transcendentals=0),
        name="center_norms",
    )(centers)


def row_norms(batch_ref):
    rows = batch_ref.shape[0]
    batch = batch_ref[...].astype(F32)
    return jnp.broadcast_to(jnp.sum(batch * batch, axis=1, keepdims=True), (rows, LANE)).T[0:1]


def product(left_ref, right_ref, total_ref, keep_ref, send_ref):
    half = keep_ref.shape[1]
    size = left_ref.shape[1] // BLOCKS
    total = 0.0
    for block in range(BLOCKS):
        at = slice(block * size, (block + 1) * size)
        total = total + dot(left_ref[:, at], right_ref[at], NN)
    total_ref[...] = total
    lower = lax.axis_index("sub") == 0
    size = keep_ref.shape[0] // CHUNKS
    for chunk in range(CHUNKS):
        at = slice(chunk * size, (chunk + 1) * size)
        first, second = [
            total_ref[pl.ds(pl.multiple_of((chunk ^ turn) * size, 8), size), part * half : (part + 1) * half]
            for part, turn in enumerate(turns())
        ]
        keep_ref[at] = jnp.where(lower, first, second)
        send_ref[at] = jnp.where(lower, second, first)


def distance_body(mine_ref, other_ref, next_ref, select_ref, centers_ref, norm_ref, total_ref, found_ref, batch_ref):
    half, depth = mine_ref.shape
    wide = select_ref.shape[1] // 2
    near = select_ref[:, :half]
    far = select_ref[:, wide : wide + half]
    batch_ref[...] = (dot(near, mine_ref[...], NN) + dot(far, other_ref[...], NN)).astype(BF16)
    total_ref[...] = norm_ref[:, 0:1] + row_norms(batch_ref) - 2.0 * dot(centers_ref[:, :depth], batch_ref[...], NT)
    found_ref[...] = dot(near, next_ref[...], NN).astype(BF16)


def predict_body(
    found_ref, other_ref, select_ref, centers_ref, before_ref, left_ref,
    keep_ref, send_ref, right_ref, batch_ref, total_ref,
):
    count, depth = centers_ref.shape
    half, part = other_ref.shape
    wide = select_ref.shape[1] // 2
    found = found_ref[...].astype(F32) + dot(select_ref[:, wide : wide + half], other_ref[...], NN)
    batch_ref[...] = found.astype(BF16)
    norm = row_norms(batch_ref)
    size = count // BLOCKS
    for block in range(BLOCKS):
        at = slice(block * size, (block + 1) * size)
        cross = dot(centers_ref[at, depth - part :], batch_ref[...], NT)
        square = jnp.maximum(before_ref[at] + norm - 2.0 * cross, 0.0)
        high, low = two(jnp.exp(jnp.sqrt(square) * (-1.0 / math.sqrt(depth))))
        for k, term in enumerate((high, low, high)):
            to = (3 * block + k) * size
            right_ref[to : to + size] = term
    product(left_ref, right_ref, total_ref, keep_ref, send_ref)


def distances(mine, other, following, select, centers, norms):
    depth = mine.shape[1]
    rows = select.shape[0]
    count = centers.shape[0]
    vmem = pl.BlockSpec(memory_space=pltpu.VMEM)
    return pl.pallas_call(
        distance_body,
        in_specs=[vmem] * 6,
        out_specs=[vmem, vmem],
        out_shape=[jax.ShapeDtypeStruct((count, rows), F32), jax.ShapeDtypeStruct((rows, depth), BF16)],
        scratch_shapes=[pltpu.VMEM((rows, depth), BF16)],
        compiler_params=params(),
        cost_estimate=pl.CostEstimate(
            flops=2 * rows * count * depth, bytes_accessed=2 * depth * (count + rows), transcendentals=0
        ),
        name="distances",
    )(mine, other, following, select, centers, norms)


def predict(found, other, select, centers, before, left):
    depth = found.shape[1]
    rows = select.shape[0]
    half = rows // 2
    count = centers.shape[0]
    padded = left.shape[0]
    out = jax.ShapeDtypeStruct((padded, half), F32)
    vmem = pl.BlockSpec(memory_space=pltpu.VMEM)
    return pl.pallas_call(
        predict_body,
        in_specs=[vmem] * 6,
        out_specs=[vmem] * 3,
        out_shape=[out, out, jax.ShapeDtypeStruct((3 * count, rows), BF16)],
        scratch_shapes=[pltpu.VMEM((rows, depth), BF16), pltpu.VMEM((padded, rows), F32)],
        compiler_params=params(),
        cost_estimate=pl.CostEstimate(
            flops=2 * rows * count * (depth + 3 * padded),
            bytes_accessed=2 * depth * (count + rows) + 4 * padded * (count + rows),
            transcendentals=2 * rows * count,
        ),
        name="predict",
    )(found, other, select, centers, before, left)


def predict_more(left, right):
    padded, count = left.shape
    rows = right.shape[1]
    out = jax.ShapeDtypeStruct((padded, rows // 2), F32)
    return pl.pallas_call(
        lambda left, right, keep, send, total: product(left, right, total, keep, send),
        out_shape=[out, out],
        scratch_shapes=[pltpu.VMEM((padded, rows), F32)],
        compiler_params=params(),
        cost_estimate=pl.CostEstimate(
            flops=2 * rows * count * padded, bytes_accessed=2 * padded * (count + rows), transcendentals=0
        ),
        name="predict_more",
    )(left, right)


def gather_total(mine_ref, other_ref, total_ref):
    lower = lax.axis_index("sub") == 0
    half = mine_ref.shape[1]
    size = mine_ref.shape[0] // CHUNKS
    for part, turn in enumerate(turns()):
        for chunk in range(CHUNKS):
            at = slice(chunk * size, (chunk + 1) * size)
            same = lower if part == 0 else jnp.logical_not(lower)
            to = pl.multiple_of((chunk ^ turn) * size, 8)
            total_ref[pl.ds(to, size), part * half : (part + 1) * half] = jnp.where(
                same, mine_ref[at], other_ref[at]
            )


def write_rows(begin, skip, total_ref, targets_ref, weights_ref, right_ref, new_hbm, out_hbm, new_ref, sems):
    rows = new_ref.shape[0]
    blocks = sems.shape[0] - 1
    bounds = [8 * (rows // 8 * k // blocks) for k in range(blocks)] + [rows]
    right = right_ref[...]
    copies = [
        pltpu.make_async_copy(
            total_ref.at[pl.ds(skip, rows)], out_hbm.at[pl.ds(begin, rows)], sems.at[blocks]
        )
    ]
    copies[0].start()
    for k in range(blocks):
        low_end, high_end = bounds[k : k + 2]
        here = slice(begin + low_end, begin + high_end)
        high, low = two(total_ref[skip + low_end : skip + high_end] - targets_ref[here])
        new_ref[low_end:high_end] = weights_ref[here] + dot(jnp.concatenate([high, high, low], axis=1), right, NN)
        copy = pltpu.make_async_copy(
            new_ref.at[pl.ds(low_end, high_end - low_end)],
            new_hbm.at[pl.ds(begin + low_end, high_end - low_end)],
            sems.at[k],
        )
        copy.start()
        copies.append(copy)
    for copy in copies:
        copy.wait()


def update_body(
    mine_ref, other_ref, targets_ref, index_ref, eigval_ref, spread_ref, weights_ref,
    new_hbm, out_hbm, right_ref, total_ref, new_ref, sems,
):
    start = (lax.axis_index("center") * 2 + lax.axis_index("sub")) * spread_ref.shape[1]
    rank, count = spread_ref.shape
    gather_total(mine_ref, other_ref, total_ref)
    value = eigval_ref[...]
    lowest = jnp.min(value, axis=1, keepdims=True)
    scaled = (1.0 - lowest / value) / value
    mixed_high, mixed_low = two(total_ref[:rank].T * (0.25 * scaled))
    spread_high, spread_low = two(spread_ref[...])
    turned = dot(mixed_high, spread_high, NN) + (
        dot(mixed_high, spread_low, NN) + dot(mixed_low, spread_high, NN)
    )
    high, low = two(turned - pick_rows(index_ref, count, start, F32, 0.25))
    for k, term in enumerate((high, low, high)):
        right_ref[k * term.shape[0] : (k + 1) * term.shape[0]] = term
    write_rows(0, rank, total_ref, targets_ref, weights_ref, right_ref, new_hbm, out_hbm, new_ref, sems)


def update(mine, other, targets, batch_index, eigval, spread, weights):
    classes, count = weights.shape
    padded, half = mine.shape
    rows = 2 * half
    rank = spread.shape[0]
    here = padded - rank
    vmem = pl.BlockSpec(memory_space=pltpu.VMEM)
    hbm = pl.BlockSpec(memory_space=pl.ANY)
    return pl.pallas_call(
        update_body,
        in_specs=[vmem] * 7,
        out_specs=[hbm, hbm, vmem],
        out_shape=[
            jax.ShapeDtypeStruct((classes, count), F32),
            jax.ShapeDtypeStruct((classes, rows), F32),
            jax.ShapeDtypeStruct((3 * rows, count), BF16),
        ],
        scratch_shapes=[
            pltpu.VMEM((padded, rows), F32),
            pltpu.VMEM((here, count), F32),
            pltpu.SemaphoreType.DMA((3,)),
        ],
        compiler_params=params(),
        cost_estimate=pl.CostEstimate(
            flops=6 * rows * count * (here + rank), bytes_accessed=8 * here * (count + rows), transcendentals=0
        ),
        name="update",
    )(mine, other, targets, batch_index, eigval, spread, weights)


def update_more_body(
    begin, mine_ref, other_ref, targets_ref, weights_ref, right_ref, new_in, out_in,
    new_hbm, out_hbm, total_ref, new_ref, sems,
):
    gather_total(mine_ref, other_ref, total_ref)
    write_rows(begin, 0, total_ref, targets_ref, weights_ref, right_ref, new_hbm, out_hbm, new_ref, sems)


def update_more(mine, other, targets, weights, right, new, out, begin):
    classes, count = weights.shape
    padded, half = mine.shape
    rows = 2 * half
    here = classes - begin
    vmem = pl.BlockSpec(memory_space=pltpu.VMEM)
    hbm = pl.BlockSpec(memory_space=pl.ANY)
    return pl.pallas_call(
        functools.partial(update_more_body, begin),
        in_specs=[vmem] * 5 + [hbm] * 2,
        out_specs=[hbm, hbm],
        out_shape=[
            jax.ShapeDtypeStruct((classes, count), F32),
            jax.ShapeDtypeStruct((classes, rows), F32),
        ],
        input_output_aliases={5: 0, 6: 1},
        scratch_shapes=[
            pltpu.VMEM((padded, rows), F32),
            pltpu.VMEM((here, count), F32),
            pltpu.SemaphoreType.DMA((3,)),
        ],
        compiler_params=params(),
        cost_estimate=pl.CostEstimate(
            flops=int(1.0 * 6) * rows * count * here, bytes_accessed=8 * here * (count + rows), transcendentals=0
        ),
        name="update_more",
    )(mine, other, targets, weights, right, new, out)


def swap(x, chips, order=None, level=0):
    flip = [2 << order(sub, chips.bit_length() - 1)[level] if order else 1 for sub in range(2)]
    return lax.ppermute(x, AXES, [(i, i ^ flip[i & 1]) for i in range(2 * chips)])


def tie(x, tied):
    x, *tied = lax.optimization_barrier((x, *tied))
    return x, tied


def total_of(keep, send, chips, tied=()):
    keep = keep + swap(send, chips)
    for level in range(chips.bit_length() - 1):
        if level >= HALVINGS:
            keep = keep + swap(keep, chips, walk, level)
            continue
        half = keep.shape[0] // 2
        keep, send = keep[:half], keep[half:]
        if level == 1 and tied:
            send, tied = tie(send, tied)
        keep = keep + swap(send, chips, walk, level)
    for level in reversed(range(HALVINGS)):
        keep = jnp.concatenate([keep, swap(keep, chips, walk, level)])
    return [keep, swap(keep, chips), *tied]


def gathered(first, second, squeeze, chips, ready):
    for level in range(chips.bit_length() - 1):
        if level == 1:
            second, ready = tie(second, ready)
        got = swap(first, chips, far_first, level)
        late = swap(second, chips, far_first, level)
        if level == 1:
            got, _ = tie(got, [second])
            first = squeeze_slots(squeeze, first, got)
            second = squeeze_slots(squeeze, second, late)
        else:
            first = jnp.concatenate([first, got])
            second = jnp.concatenate([second, late])
    return [first, swap(first, chips), second, swap(second, chips), *ready]


def one_hot(slot, slots):
    return (slot[:, None] == jnp.arange(slots, dtype=jnp.int32)[None, :]).astype(BF16)


def select_summed(rows):
    row = jnp.arange(rows, dtype=jnp.int32)
    half = rows // 2
    size = half // CHUNKS
    turn = jnp.stack(turns())[row // half]
    chunk = (row % half // size) ^ turn
    far = jnp.where(row // half == lax.axis_index("sub"), 0, half)
    return one_hot(far + chunk * size + row % size, rows)


def step(packed, chips, centers, weights, targets, batch_index, nys_index, eigvec, eigval):
    rows = batch_index.shape[1]
    classes, count = weights.shape
    depth = eigvec.shape[0]
    unit = 8 * CHUNKS
    units = -(-(classes + depth) // unit)
    first = (units + 1) // 2 * unit
    second = first
    far = [pltpu.with_memory_space_constraint(x, pltpu.HBM) for x in (batch_index, centers)]
    ready = [center_norms(centers), *spread_weights(nys_index.reshape(1, -1), eigvec, weights, first, second)]
    if packed:
        select, squeeze = select_packed(batch_index, count, chips)
        ready.append(select)
        slots = [pack_rows(*far, part) for part in range(PARTS)]
        mine, other, next_mine, next_other, *ready = gathered(*slots, squeeze, chips, ready)
        norms, left1, left2, spread, select = ready
    else:
        ready.append(select_summed(rows))
        picked = [pick_batch(*far, part) for part in range(PARTS)]
        mine, other = total_of(*picked[0], chips)
        next_mine, next_other, norms, left1, left2, spread, select = total_of(*picked[1], chips, ready)
    before, found = distances(mine, other, next_mine, select, centers, norms)
    keep, send, right = predict(found, next_other, select, centers, before, left1)
    one = total_of(keep, send, chips)
    another = total_of(*predict_more(left2, right), chips)
    new, out, right = update(*one, targets, batch_index, eigval, spread, weights)
    return update_more(*another, targets, weights, right, new, out, first - depth)


def on_device(chips, centers, weights, targets, batch_index, nys_index, eigvec, eigval):
    batch_index = batch_index.reshape(1, -1)
    new, out = lax.cond(
        rows_fit(pltpu.with_memory_space_constraint(batch_index, pltpu.HBM), centers.shape[0]) > 0,
        functools.partial(step, True, chips),
        functools.partial(step, False, chips),
        centers,
        weights.T,
        targets.T,
        batch_index,
        nys_index,
        eigvec.T,
        eigval.reshape(1, -1),
    )
    return new.T, out.T


def solution(mesh):
    return jax.shard_map(
        functools.partial(on_device, mesh.shape["center"]),
        mesh=mesh,
        in_specs=(
            P(("parts", "center", "sub"), None),
            P(("parts", "center", "sub"), None),
            P("parts", None),
            P("parts"),
            P(("parts", "center", "sub")),
            P(("parts", "center", "sub"), None),
            P("parts"),
        ),
        out_specs=(P(("parts", "center", "sub"), None), P("parts", None)),
        check_vma=False,
    )
```

```python
import functools
import math

import jax
import jax.numpy as jnp
from jax import lax
from jax.experimental import pallas as pl
from jax.experimental.pallas import tpu as pltpu
from jax.sharding import PartitionSpec as P

F32 = jnp.float32
BF16 = jnp.bfloat16
AXES = ("center", "sub")
HALVINGS = 2
CHUNKS = 1 << HALVINGS
LANE = 128
PARTS = 2
SLOTS = 32
GROUP_SLOTS = 96
BLOCKS = 3
NT = (((1,), (1,)), ((), ()))
NN = (((1,), (0,)), ((), ()))
VMEM_LIMIT = 24 * 1024 * 1024


def dot(a, b, dims):
    return lax.dot_general(a, b, dims, preferred_element_type=F32)


def walk(sub, bits):
    order = list(range(bits))
    return order if sub == 1 else order[1::-1] + order[2:]


def far_first(sub, bits):
    order = list(range(bits))[::-1]
    return order if sub == 1 else order[:-2] + order[:-3:-1]


def turns():
    center = lax.axis_index("center")
    return [
        sum(((center >> bit) & 1) << (HALVINGS - 1 - k) for k, bit in enumerate(walk(sub, HALVINGS + 1)[:HALVINGS]))
        for sub in range(2)
    ]


def column_of(row, width):
    return jnp.broadcast_to(row.astype(F32), (width, row.shape[1])).T


def two(x):
    high = x.astype(BF16)
    return high, (x - high.astype(F32)).astype(BF16)


def pick_rows(index_ref, columns, start, dtype, scale):
    column = column_of(index_ref[...] - start, LANE)
    lanes = lax.broadcasted_iota(jnp.int32, (1, LANE), 1).astype(F32)
    blocks = [
        jnp.where(column == lanes + float(LANE * k), scale, 0.0).astype(dtype)
        for k in range(columns // LANE)
    ]
    return jnp.concatenate(blocks, axis=1)


def params():
    return pltpu.CompilerParams(vmem_limit_bytes=VMEM_LIMIT)


def pick_body(first, index_hbm, centers_hbm, keep_ref, send_ref, pick_ref, index_ref, centers_ref, sems):
    sub = lax.axis_index("sub")
    blocks, count, block = centers_ref.shape
    rows = index_ref.shape[1]
    half = rows // 2
    size = half // CHUNKS
    copies = [pltpu.make_async_copy(index_hbm, index_ref, sems.at[blocks])] + [
        pltpu.make_async_copy(
            centers_hbm.at[:, pl.ds(first + k * block, block)], centers_ref.at[k], sems.at[k]
        )
        for k in range(blocks)
    ]
    for copy in copies:
        copy.start()
    copies[0].wait()
    start = (lax.axis_index("center") * 2 + sub) * count
    pick = pick_rows(index_ref, count, start, BF16, 1.0)
    for part, turn in enumerate(turns()):
        begin = jnp.where(sub == part, 0, half)
        for chunk in range(CHUNKS):
            to = pl.multiple_of(begin + (chunk ^ turn) * size, size)
            at = part * half + chunk * size
            pick_ref[pl.ds(to, size), :] = pick[at : at + size]
    for k in range(blocks):
        copies[k + 1].wait()
        found = dot(pick_ref[...], centers_ref[k], NN).astype(BF16)
        keep_ref[:, k * block : (k + 1) * block] = found[:half]
        send_ref[:, k * block : (k + 1) * block] = found[half:]


def pick_batch(batch_index, centers, part):
    rows = batch_index.shape[1]
    count, depth = centers.shape
    depth = depth // PARTS
    block = 512
    half = jax.ShapeDtypeStruct((rows // 2, depth), BF16)
    hbm = pl.BlockSpec(memory_space=pltpu.HBM)
    vmem = pl.BlockSpec(memory_space=pltpu.VMEM)
    return pl.pallas_call(
        functools.partial(pick_body, part * depth),
        in_specs=[hbm, hbm],
        out_specs=[vmem, vmem],
        out_shape=[half, half],
        scratch_shapes=[
            pltpu.VMEM((rows, count), BF16),
            pltpu.VMEM((1, rows), jnp.int32),
            pltpu.VMEM((depth // block, count, block), BF16),
            pltpu.SemaphoreType.DMA((depth // block + 1,)),
        ],
        compiler_params=params(),
        cost_estimate=pl.CostEstimate(
            flops=2 * rows * count * depth, bytes_accessed=2 * depth * (count + rows), transcendentals=0
        ),
        name="pick_batch",
    )(batch_index, centers)


def group_of(device, chips):
    bits = chips.bit_length() - 1
    masks = [sum(1 << bit for bit in far_first(sub, bits)[:2]) for sub in range(2)]
    center = device >> 1
    return (jnp.where((device & 1) == 0, center & ~masks[0], center & ~masks[1]) << 1) + (device & 1)


def owners(index, count, chips):
    owner = jnp.zeros_like(index)
    for device in range(1, 2 * chips):
        owner = owner + jnp.where(index >= device * count, 1, 0)
    return owner


def fits_body(count, index_hbm, fits_ref, index_ref, sem):
    copy = pltpu.make_async_copy(index_hbm, index_ref, sem)
    copy.start()
    copy.wait()
    chips = lax.axis_size("center")
    owner = owners(index_ref[...], count, chips)
    device = lax.broadcasted_iota(jnp.int32, (2 * chips, 1), 0)
    held = jnp.sum(jnp.where(owner == device, 1.0, 0.0), axis=1, keepdims=True)
    same = group_of(owner, chips) == group_of(device, chips)
    shared = jnp.sum(jnp.where(same, 1.0, 0.0), axis=1, keepdims=True)
    over = jnp.max(jnp.maximum(held - SLOTS, shared - GROUP_SLOTS))
    fits_ref[0] = (over <= 0.0).astype(jnp.int32)


def rows_fit(batch_index, count):
    return pl.pallas_call(
        functools.partial(fits_body, count),
        in_specs=[pl.BlockSpec(memory_space=pltpu.HBM)],
        out_specs=pl.BlockSpec(memory_space=pltpu.SMEM),
        out_shape=jax.ShapeDtypeStruct((1,), jnp.int32),
        scratch_shapes=[pltpu.VMEM(batch_index.shape, jnp.int32), pltpu.SemaphoreType.DMA],
        compiler_params=params(),
        name="rows_fit",
    )(batch_index)[0]


def pack_body(first, index_hbm, centers_hbm, out_ref, index_ref, centers_ref, sems):
    blocks, count, block = centers_ref.shape
    rows = index_ref.shape[1]
    copies = [pltpu.make_async_copy(index_hbm, index_ref, sems.at[blocks])] + [
        pltpu.make_async_copy(
            centers_hbm.at[:, pl.ds(first + k * block, block)], centers_ref.at[k], sems.at[k]
        )
        for k in range(blocks)
    ]
    for copy in copies:
        copy.start()
    copies[0].wait()
    start = (lax.axis_index("center") * 2 + lax.axis_index("sub")) * count
    local = index_ref[...] - start
    here = jnp.where((local >= 0) & (local < count), 1.0, 0.0)
    earlier = lax.broadcasted_iota(jnp.int32, (rows, rows), 0) < lax.broadcasted_iota(jnp.int32, (rows, rows), 1)
    rank = dot(jnp.broadcast_to(here, (8, rows)).astype(BF16), jnp.where(earlier, 1.0, 0.0).astype(BF16), NN)[0:1]
    slots = lax.broadcasted_iota(jnp.int32, (SLOTS, 1), 0).astype(F32)
    to_slot = jnp.where(slots == rank, here, 0.0).astype(BF16)
    pick = dot(to_slot, pick_rows(index_ref, count, start, BF16, 1.0), NN).astype(BF16)
    for k in range(blocks):
        copies[k + 1].wait()
        out_ref[:, k * block : (k + 1) * block] = dot(pick, centers_ref[k], NN).astype(BF16)


def pack_rows(batch_index, centers, part):
    rows = batch_index.shape[1]
    count, depth = centers.shape
    depth = depth // PARTS
    block = 512
    hbm = pl.BlockSpec(memory_space=pltpu.HBM)
    return pl.pallas_call(
        functools.partial(pack_body, part * depth),
        in_specs=[hbm, hbm],
        out_specs=pl.BlockSpec(memory_space=pltpu.VMEM),
        out_shape=jax.ShapeDtypeStruct((SLOTS, depth), BF16),
        scratch_shapes=[
            pltpu.VMEM((1, rows), jnp.int32),
            pltpu.VMEM((depth // block, count, block), BF16),
            pltpu.SemaphoreType.DMA((depth // block + 1,)),
        ],
        compiler_params=params(),
        cost_estimate=pl.CostEstimate(
            flops=2 * SLOTS * count * depth, bytes_accessed=2 * depth * (count + SLOTS), transcendentals=0
        ),
        name="pack_rows",
    )(batch_index, centers)


def select_body(count, index_ref, select_ref, squeeze_ref):
    rows, slots = select_ref.shape
    chips = lax.axis_size("center")
    center, sub = lax.axis_index("center"), lax.axis_index("sub")
    owner = owners(index_ref[...], count, chips)
    group = group_of(owner, chips)
    earlier = lax.broadcasted_iota(jnp.int32, (rows, rows), 0) < lax.broadcasted_iota(jnp.int32, (rows, rows), 1)

    def rank_among(key):
        column = jnp.concatenate([column_of(key, LANE)] * (rows // LANE), axis=1)
        return jnp.sum(jnp.where((column == key.astype(F32)) & earlier, 1.0, 0.0), axis=0, keepdims=True)

    away = (owner >> 1) ^ center
    orders = [far_first(side, chips.bit_length() - 1) for side in range(2)]

    def place(low, high):
        places = [
            sum(((away >> bit) & 1) << k for k, bit in enumerate(order[low:high])) + jnp.zeros_like(away)
            for order in orders
        ]
        return jnp.where((owner & 1) == 0, *places).astype(F32)

    lanes = lax.broadcasted_iota(jnp.int32, (1, LANE), 1).astype(F32)
    rank = rank_among(group)
    far = jnp.where((owner & 1) == sub, 0, slots // 2).astype(F32)
    slot = column_of(far + place(2, None) * float(GROUP_SLOTS) + rank, LANE)
    for k in range(slots // LANE):
        select_ref[:, k * LANE : (k + 1) * LANE] = jnp.where(slot == lanes + float(LANE * k), 1.0, 0.0).astype(BF16)
    before = column_of(place(0, 2) * float(SLOTS) + rank_among(owner), LANE)
    spots = lax.broadcasted_iota(jnp.int32, (GROUP_SLOTS, 1), 0).astype(F32)
    mine = group == group_of(center * 2 + sub, chips)
    to_spot = jnp.where((spots == rank) & mine, 1.0, 0.0).astype(BF16)
    squeeze_ref[...] = dot(to_spot, jnp.where(before == lanes, 1.0, 0.0).astype(BF16), NN).astype(BF16)


def select_packed(batch_index, count, chips):
    rows = batch_index.shape[1]
    half = -(-chips // 4 * GROUP_SLOTS // LANE) * LANE
    return pl.pallas_call(
        functools.partial(select_body, count),
        out_shape=[
            jax.ShapeDtypeStruct((rows, 2 * half), BF16),
            jax.ShapeDtypeStruct((GROUP_SLOTS, 4 * SLOTS), BF16),
        ],
        compiler_params=params(),
        name="select_packed",
    )(batch_index)


def squeeze_body(squeeze_ref, keep_ref, got_ref, out_ref):
    rows = keep_ref.shape[0]
    found = dot(squeeze_ref[:, :rows], keep_ref[...], NN) + dot(squeeze_ref[:, rows:], got_ref[...], NN)
    out_ref[...] = found.astype(BF16)


def squeeze_slots(squeeze, keep, got):
    depth = keep.shape[1]
    return pl.pallas_call(
        squeeze_body,
        out_shape=jax.ShapeDtypeStruct((squeeze.shape[0], depth), BF16),
        compiler_params=params(),
        cost_estimate=pl.CostEstimate(
            flops=40 * squeeze.size * depth, bytes_accessed=4 * squeeze.shape[1] * depth, transcendentals=0
        ),
        name="squeeze_slots",
    )(squeeze, keep, got)


def spread_body(
    first, classes, index_ref, eigvec_ref, weights_ref,
    left1_ref, left2_ref, spread_ref, all_ref,
):
    rank, points = eigvec_ref.shape
    count = weights_ref.shape[1]
    local = index_ref[...] - (lax.axis_index("center") * 2 + lax.axis_index("sub")) * count
    slots = lax.broadcasted_iota(jnp.int32, (count, points), 0)
    pick = jnp.where(slots == local, 1.0, 0.0).astype(BF16)
    vec = eigvec_ref[...]
    high = vec.astype(BF16)
    rest = vec - high.astype(F32)
    mid = rest.astype(BF16)
    low = (rest - mid.astype(F32)).astype(BF16)
    spread = dot(high, pick, NT) + dot(mid, pick, NT) + dot(low, pick, NT)
    spread_ref[...] = spread
    all_ref[:rank] = spread
    all_ref[rank : rank + classes] = weights_ref[...]
    all_ref[rank + classes :] = jnp.zeros((all_ref.shape[0] - rank - classes, count), F32)
    size = count // BLOCKS
    for begin, left_ref in ((0, left1_ref), (first, left2_ref)):
        for block in range(BLOCKS):
            high, low = two(all_ref[begin : begin + left_ref.shape[0], block * size : (block + 1) * size])
            for k, term in enumerate((high, high, low)):
                at = (3 * block + k) * size
                left_ref[:, at : at + size] = term


def spread_weights(nys_index, eigvec, weights, first, second):
    classes, count = weights.shape
    rank, points = eigvec.shape
    return pl.pallas_call(
        functools.partial(spread_body, first, classes),
        out_shape=[
            jax.ShapeDtypeStruct((first, 3 * count), BF16),
            jax.ShapeDtypeStruct((second, 3 * count), BF16),
            jax.ShapeDtypeStruct((rank, count), F32),
        ],
        scratch_shapes=[pltpu.VMEM((first + second, count), F32)],
        compiler_params=params(),
        cost_estimate=pl.CostEstimate(
            flops=6 * rank * points * count, bytes_accessed=8 * (first + second) * count, transcendentals=0
        ),
        name="spread_weights",
    )(nys_index, eigvec, weights)


def norms_body(centers_ref, norm_ref):
    wide = centers_ref[...].astype(F32)
    norm = jnp.sum(wide * wide, axis=1, keepdims=True)
    norm_ref[...] = jnp.broadcast_to(norm, norm_ref.shape)


def center_norms(centers):
    count, depth = centers.shape
    block = 256
    return pl.pallas_call(
        norms_body,
        grid=(count // block,),
        in_specs=[pl.BlockSpec((block, depth), lambda i: (i, 0))],
        out_specs=pl.BlockSpec((block, LANE), lambda i: (i, 0)),
        out_shape=jax.ShapeDtypeStruct((count, LANE), F32),
        compiler_params=params(),
        cost_estimate=pl.CostEstimate(flops=2 * count * depth, bytes_accessed=2 * count * depth, transcendentals=0),
        name="center_norms",
    )(centers)


def row_norms(batch_ref):
    rows = batch_ref.shape[0]
    batch = batch_ref[...].astype(F32)
    return jnp.broadcast_to(jnp.sum(batch * batch, axis=1, keepdims=True), (rows, LANE)).T[0:1]


def product(left_ref, right_ref, total_ref, keep_ref, send_ref):
    half = keep_ref.shape[1]
    size = left_ref.shape[1] // BLOCKS
    total = 0.0
    for block in range(BLOCKS):
        at = slice(block * size, (block + 1) * size)
        total = total + dot(left_ref[:, at], right_ref[at], NN)
    total_ref[...] = total
    lower = lax.axis_index("sub") == 0
    size = keep_ref.shape[0] // CHUNKS
    for chunk in range(CHUNKS):
        at = slice(chunk * size, (chunk + 1) * size)
        first, second = [
            total_ref[pl.ds(pl.multiple_of((chunk ^ turn) * size, 8), size), part * half : (part + 1) * half]
            for part, turn in enumerate(turns())
        ]
        keep_ref[at] = jnp.where(lower, first, second)
        send_ref[at] = jnp.where(lower, second, first)


def distance_body(mine_ref, other_ref, next_ref, select_ref, centers_ref, norm_ref, total_ref, found_ref, batch_ref):
    half, depth = mine_ref.shape
    wide = select_ref.shape[1] // 2
    near = select_ref[:, :half]
    far = select_ref[:, wide : wide + half]
    batch_ref[...] = (dot(near, mine_ref[...], NN) + dot(far, other_ref[...], NN)).astype(BF16)
    total_ref[...] = norm_ref[:, 0:1] + row_norms(batch_ref) - 2.0 * dot(centers_ref[:, :depth], batch_ref[...], NT)
    found_ref[...] = dot(near, next_ref[...], NN).astype(BF16)


def predict_body(
    found_ref, other_ref, select_ref, centers_ref, before_ref, left_ref,
    keep_ref, send_ref, right_ref, batch_ref, total_ref,
):
    count, depth = centers_ref.shape
    half, part = other_ref.shape
    wide = select_ref.shape[1] // 2
    found = found_ref[...].astype(F32) + dot(select_ref[:, wide : wide + half], other_ref[...], NN)
    batch_ref[...] = found.astype(BF16)
    norm = row_norms(batch_ref)
    size = count // BLOCKS
    for block in range(BLOCKS):
        at = slice(block * size, (block + 1) * size)
        cross = dot(centers_ref[at, depth - part :], batch_ref[...], NT)
        square = jnp.maximum(before_ref[at] + norm - 2.0 * cross, 0.0)
        high, low = two(jnp.exp(jnp.sqrt(square) * (-1.0 / math.sqrt(depth))))
        for k, term in enumerate((high, low, high)):
            to = (3 * block + k) * size
            right_ref[to : to + size] = term
    product(left_ref, right_ref, total_ref, keep_ref, send_ref)


def distances(mine, other, following, select, centers, norms):
    depth = mine.shape[1]
    rows = select.shape[0]
    count = centers.shape[0]
    vmem = pl.BlockSpec(memory_space=pltpu.VMEM)
    return pl.pallas_call(
        distance_body,
        in_specs=[vmem] * 6,
        out_specs=[vmem, vmem],
        out_shape=[jax.ShapeDtypeStruct((count, rows), F32), jax.ShapeDtypeStruct((rows, depth), BF16)],
        scratch_shapes=[pltpu.VMEM((rows, depth), BF16)],
        compiler_params=params(),
        cost_estimate=pl.CostEstimate(
            flops=2 * rows * count * depth, bytes_accessed=2 * depth * (count + rows), transcendentals=0
        ),
        name="distances",
    )(mine, other, following, select, centers, norms)


def predict(found, other, select, centers, before, left):
    depth = found.shape[1]
    rows = select.shape[0]
    half = rows // 2
    count = centers.shape[0]
    padded = left.shape[0]
    out = jax.ShapeDtypeStruct((padded, half), F32)
    vmem = pl.BlockSpec(memory_space=pltpu.VMEM)
    return pl.pallas_call(
        predict_body,
        in_specs=[vmem] * 6,
        out_specs=[vmem] * 3,
        out_shape=[out, out, jax.ShapeDtypeStruct((3 * count, rows), BF16)],
        scratch_shapes=[pltpu.VMEM((rows, depth), BF16), pltpu.VMEM((padded, rows), F32)],
        compiler_params=params(),
        cost_estimate=pl.CostEstimate(
            flops=2 * rows * count * (depth + 3 * padded),
            bytes_accessed=2 * depth * (count + rows) + 4 * padded * (count + rows),
            transcendentals=2 * rows * count,
        ),
        name="predict",
    )(found, other, select, centers, before, left)


def predict_more(left, right):
    padded, count = left.shape
    rows = right.shape[1]
    out = jax.ShapeDtypeStruct((padded, rows // 2), F32)
    return pl.pallas_call(
        lambda left, right, keep, send, total: product(left, right, total, keep, send),
        out_shape=[out, out],
        scratch_shapes=[pltpu.VMEM((padded, rows), F32)],
        compiler_params=params(),
        cost_estimate=pl.CostEstimate(
            flops=2 * rows * count * padded, bytes_accessed=2 * padded * (count + rows), transcendentals=0
        ),
        name="predict_more",
    )(left, right)


def gather_total(mine_ref, other_ref, total_ref):
    lower = lax.axis_index("sub") == 0
    half = mine_ref.shape[1]
    size = mine_ref.shape[0] // CHUNKS
    for part, turn in enumerate(turns()):
        for chunk in range(CHUNKS):
            at = slice(chunk * size, (chunk + 1) * size)
            same = lower if part == 0 else jnp.logical_not(lower)
            to = pl.multiple_of((chunk ^ turn) * size, 8)
            total_ref[pl.ds(to, size), part * half : (part + 1) * half] = jnp.where(
                same, mine_ref[at], other_ref[at]
            )


def write_rows(begin, skip, total_ref, targets_ref, weights_ref, right_ref, new_hbm, out_hbm, new_ref, sems):
    rows = new_ref.shape[0]
    blocks = sems.shape[0] - 1
    bounds = [8 * (rows // 8 * k // blocks) for k in range(blocks)] + [rows]
    right = right_ref[...]
    copies = [
        pltpu.make_async_copy(
            total_ref.at[pl.ds(skip, rows)], out_hbm.at[pl.ds(begin, rows)], sems.at[blocks]
        )
    ]
    copies[0].start()
    for k in range(blocks):
        low_end, high_end = bounds[k : k + 2]
        here = slice(begin + low_end, begin + high_end)
        high, low = two(total_ref[skip + low_end : skip + high_end] - targets_ref[here])
        new_ref[low_end:high_end] = weights_ref[here] + dot(jnp.concatenate([high, high, low], axis=1), right, NN)
        copy = pltpu.make_async_copy(
            new_ref.at[pl.ds(low_end, high_end - low_end)],
            new_hbm.at[pl.ds(begin + low_end, high_end - low_end)],
            sems.at[k],
        )
        copy.start()
        copies.append(copy)
    for copy in copies:
        copy.wait()


def update_body(
    mine_ref, other_ref, targets_ref, index_ref, eigval_ref, spread_ref, weights_ref,
    new_hbm, out_hbm, right_ref, total_ref, new_ref, sems,
):
    start = (lax.axis_index("center") * 2 + lax.axis_index("sub")) * spread_ref.shape[1]
    rank, count = spread_ref.shape
    gather_total(mine_ref, other_ref, total_ref)
    value = eigval_ref[...]
    lowest = jnp.min(value, axis=1, keepdims=True)
    scaled = (1.0 - lowest / value) / value
    mixed_high, mixed_low = two(total_ref[:rank].T * (0.25 * scaled))
    spread_high, spread_low = two(spread_ref[...])
    turned = dot(mixed_high, spread_high, NN) + (
        dot(mixed_high, spread_low, NN) + dot(mixed_low, spread_high, NN)
    )
    high, low = two(turned - pick_rows(index_ref, count, start, F32, 0.25))
    for k, term in enumerate((high, low, high)):
        right_ref[k * term.shape[0] : (k + 1) * term.shape[0]] = term
    write_rows(0, rank, total_ref, targets_ref, weights_ref, right_ref, new_hbm, out_hbm, new_ref, sems)


def update(mine, other, targets, batch_index, eigval, spread, weights):
    classes, count = weights.shape
    padded, half = mine.shape
    rows = 2 * half
    rank = spread.shape[0]
    here = padded - rank
    vmem = pl.BlockSpec(memory_space=pltpu.VMEM)
    hbm = pl.BlockSpec(memory_space=pl.ANY)
    return pl.pallas_call(
        update_body,
        in_specs=[vmem] * 7,
        out_specs=[hbm, hbm, vmem],
        out_shape=[
            jax.ShapeDtypeStruct((classes, count), F32),
            jax.ShapeDtypeStruct((classes, rows), F32),
            jax.ShapeDtypeStruct((3 * rows, count), BF16),
        ],
        scratch_shapes=[
            pltpu.VMEM((padded, rows), F32),
            pltpu.VMEM((here, count), F32),
            pltpu.SemaphoreType.DMA((4,)),
        ],
        compiler_params=params(),
        cost_estimate=pl.CostEstimate(
            flops=6 * rows * count * (here + rank), bytes_accessed=8 * here * (count + rows), transcendentals=0
        ),
        name="update",
    )(mine, other, targets, batch_index, eigval, spread, weights)


def update_more_body(
    begin, mine_ref, other_ref, targets_ref, weights_ref, right_ref, new_in, out_in,
    new_hbm, out_hbm, total_ref, new_ref, sems,
):
    gather_total(mine_ref, other_ref, total_ref)
    write_rows(begin, 0, total_ref, targets_ref, weights_ref, right_ref, new_hbm, out_hbm, new_ref, sems)


def update_more(mine, other, targets, weights, right, new, out, begin):
    classes, count = weights.shape
    padded, half = mine.shape
    rows = 2 * half
    here = classes - begin
    vmem = pl.BlockSpec(memory_space=pltpu.VMEM)
    hbm = pl.BlockSpec(memory_space=pl.ANY)
    return pl.pallas_call(
        functools.partial(update_more_body, begin),
        in_specs=[vmem] * 5 + [hbm] * 2,
        out_specs=[hbm, hbm],
        out_shape=[
            jax.ShapeDtypeStruct((classes, count), F32),
            jax.ShapeDtypeStruct((classes, rows), F32),
        ],
        input_output_aliases={5: 0, 6: 1},
        scratch_shapes=[
            pltpu.VMEM((padded, rows), F32),
            pltpu.VMEM((here, count), F32),
            pltpu.SemaphoreType.DMA((3,)),
        ],
        compiler_params=params(),
        cost_estimate=pl.CostEstimate(
            flops=int(1.0 * 6) * rows * count * here, bytes_accessed=8 * here * (count + rows), transcendentals=0
        ),
        name="update_more",
    )(mine, other, targets, weights, right, new, out)


def swap(x, chips, order=None, level=0):
    flip = [2 << order(sub, chips.bit_length() - 1)[level] if order else 1 for sub in range(2)]
    return lax.ppermute(x, AXES, [(i, i ^ flip[i & 1]) for i in range(2 * chips)])


def tie(x, tied):
    x, *tied = lax.optimization_barrier((x, *tied))
    return x, tied


def total_of(keep, send, chips, tied=()):
    keep = keep + swap(send, chips)
    for level in range(chips.bit_length() - 1):
        if level >= HALVINGS:
            keep = keep + swap(keep, chips, walk, level)
            continue
        half = keep.shape[0] // 2
        keep, send = keep[:half], keep[half:]
        if level == 1 and tied:
            send, tied = tie(send, tied)
        keep = keep + swap(send, chips, walk, level)
    for level in reversed(range(HALVINGS)):
        keep = jnp.concatenate([keep, swap(keep, chips, walk, level)])
    return [keep, swap(keep, chips), *tied]


def gathered(first, second, squeeze, chips, ready):
    for level in range(chips.bit_length() - 1):
        if level == 1:
            second, ready = tie(second, ready)
        got = swap(first, chips, far_first, level)
        late = swap(second, chips, far_first, level)
        if level == 1:
            got, _ = tie(got, [second])
            first = squeeze_slots(squeeze, first, got)
            second = squeeze_slots(squeeze, second, late)
        else:
            first = jnp.concatenate([first, got])
            second = jnp.concatenate([second, late])
    return [first, swap(first, chips), second, swap(second, chips), *ready]


def one_hot(slot, slots):
    return (slot[:, None] == jnp.arange(slots, dtype=jnp.int32)[None, :]).astype(BF16)


def select_summed(rows):
    row = jnp.arange(rows, dtype=jnp.int32)
    half = rows // 2
    size = half // CHUNKS
    turn = jnp.stack(turns())[row // half]
    chunk = (row % half // size) ^ turn
    far = jnp.where(row // half == lax.axis_index("sub"), 0, half)
    return one_hot(far + chunk * size + row % size, rows)


def step(packed, chips, centers, weights, targets, batch_index, nys_index, eigvec, eigval):
    rows = batch_index.shape[1]
    classes, count = weights.shape
    depth = eigvec.shape[0]
    unit = 8 * CHUNKS
    units = -(-(classes + depth) // unit)
    first = (units + 1) // 2 * unit
    second = first
    far = [pltpu.with_memory_space_constraint(x, pltpu.HBM) for x in (batch_index, centers)]
    ready = [center_norms(centers), *spread_weights(nys_index.reshape(1, -1), eigvec, weights, first, second)]
    if packed:
        select, squeeze = select_packed(batch_index, count, chips)
        ready.append(select)
        slots = [pack_rows(*far, part) for part in range(PARTS)]
        mine, other, next_mine, next_other, *ready = gathered(*slots, squeeze, chips, ready)
        norms, left1, left2, spread, select = ready
    else:
        ready.append(select_summed(rows))
        picked = [pick_batch(*far, part) for part in range(PARTS)]
        mine, other = total_of(*picked[0], chips)
        next_mine, next_other, norms, left1, left2, spread, select = total_of(*picked[1], chips, ready)
    before, found = distances(mine, other, next_mine, select, centers, norms)
    keep, send, right = predict(found, next_other, select, centers, before, left1)
    one = total_of(keep, send, chips)
    another = total_of(*predict_more(left2, right), chips)
    new, out, right = update(*one, targets, batch_index, eigval, spread, weights)
    return update_more(*another, targets, weights, right, new, out, first - depth)


def on_device(chips, centers, weights, targets, batch_index, nys_index, eigvec, eigval):
    batch_index = batch_index.reshape(1, -1)
    new, out = lax.cond(
        rows_fit(pltpu.with_memory_space_constraint(batch_index, pltpu.HBM), centers.shape[0]) > 0,
        functools.partial(step, True, chips),
        functools.partial(step, False, chips),
        centers,
        weights.T,
        targets.T,
        batch_index,
        nys_index,
        eigvec.T,
        eigval.reshape(1, -1),
    )
    return new.T, out.T


def solution(mesh):
    return jax.shard_map(
        functools.partial(on_device, mesh.shape["center"]),
        mesh=mesh,
        in_specs=(
            P(("parts", "center", "sub"), None),
            P(("parts", "center", "sub"), None),
            P("parts", None),
            P("parts"),
            P(("parts", "center", "sub")),
            P(("parts", "center", "sub"), None),
            P("parts"),
        ),
        out_specs=(P(("parts", "center", "sub"), None), P("parts", None)),
        check_vma=False,
    )
```
